32 devices in a mesh: dp: 4 (over y, core), fsdp: 8 (over z, x).
Axes of the slice: x: 2, y: 2, z: 4, core: 2. Of those that a mesh axis runs over, the one named last changes fastest.
Arguments:
- hidden_in: bfloat16 [16384, 768], P(('dp', 'fsdp')), may hold values from -6 to 6
- output_grad: bfloat16 [16384, 768], P(('dp', 'fsdp')), may hold values from -6 to 6
- encoder_states: bfloat16 [64, 512, 768], P(('dp', 'fsdp')), may hold values from -6 to 6
- language_ids: int32 [64], P(('dp', 'fsdp')), may hold values from 0 to 7
- source_index: int32 [64], P(('dp', 'fsdp')), may hold values from 0 to 1
- bucket_ids: int32 [256, 256], replicated, may hold values from 0 to 31, as said below
- language_table: bfloat16 [8, 768], P(None, ('dp', 'fsdp')), may hold values from -3 to 3
- bucket_table: bfloat16 [32, 12], replicated, may hold values from -4 to 4
- self_gain: bfloat16 [768], P(('dp', 'fsdp')), may hold values from 0.5 to 1.5
- self_query: bfloat16 [768, 768], P(('dp', 'fsdp')), may hold values from -0.02734375 to 0.02734375
- self_key: bfloat16 [768, 768], P(('dp', 'fsdp')), may hold values from -0.21875 to 0.21875
- self_value: bfloat16 [768, 768], P(('dp', 'fsdp')), may hold values from -0.21875 to 0.21875
- self_out: bfloat16 [768, 768], P(('dp', 'fsdp')), may hold values from -1.25 to 1.25
- cross_gain: bfloat16 [768], P(('dp', 'fsdp')), may hold values from 0.5 to 1.5
- cross_query: bfloat16 [768, 768], P(('dp', 'fsdp')), may hold values from -0.02734375 to 0.02734375
- cross_key: bfloat16 [768, 768], P(('dp', 'fsdp')), may hold values from -0.21875 to 0.21875
- cross_value: bfloat16 [768, 768], P(('dp', 'fsdp')), may hold values from -0.21875 to 0.21875
- cross_out: bfloat16 [768, 768], P(('dp', 'fsdp')), may hold values from -1.75 to 1.75
- feed_gain: bfloat16 [768], P(('dp', 'fsdp')), may hold values from 0.5 to 1.5
- inner_weight: bfloat16 [768, 3072], P(('dp', 'fsdp')), may hold values from -0.21875 to 0.21875
- outer_weight: bfloat16 [3072, 768], P(('dp', 'fsdp')), may hold values from -0.109375 to 0.109375
Outputs:
- hidden_out: bfloat16 [16384, 768], P(('dp', 'fsdp'))
- hidden_in_grad: float32 [16384, 768], P(('dp', 'fsdp'))
- encoder_grad: float32 [64, 512, 768], P(('dp', 'fsdp'))
- language_table_grad: float32 [8, 768], P(None, ('dp', 'fsdp'))
- bucket_table_grad: float32 [32, 12], replicated
- self_gain_grad: float32 [768], P(('dp', 'fsdp'))
- self_query_grad: float32 [768, 768], P(('dp', 'fsdp'))
- self_key_grad: float32 [768, 768], P(('dp', 'fsdp'))
- self_value_grad: float32 [768, 768], P(('dp', 'fsdp'))
- self_out_grad: float32 [768, 768], P(('dp', 'fsdp'))
- cross_gain_grad: float32 [768], P(('dp', 'fsdp'))
- cross_query_grad: float32 [768, 768], P(('dp', 'fsdp'))
- cross_key_grad: float32 [768, 768], P(('dp', 'fsdp'))
- cross_value_grad: float32 [768, 768], P(('dp', 'fsdp'))
- cross_out_grad: float32 [768, 768], P(('dp', 'fsdp'))
- feed_gain_grad: float32 [768], P(('dp', 'fsdp'))
- inner_weight_grad: float32 [768, 3072], P(('dp', 'fsdp'))
- outer_weight_grad: float32 [3072, 768], P(('dp', 'fsdp'))
The draws below stay inside these ranges and needn't reach their ends.
Inputs may be any that keep to these rules, and one draw needn't show every extreme that they name: bucket_ids[i, j] is the bucket of the distance between the positions of query i and key j, the positions rising by 1 or 2 from token to token; exact buckets below 16, logarithmic ones up to a distance of 128 and above; 0 where j > i.
All inputs are finite; a program needn't handle non-finite values.
Results may differ from the reference program's by a relative error of at most 0.019.
Values may be sent and summed in bfloat16 or wider, within the bound.
A program may use at most 192 MiB of HBM per device.

```python
import jax
import jax.numpy as jnp
import numpy as np
from jax import lax

D = 768
H = 12
HEAD = 64
FF = 3072
BUCKETS = 32
LANGS = 8
LEN = 256
ELEN = 512
SEQ_DEV = 2
ENC_DEV = 2
INNER = 768
SEQS = 64
TOKENS = 16384
ENC_SEQS = 64


def bucket_edges():
    exact_count = BUCKETS // 2
    steps_up = np.arange(1, exact_count)
    return np.ceil(exact_count * (128.0 / exact_count) ** (steps_up / exact_count)).astype(np.int32)


def draw_bucket_ids(key, part):
    key = jax.random.fold_in(key, 11)
    strides = jax.random.randint(key, (LEN,), 1, 3)
    places = jnp.cumsum(strides)
    distance = jnp.maximum(places[:, None] - places[None, :], 0)
    thresholds = jnp.asarray(bucket_edges())
    passed = jnp.sum((distance[:, :, None] >= thresholds[None, None, :]).astype(jnp.int32), axis=-1)
    return jnp.where(distance < BUCKETS // 2, distance, BUCKETS // 2 + passed).astype(jnp.int32)


def place_ends(drawn, key, low, high):
    longest = drawn.shape.index(max(drawn.shape))
    spots = []
    for shift in (0, 1):
        where = [jax.random.randint(jax.random.fold_in(key, axis), (), 0, length) for axis, length in enumerate(drawn.shape)]
        where[longest] = (where[longest] + shift) % drawn.shape[longest]
        spots.append(tuple(where))
    return drawn.at[spots[0]].set(low).at[spots[1]].set(high)


def strengthened(drawn, own_key, source, target, parts, factor):
    def block_of(dim):
        return (jnp.arange(drawn.shape[dim]) // (drawn.shape[dim] // parts)).reshape((-1,) + (1,) * (drawn.ndim - 1 - dim))

    one_side = jax.random.permutation(own_key, parts)[block_of(target)]
    other_side = (block_of(target) + parts // 2) % parts
    return jnp.where((block_of(source) == one_side) | (block_of(source) == other_side), factor * drawn, drawn)


def block_scale(rng, dims, pieces, smallest, top_value):
    def one(axis_at, parts):
        heights = jax.random.uniform(jax.random.fold_in(jax.random.fold_in(rng, 6), axis_at), (parts,), jnp.float32, smallest / len(pieces), top_value / len(pieces))
        return jnp.repeat(jnp.exp(heights), dims[axis_at] // parts).reshape((-1,) + (1,) * (len(dims) - axis_at - 1))

    level = one(*pieces[0])
    for cut in pieces[1:]:
        level = level * one(*cut)
    return level


def gaussian(key, shape, width, reach, split=(), kind=jnp.bfloat16):
    drawn = width * jax.random.normal(key, shape, jnp.float32)
    if split:
        drawn = drawn * block_scale(key, shape, split, -0.22, 0.18)
    return jnp.clip(drawn, -reach, reach).astype(kind)


def heavy_noise(stream_key, shape, spread, reach, pieces, heavy, held_as=jnp.bfloat16):
    values = spread * jax.random.normal(stream_key, shape, jnp.float32)
    if pieces:
        values = values * block_scale(stream_key, shape, pieces, -0.22, 0.18)
    return jnp.clip(strengthened(values, jax.random.fold_in(stream_key, 3), *heavy), -reach, reach).astype(held_as)


def setup_inputs(seed: int = 0) -> dict:
    arg_keys = jax.random.split(jax.random.key(seed), 22)
    hidden_in = gaussian(arg_keys[0], (TOKENS, D), 1.0, 6.0, ((0, 32),))
    output_grad = heavy_noise(arg_keys[1], (TOKENS, D), 1.0, 6.0, ((0, 32),), (0, 1, 32, 2.75))
    encoder_states = gaussian(arg_keys[2], (ENC_SEQS, ELEN, D), 1.0, 6.0, ((0, 32),))
    language_ids = place_ends(jax.random.randint(arg_keys[3], (SEQS,), 0, LANGS), jax.random.fold_in(arg_keys[3], 1), 0, LANGS - 1).astype(jnp.int32)
    source_index = place_ends(jax.random.randint(arg_keys[4], (SEQS,), 0, ENC_DEV), jax.random.fold_in(arg_keys[4], 1), 0, ENC_DEV - 1).astype(jnp.int32)
    bucket_ids = draw_bucket_ids(jax.random.fold_in(arg_keys[21], 71), 0)
    language_table = gaussian(arg_keys[6], (LANGS, D), 0.5, 3.0, ((1, 32),))
    bucket_table = gaussian(arg_keys[7], (BUCKETS, H), 1.0, 4.0)
    self_gain = jnp.clip(1.0 + 0.1 * jax.random.normal(arg_keys[8], (D,), jnp.float32), 0.5, 1.5).astype(jnp.bfloat16)
    self_query = gaussian(arg_keys[9], (D, INNER), (D * HEAD) ** -0.5, 0.02734375, ((0, 32),))
    self_key = gaussian(arg_keys[10], (D, INNER), D ** -0.5, 0.21875, ((0, 32),))
    self_value = gaussian(arg_keys[11], (D, INNER), D ** -0.5, 0.21875, ((0, 32),))
    self_out = gaussian(arg_keys[12], (INNER, D), (INNER // 32) ** -0.5, 1.25, ((0, 32),))
    cross_gain = jnp.clip(1.0 + 0.1 * jax.random.normal(arg_keys[13], (D,), jnp.float32), 0.5, 1.5).astype(jnp.bfloat16)
    cross_query = gaussian(arg_keys[14], (D, INNER), (D * HEAD) ** -0.5, 0.02734375, ((0, 32),))
    cross_key = gaussian(arg_keys[15], (D, INNER), D ** -0.5, 0.21875, ((0, 32),))
    cross_value = gaussian(arg_keys[16], (D, INNER), D ** -0.5, 0.21875, ((0, 32),))
    cross_out = gaussian(arg_keys[17], (INNER, D), (INNER // 64) ** -0.5, 1.75, ((0, 32),))
    feed_gain = jnp.clip(1.0 + 0.1 * jax.random.normal(arg_keys[18], (D,), jnp.float32), 0.5, 1.5).astype(jnp.bfloat16)
    inner_weight = gaussian(arg_keys[19], (D, FF), D ** -0.5, 0.21875, ((0, 32),))
    outer_weight = gaussian(arg_keys[20], (FF, D), FF ** -0.5, 0.109375, ((0, 32),))
    return {"hidden_in": hidden_in, "output_grad": output_grad, "encoder_states": encoder_states, "language_ids": language_ids, "source_index": source_index, "bucket_ids": bucket_ids, "language_table": language_table, "bucket_table": bucket_table, "self_gain": self_gain, "self_query": self_query, "self_key": self_key, "self_value": self_value, "self_out": self_out, "cross_gain": cross_gain, "cross_query": cross_query, "cross_key": cross_key, "cross_value": cross_value, "cross_out": cross_out, "feed_gain": feed_gain, "inner_weight": inner_weight, "outer_weight": outer_weight}


EPSILON = 1e-06
PRECISE = lax.Precision.HIGHEST
NEGATIVE = -1e+30

@jax.custom_vjp
def low(v):
    return lax.optimization_barrier(v.astype(jnp.bfloat16)).astype(jnp.float32)

@jax.custom_vjp
def low_back(v):
    return v

def low_keep(v):
    return (low(v), None)

def low_pass(kept, grad):
    return (grad,)

def back_keep(v):
    return (v, None)

def back_low(kept, grad):
    return (low(grad),)
low.defvjp(low_keep, low_pass)
low_back.defvjp(back_keep, back_low)

def norm_scale(hidden, gain):
    return hidden * lax.rsqrt(lax.optimization_barrier(jnp.mean(hidden * hidden, axis=-1, keepdims=True)) + EPSILON) * gain

def project(left, right):
    return jnp.dot(left, right, precision=PRECISE)

def split_heads(array):
    return array.reshape(array.shape[:-1] + (H, HEAD))

def attention(queries, key_rows, value_rows, offset, allowed):
    full_shape = queries.shape
    scores = jnp.einsum('sqhe,skhe->shqk', split_heads(queries), split_heads(key_rows), precision=PRECISE) + offset
    scores = low_back(jnp.where(allowed, scores, NEGATIVE))
    weights = low(jax.nn.softmax(scores, axis=-1))
    context = jnp.einsum('shqk,skhe->sqhe', weights, split_heads(value_rows), precision=PRECISE)
    return low_back(low(context.reshape(full_shape)))

def group_layer(weights, hidden, encoder, language_ids, source_index, bucket_ids):
    language_table, bucket_table, self_gain, self_query, self_key, self_value, self_out, cross_gain, cross_query, cross_key, cross_value, cross_out, feed_gain, inner_weight, outer_weight = weights
    start_state = hidden + language_table[language_ids][:, None, :]
    first_norm = low(norm_scale(start_state, self_gain))
    self_queries = low_back(low(project(first_norm, self_query)))
    self_keys = low_back(low(project(first_norm, self_key)))
    self_values = low_back(low(project(first_norm, self_value)))
    positions = jnp.arange(LEN)
    causal = positions[:, None] >= positions[None, :]
    position_bias = jnp.transpose(bucket_table[bucket_ids], (2, 0, 1))
    self_context = attention(self_queries, self_keys, self_values, position_bias, causal)
    mid_state = start_state + low_back(project(self_context, self_out))
    second_norm = low(norm_scale(mid_state, cross_gain))
    cross_queries = low_back(low(project(second_norm, cross_query)))
    source_keys = low_back(low(project(encoder, cross_key)))
    source_values = low_back(low(project(encoder, cross_value)))
    picked_keys = source_keys[source_index]
    picked_values = source_values[source_index]
    cross_context = attention(cross_queries, picked_keys, picked_values, 0.0, True)
    late_state = mid_state + low_back(project(cross_context, cross_out))
    third_norm = low(norm_scale(late_state, feed_gain))
    expanded = low_back(project(third_norm, inner_weight))
    activated = low(jax.nn.gelu(expanded, approximate=True))
    return late_state + low_back(project(activated, outer_weight))

def reference(hidden_in, output_grad, encoder_states, language_ids, source_index, bucket_ids, language_table, bucket_table, self_gain, self_query, self_key, self_value, self_out, cross_gain, cross_query, cross_key, cross_value, cross_out, feed_gain, inner_weight, outer_weight):
    weights = tuple((argument.astype(jnp.float32) for argument in (language_table, bucket_table, self_gain, self_query, self_key, self_value, self_out, cross_gain, cross_query, cross_key, cross_value, cross_out, feed_gain, inner_weight, outer_weight)))
    groups = SEQS // SEQ_DEV
    hidden = hidden_in.astype(jnp.float32).reshape(groups, SEQ_DEV, LEN, D)
    encoder = encoder_states.astype(jnp.float32).reshape(groups, ENC_DEV, ELEN, D)
    languages = language_ids.reshape(groups, SEQ_DEV)
    sources = source_index.reshape(groups, SEQ_DEV)
    layer = jax.checkpoint(group_layer)

    def whole(hidden_all, encoder_all, weight_all):

        def group_step(block_items):
            return layer(weight_all, block_items[0], block_items[1], block_items[2], block_items[3], bucket_ids)
        return lax.map(group_step, (hidden_all, encoder_all, languages, sources))
    result, backward = jax.vjp(whole, hidden, encoder, weights)
    hidden_grad, encoder_grad, weight_grads = backward(output_grad.astype(jnp.float32).reshape(groups, SEQ_DEV, LEN, D))
    return (result.reshape(TOKENS, D).astype(jnp.bfloat16), hidden_grad.reshape(TOKENS, D), encoder_grad.reshape(ENC_SEQS, ELEN, D), weight_grads[0], weight_grads[1], weight_grads[2], weight_grads[3], weight_grads[4], weight_grads[5], weight_grads[6], weight_grads[7], weight_grads[8], weight_grads[9], weight_grads[10], weight_grads[11], weight_grads[12], weight_grads[13], weight_grads[14])
```

```python
import functools

import jax
import jax.numpy as jnp
from jax import lax
from jax.experimental import pallas as pl
from jax.experimental.pallas import tpu as pltpu
from jax.sharding import PartitionSpec as P

H = 12
HEAD = 64
SEQ_BLOCK = 2


EPSILON = 1e-06
PRECISE = lax.Precision.HIGHEST
NEGATIVE = -1e30


def to_low(value):
    return value.astype(jnp.bfloat16)


def norm_scale(hidden, gain):
    return hidden * lax.rsqrt(jnp.mean(hidden * hidden, axis=-1, keepdims=True) + EPSILON) * gain


def matmul(left, right):
    return jnp.dot(left, right, preferred_element_type=jnp.float32)


def left_product(left, right):
    return lax.dot_general(
        left, right, (((0,), (0,)), ((), ())), preferred_element_type=jnp.float32
    )


def right_product(left, right):
    return lax.dot_general(
        left, right, (((1,), (1,)), ((), ())), preferred_element_type=jnp.float32
    )


def split_heads(array):
    return array.reshape(array.shape[:-1] + (H, HEAD))


def score_block(queries, key_rows, offset):
    scores = jnp.einsum(
        "sqhe,skhe->shqk",
        split_heads(queries),
        split_heads(key_rows),
        preferred_element_type=jnp.float32,
    )
    return scores + offset


def attend_forward(queries, key_rows, value_rows, offset):
    scores = score_block(queries, key_rows, offset)
    top_score = jnp.max(scores, axis=-1, keepdims=True)
    log_total = top_score + jnp.log(jnp.sum(jnp.exp(scores - top_score), axis=-1, keepdims=True))
    weights = to_low(jnp.exp(scores - log_total))
    context = jnp.einsum(
        "shqk,skhe->sqhe", weights, split_heads(value_rows), preferred_element_type=jnp.float32
    )
    return (to_low(context).reshape(queries.shape), log_total)


def attend_backward(queries, key_rows, value_rows, offset, log_total, context_grad, with_bias):
    scores = score_block(queries, key_rows, offset)
    probs = jnp.exp(scores - log_total)
    weights = to_low(probs)
    grad_heads = split_heads(context_grad)
    value_grad = jnp.einsum(
        "shqk,sqhe->skhe", weights, grad_heads, preferred_element_type=jnp.float32
    )
    prob_grad = jnp.einsum(
        "sqhe,skhe->shqk", grad_heads, split_heads(value_rows), preferred_element_type=jnp.float32
    )
    score_grad = to_low(probs * (prob_grad - jnp.sum(probs * prob_grad, axis=-1, keepdims=True)))
    query_grad = jnp.einsum(
        "shqk,skhe->sqhe", score_grad, split_heads(key_rows), preferred_element_type=jnp.float32
    )
    key_grad = jnp.einsum(
        "shqk,sqhe->skhe", score_grad, split_heads(queries), preferred_element_type=jnp.float32
    )
    grads = (
        query_grad.reshape(queries.shape),
        key_grad.reshape(key_rows.shape),
        value_grad.reshape(value_rows.shape),
    )
    if with_bias:
        return grads + (jnp.sum(score_grad.astype(jnp.float32), axis=0),)
    return grads


MESH = pl.DeviceIdType.MESH
ALL = slice(None)


class Place:
    def __init__(self, sizes):
        self.ny, self.nz = sizes
        self.dp = lax.axis_index("dp")
        self.fs = lax.axis_index("fsdp")
        self.c, self.y = lax.rem(self.dp, 2), lax.div(self.dp, 2)
        self.x, self.z = lax.rem(self.fs, 2), lax.div(self.fs, 2)

    def size(self, dim):
        return {"c": 2, "x": 2, "y": self.ny, "z": self.nz}[dim]

    def at(self, dim):
        return {"c": self.c, "x": self.x, "y": self.y, "z": self.z}[dim]

    def device(self, dim, index):
        if dim == "c":
            return (self.y * 2 + index, self.fs)
        if dim == "y":
            return (index * 2 + self.c, self.fs)
        if dim == "x":
            return (self.dp, self.z * 2 + index)
        return (self.dp, index * 2 + self.x)


def neighbour_barrier(place, far=False):
    barrier = pltpu.get_barrier_semaphore()
    links = []
    for dim in "cxyz":
        here, size = place.at(dim), place.size(dim)
        reach = 1
        while reach < size and (reach == 1 or far):
            if size == 2:
                links.append((dim, 1 - here, None))
            elif reach == 1:
                for step in (1, -1):
                    links.append((dim, here + step, (here + step >= 0) & (here + step < size)))
            else:
                links.append((dim, here + reach - 2 * reach * lax.rem(lax.div(here, reach), 2), None))
            reach *= 2

    def signal(dim, there):
        pl.semaphore_signal(barrier, inc=1, device_id=place.device(dim, there), device_id_type=MESH)

    for dim, there, condition in links:
        if condition is None:
            signal(dim, there)
        else:
            pl.when(condition)(lambda dim=dim, there=there: signal(dim, there))
    peers = sum(1 if condition is None else condition.astype(jnp.int32) for _, _, condition in links)
    pl.semaphore_wait(barrier, peers)


PATHS = ("zxy", "zyx", "xzy", "yzx")


class Link:
    def __init__(self, copy, sends=None, receives=None):
        self.copy, self.sends, self.receives = copy, sends, receives

    @staticmethod
    def when(condition, run):
        if condition is None:
            run()
        else:
            pl.when(condition)(run)

    def start(self):
        self.when(self.sends, lambda: self.copy.start())

    def wait_send(self):
        self.when(self.sends, lambda: self.copy.wait_send())

    def wait_recv(self):
        self.when(self.receives, lambda: self.copy.wait_recv())


def pick(held, place, **fixed):
    return tuple(fixed.get(dim, ALL if dim in held else place.at(dim)) for dim in "yczx")


def gather_steps(place, blocks, path, sems):
    steps, slot, held = [], 0, ""
    for dim in path + "c":
        here, size = place.at(dim), place.size(dim)
        if size == 2:
            there = 1 - here
            index = pick(held, place)
            copy = pltpu.make_async_remote_copy(
                blocks(index), blocks(index), sems[0].at[slot], sems[1].at[slot],
                device_id=place.device(dim, there), device_id_type=MESH,
            )
            steps.append([Link(copy)])
            slot += 1
        else:
            for hop in range(1, size):
                links = []
                for way in (1, -1):
                    origin = here - way * (hop - 1)
                    there = here + way
                    source = here - way * hop
                    index = pick(held, place, **{dim: jnp.clip(origin, 0, size - 1)})
                    copy = pltpu.make_async_remote_copy(
                        blocks(index), blocks(index), sems[0].at[slot], sems[1].at[slot],
                        device_id=place.device(dim, jnp.clip(there, 0, size - 1)), device_id_type=MESH,
                    )
                    sends = (origin >= 0) & (origin < size) & (there >= 0) & (there < size)
                    links.append(Link(copy, sends, (source >= 0) & (source < size)))
                    slot += 1
                steps.append(links)
        held += dim
    return steps


def slot_count(sizes):
    ny, nz = sizes
    return 2 + (1 if ny == 2 else 2 * (ny - 1)) + (1 if nz == 2 else 2 * (nz - 1))


def run_steps(plans, lag):
    rounds = max(lag[i] + len(plan) for i, plan in enumerate(plans)) + 1
    for now in range(rounds):
        for offset, plan in zip(lag, plans):
            at = now - offset
            if 1 <= at <= len(plan):
                for link in plan[at - 1]:
                    link.wait_recv()
            if 0 <= at < len(plan):
                for link in plan[at]:
                    link.start()
    for plan in plans:
        for links in plan:
            for link in links:
                link.wait_send()


def gather_kernel(sizes, *refs):
    shards, wholes = refs[:11], refs[11:22]
    own_sem, send_sem, recv_sem = refs[22:]
    place = Place(sizes)
    own = (place.y, place.c, place.z, place.x)
    owns = [
        pltpu.make_async_copy(shard, whole.at[own], own_sem.at[i])
        for i, (shard, whole) in enumerate(zip(shards, wholes))
    ]
    for copy in owns:
        copy.start()
    neighbour_barrier(place)
    views = [lambda index, ref=ref: ref.at[index] for ref in wholes[:9]]
    width = wholes[8].shape[-1]
    for q in range(4):
        views.append(
            lambda index, q=q: wholes[9].at[index + (ALL, pl.ds(q * width, width))]
        )
    for q in range(4):
        views.append(lambda index, q=q: wholes[10].at[index + (q,)])
    plans, lag = [], []
    for i, view in enumerate(views):
        path = PATHS[0] if i == 0 else PATHS[(i - 1) % 4]
        plans.append(gather_steps(place, view, path, (send_sem.at[i], recv_sem.at[i])))
        lag.append(0 if i == 0 else 3 * ((i - 1) // 4))
    for copy in owns:
        copy.wait()
    run_steps(plans, lag)


def gather_weights(sizes, table, gains, squares, inner, outer):
    ny, nz = sizes
    grid = (ny, 2, nz, 2)
    part, width = squares[0].shape
    small = jnp.zeros((16, 128), table.dtype)
    small = small.at[: table.shape[0], :part].set(table)
    for i, gain in enumerate(gains):
        small = small.at[table.shape[0] + i, :part].set(gain)
    shards = (small,) + tuple(squares) + (inner, outer.reshape(4, part, width))
    anywhere = pl.BlockSpec(memory_space=pl.ANY)
    slots = slot_count(sizes)
    wholes = pl.pallas_call(
        functools.partial(gather_kernel, sizes),
        out_shape=[jax.ShapeDtypeStruct(grid + s.shape, s.dtype) for s in shards],
        in_specs=[anywhere] * 11,
        out_specs=[anywhere] * 11,
        scratch_shapes=[
            pltpu.SemaphoreType.DMA((11,)),
            pltpu.SemaphoreType.DMA((17, slots)),
            pltpu.SemaphoreType.DMA((17, slots)),
        ],
        compiler_params=pltpu.CompilerParams(collective_id=0, has_side_effects=True),
    )(*shards)
    count = ny * nz * 4
    tiny = wholes[0].reshape(count, 16, 128)[:, :, :part].transpose(1, 0, 2).reshape(16, count * part)
    rows = table.shape[0]
    return (
        (tiny[rows], tiny[rows + 1], tiny[rows + 2], tiny[:rows])
        + tuple(w.reshape(count * part, width) for w in wholes[1:9])
        + (wholes[9].reshape(count * part, 4 * width), wholes[10].reshape(4 * count * part, width))
    )


class Reduce:
    def __init__(self, place, path, source, total, core_in, boxes, out, sems):
        self.place, self.path, self.source, self.total = place, path, source, total
        self.core_in, self.boxes, self.out, self.sems = core_in, boxes, out, sems
        self.slot = 0
        self.sent = []

    def copy(self, source, target, dim, there):
        slot = self.slot
        self.slot += 1
        return pltpu.make_async_remote_copy(
            source, target, self.sems[0].at[slot], self.sems[1].at[slot],
            device_id=self.place.device(dim, there), device_id_type=MESH,
        )

    def index(self, fixed):
        return tuple(fixed.get(dim, ALL) for dim in "yzx")

    def add(self, target, box):
        shape = box.shape[:-2]
        count = 1
        for size in shape:
            count *= size
        free = [i for i, entry in enumerate(target) if entry is ALL]

        def body(n, _):
            spots, rest = [], n
            for size in reversed(shape):
                spots.append(lax.rem(rest, size))
                rest = lax.div(rest, size)
            spots = spots[::-1]
            full = list(target)
            for place_at, spot in zip(free, spots):
                full[place_at] = spot
            mine = self.total[tuple(full)].astype(jnp.float32)
            got = box[tuple(spots)].astype(jnp.float32)
            self.total[tuple(full)] = (mine + got).astype(jnp.bfloat16)
            return 0

        if count == 1:
            body(0, 0)
        else:
            lax.fori_loop(0, count, body, 0)

    def steps(self):
        place, listing = self.place, []
        own = pltpu.make_async_copy(self.source(place.c), self.total, self.sems[2])
        core = self.copy(self.source(1 - place.c), self.core_in, "c", 1 - place.c)

        def start():
            own.start()
            core.start()

        def finish():
            own.wait()
            core.wait_recv()
            self.add((ALL, ALL, ALL), self.core_in)

        self.sent.append(Link(core))
        listing.append((start, finish))
        fixed, box = {}, 0
        for dim in self.path:
            here, size = place.at(dim), place.size(dim)
            if size == 2:
                target = self.index({**fixed, dim: 1 - here})
                link = Link(self.copy(self.total.at[target], self.boxes[box], dim, 1 - here))
                self.sent.append(link)
                listing.append(self.pair([link], [(self.index({**fixed, dim: here}), box, None)]))
                box += 1
            else:
                for hop in range(size - 1, 0, -1):
                    links, adds = [], []
                    for way in (1, -1):
                        there = here - way
                        goal = here - way * hop
                        sends = (goal >= 0) & (goal < size)
                        source = here + way
                        got = source - way * hop
                        receives = (source >= 0) & (source < size) & (got >= 0) & (got < size)
                        target = self.index({**fixed, dim: jnp.clip(goal, 0, size - 1)})
                        copy = self.copy(
                            self.total.at[target], self.boxes[box], dim, jnp.clip(there, 0, size - 1)
                        )
                        link = Link(copy, sends, receives)
                        self.sent.append(link)
                        links.append(link)
                        adds.append((self.index({**fixed, dim: jnp.clip(got, 0, size - 1)}), box, receives))
                        box += 1
                    listing.append(self.pair(links, adds))
            fixed = {**fixed, dim: here}
        return listing

    def pair(self, links, adds):
        def start():
            for link in links:
                link.start()

        def finish():
            for link in links:
                link.wait_recv()
            for target, box, condition in adds:
                Link.when(condition, functools.partial(self.add, target, self.boxes[box]))

        return start, finish

    def close(self):
        own = (self.place.y, self.place.z, self.place.x)
        self.out(self.total[own].astype(jnp.float32))
        for link in self.sent:
            link.wait_send()


def box_shapes(sizes, path):
    ny, nz = sizes
    size = {"y": ny, "z": nz, "x": 2}
    left, shapes = "yzx", []
    for dim in path:
        left = left.replace(dim, "")
        lead = tuple(size[d] for d in left)
        shapes += [lead] * (1 if size[dim] == 2 else 2 * (size[dim] - 1))
    return shapes


BACK_PATHS = tuple(path[::-1] for path in PATHS)


def reduce_kernel(sizes, box_counts, *refs):
    sources, small_in = refs[:10], refs[10]
    outs, small_out = refs[11:21], refs[21]
    totals, core_boxes = refs[22], refs[23]
    at = 24
    boxes = []
    for count in box_counts:
        boxes.append(refs[at : at + count])
        at += count
    small_box, own_sem, send_sem, recv_sem, small_send, small_recv = refs[at:]
    place = Place(sizes)
    neighbour_barrier(place, far=True)
    width = outs[0].shape[-1]

    def square(ref):
        return lambda core: ref.at[:, core]

    def inner(q):
        return lambda core: sources[8].at[:, core, :, :, :, pl.ds(q * width, width)]

    def outer(q):
        return lambda core: sources[9].at[:, core, :, :, q]

    views = [inner(q) for q in range(4)] + [outer(q) for q in range(4)]
    views += [square(sources[i]) for i in (4, 5, 6, 7, 0, 1, 2, 3)]

    def store_square(i):
        def run(value):
            outs[i][...] = value

        return run

    def store_inner(q):
        def run(value):
            outs[8][:, q * width : (q + 1) * width] = value

        return run

    def store_outer(q):
        def run(value):
            outs[9][q] = value

        return run

    stores = [store_inner(q) for q in range(4)] + [store_outer(q) for q in range(4)]
    stores += [store_square(i) for i in (4, 5, 6, 7, 0, 1, 2, 3)]
    plans, lag = [], []
    reduces = []
    for m in range(16):
        group, kind = m // 4, m % 4
        reduce = Reduce(
            place, BACK_PATHS[kind], views[m], totals.at[m], core_boxes.at[m],
            [box.at[group] for box in boxes[kind]], stores[m],
            (send_sem.at[m], recv_sem.at[m], own_sem.at[m]),
        )
        reduces.append(reduce)
        plans.append(reduce.steps())
        lag.append(3 * group)
    small_out[...] = small_in[...]
    small = []
    moves = [("c", 1 - place.c), ("x", 1 - place.x), ("y", None), ("z", None)]
    for dim, there in moves:
        size, here, reach = place.size(dim), place.at(dim), 1
        while reach < size:
            partner = here + reach - 2 * reach * lax.rem(lax.div(here, reach), 2)
            small.append((dim, partner))
            reach *= 2
    rounds = max(max(lag[i] + len(plan) for i, plan in enumerate(plans)) + 1, len(small) + 1)
    copies = []
    for now in range(rounds):
        for offset, plan in zip(lag, plans):
            step = now - offset
            if 1 <= step <= len(plan):
                plan[step - 1][1]()
            if 0 <= step < len(plan):
                plan[step][0]()
        if 1 <= now <= len(small):
            copies[-1].wait()
            small_out[...] += small_box[now - 1]
        if now < len(small):
            dim, partner = small[now]
            copies.append(
                pltpu.make_async_remote_copy(
                    small_out, small_box.at[now], small_send.at[now], small_recv.at[now],
                    device_id=place.device(dim, partner), device_id_type=MESH,
                )
            )
            copies[-1].start()
    for reduce in reduces:
        reduce.close()


def reduce_grads(sizes, language, bucket, gains, squares, inner, outer):
    ny, nz = sizes
    grid = (ny, 2, nz, 2)
    count = ny * nz * 4
    width = squares[0].shape[1]
    part = squares[0].shape[0] // count
    langs = language.shape[0]
    flat = jnp.zeros((width,), jnp.float32).at[: bucket.size].set(bucket.reshape(-1))
    small = jnp.concatenate(
        [language] + [g.reshape(1, width) for g in gains] + [flat[None], jnp.zeros((4, width), jnp.float32)], axis=0
    )
    sources = [to_low(s).reshape(grid + (part, width)) for s in squares]
    sources += [
        to_low(inner).reshape(grid + (part, 4 * width)),
        to_low(outer).reshape(grid + (4, part, width)),
    ]
    anywhere = pl.BlockSpec(memory_space=pl.ANY)
    vmem = pl.BlockSpec(memory_space=pltpu.VMEM)
    shapes = [(part, width)] * 8 + [(part, 4 * width), (4, part, width), small.shape]
    lead = [box_shapes(sizes, path) for path in BACK_PATHS]
    slots = slot_count(sizes)
    hops = (ny * nz * 4).bit_length() - 1
    outs = pl.pallas_call(
        functools.partial(reduce_kernel, sizes, tuple(len(s) for s in lead)),
        out_shape=[jax.ShapeDtypeStruct(s, jnp.float32) for s in shapes],
        in_specs=[anywhere] * 10 + [vmem],
        out_specs=[vmem] * 11,
        scratch_shapes=[
            pltpu.VMEM((16, ny, nz, 2, part, width), jnp.bfloat16),
            pltpu.VMEM((16, ny, nz, 2, part, width), jnp.bfloat16),
        ]
        + [pltpu.VMEM((4,) + s + (part, width), jnp.bfloat16) for one in lead for s in one]
        + [
            pltpu.VMEM((hops,) + small.shape, jnp.float32),
            pltpu.SemaphoreType.DMA((16,)),
            pltpu.SemaphoreType.DMA((16, slots)),
            pltpu.SemaphoreType.DMA((16, slots)),
            pltpu.SemaphoreType.DMA((hops,)),
            pltpu.SemaphoreType.DMA((hops,)),
        ],
        compiler_params=pltpu.CompilerParams(
            collective_id=1, has_side_effects=True, vmem_limit_bytes=60 * 1024 * 1024
        ),
    )(*sources, small)
    start = (lax.axis_index("dp") * nz * 2 + lax.axis_index("fsdp")) * part
    total = outs[10]
    mine = lax.dynamic_slice(total, (0, start), (langs + 3, part))
    return (
        mine[:langs],
        total[langs + 3, : bucket.size].reshape(bucket.shape),
        mine[langs], mine[langs + 1], mine[langs + 2],
        outs[:8], outs[8], outs[9].reshape(4 * part, width),
    )


def local(
    sizes,
    hidden_in,
    output_grad,
    encoder_states,
    language_ids,
    source_index,
    bucket_ids,
    language_table,
    bucket_table,
    self_gain,
    self_query,
    self_key,
    self_value,
    self_out,
    cross_gain,
    cross_query,
    cross_key,
    cross_value,
    cross_out,
    feed_gain,
    inner_weight,
    outer_weight,
):
    seq_count = language_ids.shape[0]
    length = bucket_ids.shape[0]
    tokens = seq_count * length
    enc_count = encoder_states.shape[0]
    enc_length = encoder_states.shape[1]
    width = hidden_in.shape[1]
    blocks = seq_count // SEQ_BLOCK
    (
        gain_one, gain_two, gain_three, table_whole, query_whole, key_whole, value_whole, out_whole,
        cquery_whole, ckey_whole, cvalue_whole, cout_whole, inner_whole, outer_whole,
    ) = gather_weights(
        sizes, language_table, (self_gain, cross_gain, feed_gain),
        (self_query, self_key, self_value, self_out, cross_query, cross_key, cross_value, cross_out),
        inner_weight, outer_weight,
    )

    def to_blocks(array, rows):
        return array.reshape(blocks, SEQ_BLOCK, rows, array.shape[-1])

    language_hot = (language_ids[:, None] == jnp.arange(table_whole.shape[0])[None, :]).astype(
        jnp.float32
    )
    language_rows = jnp.dot(language_hot, table_whole.astype(jnp.float32), precision=PRECISE)
    start_state = (
        hidden_in.astype(jnp.float32).reshape(seq_count, length, width) + language_rows[:, None, :]
    ).reshape(tokens, width)
    first_norm = to_low(norm_scale(start_state, gain_one.astype(jnp.float32)))
    self_queries = to_low(matmul(first_norm, query_whole))
    self_keys = to_low(matmul(first_norm, key_whole))
    self_values = to_low(matmul(first_norm, value_whole))
    bucket_hot = (
        bucket_ids[:, :, None] == jnp.arange(bucket_table.shape[0])[None, None, :]
    ).astype(jnp.float32)
    position_bias = jnp.einsum(
        "ijb,bh->hij", bucket_hot, bucket_table.astype(jnp.float32), precision=PRECISE
    )
    positions = jnp.arange(length)
    masked_bias = jnp.where(
        (positions[:, None] >= positions[None, :])[None], position_bias, NEGATIVE
    )

    def self_forward(block_items):
        return attend_forward(block_items[0], block_items[1], block_items[2], masked_bias)

    self_context, self_total = lax.map(
        self_forward,
        (
            to_blocks(self_queries, length),
            to_blocks(self_keys, length),
            to_blocks(self_values, length),
        ),
    )
    self_context = self_context.reshape(tokens, -1)
    mid_state = start_state + matmul(self_context, out_whole)
    second_norm = to_low(norm_scale(mid_state, gain_two.astype(jnp.float32)))
    cross_queries = to_low(matmul(second_norm, cquery_whole))
    encoder_flat = encoder_states.reshape(enc_count * enc_length, width)
    source_keys = to_low(matmul(encoder_flat, ckey_whole)).reshape(enc_count, enc_length, -1)
    source_values = to_low(matmul(encoder_flat, cvalue_whole)).reshape(enc_count, enc_length, -1)
    source_hot = (source_index[:, None] == jnp.arange(enc_count)[None, :]).astype(jnp.float32)
    source_low = to_low(source_hot)
    picked_keys = to_low(
        jnp.einsum("se,emc->smc", source_low, source_keys, preferred_element_type=jnp.float32)
    )
    picked_values = to_low(
        jnp.einsum("se,emc->smc", source_low, source_values, preferred_element_type=jnp.float32)
    )

    def cross_forward(block_items):
        return attend_forward(block_items[0], block_items[1], block_items[2], 0.0)

    cross_context, cross_total = lax.map(
        cross_forward,
        (
            to_blocks(cross_queries, length),
            picked_keys.reshape(blocks, SEQ_BLOCK, enc_length, -1),
            picked_values.reshape(blocks, SEQ_BLOCK, enc_length, -1),
        ),
    )
    cross_context = cross_context.reshape(tokens, -1)
    late_state = mid_state + matmul(cross_context, cout_whole)
    third_norm = to_low(norm_scale(late_state, gain_three.astype(jnp.float32)))
    expanded = matmul(third_norm, inner_whole)
    activated = to_low(jax.nn.gelu(expanded, approximate=True))
    hidden_out = (late_state + matmul(activated, outer_whole)).astype(jnp.bfloat16)
    top_grad = output_grad.astype(jnp.float32)
    outer_full = left_product(activated, output_grad)
    activated_grad = right_product(output_grad, outer_whole)
    gelu_value, gelu_back = jax.vjp(jax.nn.gelu, expanded)
    expanded_grad = to_low(gelu_back(activated_grad)[0])
    inner_full = left_product(third_norm, expanded_grad)
    third_grad = right_product(expanded_grad, inner_whole)
    norm_value, norm_back = jax.vjp(norm_scale, late_state, gain_three.astype(jnp.float32))
    state_back, feed_gain_full = norm_back(third_grad)
    late_grad = top_grad + state_back
    cross_low = to_low(late_grad)
    cout_full = left_product(cross_context, cross_low)
    cross_context_grad = to_low(right_product(cross_low, cout_whole))

    def cross_backward(block_items):
        return attend_backward(
            block_items[0],
            block_items[1],
            block_items[2],
            0.0,
            block_items[3],
            block_items[4],
            False,
        )

    cquery_part, ckey_part, cvalue_part = lax.map(
        cross_backward,
        (
            to_blocks(cross_queries, length),
            picked_keys.reshape(blocks, SEQ_BLOCK, enc_length, -1),
            picked_values.reshape(blocks, SEQ_BLOCK, enc_length, -1),
            cross_total,
            to_blocks(cross_context_grad, length),
        ),
    )
    cquery_low = to_low(cquery_part.reshape(tokens, -1))
    source_key_grad = to_low(
        jnp.einsum(
            "se,smc->emc",
            source_hot,
            ckey_part.reshape(seq_count, enc_length, -1),
            precision=PRECISE,
        ).reshape(enc_count * enc_length, -1)
    )
    source_value_grad = to_low(
        jnp.einsum(
            "se,smc->emc",
            source_hot,
            cvalue_part.reshape(seq_count, enc_length, -1),
            precision=PRECISE,
        ).reshape(enc_count * enc_length, -1)
    )
    cquery_full = left_product(second_norm, cquery_low)
    ckey_full = left_product(encoder_flat, source_key_grad)
    cvalue_full = left_product(encoder_flat, source_value_grad)
    encoder_grad = (
        right_product(source_key_grad, ckey_whole) + right_product(source_value_grad, cvalue_whole)
    ).reshape(enc_count, enc_length, width)
    second_grad = right_product(cquery_low, cquery_whole)
    norm_value, norm_back = jax.vjp(norm_scale, mid_state, gain_two.astype(jnp.float32))
    state_back, cross_gain_full = norm_back(second_grad)
    mid_grad = late_grad + state_back
    self_low = to_low(mid_grad)
    out_full = left_product(self_context, self_low)
    self_context_grad = to_low(right_product(self_low, out_whole))

    def self_backward(block_items):
        return attend_backward(
            block_items[0],
            block_items[1],
            block_items[2],
            masked_bias,
            block_items[3],
            block_items[4],
            True,
        )

    query_part, key_part, value_part, bias_part = lax.map(
        self_backward,
        (
            to_blocks(self_queries, length),
            to_blocks(self_keys, length),
            to_blocks(self_values, length),
            self_total,
            to_blocks(self_context_grad, length),
        ),
    )
    query_low = to_low(query_part.reshape(tokens, -1))
    key_low = to_low(key_part.reshape(tokens, -1))
    value_low = to_low(value_part.reshape(tokens, -1))
    table_full = jnp.einsum(
        "hij,ijb->bh", jnp.sum(bias_part, axis=0), bucket_hot, precision=PRECISE
    )
    query_full = left_product(first_norm, query_low)
    key_full = left_product(first_norm, key_low)
    value_full = left_product(first_norm, value_low)
    first_grad = (
        right_product(query_low, query_whole)
        + right_product(key_low, key_whole)
        + right_product(value_low, value_whole)
    )
    norm_value, norm_back = jax.vjp(norm_scale, start_state, gain_one.astype(jnp.float32))
    state_back, self_gain_full = norm_back(first_grad)
    hidden_in_grad = mid_grad + state_back
    sequence_sums = jnp.sum(hidden_in_grad.reshape(seq_count, length, width), axis=1)
    language_full = left_product(language_hot, sequence_sums)
    (
        language_part, bucket_table_grad, sgain_part, cgain_part, feed_gain_part, whole_parts, inner_part, outer_part,
    ) = reduce_grads(
        sizes, language_full, table_full, (self_gain_full, cross_gain_full, feed_gain_full),
        (query_full, key_full, value_full, out_full, cquery_full, ckey_full, cvalue_full, cout_full),
        inner_full, outer_full,
    )
    query_sum, key_sum, value_sum, out_part, cquery_part_sum, ckey_part_sum, cvalue_part_sum, cout_part = whole_parts
    return (
        hidden_out,
        hidden_in_grad,
        encoder_grad,
        language_part,
        bucket_table_grad,
        sgain_part,
        query_sum,
        key_sum,
        value_sum,
        out_part,
        cgain_part,
        cquery_part_sum,
        ckey_part_sum,
        cvalue_part_sum,
        cout_part,
        feed_gain_part,
        inner_part,
        outer_part,
    )


def solution(mesh):
    sizes = (mesh.shape["dp"] // 2, mesh.shape["fsdp"] // 2)
    in_specs = (
        P(("dp", "fsdp"), None),
        P(("dp", "fsdp"), None),
        P(("dp", "fsdp"), None, None),
        P(("dp", "fsdp")),
        P(("dp", "fsdp")),
        P(),
        P(None, ("dp", "fsdp")),
        P(),
        P(("dp", "fsdp")),
        P(("dp", "fsdp"), None),
        P(("dp", "fsdp"), None),
        P(("dp", "fsdp"), None),
        P(("dp", "fsdp"), None),
        P(("dp", "fsdp")),
        P(("dp", "fsdp"), None),
        P(("dp", "fsdp"), None),
        P(("dp", "fsdp"), None),
        P(("dp", "fsdp"), None),
        P(("dp", "fsdp")),
        P(("dp", "fsdp"), None),
        P(("dp", "fsdp"), None),
    )
    out_specs = (
        P(("dp", "fsdp"), None),
        P(("dp", "fsdp"), None),
        P(("dp", "fsdp"), None, None),
        P(None, ("dp", "fsdp")),
        P(),
        P(("dp", "fsdp")),
        P(("dp", "fsdp"), None),
        P(("dp", "fsdp"), None),
        P(("dp", "fsdp"), None),
        P(("dp", "fsdp"), None),
        P(("dp", "fsdp")),
        P(("dp", "fsdp"), None),
        P(("dp", "fsdp"), None),
        P(("dp", "fsdp"), None),
        P(("dp", "fsdp"), None),
        P(("dp", "fsdp")),
        P(("dp", "fsdp"), None),
        P(("dp", "fsdp"), None),
    )
    return jax.shard_map(functools.partial(local, sizes), mesh=mesh, in_specs=in_specs, out_specs=out_specs, check_vma=False)
```

```python
import functools

import jax
import jax.numpy as jnp
from jax import lax
from jax.experimental import pallas as pl
from jax.experimental.pallas import tpu as pltpu
from jax.sharding import PartitionSpec as P

H = 12
HEAD = 64
SEQ_BLOCK = 2


EPSILON = 1e-06
PRECISE = lax.Precision.HIGHEST
NEGATIVE = -1e30


def to_low(value):
    return value.astype(jnp.bfloat16)


def norm_scale(hidden, gain):
    return hidden * lax.rsqrt(jnp.mean(hidden * hidden, axis=-1, keepdims=True) + EPSILON) * gain


def matmul(left, right):
    return jnp.dot(left, right, preferred_element_type=jnp.float32)


def left_product(left, right):
    return lax.dot_general(
        left, right, (((0,), (0,)), ((), ())), preferred_element_type=jnp.float32
    )


def right_product(left, right):
    return lax.dot_general(
        left, right, (((1,), (1,)), ((), ())), preferred_element_type=jnp.float32
    )


def split_heads(array):
    return array.reshape(array.shape[:-1] + (H, HEAD))


def score_block(queries, key_rows, offset):
    scores = jnp.einsum(
        "sqhe,skhe->shqk",
        split_heads(queries),
        split_heads(key_rows),
        preferred_element_type=jnp.float32,
    )
    return scores + offset


def attend_forward(queries, key_rows, value_rows, offset):
    scores = score_block(queries, key_rows, offset)
    top_score = jnp.max(scores, axis=-1, keepdims=True)
    log_total = top_score + jnp.log(jnp.sum(jnp.exp(scores - top_score), axis=-1, keepdims=True))
    weights = to_low(jnp.exp(scores - log_total))
    context = jnp.einsum(
        "shqk,skhe->sqhe", weights, split_heads(value_rows), preferred_element_type=jnp.float32
    )
    return (to_low(context).reshape(queries.shape), log_total)


def attend_backward(queries, key_rows, value_rows, offset, log_total, context_grad, with_bias):
    scores = score_block(queries, key_rows, offset)
    probs = jnp.exp(scores - log_total)
    weights = to_low(probs)
    grad_heads = split_heads(context_grad)
    value_grad = jnp.einsum(
        "shqk,sqhe->skhe", weights, grad_heads, preferred_element_type=jnp.float32
    )
    prob_grad = jnp.einsum(
        "sqhe,skhe->shqk", grad_heads, split_heads(value_rows), preferred_element_type=jnp.float32
    )
    score_grad = to_low(probs * (prob_grad - jnp.sum(probs * prob_grad, axis=-1, keepdims=True)))
    query_grad = jnp.einsum(
        "shqk,skhe->sqhe", score_grad, split_heads(key_rows), preferred_element_type=jnp.float32
    )
    key_grad = jnp.einsum(
        "shqk,sqhe->skhe", score_grad, split_heads(queries), preferred_element_type=jnp.float32
    )
    grads = (
        query_grad.reshape(queries.shape),
        key_grad.reshape(key_rows.shape),
        value_grad.reshape(value_rows.shape),
    )
    if with_bias:
        return grads + (jnp.sum(score_grad.astype(jnp.float32), axis=0),)
    return grads


MESH = pl.DeviceIdType.MESH
ALL = slice(None)


class Place:
    def __init__(self, sizes):
        self.ny, self.nz = sizes
        self.dp = lax.axis_index("dp")
        self.fs = lax.axis_index("fsdp")
        self.c, self.y = lax.rem(self.dp, 2), lax.div(self.dp, 2)
        self.x, self.z = lax.rem(self.fs, 2), lax.div(self.fs, 2)

    def size(self, dim):
        return {"c": 2, "x": 2, "y": self.ny, "z": self.nz}[dim]

    def at(self, dim):
        return {"c": self.c, "x": self.x, "y": self.y, "z": self.z}[dim]

    def device(self, dim, index):
        if dim == "c":
            return (self.y * 2 + index, self.fs)
        if dim == "y":
            return (index * 2 + self.c, self.fs)
        if dim == "x":
            return (self.dp, self.z * 2 + index)
        return (self.dp, index * 2 + self.x)


def neighbour_barrier(place, far=False):
    barrier = pltpu.get_barrier_semaphore()
    links = []
    for dim in "cxyz":
        here, size = place.at(dim), place.size(dim)
        reach = 1
        while reach < size and (reach == 1 or far):
            if size == 2:
                links.append((dim, 1 - here, None))
            elif reach == 1:
                for step in (1, -1):
                    links.append((dim, here + step, (here + step >= 0) & (here + step < size)))
            else:
                links.append((dim, here + reach - 2 * reach * lax.rem(lax.div(here, reach), 2), None))
            reach *= 2

    def signal(dim, there):
        pl.semaphore_signal(barrier, inc=1, device_id=place.device(dim, there), device_id_type=MESH)

    for dim, there, condition in links:
        if condition is None:
            signal(dim, there)
        else:
            pl.when(condition)(lambda dim=dim, there=there: signal(dim, there))
    peers = sum(1 if condition is None else condition.astype(jnp.int32) for _, _, condition in links)
    pl.semaphore_wait(barrier, peers)


PATHS = ("zxy", "zyx", "xzy", "yzx")


class Link:
    def __init__(self, copy, sends=None, receives=None):
        self.copy, self.sends, self.receives = copy, sends, receives

    @staticmethod
    def when(condition, run):
        if condition is None:
            run()
        else:
            pl.when(condition)(run)

    def start(self):
        self.when(self.sends, lambda: self.copy.start())

    def wait_send(self):
        self.when(self.sends, lambda: self.copy.wait_send())

    def wait_recv(self):
        self.when(self.receives, lambda: self.copy.wait_recv())


def pick(held, place, **fixed):
    return tuple(fixed.get(dim, ALL if dim in held else place.at(dim)) for dim in "yczx")


def gather_steps(place, blocks, path, sems):
    steps, slot, held = [], 0, ""
    for dim in path + "c":
        here, size = place.at(dim), place.size(dim)
        if size == 2:
            there = 1 - here
            index = pick(held, place)
            copy = pltpu.make_async_remote_copy(
                blocks(index), blocks(index), sems[0].at[slot], sems[1].at[slot],
                device_id=place.device(dim, there), device_id_type=MESH,
            )
            steps.append([Link(copy)])
            slot += 1
        else:
            for hop in range(1, size):
                links = []
                for way in (1, -1):
                    origin = here - way * (hop - 1)
                    there = here + way
                    source = here - way * hop
                    index = pick(held, place, **{dim: jnp.clip(origin, 0, size - 1)})
                    copy = pltpu.make_async_remote_copy(
                        blocks(index), blocks(index), sems[0].at[slot], sems[1].at[slot],
                        device_id=place.device(dim, jnp.clip(there, 0, size - 1)), device_id_type=MESH,
                    )
                    sends = (origin >= 0) & (origin < size) & (there >= 0) & (there < size)
                    links.append(Link(copy, sends, (source >= 0) & (source < size)))
                    slot += 1
                steps.append(links)
        held += dim
    return steps


def slot_count(sizes):
    ny, nz = sizes
    return 2 + (1 if ny == 2 else 2 * (ny - 1)) + (1 if nz == 2 else 2 * (nz - 1))


def run_steps(plans, lag):
    rounds = max(lag[i] + len(plan) for i, plan in enumerate(plans)) + 1
    for now in range(rounds):
        for offset, plan in zip(lag, plans):
            at = now - offset
            if 1 <= at <= len(plan):
                for link in plan[at - 1]:
                    link.wait_recv()
            if 0 <= at < len(plan):
                for link in plan[at]:
                    link.start()
    for plan in plans:
        for links in plan:
            for link in links:
                link.wait_send()


def gather_kernel(sizes, *refs):
    shards, wholes = refs[:11], refs[11:22]
    own_sem, send_sem, recv_sem = refs[22:]
    place = Place(sizes)
    own = (place.y, place.c, place.z, place.x)
    owns = [
        pltpu.make_async_copy(shard, whole.at[own], own_sem.at[i])
        for i, (shard, whole) in enumerate(zip(shards, wholes))
    ]
    for copy in owns:
        copy.start()
    neighbour_barrier(place)
    views = [lambda index, ref=ref: ref.at[index] for ref in wholes[:9]]
    width = wholes[8].shape[-1]
    for q in range(4):
        views.append(
            lambda index, q=q: wholes[9].at[index + (ALL, pl.ds(q * width, width))]
        )
    for q in range(4):
        views.append(lambda index, q=q: wholes[10].at[index + (q,)])
    plans, lag = [], []
    for i, view in enumerate(views):
        path = PATHS[0] if i == 0 else PATHS[(i - 1) % 4]
        plans.append(gather_steps(place, view, path, (send_sem.at[i], recv_sem.at[i])))
        lag.append(0 if i == 0 else 3 * ((i - 1) // 4))
    for copy in owns:
        copy.wait()
    run_steps(plans, lag)


def gather_weights(sizes, table, gains, squares, inner, outer):
    ny, nz = sizes
    grid = (ny, 2, nz, 2)
    part, width = squares[0].shape
    small = jnp.zeros((16, 128), table.dtype)
    small = small.at[: table.shape[0], :part].set(table)
    for i, gain in enumerate(gains):
        small = small.at[table.shape[0] + i, :part].set(gain)
    shards = (small,) + tuple(squares) + (inner, outer.reshape(4, part, width))
    anywhere = pl.BlockSpec(memory_space=pl.ANY)
    slots = slot_count(sizes)
    wholes = pl.pallas_call(
        functools.partial(gather_kernel, sizes),
        out_shape=[jax.ShapeDtypeStruct(grid + s.shape, s.dtype) for s in shards],
        in_specs=[anywhere] * 11,
        out_specs=[anywhere] * 11,
        scratch_shapes=[
            pltpu.SemaphoreType.DMA((11,)),
            pltpu.SemaphoreType.DMA((17, slots)),
            pltpu.SemaphoreType.DMA((17, slots)),
        ],
        compiler_params=pltpu.CompilerParams(collective_id=0, has_side_effects=True),
    )(*shards)
    count = ny * nz * 4
    tiny = wholes[0].reshape(count, 16, 128)[:, :, :part].transpose(1, 0, 2).reshape(16, count * part)
    rows = table.shape[0]
    return (
        (tiny[rows], tiny[rows + 1], tiny[rows + 2], tiny[:rows])
        + tuple(w.reshape(count * part, width) for w in wholes[1:9])
        + (wholes[9].reshape(count * part, 4 * width), wholes[10].reshape(4 * count * part, width))
    )


class Reduce:
    def __init__(self, place, path, source, total, core_in, boxes, out, sems):
        self.place, self.path, self.source, self.total = place, path, source, total
        self.core_in, self.boxes, self.out, self.sems = core_in, boxes, out, sems
        self.slot = 0
        self.sent = []

    def copy(self, source, target, dim, there):
        slot = self.slot
        self.slot += 1
        return pltpu.make_async_remote_copy(
            source, target, self.sems[0].at[slot], self.sems[1].at[slot],
            device_id=self.place.device(dim, there), device_id_type=MESH,
        )

    def index(self, fixed):
        return tuple(fixed.get(dim, ALL) for dim in "yzx")

    def add(self, target, box):
        shape = box.shape[:-2]
        count = 1
        for size in shape:
            count *= size
        free = [i for i, entry in enumerate(target) if entry is ALL]

        def body(n, _):
            spots, rest = [], n
            for size in reversed(shape):
                spots.append(lax.rem(rest, size))
                rest = lax.div(rest, size)
            spots = spots[::-1]
            full = list(target)
            for place_at, spot in zip(free, spots):
                full[place_at] = spot
            mine = self.total[tuple(full)].astype(jnp.float32)
            got = box[tuple(spots)].astype(jnp.float32)
            self.total[tuple(full)] = (mine + got).astype(jnp.bfloat16)
            return 0

        if count == 1:
            body(0, 0)
        else:
            lax.fori_loop(0, count, body, 0)

    def steps(self):
        place, listing = self.place, []
        own = pltpu.make_async_copy(self.source(place.c), self.total, self.sems[2])
        core = self.copy(self.source(1 - place.c), self.core_in, "c", 1 - place.c)

        def start():
            own.start()
            core.start()

        def finish():
            own.wait()
            core.wait_recv()
            self.add((ALL, ALL, ALL), self.core_in)

        self.sent.append(Link(core))
        listing.append((start, finish))
        fixed, box = {}, 0
        for dim in self.path:
            here, size = place.at(dim), place.size(dim)
            if size == 2:
                target = self.index({**fixed, dim: 1 - here})
                link = Link(self.copy(self.total.at[target], self.boxes[box], dim, 1 - here))
                self.sent.append(link)
                listing.append(self.pair([link], [(self.index({**fixed, dim: here}), box, None)]))
                box += 1
            else:
                for hop in range(size - 1, 0, -1):
                    links, adds = [], []
                    for way in (1, -1):
                        there = here - way
                        goal = here - way * hop
                        sends = (goal >= 0) & (goal < size)
                        source = here + way
                        got = source - way * hop
                        receives = (source >= 0) & (source < size) & (got >= 0) & (got < size)
                        target = self.index({**fixed, dim: jnp.clip(goal, 0, size - 1)})
                        copy = self.copy(
                            self.total.at[target], self.boxes[box], dim, jnp.clip(there, 0, size - 1)
                        )
                        link = Link(copy, sends, receives)
                        self.sent.append(link)
                        links.append(link)
                        adds.append((self.index({**fixed, dim: jnp.clip(got, 0, size - 1)}), box, receives))
                        box += 1
                    listing.append(self.pair(links, adds))
            fixed = {**fixed, dim: here}
        return listing

    def pair(self, links, adds):
        def start():
            for link in links:
                link.start()

        def finish():
            for link in links:
                link.wait_recv()
            for target, box, condition in adds:
                Link.when(condition, functools.partial(self.add, target, self.boxes[box]))

        return start, finish

    def close(self):
        own = (self.place.y, self.place.z, self.place.x)
        self.out(self.total[own].astype(jnp.float32))
        for link in self.sent:
            link.wait_send()


def box_shapes(sizes, path):
    ny, nz = sizes
    size = {"y": ny, "z": nz, "x": 2}
    left, shapes = "yzx", []
    for dim in path:
        left = left.replace(dim, "")
        lead = tuple(size[d] for d in left)
        shapes += [lead] * (1 if size[dim] == 2 else 2 * (size[dim] - 1))
    return shapes


BACK_PATHS = tuple(path[::-1] for path in PATHS)


def reduce_kernel(sizes, box_counts, *refs):
    sources, small_in = refs[:10], refs[10]
    outs, small_out = refs[11:21], refs[21]
    totals, core_boxes = refs[22], refs[23]
    at = 24
    boxes = []
    for count in box_counts:
        boxes.append(refs[at : at + count])
        at += count
    small_box, own_sem, send_sem, recv_sem, small_send, small_recv = refs[at:]
    place = Place(sizes)
    neighbour_barrier(place, far=True)
    width = outs[0].shape[-1]

    def square(ref):
        return lambda core: ref.at[:, core]

    def inner(q):
        return lambda core: sources[8].at[:, core, :, :, :, pl.ds(q * width, width)]

    def outer(q):
        return lambda core: sources[9].at[:, core, :, :, q]

    views = [inner(q) for q in range(4)] + [outer(q) for q in range(4)]
    views += [square(sources[i]) for i in (4, 5, 6, 7, 0, 1, 2, 3)]

    def store_square(i):
        def run(value):
            outs[i][...] = value

        return run

    def store_inner(q):
        def run(value):
            outs[8][:, q * width : (q + 1) * width] = value

        return run

    def store_outer(q):
        def run(value):
            outs[9][q] = value

        return run

    stores = [store_inner(q) for q in range(4)] + [store_outer(q) for q in range(4)]
    stores += [store_square(i) for i in (4, 5, 6, 7, 0, 1, 2, 3)]
    plans, lag = [], []
    reduces = []
    for m in range(16):
        group, kind = m // 4, m % 4
        reduce = Reduce(
            place, BACK_PATHS[kind], views[m], totals.at[m], core_boxes.at[m],
            [box.at[group] for box in boxes[kind]], stores[m],
            (send_sem.at[m], recv_sem.at[m], own_sem.at[m]),
        )
        reduces.append(reduce)
        plans.append(reduce.steps())
        lag.append(3 * group)
    small_out[...] = small_in[...]
    small = []
    moves = [("c", 1 - place.c), ("x", 1 - place.x), ("y", None), ("z", None)]
    for dim, there in moves:
        size, here, reach = place.size(dim), place.at(dim), 1
        while reach < size:
            partner = here + reach - 2 * reach * lax.rem(lax.div(here, reach), 2)
            small.append((dim, partner))
            reach *= 2
    rounds = max(max(lag[i] + len(plan) for i, plan in enumerate(plans)) + 1, len(small) + 1)
    copies = []
    for now in range(rounds):
        for offset, plan in zip(lag, plans):
            step = now - offset
            if 1 <= step <= len(plan):
                plan[step - 1][1]()
            if 0 <= step < len(plan):
                plan[step][0]()
        if 1 <= now <= len(small):
            copies[-1].wait()
            small_out[...] += small_box[now - 1]
        if now < len(small):
            dim, partner = small[now]
            copies.append(
                pltpu.make_async_remote_copy(
                    small_out, small_box.at[now], small_send.at[now], small_recv.at[now],
                    device_id=place.device(dim, partner), device_id_type=MESH,
                )
            )
            copies[-1].start()
    for reduce in reduces:
        reduce.close()


def reduce_grads(sizes, language, bucket, gains, squares, inner, outer):
    ny, nz = sizes
    grid = (ny, 2, nz, 2)
    count = ny * nz * 4
    width = squares[0].shape[1]
    part = squares[0].shape[0] // count
    langs = language.shape[0]
    flat = jnp.zeros((width,), jnp.float32).at[: bucket.size].set(bucket.reshape(-1))
    small = jnp.concatenate(
        [language] + [g.reshape(1, width) for g in gains] + [flat[None], jnp.zeros((4, width), jnp.float32)], axis=0
    )
    sources = [to_low(s).reshape(grid + (part, width)) for s in squares]
    sources += [
        to_low(inner).reshape(grid + (part, 4 * width)),
        to_low(outer).reshape(grid + (4, part, width)),
    ]
    anywhere = pl.BlockSpec(memory_space=pl.ANY)
    vmem = pl.BlockSpec(memory_space=pltpu.VMEM)
    shapes = [(part, width)] * 8 + [(part, 4 * width), (4, part, width), small.shape]
    lead = [box_shapes(sizes, path) for path in BACK_PATHS]
    slots = slot_count(sizes)
    hops = (ny * nz * 4).bit_length() - 1
    outs = pl.pallas_call(
        functools.partial(reduce_kernel, sizes, tuple(len(s) for s in lead)),
        out_shape=[jax.ShapeDtypeStruct(s, jnp.float32) for s in shapes],
        in_specs=[anywhere] * 10 + [vmem],
        out_specs=[vmem] * 11,
        scratch_shapes=[
            pltpu.VMEM((16, ny, nz, 2, part, width), jnp.bfloat16),
            pltpu.VMEM((16, ny, nz, 2, part, width), jnp.bfloat16),
        ]
        + [pltpu.VMEM((4,) + s + (part, width), jnp.bfloat16) for one in lead for s in one]
        + [
            pltpu.VMEM((hops,) + small.shape, jnp.float32),
            pltpu.SemaphoreType.DMA((16,)),
            pltpu.SemaphoreType.DMA((16, slots)),
            pltpu.SemaphoreType.DMA((16, slots)),
            pltpu.SemaphoreType.DMA((hops,)),
            pltpu.SemaphoreType.DMA((hops,)),
        ],
        compiler_params=pltpu.CompilerParams(
            collective_id=1, has_side_effects=True, vmem_limit_bytes=60 * 1024 * 1024
        ),
    )(*sources, small)
    start = (lax.axis_index("dp") * nz * 2 + lax.axis_index("fsdp")) * part
    total = outs[10]
    mine = lax.dynamic_slice(total, (0, start), (langs + 3, part))
    return (
        mine[:langs],
        total[langs + 3, : bucket.size].reshape(bucket.shape),
        mine[langs], mine[langs + 1], mine[langs + 2],
        outs[:8], outs[8], outs[9].reshape(4 * part, width),
    )


LOW = jnp.bfloat16
FULL = jnp.float32
PAIR = 2 * HEAD


def nt_dot(left, right):
    return lax.dot_general(left, right, (((1,), (1,)), ((), ())), preferred_element_type=FULL)


def tn_dot(left, right):
    return lax.dot_general(left, right, (((0,), (0,)), ((), ())), preferred_element_type=FULL)


def flat(ref, *suffix):
    value = ref[(ALL,) * (len(ref.shape) - 1) + suffix] if suffix else ref[...]
    rows = 1
    for size in value.shape[:-1]:
        rows *= size
    return value.reshape(rows, value.shape[-1])


def each(count, body):
    def run(i, _):
        body(pl.ds(pl.multiple_of(i * 128, 128), 128))
        return 0

    lax.fori_loop(0, count, run, 0)


def unit_rows(hidden):
    return hidden * lax.rsqrt(jnp.mean(hidden * hidden, axis=-1, keepdims=True) + EPSILON)


def spread_small(tiny, table):
    part = table.shape[1] // (tiny.shape[0] * tiny.shape[2] * 4)
    table[...] = jnp.zeros_like(table)
    lane = lax.broadcasted_iota(jnp.int32, (16, 128), 1)
    at = 0
    for y in range(tiny.shape[0]):
        for core in range(2):
            for z in range(tiny.shape[2]):
                for x in range(2):
                    slab = jnp.where(lane < part, tiny[y, core, z, x].astype(FULL), 0.0)
                    base, shift = at // 128 * 128, at % 128
                    if shift:
                        slab = pltpu.roll(slab, shift, 1)
                    if shift + part <= 128:
                        table[:, base : base + 128] += slab
                    else:
                        table[:, base : base + 128] += jnp.where(lane >= part, slab, 0.0)
                        table[:, base + 128 : base + 256] += jnp.where(lane < part, slab, 0.0)
                    at += part


def build_bias(ids, values, bias):
    heads, keys, queries = bias.shape
    rows = 32

    def block(n, _):
        at = pl.ds(pl.multiple_of(n * rows, rows), rows)
        bucket = ids[at, :]
        bits = [lax.bitwise_and(bucket, 1 << b) != 0 for b in range(5)]
        key = n * rows + lax.broadcasted_iota(jnp.int32, (rows, queries), 0)
        query = lax.broadcasted_iota(jnp.int32, (rows, queries), 1)
        hidden = key > query

        def head(h, _):
            level = [values[h, c] for c in range(32)]
            for bit in bits:
                level = [jnp.where(bit, level[i + 1], level[i]) for i in range(0, len(level), 2)]
            bias[h, at, :] = jnp.where(hidden, NEGATIVE, level[0]).astype(LOW)
            return 0

        return lax.fori_loop(0, heads, head, 0)

    lax.fori_loop(0, keys // rows, block, 0)


def head_pair(value):
    lane = lax.broadcasted_iota(jnp.int32, value.shape, 1)
    zero = jnp.zeros_like(value)
    return jnp.concatenate([jnp.where(lane < HEAD, value, zero), jnp.where(lane < HEAD, zero, value)], axis=0)


def pair_forward(queries, keys, values, offset, weights, inverse_row):
    count = queries.shape[0]
    scores = nt_dot(keys, head_pair(queries))
    if offset is not None:
        scores = scores + offset
    grown = jnp.exp(scores - jnp.max(scores, axis=0, keepdims=True))
    inverse_row[...] = 1.0 / jnp.sum(grown, axis=0, keepdims=True)
    low = grown.astype(LOW)
    weights[...] = low
    lane = lax.broadcasted_iota(jnp.int32, values.shape, 1)
    one = jnp.ones_like(values)
    first = tn_dot(low[:, :count], jnp.where(lane < HEAD, values, one))
    second = tn_dot(low[:, count:], jnp.where(lane < HEAD, one, values))
    lane = lax.broadcasted_iota(jnp.int32, first.shape, 1)
    total = pltpu.roll(jnp.where(lane < HEAD, second, first), HEAD, 1)
    inverse = 1.0 / total
    return jnp.where(lane < HEAD, first, second) * inverse, inverse


def gelu_parts(u):
    a, b = 0.7978845608028654, 0.044715
    square = u * u
    t = jnp.tanh(a * u * (1.0 + b * square))
    half = 0.5 * (1.0 + t)
    slope = half + 0.5 * u * (1.0 - t * t) * (a * (1.0 + 3.0 * b * square))
    return u * half, slope


def gather_plans(place, wholes, small, sems):
    views = [lambda index, ref=ref: ref.at[index] for ref in [small] + list(wholes[:8])]
    width = wholes[0].shape[-1]
    for q in range(4):
        views.append(lambda index, q=q: wholes[8].at[index + (ALL, pl.ds(q * width, width))])
    for q in range(4):
        views.append(lambda index, q=q: wholes[9].at[index + (q,)])
    plans, lag = [], []
    for i, view in enumerate(views):
        path = PATHS[0] if i == 0 else PATHS[(i - 1) % 4]
        plans.append(gather_steps(place, view, path, (sems[0].at[i], sems[1].at[i])))
        lag.append(0 if i == 0 else 2 * ((i - 1) // 4))
    return plans, lag


SAVED = (
    "first_norm", "queries", "keys", "values", "self_context", "second_norm", "cross_queries",
    "source_keys", "source_values", "cross_context", "third_norm", "activated", "slope",
    "start", "mid", "late", "self_inverse", "cross_inverse", "self_rows", "cross_rows", "table",
)


def saved_shapes(tokens, sources, width, length):
    low, full = LOW, FULL
    row = (tokens, width)
    pairs = tokens // length * (width // PAIR)
    shapes = {name: (row, low) for name in SAVED}
    shapes["source_keys"] = shapes["source_values"] = ((2, sources // 2, width), low)
    shapes["activated"] = shapes["slope"] = ((4,) + row, low)
    for name in ("start", "mid", "late", "self_inverse", "cross_inverse"):
        shapes[name] = (row, full)
    shapes["self_rows"] = shapes["cross_rows"] = ((pairs, 1, 2 * length), full)
    shapes["table"] = ((16, width), full)
    return shapes


def forward_kernel(sizes, *refs):
    n = len(SAVED)
    small_shard, shards = refs[0], refs[1:11]
    hidden, encoder, languages, sources, ids, bucket_values = refs[11:17]
    hidden_out, whole_outs = refs[17], refs[18:28]
    self_weights, cross_weights = refs[28:30]
    saved_outs = dict(zip(SAVED, refs[30 : 30 + n]))
    at = 30 + n
    tiny, wholes = refs[at], refs[at + 1 : at + 11]
    at += 11
    v = dict(zip(SAVED, refs[at : at + n]))
    at += n
    bias, stage, out_buffer = refs[at : at + 3]
    own_sem, send_sem, recv_sem, out_sem, stage_sem, hidden_sem = refs[at + 3 :]
    tokens, width = hidden.shape
    length = ids.shape[0]
    per_seq = width // PAIR
    seqs = tokens // length
    enc_length = encoder.shape[0] // 2
    blocks = tokens // 128

    place = Place(sizes)
    own = (place.y, place.c, place.z, place.x)
    owns = [
        pltpu.make_async_copy(shard, whole.at[own], own_sem.at[i])
        for i, (shard, whole) in enumerate(zip((small_shard,) + shards, (tiny,) + wholes))
    ]
    for copy in owns:
        copy.start()
    neighbour_barrier(place)
    plans, lag = gather_plans(place, wholes, tiny, (send_sem, recv_sem))
    for copy in owns:
        copy.wait()
    copies = []

    def keep(name):
        copy = pltpu.make_async_copy(v[name], saved_outs[name], out_sem.at[len(copies)])
        copy.start()
        copies.append(copy)

    def keep_whole(i):
        copy = pltpu.make_async_copy(wholes[i], whole_outs[i], out_sem.at[len(copies)])
        copy.start()
        copies.append(copy)

    def opening():
        spread_small(tiny, v["table"])
        for s in range(seqs):
            row = jnp.zeros((1, width), FULL)
            for l in range(8):
                row = row + jnp.where(languages[s] == l, v["table"][l : l + 1, :], 0.0)

            def body(at):
                start = hidden[at, :].astype(FULL) + row
                v["start"][at, :] = start
                v["first_norm"][at, :] = (unit_rows(start) * v["table"][8:9, :]).astype(LOW)

            def run(i, _):
                body(pl.ds(pl.multiple_of(s * length + i * 128, 128), 128))
                return 0

            lax.fori_loop(0, length // 128, run, 0)
        keep("table")
        keep("start")
        keep("first_norm")

    def project(source, weight, target):
        target[...] = jnp.dot(source[...], flat(weight), preferred_element_type=FULL).astype(LOW)

    def attention(queries, keys, values, context, inverse, rows, weights_out, seq, picked):
        lanes_of = lambda p: pl.ds(pl.multiple_of(p * PAIR, PAIR), PAIR)
        row_at = pl.ds(seq * length, length)
        key_rows = length if picked is None else enc_length

        def out_copy(slot, index):
            return pltpu.make_async_copy(
                stage.at[slot, pl.ds(0, key_rows)], weights_out.at[index], stage_sem.at[slot]
            )

        def body(p, _):
            lanes = lanes_of(p)
            slot = lax.rem(p, 2)
            index = seq * per_seq + p

            @pl.when(p >= 2)
            def _():
                out_copy(slot, index).wait()

            offset = None
            if picked is not None:
                key_block, value_block = keys[picked, :, lanes], values[picked, :, lanes]
            else:
                key_block, value_block = keys[row_at, lanes], values[row_at, lanes]
                offset = jnp.concatenate([bias[2 * p], bias[2 * p + 1]], axis=1).astype(FULL)
            out, total = pair_forward(
                queries[row_at, lanes], key_block, value_block, offset,
                stage.at[slot, pl.ds(0, key_rows)], rows.at[index],
            )
            context[row_at, lanes] = out.astype(LOW)
            inverse[row_at, lanes] = total
            out_copy(slot, index).start()
            return 0

        lax.fori_loop(0, per_seq, body, 0)
        for slot in range(2):
            out_copy(slot, 0).wait()

    def residual(context, weight, before, after, gain_row, norm):
        def body(at):
            state = before[at, :] + jnp.dot(context[at, :], flat(weight), preferred_element_type=FULL)
            after[at, :] = state
            norm[at, :] = (unit_rows(state) * v["table"][gain_row : gain_row + 1, :]).astype(LOW)

        each(blocks, body)

    def self_projections():
        project(v["first_norm"], wholes[0], v["queries"])
        project(v["first_norm"], wholes[1], v["keys"])
        project(v["first_norm"], wholes[2], v["values"])
        for i in range(3):
            keep_whole(i)
        keep_whole(3)
        for name in ("queries", "keys", "values"):
            keep(name)

    def self_attention(s):
        attention(
            v["queries"], v["keys"], v["values"], v["self_context"], v["self_inverse"], v["self_rows"],
            self_weights, s, None,
        )

    def self_end():
        for name in ("self_context", "self_inverse", "self_rows"):
            keep(name)
        residual(v["self_context"], wholes[3], v["start"], v["mid"], 9, v["second_norm"])
        keep("mid")
        keep("second_norm")

    def cross_sources():
        for name, i in (("source_keys", 5), ("source_values", 6)):
            for half in range(2):
                v[name][half] = jnp.dot(
                    encoder[pl.ds(half * enc_length, enc_length), :], flat(wholes[i]), preferred_element_type=FULL
                ).astype(LOW)
            keep(name)
        for i in (4, 5, 6, 7):
            keep_whole(i)

    def cross_projection():
        project(v["second_norm"], wholes[4], v["cross_queries"])
        keep("cross_queries")

    def cross_attention(s):
        attention(
            v["cross_queries"], v["source_keys"], v["source_values"], v["cross_context"], v["cross_inverse"],
            v["cross_rows"], cross_weights, s, sources[s],
        )

    def cross_end():
        for name in ("cross_context", "cross_inverse", "cross_rows"):
            keep(name)
        residual(v["cross_context"], wholes[7], v["mid"], v["late"], 10, v["third_norm"])
        keep("late")
        keep("third_norm")

    def feed_inner():
        for q in range(4):

            def body(at, q=q):
                expanded = jnp.dot(
                    v["third_norm"][at, :], flat(wholes[8], pl.ds(q * width, width)), preferred_element_type=FULL
                )
                value, slope = gelu_parts(expanded)
                v["activated"][q, at, :] = value.astype(LOW)
                v["slope"][q, at, :] = slope.astype(LOW)

            each(blocks, body)
        keep("activated")
        keep("slope")
        keep_whole(8)

    def feed_outer():
        weight = flat(wholes[9])

        def body(at):
            state = v["late"][at, :]
            for q in range(4):
                state = state + jnp.dot(
                    v["activated"][q, at, :], weight[q * width : (q + 1) * width], preferred_element_type=FULL
                )
            out_buffer[at, :] = state.astype(LOW)

        each(blocks, body)
        keep_whole(9)

    tasks = {
        1: [lambda: build_bias(ids, bucket_values, bias)],
        6: [opening, self_projections],
        7: [lambda: self_attention(0), lambda: self_attention(1)],
        8: [self_end, cross_sources, cross_projection],
        9: [lambda: cross_attention(0)],
        10: [lambda: cross_attention(1)],
        11: [cross_end, feed_inner],
        12: [feed_outer],
    }
    rounds = max(offset + len(plan) for offset, plan in zip(lag, plans)) + 1
    for now in range(max(rounds, 13)):
        for offset, plan in zip(lag, plans):
            step = now - offset
            if 1 <= step <= len(plan):
                for link in plan[step - 1]:
                    link.wait_recv()
            if 0 <= step < len(plan):
                for link in plan[step]:
                    link.start()
        for task in tasks.get(now, ()):
            task()
    last = pltpu.make_async_copy(out_buffer, hidden_out, hidden_sem)
    last.start()
    for plan in plans:
        for links in plan:
            for link in links:
                link.wait_send()
    for copy in copies:
        copy.wait()
    last.wait()


def small_slab(table, gains):
    rows, part = table.shape
    small = jnp.concatenate([table] + [g.reshape(1, part) for g in gains], axis=0)
    return jnp.pad(small, ((0, 16 - rows - len(gains)), (0, 128 - part)))


def forward(
    sizes, hidden_in, encoder_states, language_ids, source_index, bucket_ids, language_table, bucket_table, gains,
    squares, inner, outer,
):
    ny, nz = sizes
    grid = (ny, 2, nz, 2)
    part, width = squares[0].shape
    tokens = hidden_in.shape[0]
    length = bucket_ids.shape[0]
    encoder = encoder_states.reshape(-1, width)
    enc_length = encoder_states.shape[1]
    shards = [small_slab(language_table, gains)] + list(squares) + [inner, outer.reshape(4, part, width)]
    wholes = [jax.ShapeDtypeStruct(grid + s.shape, LOW) for s in shards]
    shapes = saved_shapes(tokens, encoder.shape[0], width, length)
    pairs = tokens // length * (width // PAIR)
    anywhere = pl.BlockSpec(memory_space=pl.ANY)
    vmem = pl.BlockSpec(memory_space=pltpu.VMEM)
    smem = pl.BlockSpec(memory_space=pltpu.SMEM)
    slots = slot_count(sizes)
    out_shape = [jax.ShapeDtypeStruct((tokens, width), LOW)] + wholes[1:]
    out_shape += [jax.ShapeDtypeStruct((pairs, rows, 2 * length), LOW) for rows in (length, enc_length)]
    out_shape += [jax.ShapeDtypeStruct(*shapes[name]) for name in SAVED]
    outs = pl.pallas_call(
        functools.partial(forward_kernel, sizes),
        out_shape=out_shape,
        in_specs=[anywhere] * 11 + [vmem, vmem, smem, smem, vmem, smem],
        out_specs=[anywhere] * len(out_shape),
        scratch_shapes=[pltpu.VMEM(w.shape, w.dtype) for w in wholes]
        + [pltpu.VMEM(*shapes[name]) for name in SAVED]
        + [
            pltpu.VMEM((H, length, length), LOW),
            pltpu.VMEM((2, enc_length, 2 * length), LOW),
            pltpu.VMEM((tokens, width), LOW),
            pltpu.SemaphoreType.DMA((11,)),
            pltpu.SemaphoreType.DMA((17, slots)),
            pltpu.SemaphoreType.DMA((17, slots)),
            pltpu.SemaphoreType.DMA((len(SAVED) + 10,)),
            pltpu.SemaphoreType.DMA((2,)),
            pltpu.SemaphoreType.DMA,
        ],
        compiler_params=pltpu.CompilerParams(
            collective_id=2, has_side_effects=True, vmem_limit_bytes=62 * 1024 * 1024
        ),
    )(
        *shards, hidden_in, encoder, language_ids, source_index, bucket_ids.T,
        bucket_table.astype(FULL).T,
    )
    return outs


class Summed:
    def __init__(self, place, path, blocks, core_in, boxes, sems):
        self.place, self.blocks, self.sems = place, blocks, sems
        self.slot, self.links, self.stages = 0, [], []
        c = place.c
        core = self.copy(blocks((ALL, 1 - c, ALL, ALL)), core_in, "c", 1 - c)
        self.stage([Link(core)], [((ALL, c, ALL, ALL), core_in, None)])
        fixed, box = {"c": c}, 0
        for dim in path:
            here, size = place.at(dim), place.size(dim)
            if size == 2:
                copy = self.copy(blocks(self.index({**fixed, dim: 1 - here})), boxes[box], dim, 1 - here)
                self.stage([Link(copy)], [(self.index({**fixed, dim: here}), boxes[box], None)])
                box += 1
            else:
                for hop in range(size - 1, 0, -1):
                    links, adds = [], []
                    for way in (1, -1):
                        there, goal = here - way, here - way * hop
                        sends = (goal >= 0) & (goal < size)
                        source = here + way
                        got = source - way * hop
                        receives = (source >= 0) & (source < size) & (got >= 0) & (got < size)
                        copy = self.copy(
                            blocks(self.index({**fixed, dim: jnp.clip(goal, 0, size - 1)})), boxes[box], dim,
                            jnp.clip(there, 0, size - 1),
                        )
                        links.append(Link(copy, sends, receives))
                        adds.append((self.index({**fixed, dim: jnp.clip(got, 0, size - 1)}), boxes[box], receives))
                        box += 1
                    self.stage(links, adds)
            fixed = {**fixed, dim: here}
        self.own = self.index(fixed)

    def index(self, fixed):
        return tuple(fixed.get(dim, ALL) for dim in "yczx")

    def copy(self, source, target, dim, there):
        slot = self.slot
        self.slot += 1
        return pltpu.make_async_remote_copy(
            source, target, self.sems[0].at[slot], self.sems[1].at[slot],
            device_id=self.place.device(dim, there), device_id_type=MESH,
        )

    def stage(self, links, adds):
        self.links += links
        self.stages.append((links, adds))

    def start(self, step):
        for link in self.stages[step][0]:
            link.start()

    def finish(self, step):
        links, adds = self.stages[step]
        for link in links:
            link.wait_recv()

        def add(target, box):
            view = self.blocks(target)
            view[...] = view[...] + box[...]

        for target, box, condition in adds:
            Link.when(condition, functools.partial(add, target, box))

    def close(self, store):
        store(self.blocks(self.own)[...].astype(FULL))
        for link in self.links:
            link.wait_send()


def pair_backward(weights, queries, keys, values, grads, inverse_row):
    count = queries.shape[0]
    stacked = head_pair(grads)
    prob_grad = nt_dot(values, stacked)
    grown = weights.astype(FULL)
    centre = jnp.sum(grown * prob_grad, axis=0, keepdims=True) * inverse_row
    score_grad = (grown * (prob_grad - centre)).astype(LOW)
    value_part = jnp.dot(weights, stacked, preferred_element_type=FULL)
    key_part = jnp.dot(score_grad, head_pair(queries), preferred_element_type=FULL)
    both = jnp.concatenate([score_grad[:, :count], score_grad[:, count:]], axis=0)
    query_part = tn_dot(both, head_pair(keys))
    return query_part, key_part, value_part, score_grad


def backward_kernel(sizes, box_counts, *refs):
    n = len(SAVED)
    grads, encoder, languages, sources, ids = refs[:5]
    wholes = refs[5:15]
    self_weights, cross_weights = refs[15:17]
    saved = dict(zip(SAVED, refs[17 : 17 + n]))
    at = 17 + n
    hidden_grad, encoder_grad, small_out, square_outs, inner_out, outer_out = (
        refs[at], refs[at + 1], refs[at + 2], refs[at + 3 : at + 11], refs[at + 11], refs[at + 12],
    )
    at += 13
    squares, outers, core_boxes = refs[at : at + 3]
    at += 3
    boxes = []
    for count in box_counts:
        boxes.append(refs[at : at + count])
        at += count
    small_box, pool, pairs_in, run_a, run_b, run_c, w, wo, stage, score_sum, bucket_rows, table, self_rows, cross_rows = refs[at : at + 14]
    send_sem, recv_sem, small_send, small_recv, load_sem, stage_sem, store_sem = refs[at + 14 :]
    place = Place(sizes)
    length = ids.shape[0]
    seqs, tokens = languages.shape[0], pool.shape[1]
    width = pool.shape[2]
    blocks = tokens // 128
    per_seq = width // PAIR
    part = inner_out.shape[0]
    loads = []

    def load(source, target):
        copy = pltpu.make_async_copy(source, target, load_sem.at[len(loads)])
        loads.append(copy)
        copy.start()
        return copy

    X = [pool.at[i] for i in range(11)] + [pairs_in.at[i] for i in range(4)]
    og, tn = X[0], X[1]
    get_og = load(grads, og)
    get_act = [load(saved["activated"].at[q], X[2 + q]) for q in range(4)]
    get_table = load(saved["table"], table)
    get_slope = [load(saved["slope"].at[q], X[6 + q]) for q in range(4)]

    def outer_chunk(q):
        return wholes[9].at[q // 2, q % 2]

    def inner_chunk(q):
        return wholes[8].at[:, :, :, :, :, pl.ds(q * width, width)]

    get_wo = [load(outer_chunk(q), wo.at[q]) for q in range(2)]
    get_tn = load(saved["third_norm"], tn)
    get_wi = [load(inner_chunk(q), w.at[q]) for q in range(2)]
    get_late = load(saved["late"], run_c)
    got = {}
    got["cross_rows"] = load(saved["cross_rows"], cross_rows)
    got["self_rows"] = load(saved["self_rows"], self_rows)
    got["co"] = load(wholes[7], w.at[2])
    got["cq_w"] = load(wholes[4], w.at[3])
    got["keys"] = load(saved["source_keys"], pairs_in.at[pl.ds(0, 2)])
    got["values"] = load(saved["source_values"], pairs_in.at[pl.ds(2, 2)])
    neighbour_barrier(place, far=True)

    def view_of(m):
        if m < 4:
            return lambda index: outers.at[index + (m,)]
        return lambda index: squares.at[(m - 4,) + index]

    plans = []
    for m in range(16):
        group, kind = m // 4, m % 4
        slot = group % 2
        plans.append(
            Summed(
                place, BACK_PATHS[kind], view_of(m), core_boxes.at[slot, kind], [box.at[slot] for box in boxes[kind]],
                (send_sem.at[m], recv_sem.at[m]),
            )
        )

    def put(i, value):
        squares[i] = value.reshape(squares.shape[1:]).astype(LOW)

    small_out[...] = jnp.zeros_like(small_out)

    def norm_backward(state, inflow, gain_row, before, after):
        def body(at):
            hidden, flow, gain = state[at, :], inflow[at, :], table[gain_row : gain_row + 1, :]
            scale = lax.rsqrt(jnp.mean(hidden * hidden, axis=-1, keepdims=True) + EPSILON)
            unit = hidden * scale
            small_out[gain_row : gain_row + 1, :] += jnp.sum(flow * unit, axis=0, keepdims=True)
            flow = flow * gain
            flow = (flow - unit * jnp.mean(unit * flow, axis=-1, keepdims=True)) * scale
            after[at, :] = before[at, :].astype(FULL) + flow

        each(blocks, body)

    def outer_grads():
        get_og.wait()
        for q in range(4):
            get_act[q].wait()
            value = tn_dot(X[2 + q][...], og[...])
            outers[q // 2, q % 2] = value.reshape(outers.shape[2:]).astype(LOW)
        got["cross_context"] = load(saved["cross_context"], X[2])
        got["cross_queries"] = load(saved["cross_queries"], X[3])
        got["second_norm"] = load(saved["second_norm"], X[4])
        got["first_norm"] = load(saved["first_norm"], X[5])

    def inner_grads():
        get_tn.wait()
        eg = X[10]
        for q in range(4):
            get_wo[q].wait()
            get_slope[q].wait()
            out_w = wo[q % 2].reshape(width, width)
            eg[...] = (nt_dot(og[...], out_w) * X[6 + q][...].astype(FULL)).astype(LOW)
            if q + 2 < 4:
                get_wo.append(load(outer_chunk(q + 2), wo.at[q % 2]))
            put(q, tn_dot(tn[...], eg[...]))
            get_wi[q].wait()
            back = nt_dot(eg[...], flat(w.at[q % 2]))
            if q == 0:
                run_b[...] = back
            else:
                run_b[...] += back
            if q + 2 < 4:
                get_wi.append(load(inner_chunk(q + 2), w.at[q % 2]))
        got["so"] = load(wholes[3], w.at[0])
        got["q_w"] = load(wholes[0], w.at[1])
        got["encoder"] = load(encoder, pool.at[pl.ds(6, 2)])

    def cross_opening():
        get_table.wait()
        get_late.wait()
        norm_backward(run_c, run_b, 10, og, run_a)
        get_inverse = load(saved["cross_inverse"], run_c)
        branch = X[1]
        branch[...] = run_a[...].astype(LOW)
        got["cross_context"].wait()
        put(4, tn_dot(X[2][...], branch[...]))
        got["co"].wait()
        got["k_w"] = None
        get_inverse.wait()
        X[0][...] = (nt_dot(branch[...], flat(w.at[2])).astype(LOW).astype(FULL) * run_c[...]).astype(LOW)
        got["k_w"] = load(wholes[1], w.at[2])
        got["mid"] = load(saved["mid"], run_c)

    def weight_copy(source, index, slot, rows):
        return pltpu.make_async_copy(source.at[index], stage.at[slot, pl.ds(0, rows)], stage_sem.at[slot])

    def attention(weights, rows, key_rows, one, finish_pair):
        for s in range(seqs):
            weight_copy(weights, s * per_seq, s, key_rows).start()

        def body(p, _):
            lanes = pl.ds(pl.multiple_of(p * PAIR, PAIR), PAIR)
            results = []
            for s in range(seqs):
                index = s * per_seq + p
                weight_copy(weights, index, s, key_rows).wait()
                queries, keys, values, grad = one(s, lanes)
                results.append(
                    pair_backward(stage[s, pl.ds(0, key_rows)], queries, keys, values, grad, rows[index])
                )

                @pl.when(p + 1 < per_seq)
                def _():
                    weight_copy(weights, index + 1, s, key_rows).start()

            finish_pair(p, lanes, results)
            return 0

        lax.fori_loop(0, per_seq, body, 0)

    enc_length = pool.shape[1]

    def cross_attention():
        got["cross_rows"].wait()
        got["cross_queries"].wait()
        got["keys"].wait()
        got["values"].wait()

        def one(s, lanes):
            at = pl.ds(s * length, length)
            source = sources[s]
            return X[3][at, lanes], pairs_in[source, :, lanes], pairs_in[2 + source, :, lanes], X[0][at, lanes]

        def finish_pair(p, lanes, results):
            for s in range(seqs):
                X[1][pl.ds(s * length, length), lanes] = results[s][0].astype(LOW)
            for e in range(2):
                for target, part_at in ((8, 1), (11, 2)):
                    total = jnp.where(sources[0] == e, results[0][part_at], 0.0)
                    total = total + jnp.where(sources[1] == e, results[1][part_at], 0.0)
                    pool[target + e, :, lanes] = total.astype(LOW)

        attention(cross_weights, cross_rows, enc_length, one, finish_pair)
        got["queries"] = load(saved["queries"], X[11])
        got["keys"] = load(saved["keys"], X[12])
        got["values"] = load(saved["values"], X[13])
        got["self_context"] = load(saved["self_context"], X[14])

    def cross_grads():
        got["second_norm"].wait()
        put(5, tn_dot(X[4][...], X[1][...]))
        got["encoder"].wait()
        for i, target in ((6, 8), (7, 11)):
            put(i, tn_dot(pool[6], pool[target]) + tn_dot(pool[7], pool[target + 1]))

    def self_opening():
        got["cq_w"].wait()
        run_b[...] = nt_dot(X[1][...], flat(w.at[3]))
        got["v_w"] = load(wholes[2], w.at[3])
        got["mid"].wait()
        norm_backward(run_c, run_b, 9, run_a, run_a)
        get_inverse = load(saved["self_inverse"], run_c)
        branch = X[1]
        branch[...] = run_a[...].astype(LOW)
        got["self_context"].wait()
        put(8, tn_dot(X[14][...], branch[...]))
        got["so"].wait()
        get_inverse.wait()
        X[0][...] = (nt_dot(branch[...], flat(w.at[0])).astype(LOW).astype(FULL) * run_c[...]).astype(LOW)
        got["ck_w"] = load(wholes[5], w.at[0])
        got["start"] = load(saved["start"], run_c)

    def self_attention():
        for name in ("self_rows", "queries", "keys", "values"):
            got[name].wait()

        def one(s, lanes):
            at = pl.ds(s * length, length)
            return tuple(X[i][at, lanes] for i in (11, 12, 13, 0))

        def finish_pair(p, lanes, results):
            for s in range(seqs):
                for i in range(3):
                    X[2 + i][pl.ds(s * length, length), lanes] = results[s][i].astype(LOW)
            score_sum[p] = results[0][3].astype(FULL) + results[1][3].astype(FULL)

        attention(self_weights, self_rows, length, one, finish_pair)

    def self_grads():
        got["first_norm"].wait()
        for i in range(3):
            put(9 + i, tn_dot(X[5][...], X[2 + i][...]))

    stores = []

    def store(source, target):
        copy = pltpu.make_async_copy(source, target, store_sem.at[len(stores)])
        stores.append(copy)
        copy.start()

    def closing():
        for name in ("q_w", "k_w", "v_w", "start"):
            got[name].wait()
        run_b[...] = nt_dot(X[2][...], flat(w.at[1]))
        run_b[...] += nt_dot(X[3][...], flat(w.at[2]))
        run_b[...] += nt_dot(X[4][...], flat(w.at[3]))
        got["cv_w"] = load(wholes[6], w.at[1])
        norm_backward(run_c, run_b, 8, run_a, run_a)
        store(run_a, hidden_grad)
        for s in range(seqs):
            row = jnp.sum(run_a[pl.ds(s * length, length), :], axis=0, keepdims=True)
            for l in range(8):
                small_out[l : l + 1, :] += jnp.where(languages[s] == l, row, 0.0)

    def encoder_end():
        got["ck_w"].wait()
        got["cv_w"].wait()
        for e, run in ((0, run_b), (1, run_c)):
            run[...] = nt_dot(pool[8 + e], flat(w.at[0]))
            run[...] += nt_dot(pool[11 + e], flat(w.at[1]))
            store(run, encoder_grad.at[e])

    def bucket_sums():
        half = length // 2

        def pair(p, _):
            def bucket(c, _):
                here = ids[...] == c
                for h in range(2):
                    kept = jnp.where(here, score_sum[p, :, h * length : (h + 1) * length], 0.0)
                    lanes = jnp.sum(kept.reshape(length // 8, 8, length), axis=0)
                    row = jnp.sum(lanes[:, :half] + lanes[:, half:], axis=0, keepdims=True)
                    bucket_rows[pl.ds((2 * p + h) * 32 + c, 1), :] = row
                return 0

            return lax.fori_loop(0, 32, bucket, 0)

        lax.fori_loop(0, per_seq, pair, 0)
        ones = jnp.ones((8, 128), FULL)
        totals = lax.dot_general(
            ones, bucket_rows[...], (((1,), (1,)), ((), ())), precision=PRECISE, preferred_element_type=FULL
        )
        small_out[11:12, : bucket_rows.shape[0]] = totals[:1, :]

    small = []
    for dim in "cxyz":
        here, reach = place.at(dim), 1
        while reach < place.size(dim):
            small.append((dim, here + reach - 2 * reach * lax.rem(lax.div(here, reach), 2)))
            reach *= 2

    def small_copy(i):
        dim, partner = small[i]
        return pltpu.make_async_remote_copy(
            small_out, small_box.at[i], small_send.at[i], small_recv.at[i],
            device_id=place.device(dim, partner), device_id_type=MESH,
        )

    def small_step(i):
        def run():
            if i > 0:
                small_copy(i - 1).wait()
                small_out[...] += small_box[i - 1]
            if i < len(small):
                small_copy(i).start()

        return run

    tasks = {
        -1: [outer_grads],
        0: [inner_grads],
        1: [cross_opening],
        2: [cross_attention],
        3: [cross_grads],
        4: [self_opening],
        5: [self_attention, self_grads],
        6: [closing],
        7: [bucket_sums, small_step(0)],
        8: [encoder_end, small_step(1)],
        9: [small_step(2)],
        10: [small_step(3)],
        11: [small_step(4)],
        12: [small_step(5)],
    }
    steps = len(plans[0].stages)
    for task in tasks[-1]:
        task()
    for now in range(6 + steps + 1):
        for m, plan in enumerate(plans):
            step = now - 2 * (m // 4)
            if 1 <= step <= steps:
                plan.finish(step - 1)
            if 0 <= step < steps:
                plan.start(step)
        for task in tasks.get(now, ()):
            task()

    def into(ref, *index):
        def run(value):
            ref[index if index else ...] = value

        return run

    out_at = [into(outer_out, q) for q in range(4)]
    out_at += [into(inner_out, ALL, pl.ds(q * width, width)) for q in range(4)]
    out_at += [into(square_outs[i]) for i in (7, 4, 5, 6, 3, 0, 1, 2)]
    for plan, target in zip(plans, out_at):
        plan.close(target)
    for copy in stores:
        copy.wait()


def backward(sizes, output_grad, encoder_states, language_ids, source_index, bucket_ids, forward_outs):
    ny, nz = sizes
    grid = (ny, 2, nz, 2)
    tokens, width = output_grad.shape
    length = bucket_ids.shape[0]
    part = width // (ny * nz * 4)
    wholes, score_weights, saved = forward_outs[1:11], forward_outs[11:13], dict(zip(SAVED, forward_outs[13:]))
    enc_count, enc_length = encoder_states.shape[:2]
    anywhere = pl.BlockSpec(memory_space=pl.ANY)
    vmem = pl.BlockSpec(memory_space=pltpu.VMEM)
    smem = pl.BlockSpec(memory_space=pltpu.SMEM)
    lead = [box_shapes(sizes, path) for path in BACK_PATHS]
    slots = slot_count(sizes)
    hops = (ny * nz * 4).bit_length() - 1
    pairs = tokens // length * (width // PAIR)
    shapes = [(tokens, width), (enc_count, enc_length, width), (16, width)] + [(part, width)] * 8
    shapes += [(part, 4 * width), (4, part, width)]
    row = (tokens, width)
    outs = pl.pallas_call(
        functools.partial(backward_kernel, sizes, tuple(len(s) for s in lead)),
        out_shape=[jax.ShapeDtypeStruct(s, FULL) for s in shapes],
        in_specs=[anywhere, anywhere, smem, smem, vmem] + [anywhere] * (12 + len(SAVED)),
        out_specs=[anywhere, anywhere] + [vmem] * 11,
        scratch_shapes=[
            pltpu.VMEM((12,) + grid + (part, width), LOW),
            pltpu.VMEM(grid + (4, part, width), LOW),
            pltpu.VMEM((2, 4, ny, nz, 2, part, width), LOW),
        ]
        + [pltpu.VMEM((2,) + s + (part, width), LOW) for one in lead for s in one]
        + [
            pltpu.VMEM((hops, 16, width), FULL),
            pltpu.VMEM((13,) + row, LOW),
            pltpu.VMEM((4,) + row, LOW),
            pltpu.VMEM(row, FULL),
            pltpu.VMEM(row, FULL),
            pltpu.VMEM(row, FULL),
            pltpu.VMEM((4,) + grid + (part, width), LOW),
            pltpu.VMEM((2, nz, 2, 4, part, width), LOW),
            pltpu.VMEM((2, enc_length, 2 * length), LOW),
            pltpu.VMEM((width // PAIR, length, 2 * length), FULL),
            pltpu.VMEM((32 * H, 128), FULL),
            pltpu.VMEM((16, width), FULL),
            pltpu.VMEM((pairs, 1, 2 * length), FULL),
            pltpu.VMEM((pairs, 1, 2 * length), FULL),
            pltpu.SemaphoreType.DMA((16, slots)),
            pltpu.SemaphoreType.DMA((16, slots)),
            pltpu.SemaphoreType.DMA((hops,)),
            pltpu.SemaphoreType.DMA((hops,)),
            pltpu.SemaphoreType.DMA((48,)),
            pltpu.SemaphoreType.DMA((2,)),
            pltpu.SemaphoreType.DMA((4,)),
        ],
        compiler_params=pltpu.CompilerParams(
            collective_id=3, has_side_effects=True, vmem_limit_bytes=63 * 1024 * 1024
        ),
    )(
        output_grad, encoder_states, language_ids, source_index, bucket_ids.T, *wholes, *score_weights,
        *[saved[name] for name in SAVED],
    )
    start = (lax.axis_index("dp") * nz * 2 + lax.axis_index("fsdp")) * part
    total = outs[2]
    mine = lax.dynamic_slice(total, (0, start), (16, part))
    return (
        outs[0], outs[1], mine[:8], total[11, : 32 * H].reshape(H, 32).T, mine[8], mine[9], mine[10],
        outs[3:11], outs[11], outs[12].reshape(4 * part, width),
    )


def local_general(
    sizes,
    hidden_in,
    output_grad,
    encoder_states,
    language_ids,
    source_index,
    bucket_ids,
    language_table,
    bucket_table,
    self_gain,
    self_query,
    self_key,
    self_value,
    self_out,
    cross_gain,
    cross_query,
    cross_key,
    cross_value,
    cross_out,
    feed_gain,
    inner_weight,
    outer_weight,
):
    seq_count = language_ids.shape[0]
    length = bucket_ids.shape[0]
    tokens = seq_count * length
    enc_count = encoder_states.shape[0]
    enc_length = encoder_states.shape[1]
    width = hidden_in.shape[1]
    blocks = seq_count // SEQ_BLOCK
    (
        gain_one, gain_two, gain_three, table_whole, query_whole, key_whole, value_whole, out_whole,
        cquery_whole, ckey_whole, cvalue_whole, cout_whole, inner_whole, outer_whole,
    ) = gather_weights(
        sizes, language_table, (self_gain, cross_gain, feed_gain),
        (self_query, self_key, self_value, self_out, cross_query, cross_key, cross_value, cross_out),
        inner_weight, outer_weight,
    )

    def to_blocks(array, rows):
        return array.reshape(blocks, SEQ_BLOCK, rows, array.shape[-1])

    language_hot = (language_ids[:, None] == jnp.arange(table_whole.shape[0])[None, :]).astype(
        jnp.float32
    )
    language_rows = jnp.dot(language_hot, table_whole.astype(jnp.float32), precision=PRECISE)
    start_state = (
        hidden_in.astype(jnp.float32).reshape(seq_count, length, width) + language_rows[:, None, :]
    ).reshape(tokens, width)
    first_norm = to_low(norm_scale(start_state, gain_one.astype(jnp.float32)))
    self_queries = to_low(matmul(first_norm, query_whole))
    self_keys = to_low(matmul(first_norm, key_whole))
    self_values = to_low(matmul(first_norm, value_whole))
    bucket_hot = (
        bucket_ids[:, :, None] == jnp.arange(bucket_table.shape[0])[None, None, :]
    ).astype(jnp.float32)
    position_bias = jnp.einsum(
        "ijb,bh->hij", bucket_hot, bucket_table.astype(jnp.float32), precision=PRECISE
    )
    positions = jnp.arange(length)
    masked_bias = jnp.where(
        (positions[:, None] >= positions[None, :])[None], position_bias, NEGATIVE
    )

    def self_forward(block_items):
        return attend_forward(block_items[0], block_items[1], block_items[2], masked_bias)

    self_context, self_total = lax.map(
        self_forward,
        (
            to_blocks(self_queries, length),
            to_blocks(self_keys, length),
            to_blocks(self_values, length),
        ),
    )
    self_context = self_context.reshape(tokens, -1)
    mid_state = start_state + matmul(self_context, out_whole)
    second_norm = to_low(norm_scale(mid_state, gain_two.astype(jnp.float32)))
    cross_queries = to_low(matmul(second_norm, cquery_whole))
    encoder_flat = encoder_states.reshape(enc_count * enc_length, width)
    source_keys = to_low(matmul(encoder_flat, ckey_whole)).reshape(enc_count, enc_length, -1)
    source_values = to_low(matmul(encoder_flat, cvalue_whole)).reshape(enc_count, enc_length, -1)
    source_hot = (source_index[:, None] == jnp.arange(enc_count)[None, :]).astype(jnp.float32)
    source_low = to_low(source_hot)
    picked_keys = to_low(
        jnp.einsum("se,emc->smc", source_low, source_keys, preferred_element_type=jnp.float32)
    )
    picked_values = to_low(
        jnp.einsum("se,emc->smc", source_low, source_values, preferred_element_type=jnp.float32)
    )

    def cross_forward(block_items):
        return attend_forward(block_items[0], block_items[1], block_items[2], 0.0)

    cross_context, cross_total = lax.map(
        cross_forward,
        (
            to_blocks(cross_queries, length),
            picked_keys.reshape(blocks, SEQ_BLOCK, enc_length, -1),
            picked_values.reshape(blocks, SEQ_BLOCK, enc_length, -1),
        ),
    )
    cross_context = cross_context.reshape(tokens, -1)
    late_state = mid_state + matmul(cross_context, cout_whole)
    third_norm = to_low(norm_scale(late_state, gain_three.astype(jnp.float32)))
    expanded = matmul(third_norm, inner_whole)
    activated = to_low(jax.nn.gelu(expanded, approximate=True))
    hidden_out = (late_state + matmul(activated, outer_whole)).astype(jnp.bfloat16)
    top_grad = output_grad.astype(jnp.float32)
    outer_full = left_product(activated, output_grad)
    activated_grad = right_product(output_grad, outer_whole)
    gelu_value, gelu_back = jax.vjp(jax.nn.gelu, expanded)
    expanded_grad = to_low(gelu_back(activated_grad)[0])
    inner_full = left_product(third_norm, expanded_grad)
    third_grad = right_product(expanded_grad, inner_whole)
    norm_value, norm_back = jax.vjp(norm_scale, late_state, gain_three.astype(jnp.float32))
    state_back, feed_gain_full = norm_back(third_grad)
    late_grad = top_grad + state_back
    cross_low = to_low(late_grad)
    cout_full = left_product(cross_context, cross_low)
    cross_context_grad = to_low(right_product(cross_low, cout_whole))

    def cross_backward(block_items):
        return attend_backward(
            block_items[0],
            block_items[1],
            block_items[2],
            0.0,
            block_items[3],
            block_items[4],
            False,
        )

    cquery_part, ckey_part, cvalue_part = lax.map(
        cross_backward,
        (
            to_blocks(cross_queries, length),
            picked_keys.reshape(blocks, SEQ_BLOCK, enc_length, -1),
            picked_values.reshape(blocks, SEQ_BLOCK, enc_length, -1),
            cross_total,
            to_blocks(cross_context_grad, length),
        ),
    )
    cquery_low = to_low(cquery_part.reshape(tokens, -1))
    source_key_grad = to_low(
        jnp.einsum(
            "se,smc->emc",
            source_hot,
            ckey_part.reshape(seq_count, enc_length, -1),
            precision=PRECISE,
        ).reshape(enc_count * enc_length, -1)
    )
    source_value_grad = to_low(
        jnp.einsum(
            "se,smc->emc",
            source_hot,
            cvalue_part.reshape(seq_count, enc_length, -1),
            precision=PRECISE,
        ).reshape(enc_count * enc_length, -1)
    )
    cquery_full = left_product(second_norm, cquery_low)
    ckey_full = left_product(encoder_flat, source_key_grad)
    cvalue_full = left_product(encoder_flat, source_value_grad)
    encoder_grad = (
        right_product(source_key_grad, ckey_whole) + right_product(source_value_grad, cvalue_whole)
    ).reshape(enc_count, enc_length, width)
    second_grad = right_product(cquery_low, cquery_whole)
    norm_value, norm_back = jax.vjp(norm_scale, mid_state, gain_two.astype(jnp.float32))
    state_back, cross_gain_full = norm_back(second_grad)
    mid_grad = late_grad + state_back
    self_low = to_low(mid_grad)
    out_full = left_product(self_context, self_low)
    self_context_grad = to_low(right_product(self_low, out_whole))

    def self_backward(block_items):
        return attend_backward(
            block_items[0],
            block_items[1],
            block_items[2],
            masked_bias,
            block_items[3],
            block_items[4],
            True,
        )

    query_part, key_part, value_part, bias_part = lax.map(
        self_backward,
        (
            to_blocks(self_queries, length),
            to_blocks(self_keys, length),
            to_blocks(self_values, length),
            self_total,
            to_blocks(self_context_grad, length),
        ),
    )
    query_low = to_low(query_part.reshape(tokens, -1))
    key_low = to_low(key_part.reshape(tokens, -1))
    value_low = to_low(value_part.reshape(tokens, -1))
    table_full = jnp.einsum(
        "hij,ijb->bh", jnp.sum(bias_part, axis=0), bucket_hot, precision=PRECISE
    )
    query_full = left_product(first_norm, query_low)
    key_full = left_product(first_norm, key_low)
    value_full = left_product(first_norm, value_low)
    first_grad = (
        right_product(query_low, query_whole)
        + right_product(key_low, key_whole)
        + right_product(value_low, value_whole)
    )
    norm_value, norm_back = jax.vjp(norm_scale, start_state, gain_one.astype(jnp.float32))
    state_back, self_gain_full = norm_back(first_grad)
    hidden_in_grad = mid_grad + state_back
    sequence_sums = jnp.sum(hidden_in_grad.reshape(seq_count, length, width), axis=1)
    language_full = left_product(language_hot, sequence_sums)
    (
        language_part, bucket_table_grad, sgain_part, cgain_part, feed_gain_part, whole_parts, inner_part, outer_part,
    ) = reduce_grads(
        sizes, language_full, table_full, (self_gain_full, cross_gain_full, feed_gain_full),
        (query_full, key_full, value_full, out_full, cquery_full, ckey_full, cvalue_full, cout_full),
        inner_full, outer_full,
    )
    query_sum, key_sum, value_sum, out_part, cquery_part_sum, ckey_part_sum, cvalue_part_sum, cout_part = whole_parts
    return (
        hidden_out,
        hidden_in_grad,
        encoder_grad,
        language_part,
        bucket_table_grad,
        sgain_part,
        query_sum,
        key_sum,
        value_sum,
        out_part,
        cgain_part,
        cquery_part_sum,
        ckey_part_sum,
        cvalue_part_sum,
        cout_part,
        feed_gain_part,
        inner_part,
        outer_part,
    )


def local(sizes, *args):
    if sizes == (2, 4) and args[8].shape[0] % 8 == 0:
        return local_fused(sizes, *args)
    return local_general(sizes, *args)


def local_fused(
    sizes, hidden_in, output_grad, encoder_states, language_ids, source_index, bucket_ids, language_table,
    bucket_table, self_gain, self_query, self_key, self_value, self_out, cross_gain, cross_query, cross_key,
    cross_value, cross_out, feed_gain, inner_weight, outer_weight,
):
    kept = forward(
        sizes, hidden_in, encoder_states, language_ids, source_index, bucket_ids, language_table, bucket_table,
        (self_gain, cross_gain, feed_gain),
        (self_query, self_key, self_value, self_out, cross_query, cross_key, cross_value, cross_out),
        inner_weight, outer_weight,
    )
    (
        hidden_grad, encoder_grad, language_part, bucket_grad, gain_one, gain_two, gain_three, squares, inner, outer,
    ) = backward(sizes, output_grad, encoder_states, language_ids, source_index, bucket_ids, kept)
    return (
        kept[0], hidden_grad, encoder_grad, language_part, bucket_grad, gain_one, *squares[:4], gain_two,
        *squares[4:], gain_three, inner, outer,
    )


def solution(mesh):
    sizes = (mesh.shape["dp"] // 2, mesh.shape["fsdp"] // 2)
    in_specs = (
        P(("dp", "fsdp"), None),
        P(("dp", "fsdp"), None),
        P(("dp", "fsdp"), None, None),
        P(("dp", "fsdp")),
        P(("dp", "fsdp")),
        P(),
        P(None, ("dp", "fsdp")),
        P(),
        P(("dp", "fsdp")),
        P(("dp", "fsdp"), None),
        P(("dp", "fsdp"), None),
        P(("dp", "fsdp"), None),
        P(("dp", "fsdp"), None),
        P(("dp", "fsdp")),
        P(("dp", "fsdp"), None),
        P(("dp", "fsdp"), None),
        P(("dp", "fsdp"), None),
        P(("dp", "fsdp"), None),
        P(("dp", "fsdp")),
        P(("dp", "fsdp"), None),
        P(("dp", "fsdp"), None),
    )
    out_specs = (
        P(("dp", "fsdp"), None),
        P(("dp", "fsdp"), None),
        P(("dp", "fsdp"), None, None),
        P(None, ("dp", "fsdp")),
        P(),
        P(("dp", "fsdp")),
        P(("dp", "fsdp"), None),
        P(("dp", "fsdp"), None),
        P(("dp", "fsdp"), None),
        P(("dp", "fsdp"), None),
        P(("dp", "fsdp")),
        P(("dp", "fsdp"), None),
        P(("dp", "fsdp"), None),
        P(("dp", "fsdp"), None),
        P(("dp", "fsdp"), None),
        P(("dp", "fsdp")),
        P(("dp", "fsdp"), None),
        P(("dp", "fsdp"), None),
    )
    return jax.shard_map(functools.partial(local, sizes), mesh=mesh, in_specs=in_specs, out_specs=out_specs, check_vma=False)
```

```python
import functools

import jax
import jax.numpy as jnp
from jax import lax
from jax.experimental import pallas as pl
from jax.experimental.pallas import tpu as pltpu
from jax.sharding import PartitionSpec as P

H = 12
HEAD = 64
SEQ_BLOCK = 2


EPSILON = 1e-06
PRECISE = lax.Precision.HIGHEST
NEGATIVE = -1e30


def to_low(value):
    return value.astype(jnp.bfloat16)


def norm_scale(hidden, gain):
    return hidden * lax.rsqrt(jnp.mean(hidden * hidden, axis=-1, keepdims=True) + EPSILON) * gain


def matmul(left, right):
    return jnp.dot(left, right, preferred_element_type=jnp.float32)


def left_product(left, right):
    return lax.dot_general(
        left, right, (((0,), (0,)), ((), ())), preferred_element_type=jnp.float32
    )


def right_product(left, right):
    return lax.dot_general(
        left, right, (((1,), (1,)), ((), ())), preferred_element_type=jnp.float32
    )


def split_heads(array):
    return array.reshape(array.shape[:-1] + (H, HEAD))


def score_block(queries, key_rows, offset):
    scores = jnp.einsum(
        "sqhe,skhe->shqk",
        split_heads(queries),
        split_heads(key_rows),
        preferred_element_type=jnp.float32,
    )
    return scores + offset


def attend_forward(queries, key_rows, value_rows, offset):
    scores = score_block(queries, key_rows, offset)
    top_score = jnp.max(scores, axis=-1, keepdims=True)
    log_total = top_score + jnp.log(jnp.sum(jnp.exp(scores - top_score), axis=-1, keepdims=True))
    weights = to_low(jnp.exp(scores - log_total))
    context = jnp.einsum(
        "shqk,skhe->sqhe", weights, split_heads(value_rows), preferred_element_type=jnp.float32
    )
    return (to_low(context).reshape(queries.shape), log_total)


def attend_backward(queries, key_rows, value_rows, offset, log_total, context_grad, with_bias):
    scores = score_block(queries, key_rows, offset)
    probs = jnp.exp(scores - log_total)
    weights = to_low(probs)
    grad_heads = split_heads(context_grad)
    value_grad = jnp.einsum(
        "shqk,sqhe->skhe", weights, grad_heads, preferred_element_type=jnp.float32
    )
    prob_grad = jnp.einsum(
        "sqhe,skhe->shqk", grad_heads, split_heads(value_rows), preferred_element_type=jnp.float32
    )
    score_grad = to_low(probs * (prob_grad - jnp.sum(probs * prob_grad, axis=-1, keepdims=True)))
    query_grad = jnp.einsum(
        "shqk,skhe->sqhe", score_grad, split_heads(key_rows), preferred_element_type=jnp.float32
    )
    key_grad = jnp.einsum(
        "shqk,sqhe->skhe", score_grad, split_heads(queries), preferred_element_type=jnp.float32
    )
    grads = (
        query_grad.reshape(queries.shape),
        key_grad.reshape(key_rows.shape),
        value_grad.reshape(value_rows.shape),
    )
    if with_bias:
        return grads + (jnp.sum(score_grad.astype(jnp.float32), axis=0),)
    return grads


MESH = pl.DeviceIdType.MESH
ALL = slice(None)


class Place:
    def __init__(self, sizes):
        self.ny, self.nz = sizes
        self.dp = lax.axis_index("dp")
        self.fs = lax.axis_index("fsdp")
        self.c, self.y = lax.rem(self.dp, 2), lax.div(self.dp, 2)
        self.x, self.z = lax.rem(self.fs, 2), lax.div(self.fs, 2)

    def size(self, dim):
        return {"c": 2, "x": 2, "y": self.ny, "z": self.nz}[dim]

    def at(self, dim):
        return {"c": self.c, "x": self.x, "y": self.y, "z": self.z}[dim]

    def device(self, dim, index):
        if dim == "c":
            return (self.y * 2 + index, self.fs)
        if dim == "y":
            return (index * 2 + self.c, self.fs)
        if dim == "x":
            return (self.dp, self.z * 2 + index)
        return (self.dp, index * 2 + self.x)


def neighbour_barrier(place, far=False):
    barrier = pltpu.get_barrier_semaphore()
    links = []
    for dim in "cxyz":
        here, size = place.at(dim), place.size(dim)
        reach = 1
        while reach < size and (reach == 1 or far):
            if size == 2:
                links.append((dim, 1 - here, None))
            elif reach == 1:
                for step in (1, -1):
                    links.append((dim, here + step, (here + step >= 0) & (here + step < size)))
            else:
                links.append((dim, here + reach - 2 * reach * lax.rem(lax.div(here, reach), 2), None))
            reach *= 2

    def signal(dim, there):
        pl.semaphore_signal(barrier, inc=1, device_id=place.device(dim, there), device_id_type=MESH)

    for dim, there, condition in links:
        if condition is None:
            signal(dim, there)
        else:
            pl.when(condition)(lambda dim=dim, there=there: signal(dim, there))
    peers = sum(1 if condition is None else condition.astype(jnp.int32) for _, _, condition in links)
    pl.semaphore_wait(barrier, peers)


PATHS = ("zxy", "zyx", "xzy", "yzx")


class Link:
    def __init__(self, copy, sends=None, receives=None):
        self.copy, self.sends, self.receives = copy, sends, receives

    @staticmethod
    def when(condition, run):
        if condition is None:
            run()
        else:
            pl.when(condition)(run)

    def start(self):
        self.when(self.sends, lambda: self.copy.start())

    def wait_send(self):
        self.when(self.sends, lambda: self.copy.wait_send())

    def wait_recv(self):
        self.when(self.receives, lambda: self.copy.wait_recv())


def pick(held, place, **fixed):
    return tuple(fixed.get(dim, ALL if dim in held else place.at(dim)) for dim in "yczx")


def gather_steps(place, blocks, path, sems):
    steps, slot, held = [], 0, ""
    for dim in path + "c":
        here, size = place.at(dim), place.size(dim)
        if size == 2:
            there = 1 - here
            index = pick(held, place)
            copy = pltpu.make_async_remote_copy(
                blocks(index), blocks(index), sems[0].at[slot], sems[1].at[slot],
                device_id=place.device(dim, there), device_id_type=MESH,
            )
            steps.append([Link(copy)])
            slot += 1
        else:
            for hop in range(1, size):
                links = []
                for way in (1, -1):
                    origin = here - way * (hop - 1)
                    there = here + way
                    source = here - way * hop
                    index = pick(held, place, **{dim: jnp.clip(origin, 0, size - 1)})
                    copy = pltpu.make_async_remote_copy(
                        blocks(index), blocks(index), sems[0].at[slot], sems[1].at[slot],
                        device_id=place.device(dim, jnp.clip(there, 0, size - 1)), device_id_type=MESH,
                    )
                    sends = (origin >= 0) & (origin < size) & (there >= 0) & (there < size)
                    links.append(Link(copy, sends, (source >= 0) & (source < size)))
                    slot += 1
                steps.append(links)
        held += dim
    return steps


def slot_count(sizes):
    ny, nz = sizes
    return 2 + (1 if ny == 2 else 2 * (ny - 1)) + (1 if nz == 2 else 2 * (nz - 1))


def run_steps(plans, lag):
    rounds = max(lag[i] + len(plan) for i, plan in enumerate(plans)) + 1
    for now in range(rounds):
        for offset, plan in zip(lag, plans):
            at = now - offset
            if 1 <= at <= len(plan):
                for link in plan[at - 1]:
                    link.wait_recv()
            if 0 <= at < len(plan):
                for link in plan[at]:
                    link.start()
    for plan in plans:
        for links in plan:
            for link in links:
                link.wait_send()


def gather_kernel(sizes, *refs):
    shards, wholes = refs[:11], refs[11:22]
    own_sem, send_sem, recv_sem = refs[22:]
    place = Place(sizes)
    own = (place.y, place.c, place.z, place.x)
    owns = [
        pltpu.make_async_copy(shard, whole.at[own], own_sem.at[i])
        for i, (shard, whole) in enumerate(zip(shards, wholes))
    ]
    for copy in owns:
        copy.start()
    neighbour_barrier(place)
    views = [lambda index, ref=ref: ref.at[index] for ref in wholes[:9]]
    width = wholes[8].shape[-1]
    for q in range(4):
        views.append(
            lambda index, q=q: wholes[9].at[index + (ALL, pl.ds(q * width, width))]
        )
    for q in range(4):
        views.append(lambda index, q=q: wholes[10].at[index + (q,)])
    plans, lag = [], []
    for i, view in enumerate(views):
        path = PATHS[0] if i == 0 else PATHS[(i - 1) % 4]
        plans.append(gather_steps(place, view, path, (send_sem.at[i], recv_sem.at[i])))
        lag.append(0 if i == 0 else 3 * ((i - 1) // 4))
    for copy in owns:
        copy.wait()
    run_steps(plans, lag)


def gather_weights(sizes, table, gains, squares, inner, outer):
    ny, nz = sizes
    grid = (ny, 2, nz, 2)
    part, width = squares[0].shape
    small = jnp.zeros((16, 128), table.dtype)
    small = small.at[: table.shape[0], :part].set(table)
    for i, gain in enumerate(gains):
        small = small.at[table.shape[0] + i, :part].set(gain)
    shards = (small,) + tuple(squares) + (inner, outer.reshape(4, part, width))
    anywhere = pl.BlockSpec(memory_space=pl.ANY)
    slots = slot_count(sizes)
    wholes = pl.pallas_call(
        functools.partial(gather_kernel, sizes),
        out_shape=[jax.ShapeDtypeStruct(grid + s.shape, s.dtype) for s in shards],
        in_specs=[anywhere] * 11,
        out_specs=[anywhere] * 11,
        scratch_shapes=[
            pltpu.SemaphoreType.DMA((11,)),
            pltpu.SemaphoreType.DMA((17, slots)),
            pltpu.SemaphoreType.DMA((17, slots)),
        ],
        compiler_params=pltpu.CompilerParams(collective_id=0, has_side_effects=True),
    )(*shards)
    count = ny * nz * 4
    tiny = wholes[0].reshape(count, 16, 128)[:, :, :part].transpose(1, 0, 2).reshape(16, count * part)
    rows = table.shape[0]
    return (
        (tiny[rows], tiny[rows + 1], tiny[rows + 2], tiny[:rows])
        + tuple(w.reshape(count * part, width) for w in wholes[1:9])
        + (wholes[9].reshape(count * part, 4 * width), wholes[10].reshape(4 * count * part, width))
    )


class Reduce:
    def __init__(self, place, path, source, total, core_in, boxes, out, sems):
        self.place, self.path, self.source, self.total = place, path, source, total
        self.core_in, self.boxes, self.out, self.sems = core_in, boxes, out, sems
        self.slot = 0
        self.sent = []

    def copy(self, source, target, dim, there):
        slot = self.slot
        self.slot += 1
        return pltpu.make_async_remote_copy(
            source, target, self.sems[0].at[slot], self.sems[1].at[slot],
            device_id=self.place.device(dim, there), device_id_type=MESH,
        )

    def index(self, fixed):
        return tuple(fixed.get(dim, ALL) for dim in "yzx")

    def add(self, target, box):
        shape = box.shape[:-2]
        count = 1
        for size in shape:
            count *= size
        free = [i for i, entry in enumerate(target) if entry is ALL]

        def body(n, _):
            spots, rest = [], n
            for size in reversed(shape):
                spots.append(lax.rem(rest, size))
                rest = lax.div(rest, size)
            spots = spots[::-1]
            full = list(target)
            for place_at, spot in zip(free, spots):
                full[place_at] = spot
            mine = self.total[tuple(full)].astype(jnp.float32)
            got = box[tuple(spots)].astype(jnp.float32)
            self.total[tuple(full)] = (mine + got).astype(jnp.bfloat16)
            return 0

        if count == 1:
            body(0, 0)
        else:
            lax.fori_loop(0, count, body, 0)

    def steps(self):
        place, listing = self.place, []
        own = pltpu.make_async_copy(self.source(place.c), self.total, self.sems[2])
        core = self.copy(self.source(1 - place.c), self.core_in, "c", 1 - place.c)

        def start():
            own.start()
            core.start()

        def finish():
            own.wait()
            core.wait_recv()
            self.add((ALL, ALL, ALL), self.core_in)

        self.sent.append(Link(core))
        listing.append((start, finish))
        fixed, box = {}, 0
        for dim in self.path:
            here, size = place.at(dim), place.size(dim)
            if size == 2:
                target = self.index({**fixed, dim: 1 - here})
                link = Link(self.copy(self.total.at[target], self.boxes[box], dim, 1 - here))
                self.sent.append(link)
                listing.append(self.pair([link], [(self.index({**fixed, dim: here}), box, None)]))
                box += 1
            else:
                for hop in range(size - 1, 0, -1):
                    links, adds = [], []
                    for way in (1, -1):
                        there = here - way
                        goal = here - way * hop
                        sends = (goal >= 0) & (goal < size)
                        source = here + way
                        got = source - way * hop
                        receives = (source >= 0) & (source < size) & (got >= 0) & (got < size)
                        target = self.index({**fixed, dim: jnp.clip(goal, 0, size - 1)})
                        copy = self.copy(
                            self.total.at[target], self.boxes[box], dim, jnp.clip(there, 0, size - 1)
                        )
                        link = Link(copy, sends, receives)
                        self.sent.append(link)
                        links.append(link)
                        adds.append((self.index({**fixed, dim: jnp.clip(got, 0, size - 1)}), box, receives))
                        box += 1
                    listing.append(self.pair(links, adds))
            fixed = {**fixed, dim: here}
        return listing

    def pair(self, links, adds):
        def start():
            for link in links:
                link.start()

        def finish():
            for link in links:
                link.wait_recv()
            for target, box, condition in adds:
                Link.when(condition, functools.partial(self.add, target, self.boxes[box]))

        return start, finish

    def close(self):
        own = (self.place.y, self.place.z, self.place.x)
        self.out(self.total[own].astype(jnp.float32))
        for link in self.sent:
            link.wait_send()


def box_shapes(sizes, path):
    ny, nz = sizes
    size = {"y": ny, "z": nz, "x": 2}
    left, shapes = "yzx", []
    for dim in path:
        left = left.replace(dim, "")
        lead = tuple(size[d] for d in left)
        shapes += [lead] * (1 if size[dim] == 2 else 2 * (size[dim] - 1))
    return shapes


BACK_PATHS = tuple(path[::-1] for path in PATHS)


def reduce_kernel(sizes, box_counts, *refs):
    sources, small_in = refs[:10], refs[10]
    outs, small_out = refs[11:21], refs[21]
    totals, core_boxes = refs[22], refs[23]
    at = 24
    boxes = []
    for count in box_counts:
        boxes.append(refs[at : at + count])
        at += count
    small_box, own_sem, send_sem, recv_sem, small_send, small_recv = refs[at:]
    place = Place(sizes)
    neighbour_barrier(place, far=True)
    width = outs[0].shape[-1]

    def square(ref):
        return lambda core: ref.at[:, core]

    def inner(q):
        return lambda core: sources[8].at[:, core, :, :, :, pl.ds(q * width, width)]

    def outer(q):
        return lambda core: sources[9].at[:, core, :, :, q]

    views = [inner(q) for q in range(4)] + [outer(q) for q in range(4)]
    views += [square(sources[i]) for i in (4, 5, 6, 7, 0, 1, 2, 3)]

    def store_square(i):
        def run(value):
            outs[i][...] = value

        return run

    def store_inner(q):
        def run(value):
            outs[8][:, q * width : (q + 1) * width] = value

        return run

    def store_outer(q):
        def run(value):
            outs[9][q] = value

        return run

    stores = [store_inner(q) for q in range(4)] + [store_outer(q) for q in range(4)]
    stores += [store_square(i) for i in (4, 5, 6, 7, 0, 1, 2, 3)]
    plans, lag = [], []
    reduces = []
    for m in range(16):
        group, kind = m // 4, m % 4
        reduce = Reduce(
            place, BACK_PATHS[kind], views[m], totals.at[m], core_boxes.at[m],
            [box.at[group] for box in boxes[kind]], stores[m],
            (send_sem.at[m], recv_sem.at[m], own_sem.at[m]),
        )
        reduces.append(reduce)
        plans.append(reduce.steps())
        lag.append(3 * group)
    small_out[...] = small_in[...]
    small = []
    moves = [("c", 1 - place.c), ("x", 1 - place.x), ("y", None), ("z", None)]
    for dim, there in moves:
        size, here, reach = place.size(dim), place.at(dim), 1
        while reach < size:
            partner = here + reach - 2 * reach * lax.rem(lax.div(here, reach), 2)
            small.append((dim, partner))
            reach *= 2
    rounds = max(max(lag[i] + len(plan) for i, plan in enumerate(plans)) + 1, len(small) + 1)
    copies = []
    for now in range(rounds):
        for offset, plan in zip(lag, plans):
            step = now - offset
            if 1 <= step <= len(plan):
                plan[step - 1][1]()
            if 0 <= step < len(plan):
                plan[step][0]()
        if 1 <= now <= len(small):
            copies[-1].wait()
            small_out[...] += small_box[now - 1]
        if now < len(small):
            dim, partner = small[now]
            copies.append(
                pltpu.make_async_remote_copy(
                    small_out, small_box.at[now], small_send.at[now], small_recv.at[now],
                    device_id=place.device(dim, partner), device_id_type=MESH,
                )
            )
            copies[-1].start()
    for reduce in reduces:
        reduce.close()


def reduce_grads(sizes, language, bucket, gains, squares, inner, outer):
    ny, nz = sizes
    grid = (ny, 2, nz, 2)
    count = ny * nz * 4
    width = squares[0].shape[1]
    part = squares[0].shape[0] // count
    langs = language.shape[0]
    flat = jnp.zeros((width,), jnp.float32).at[: bucket.size].set(bucket.reshape(-1))
    small = jnp.concatenate(
        [language] + [g.reshape(1, width) for g in gains] + [flat[None], jnp.zeros((4, width), jnp.float32)], axis=0
    )
    sources = [to_low(s).reshape(grid + (part, width)) for s in squares]
    sources += [
        to_low(inner).reshape(grid + (part, 4 * width)),
        to_low(outer).reshape(grid + (4, part, width)),
    ]
    anywhere = pl.BlockSpec(memory_space=pl.ANY)
    vmem = pl.BlockSpec(memory_space=pltpu.VMEM)
    shapes = [(part, width)] * 8 + [(part, 4 * width), (4, part, width), small.shape]
    lead = [box_shapes(sizes, path) for path in BACK_PATHS]
    slots = slot_count(sizes)
    hops = (ny * nz * 4).bit_length() - 1
    outs = pl.pallas_call(
        functools.partial(reduce_kernel, sizes, tuple(len(s) for s in lead)),
        out_shape=[jax.ShapeDtypeStruct(s, jnp.float32) for s in shapes],
        in_specs=[anywhere] * 10 + [vmem],
        out_specs=[vmem] * 11,
        scratch_shapes=[
            pltpu.VMEM((16, ny, nz, 2, part, width), jnp.bfloat16),
            pltpu.VMEM((16, ny, nz, 2, part, width), jnp.bfloat16),
        ]
        + [pltpu.VMEM((4,) + s + (part, width), jnp.bfloat16) for one in lead for s in one]
        + [
            pltpu.VMEM((hops,) + small.shape, jnp.float32),
            pltpu.SemaphoreType.DMA((16,)),
            pltpu.SemaphoreType.DMA((16, slots)),
            pltpu.SemaphoreType.DMA((16, slots)),
            pltpu.SemaphoreType.DMA((hops,)),
            pltpu.SemaphoreType.DMA((hops,)),
        ],
        compiler_params=pltpu.CompilerParams(
            collective_id=1, has_side_effects=True, vmem_limit_bytes=60 * 1024 * 1024
        ),
    )(*sources, small)
    start = (lax.axis_index("dp") * nz * 2 + lax.axis_index("fsdp")) * part
    total = outs[10]
    mine = lax.dynamic_slice(total, (0, start), (langs + 3, part))
    return (
        mine[:langs],
        total[langs + 3, : bucket.size].reshape(bucket.shape),
        mine[langs], mine[langs + 1], mine[langs + 2],
        outs[:8], outs[8], outs[9].reshape(4 * part, width),
    )


FORWARD_PATHS = (
    "yzx", "zxy", "zxy", "zyx", "xzy", "zyx", "zxy", "zyx", "xyz", "yzx", "yxz", "zyx", "zyx", "xzy", "yxz",
    "zxy", "zxy",
)
FORWARD_ORDER = (
    3, 4, 0, 8, 14, 2, 10, 7, 13, 3, 2, 14, 9, 10, 8, 12, 3, 3, 5, 2, 7, 2, 7, 12, 0, 7, 1, 5, 4, 3, 0, 2, 5, 6,
    11, 1, 1, 0, 11, 1, 0, 6, "bias", 5, 16, 6, 2, 9, 6, 16, 4, 1, 13, 11, 0, 3, 15, 5, 0, 9, 2, 16, 3, 7,
    "open", 11, 4, "k", 13, 6, 1, 12, 9, 10, 15, "v", 16, 5, 8, 4, 1, "q", 13, "sa0", "sa1", 7, 11, 15, "sa2",
    14, 12, 5, 7, "V", 13, 16, 15, 4, 10, 8, 9, 6, "sa3", 12, 4, "send", 11, 6, 10, "cq", "K", "ca0", 8, 9,
    "ca1", 10, 14, 11, 9, "ca2", 8, 13, 16, 15, 10, "ca3", 8, 14, "cend", 12, "in0", "og0", 15, "in1", 12,
    "in2", 15, 14, "og1", "in3", "og3", 13, "og2", 14, 16,
)
BACKWARD_ORDER = (
    0, 1, 3, 2, "in0", "in1", 1, 0, "in2", "in3", 4, 2, "n3", 7, 6, "co", 3, "ccg", 0, 4, "ca0", 8, 7, 6, 3, 2,
    "ca1", 5, 1, "ca2", 7, "cv", 0, 6, 5, 8, "cq", 0, 11, "n2", "so", 2, 4, "scg", 3, 7, 9, "sa0", 2, 5, 3, 0,
    11, 7, 12, "sa1", "sa2", 4, "v", 15, 5, "k", 14, 3, 8, 7, 5, 6, "ck", 11, 14, 10, 15, 1, 9, "q", 5, 6, 8, 0,
    4, 13, 11, 10, 1, "close", 4, 15, 6, 12, 8, 11, 14, "bucket", 2, 1, 10, 15, 13, 16, 9, 14, "hid", 1, 10, 15,
    4, 5, 16, 2, 7, 3, 6, 12, 9, 13, 10, 14, 16, 9, "enc", 13, 12, 8, 11, 16, 13, 15, 12, 10, 8, 9, 16, 13, 14,
    10, 12, 14, 9, 15, 11, 16, 13, 12,
)


LOW = jnp.bfloat16
FULL = jnp.float32
PAIR = 2 * HEAD


def nt_dot(left, right):
    return lax.dot_general(left, right, (((1,), (1,)), ((), ())), preferred_element_type=FULL)


def tn_dot(left, right):
    return lax.dot_general(left, right, (((0,), (0,)), ((), ())), preferred_element_type=FULL)


def flat(ref, *suffix):
    value = ref[(ALL,) * (len(ref.shape) - 1) + suffix] if suffix else ref[...]
    rows = 1
    for size in value.shape[:-1]:
        rows *= size
    return value.reshape(rows, value.shape[-1])


def each(count, body):
    def run(i, _):
        body(pl.ds(pl.multiple_of(i * 128, 128), 128))
        return 0

    lax.fori_loop(0, count, run, 0)


def unit_rows(hidden):
    return hidden * lax.rsqrt(jnp.mean(hidden * hidden, axis=-1, keepdims=True) + EPSILON)


def spread_small(tiny, table):
    part = table.shape[1] // (tiny.shape[0] * tiny.shape[2] * 4)
    table[...] = jnp.zeros_like(table)
    lane = lax.broadcasted_iota(jnp.int32, (16, 128), 1)
    at = 0
    for y in range(tiny.shape[0]):
        for core in range(2):
            for z in range(tiny.shape[2]):
                for x in range(2):
                    slab = jnp.where(lane < part, tiny[y, core, z, x].astype(FULL), 0.0)
                    base, shift = at // 128 * 128, at % 128
                    if shift:
                        slab = pltpu.roll(slab, shift, 1)
                    if shift + part <= 128:
                        table[:, base : base + 128] += slab
                    else:
                        table[:, base : base + 128] += jnp.where(lane >= part, slab, 0.0)
                        table[:, base + 128 : base + 256] += jnp.where(lane < part, slab, 0.0)
                    at += part


def build_bias(ids, values, bias):
    heads, keys, queries = bias.shape
    rows = 32

    def block(n, _):
        at = pl.ds(pl.multiple_of(n * rows, rows), rows)
        bucket = ids[at, :]
        bits = [lax.bitwise_and(bucket, 1 << b) != 0 for b in range(5)]
        key = n * rows + lax.broadcasted_iota(jnp.int32, (rows, queries), 0)
        query = lax.broadcasted_iota(jnp.int32, (rows, queries), 1)
        hidden = key > query

        def head(h, _):
            level = [values[h, c] for c in range(32)]
            for bit in bits:
                level = [jnp.where(bit, level[i + 1], level[i]) for i in range(0, len(level), 2)]
            bias[h, at, :] = jnp.where(hidden, NEGATIVE, level[0]).astype(LOW)
            return 0

        return lax.fori_loop(0, heads, head, 0)

    lax.fori_loop(0, keys // rows, block, 0)


def head_pair(value):
    lane = lax.broadcasted_iota(jnp.int32, value.shape, 1)
    zero = jnp.zeros_like(value)
    return jnp.concatenate([jnp.where(lane < HEAD, value, zero), jnp.where(lane < HEAD, zero, value)], axis=0)


def pair_forward(queries, keys, values, offset, weights, inverse_row):
    count = queries.shape[0]
    scores = nt_dot(keys, head_pair(queries))
    if offset is not None:
        scores = scores + offset
    grown = jnp.exp(scores - jnp.max(scores, axis=0, keepdims=True))
    inverse_row[...] = 1.0 / jnp.sum(grown, axis=0, keepdims=True)
    low = grown.astype(LOW)
    weights[...] = low
    lane = lax.broadcasted_iota(jnp.int32, values.shape, 1)
    one = jnp.ones_like(values)
    first = tn_dot(low[:, :count], jnp.where(lane < HEAD, values, one))
    second = tn_dot(low[:, count:], jnp.where(lane < HEAD, one, values))
    lane = lax.broadcasted_iota(jnp.int32, first.shape, 1)
    total = pltpu.roll(jnp.where(lane < HEAD, second, first), HEAD, 1)
    inverse = 1.0 / total
    return jnp.where(lane < HEAD, first, second) * inverse, inverse


def gelu_parts(u):
    a, b = 0.7978845608028654, 0.044715
    square = u * u
    t = jnp.tanh(a * u * (1.0 + b * square))
    half = 0.5 * (1.0 + t)
    slope = half + 0.5 * u * (1.0 - t * t) * (a * (1.0 + 3.0 * b * square))
    return u * half, slope


def gather_plans(place, wholes, small, sems):
    views = [lambda index, ref=ref: ref.at[index] for ref in [small] + list(wholes[:8])]
    width = wholes[0].shape[-1]
    for q in range(4):
        views.append(lambda index, q=q: wholes[8].at[index + (ALL, pl.ds(q * width, width))])
    for q in range(4):
        views.append(lambda index, q=q: wholes[9].at[index + (q,)])
    return [
        gather_steps(place, view, path, (sems[0].at[i], sems[1].at[i]))
        for i, (view, path) in enumerate(zip(views, FORWARD_PATHS))
    ]


def run_order(order, plans, tasks):
    at = [0] * len(plans)
    for entry in order:
        if isinstance(entry, str):
            tasks[entry]()
            continue
        step, plan = at[entry], plans[entry]
        at[entry] += 1
        if step >= 1:
            for link in plan[step - 1]:
                link.wait_recv()
        if step < len(plan):
            for link in plan[step]:
                link.start()


SAVED = (
    "first_norm", "queries", "keys", "values", "self_context", "second_norm", "cross_queries",
    "source_keys", "source_values", "cross_context", "third_norm", "activated", "slope",
    "start", "mid", "late", "self_inverse", "cross_inverse", "self_rows", "cross_rows", "table",
)


def saved_shapes(tokens, sources, width, length):
    low, full = LOW, FULL
    row = (tokens, width)
    pairs = tokens // length * (width // PAIR)
    shapes = {name: (row, low) for name in SAVED}
    shapes["source_keys"] = shapes["source_values"] = ((2, sources // 2, width), low)
    shapes["activated"] = shapes["slope"] = ((4,) + row, low)
    for name in ("start", "mid", "late", "self_inverse", "cross_inverse"):
        shapes[name] = (row, full)
    shapes["self_rows"] = shapes["cross_rows"] = ((pairs, 1, 2 * length), full)
    shapes["table"] = ((16, width), full)
    return shapes


def forward_kernel(sizes, *refs):
    n = len(SAVED)
    small_shard, shards = refs[0], refs[1:11]
    hidden, upstream, encoder, languages, sources, ids, bucket_values = refs[11:18]
    outer_grads, whole_outs = refs[18], refs[19:29]
    self_weights, cross_weights = refs[29:31]
    saved_outs = dict(zip(SAVED, refs[31 : 31 + n]))
    at = 31 + n
    tiny, wholes = refs[at], refs[at + 1 : at + 11]
    at += 11
    v = dict(zip(SAVED, refs[at : at + n]))
    at += n
    bias, stage, outer_blocks = refs[at : at + 3]
    own_sem, send_sem, recv_sem, out_sem, stage_sem, hidden_sem = refs[at + 3 :]
    tokens, width = hidden.shape
    length = ids.shape[0]
    per_seq = width // PAIR
    seqs = tokens // length
    enc_length = encoder.shape[0] // 2
    blocks = tokens // 128

    place = Place(sizes)
    own = (place.y, place.c, place.z, place.x)
    owns = [
        pltpu.make_async_copy(shard, whole.at[own], own_sem.at[i])
        for i, (shard, whole) in enumerate(zip((small_shard,) + shards, (tiny,) + wholes))
    ]
    for copy in owns:
        copy.start()
    neighbour_barrier(place)
    plans = gather_plans(place, wholes, tiny, (send_sem, recv_sem))
    for copy in owns:
        copy.wait()
    copies = []

    def keep(name):
        copy = pltpu.make_async_copy(v[name], saved_outs[name], out_sem.at[len(copies)])
        copy.start()
        copies.append(copy)

    def keep_whole(i):
        copy = pltpu.make_async_copy(wholes[i], whole_outs[i], out_sem.at[len(copies)])
        copy.start()
        copies.append(copy)

    def opening():
        spread_small(tiny, v["table"])
        for s in range(seqs):
            row = jnp.zeros((1, width), FULL)
            for l in range(8):
                row = row + jnp.where(languages[s] == l, v["table"][l : l + 1, :], 0.0)

            def body(at):
                start = hidden[at, :].astype(FULL) + row
                v["start"][at, :] = start
                v["first_norm"][at, :] = (unit_rows(start) * v["table"][8:9, :]).astype(LOW)

            def run(i, _):
                body(pl.ds(pl.multiple_of(s * length + i * 128, 128), 128))
                return 0

            lax.fori_loop(0, length // 128, run, 0)
        keep("table")
        keep("start")
        keep("first_norm")

    def project(source, weight, target):
        target[...] = jnp.dot(source[...], flat(weight), preferred_element_type=FULL).astype(LOW)

    def attention(queries, keys, values, context, inverse, rows, weights_out, seq, first, last, picked):
        row_at = pl.ds(seq * length, length)
        key_rows = length if picked is None else enc_length

        def out_copy(slot, index):
            return pltpu.make_async_copy(
                stage.at[slot, pl.ds(0, key_rows)], weights_out.at[index], stage_sem.at[slot]
            )

        def body(p, _):
            lanes = pl.ds(pl.multiple_of(p * PAIR, PAIR), PAIR)
            slot = lax.rem(p - first, 2)
            index = seq * per_seq + p

            @pl.when(p - first >= 2)
            def _():
                out_copy(slot, index).wait()

            offset = None
            if picked is not None:
                key_block, value_block = keys[picked, :, lanes], values[picked, :, lanes]
            else:
                key_block, value_block = keys[row_at, lanes], values[row_at, lanes]
                offset = jnp.concatenate([bias[2 * p], bias[2 * p + 1]], axis=1).astype(FULL)
            out, total = pair_forward(
                queries[row_at, lanes], key_block, value_block, offset,
                stage.at[slot, pl.ds(0, key_rows)], rows.at[index],
            )
            context[row_at, lanes] = out.astype(LOW)
            inverse[row_at, lanes] = total
            out_copy(slot, index).start()
            return 0

        lax.fori_loop(first, last, body, 0)
        for slot in range(min(2, last - first)):
            out_copy(slot, 0).wait()

    def residual(context, weight, before, after, gain_row, norm):
        def body(at):
            state = before[at, :] + jnp.dot(context[at, :], flat(weight), preferred_element_type=FULL)
            after[at, :] = state
            norm[at, :] = (unit_rows(state) * v["table"][gain_row : gain_row + 1, :]).astype(LOW)

        each(blocks, body)

    def self_projection(i, name):
        project(v["first_norm"], wholes[i], v[name])
        keep_whole(i)
        keep(name)

    def self_attention(s, first, last):
        attention(
            v["queries"], v["keys"], v["values"], v["self_context"], v["self_inverse"], v["self_rows"],
            self_weights, s, first, last, None,
        )

    def self_end():
        for name in ("self_context", "self_inverse", "self_rows"):
            keep(name)
        residual(v["self_context"], wholes[3], v["start"], v["mid"], 9, v["second_norm"])
        keep("mid")
        keep("second_norm")
        keep_whole(3)

    def cross_source(i, name):
        for half in range(2):
            v[name][half] = jnp.dot(
                encoder[pl.ds(half * enc_length, enc_length), :], flat(wholes[i]), preferred_element_type=FULL
            ).astype(LOW)
        keep(name)
        keep_whole(i)

    def cross_projection():
        project(v["second_norm"], wholes[4], v["cross_queries"])
        keep("cross_queries")
        keep_whole(4)

    def cross_attention(s, first, last):
        attention(
            v["cross_queries"], v["source_keys"], v["source_values"], v["cross_context"], v["cross_inverse"],
            v["cross_rows"], cross_weights, s, first, last, sources[s],
        )

    def cross_end():
        for name in ("cross_context", "cross_inverse", "cross_rows"):
            keep(name)
        residual(v["cross_context"], wholes[7], v["mid"], v["late"], 10, v["third_norm"])
        keep("late")
        keep("third_norm")
        keep_whole(7)

    def feed_inner(q):
        weight = flat(wholes[8], pl.ds(q * width, width))
        for half in range(2):
            at = pl.ds(half * tokens // 2, tokens // 2)
            expanded = jnp.dot(v["third_norm"][at, :], weight, preferred_element_type=FULL)
            value, slope = gelu_parts(expanded)
            v["activated"][q, at, :] = value.astype(LOW)
            v["slope"][q, at, :] = slope.astype(LOW)
        if q == 3:
            keep("activated")
            keep("slope")
            keep_whole(8)

    def outer_grad(q):
        value = tn_dot(v["activated"][q], upstream[...])
        outer_blocks[q // 2, q % 2] = value.reshape(outer_blocks.shape[2:]).astype(LOW)

    tasks = {"bias": lambda: build_bias(ids, bucket_values, bias), "open": opening, "send": self_end}
    tasks.update(cq=cross_projection, cend=cross_end)
    for i, (task, name) in enumerate((("q", "queries"), ("k", "keys"), ("v", "values"))):
        tasks[task] = functools.partial(self_projection, i, name)
    for i in range(4):
        first = per_seq // 2 * (i % 2)
        tasks[f"sa{i}"] = functools.partial(self_attention, i // 2, first, first + per_seq // 2)
        tasks[f"ca{i}"] = functools.partial(cross_attention, i // 2, first, first + per_seq // 2)
        tasks[f"in{i}"] = functools.partial(feed_inner, i)
        tasks[f"og{i}"] = functools.partial(outer_grad, i)
    tasks["K"] = functools.partial(cross_source, 5, "source_keys")
    tasks["V"] = functools.partial(cross_source, 6, "source_values")
    run_order(FORWARD_ORDER, plans, tasks)
    keep_whole(9)
    last = pltpu.make_async_copy(outer_blocks, outer_grads, hidden_sem)
    last.start()
    for plan in plans:
        for links in plan:
            for link in links:
                link.wait_send()
    for copy in copies:
        copy.wait()
    last.wait()


def small_slab(table, gains):
    rows, part = table.shape
    small = jnp.concatenate([table] + [g.reshape(1, part) for g in gains], axis=0)
    return jnp.pad(small, ((0, 16 - rows - len(gains)), (0, 128 - part)))


def forward(
    sizes, hidden_in, output_grad, encoder_states, language_ids, source_index, bucket_ids, language_table, bucket_table, gains,
    squares, inner, outer,
):
    ny, nz = sizes
    grid = (ny, 2, nz, 2)
    part, width = squares[0].shape
    tokens = hidden_in.shape[0]
    length = bucket_ids.shape[0]
    encoder = encoder_states.reshape(-1, width)
    enc_length = encoder_states.shape[1]
    shards = [small_slab(language_table, gains)] + list(squares) + [inner, outer.reshape(4, part, width)]
    wholes = [jax.ShapeDtypeStruct(grid + s.shape, LOW) for s in shards]
    shapes = saved_shapes(tokens, encoder.shape[0], width, length)
    pairs = tokens // length * (width // PAIR)
    anywhere = pl.BlockSpec(memory_space=pl.ANY)
    vmem = pl.BlockSpec(memory_space=pltpu.VMEM)
    smem = pl.BlockSpec(memory_space=pltpu.SMEM)
    slots = slot_count(sizes)
    out_shape = [wholes[10]] + wholes[1:]
    out_shape += [jax.ShapeDtypeStruct((pairs, rows, 2 * length), LOW) for rows in (length, enc_length)]
    out_shape += [jax.ShapeDtypeStruct(*shapes[name]) for name in SAVED]
    outs = pl.pallas_call(
        functools.partial(forward_kernel, sizes),
        out_shape=out_shape,
        in_specs=[anywhere] * 11 + [vmem, vmem, vmem, smem, smem, vmem, smem],
        out_specs=[anywhere] * len(out_shape),
        scratch_shapes=[pltpu.VMEM(w.shape, w.dtype) for w in wholes]
        + [pltpu.VMEM(*shapes[name]) for name in SAVED]
        + [
            pltpu.VMEM((H, length, length), LOW),
            pltpu.VMEM((2, enc_length, 2 * length), LOW),
            pltpu.VMEM(wholes[10].shape, LOW),
            pltpu.SemaphoreType.DMA((11,)),
            pltpu.SemaphoreType.DMA((17, slots)),
            pltpu.SemaphoreType.DMA((17, slots)),
            pltpu.SemaphoreType.DMA((len(SAVED) + 10,)),
            pltpu.SemaphoreType.DMA((2,)),
            pltpu.SemaphoreType.DMA,
        ],
        compiler_params=pltpu.CompilerParams(
            collective_id=2, has_side_effects=True, vmem_limit_bytes=62 * 1024 * 1024
        ),
    )(
        *shards, hidden_in, output_grad, encoder, language_ids, source_index, bucket_ids.T,
        bucket_table.astype(FULL).T,
    )
    return outs


class Summed:
    def __init__(self, place, path, blocks, core_in, boxes, sems):
        self.place, self.blocks, self.sems = place, blocks, sems
        self.slot, self.links, self.stages = 0, [], []
        c = place.c
        core = self.copy(blocks((ALL, 1 - c, ALL, ALL)), core_in, "c", 1 - c)
        self.stage([Link(core)], [((ALL, c, ALL, ALL), core_in, None)])
        fixed, box = {"c": c}, 0
        for dim in path:
            here, size = place.at(dim), place.size(dim)
            if size == 2:
                copy = self.copy(blocks(self.index({**fixed, dim: 1 - here})), boxes[box], dim, 1 - here)
                self.stage([Link(copy)], [(self.index({**fixed, dim: here}), boxes[box], None)])
                box += 1
            else:
                for hop in range(size - 1, 0, -1):
                    links, adds = [], []
                    for way in (1, -1):
                        there, goal = here - way, here - way * hop
                        sends = (goal >= 0) & (goal < size)
                        source = here + way
                        got = source - way * hop
                        receives = (source >= 0) & (source < size) & (got >= 0) & (got < size)
                        copy = self.copy(
                            blocks(self.index({**fixed, dim: jnp.clip(goal, 0, size - 1)})), boxes[box], dim,
                            jnp.clip(there, 0, size - 1),
                        )
                        links.append(Link(copy, sends, receives))
                        adds.append((self.index({**fixed, dim: jnp.clip(got, 0, size - 1)}), boxes[box], receives))
                        box += 1
                    self.stage(links, adds)
            fixed = {**fixed, dim: here}
        self.own = self.index(fixed)

    def index(self, fixed):
        return tuple(fixed.get(dim, ALL) for dim in "yczx")

    def copy(self, source, target, dim, there):
        slot = self.slot
        self.slot += 1
        return pltpu.make_async_remote_copy(
            source, target, self.sems[0].at[slot], self.sems[1].at[slot],
            device_id=self.place.device(dim, there), device_id_type=MESH,
        )

    def stage(self, links, adds):
        self.links += links
        self.stages.append((links, adds))

    def start(self, step):
        for link in self.stages[step][0]:
            link.start()

    def finish(self, step):
        links, adds = self.stages[step]
        for link in links:
            link.wait_recv()

        def add(target, box):
            view = self.blocks(target)
            view[...] = view[...] + box[...]

        for target, box, condition in adds:
            Link.when(condition, functools.partial(add, target, box))

    def close(self):
        for link in self.links:
            link.wait_send()


def pair_backward(weights, queries, keys, values, grads, inverse_row):
    count = queries.shape[0]
    stacked = head_pair(grads)
    prob_grad = nt_dot(values, stacked)
    grown = weights.astype(FULL)
    centre = jnp.sum(grown * prob_grad, axis=0, keepdims=True) * inverse_row
    score_grad = (grown * (prob_grad - centre)).astype(LOW)
    value_part = jnp.dot(weights, stacked, preferred_element_type=FULL)
    key_part = jnp.dot(score_grad, head_pair(queries), preferred_element_type=FULL)
    both = jnp.concatenate([score_grad[:, :count], score_grad[:, count:]], axis=0)
    query_part = tn_dot(both, head_pair(keys))
    return query_part, key_part, value_part, score_grad


def backward_kernel(sizes, box_counts, *refs):
    n = len(SAVED)
    grads, encoder, languages, sources, ids, outer_grads = refs[:6]
    wholes = refs[6:16]
    self_weights, cross_weights = refs[16:18]
    saved = dict(zip(SAVED, refs[18 : 18 + n]))
    at = 18 + n
    hidden_out, hidden_grad, encoder_grad, small_out, packed = refs[at : at + 5]
    at += 5
    squares, outers, core_boxes = refs[at : at + 3]
    at += 3
    boxes = []
    for count in box_counts:
        boxes.append(refs[at : at + count])
        at += count
    small_box, pool, pairs_in, run_a, run_b, run_c, w, wo, stage, score_sum, bucket_rows, table, self_rows, cross_rows = refs[at : at + 14]
    send_sem, recv_sem, small_send, small_recv, load_sem, stage_sem, store_sem = refs[at + 14 :]
    place = Place(sizes)
    length = ids.shape[0]
    seqs, tokens = languages.shape[0], pool.shape[1]
    width = pool.shape[2]
    blocks = tokens // 128
    per_seq = width // PAIR
    loads = []

    def load(source, target):
        copy = pltpu.make_async_copy(source, target, load_sem.at[len(loads)])
        loads.append(copy)
        copy.start()
        return copy

    X = [pool.at[i] for i in range(11)] + [pairs_in.at[i] for i in range(4)]
    og, tn = X[0], X[1]
    get_outers = load(outer_grads, outers)
    get_og = load(grads, og)
    get_table = load(saved["table"], table)
    get_slope = [load(saved["slope"].at[q], X[6 + q]) for q in range(4)]

    def outer_chunk(q):
        return wholes[9].at[q // 2, q % 2]

    def inner_chunk(q):
        return wholes[8].at[:, :, :, :, :, pl.ds(q * width, width)]

    get_wo = [load(outer_chunk(q), wo.at[q]) for q in range(2)]
    get_tn = load(saved["third_norm"], tn)
    got = {}
    get_wi = [load(inner_chunk(q), w.at[q]) for q in range(2)]
    get_late = load(saved["late"], run_c)
    got["cross_rows"] = load(saved["cross_rows"], cross_rows)
    got["self_rows"] = load(saved["self_rows"], self_rows)
    got["co"] = load(wholes[7], w.at[2])
    got["cq_w"] = load(wholes[4], w.at[3])
    got["keys"] = load(saved["source_keys"], pairs_in.at[pl.ds(0, 2)])
    got["values"] = load(saved["source_values"], pairs_in.at[pl.ds(2, 2)])
    got["cross_context"] = load(saved["cross_context"], X[2])
    got["cross_queries"] = load(saved["cross_queries"], X[3])
    got["second_norm"] = load(saved["second_norm"], X[4])
    got["first_norm"] = load(saved["first_norm"], X[5])
    neighbour_barrier(place, far=True)

    def view_of(m):
        if m < 4:
            return lambda index: outers.at[index + (m,)]
        return lambda index: squares.at[(m - 4,) + index]

    plans = []
    for m in range(16):
        group, kind = m // 4, m % 4
        slot = group % 2
        plans.append(
            Summed(
                place, BACK_PATHS[kind], view_of(m), core_boxes.at[slot, kind], [box.at[slot] for box in boxes[kind]],
                (send_sem.at[m], recv_sem.at[m]),
            )
        )

    def put(i, value):
        squares[i] = value.reshape(squares.shape[1:]).astype(LOW)

    small_out[...] = jnp.zeros_like(small_out)

    def norm_backward(state, inflow, gain_row, before, after):
        def body(at):
            hidden, flow, gain = state[at, :], inflow[at, :], table[gain_row : gain_row + 1, :]
            scale = lax.rsqrt(jnp.mean(hidden * hidden, axis=-1, keepdims=True) + EPSILON)
            unit = hidden * scale
            small_out[gain_row : gain_row + 1, :] += jnp.sum(flow * unit, axis=0, keepdims=True)
            flow = flow * gain
            flow = (flow - unit * jnp.mean(unit * flow, axis=-1, keepdims=True)) * scale
            after[at, :] = before[at, :].astype(FULL) + flow

        each(blocks, body)

    branch = X[1]

    def inner_grad(q):
        eg = X[10]
        if q == 0:
            get_og.wait()
            get_tn.wait()
        get_wo[q].wait()
        get_slope[q].wait()
        out_w = wo[q % 2].reshape(width, width)
        eg[...] = (nt_dot(og[...], out_w) * X[6 + q][...].astype(FULL)).astype(LOW)
        get_wo.append(load(outer_chunk((q + 2) % 4), wo.at[q % 2]))
        put(q, tn_dot(tn[...], eg[...]))
        get_wi[q].wait()
        back = nt_dot(eg[...], flat(w.at[q % 2]))
        if q == 0:
            run_b[...] = back
        else:
            run_b[...] += back
        if q + 2 < 4:
            get_wi.append(load(inner_chunk(q + 2), w.at[q % 2]))
        if q == 3:
            got["so"] = load(wholes[3], w.at[0])
            got["q_w"] = load(wholes[0], w.at[1])
            got["encoder"] = load(encoder, pool.at[pl.ds(6, 2)])

    def third_backward():
        get_table.wait()
        get_late.wait()
        norm_backward(run_c, run_b, 10, og, run_a)
        got["inverse"] = load(saved["cross_inverse"], run_c)
        branch[...] = run_a[...].astype(LOW)

    def context_grad(weight, slot):
        got[weight].wait()
        got["inverse"].wait()
        X[0][...] = (nt_dot(branch[...], flat(w.at[slot])).astype(LOW).astype(FULL) * run_c[...]).astype(LOW)

    def cross_out_grad():
        got["cross_context"].wait()
        put(4, tn_dot(X[2][...], branch[...]))

    def cross_context_grad():
        context_grad("co", 2)
        got["k_w"] = load(wholes[1], w.at[2])
        got["mid"] = load(saved["mid"], run_c)

    def weight_copy(source, index, slot, rows):
        return pltpu.make_async_copy(source.at[index], stage.at[slot, pl.ds(0, rows)], stage_sem.at[slot])

    def attention(weights, rows, key_rows, one, finish_pair, first, last):
        if first == 0:
            for s in range(seqs):
                weight_copy(weights, s * per_seq, s, key_rows).start()

        def body(p, _):
            lanes = pl.ds(pl.multiple_of(p * PAIR, PAIR), PAIR)
            results = []
            for s in range(seqs):
                index = s * per_seq + p
                weight_copy(weights, index, s, key_rows).wait()
                queries, keys, values, grad = one(s, lanes)
                results.append(
                    pair_backward(stage[s, pl.ds(0, key_rows)], queries, keys, values, grad, rows[index])
                )

                @pl.when(p + 1 < per_seq)
                def _():
                    weight_copy(weights, index + 1, s, key_rows).start()

            finish_pair(p, lanes, results)
            return 0

        lax.fori_loop(first, last, body, 0)

    enc_length = pool.shape[1]

    def cross_attention(first, last):
        if first == 0:
            for name in ("cross_rows", "cross_queries", "keys", "values"):
                got[name].wait()

        def one(s, lanes):
            at = pl.ds(s * length, length)
            source = sources[s]
            return X[3][at, lanes], pairs_in[source, :, lanes], pairs_in[2 + source, :, lanes], X[0][at, lanes]

        def finish_pair(p, lanes, results):
            for s in range(seqs):
                X[1][pl.ds(s * length, length), lanes] = results[s][0].astype(LOW)
            for e in range(2):
                for target, part_at in ((8, 1), (11, 2)):
                    total = jnp.where(sources[0] == e, results[0][part_at], 0.0)
                    total = total + jnp.where(sources[1] == e, results[1][part_at], 0.0)
                    pool[target + e, :, lanes] = total.astype(LOW)

        attention(cross_weights, cross_rows, enc_length, one, finish_pair, first, last)
        if last < per_seq:
            return
        got["queries"] = load(saved["queries"], X[11])
        got["keys"] = load(saved["keys"], X[12])
        got["values"] = load(saved["values"], X[13])
        got["self_context"] = load(saved["self_context"], X[14])

    def cross_query_grad():
        got["second_norm"].wait()
        put(5, tn_dot(X[4][...], X[1][...]))

    def source_grad(i, target):
        copy = got.pop("encoder", None)
        if copy is not None:
            copy.wait()
        put(i, tn_dot(pool[6], pool[target]) + tn_dot(pool[7], pool[target + 1]))

    def second_backward():
        got["cq_w"].wait()
        run_b[...] = nt_dot(X[1][...], flat(w.at[3]))
        got["v_w"] = load(wholes[2], w.at[3])
        got["mid"].wait()
        norm_backward(run_c, run_b, 9, run_a, run_a)
        got["inverse"] = load(saved["self_inverse"], run_c)
        branch[...] = run_a[...].astype(LOW)

    def self_out_grad():
        got["self_context"].wait()
        put(8, tn_dot(X[14][...], branch[...]))

    def self_context_grad():
        context_grad("so", 0)
        got["ck_w"] = load(wholes[5], w.at[0])
        got["start"] = load(saved["start"], run_c)

    def self_attention(first, last):
        if first == 0:
            for name in ("self_rows", "queries", "keys", "values"):
                got[name].wait()

        def one(s, lanes):
            at = pl.ds(s * length, length)
            return tuple(X[i][at, lanes] for i in (11, 12, 13, 0))

        def finish_pair(p, lanes, results):
            for s in range(seqs):
                for i in range(3):
                    X[2 + i][pl.ds(s * length, length), lanes] = results[s][i].astype(LOW)
            score_sum[p] = results[0][3].astype(FULL) + results[1][3].astype(FULL)

        attention(self_weights, self_rows, length, one, finish_pair, first, last)

    def self_grad(i):
        copy = got.pop("first_norm", None)
        if copy is not None:
            copy.wait()
        put(9 + i, tn_dot(X[5][...], X[2 + i][...]))

    stores = []

    def store(source, target):
        copy = pltpu.make_async_copy(source, target, store_sem.at[len(stores)])
        stores.append(copy)
        copy.start()

    def closing():
        for name in ("q_w", "k_w", "v_w", "start"):
            got[name].wait()
        run_b[...] = nt_dot(X[2][...], flat(w.at[1]))
        run_b[...] += nt_dot(X[3][...], flat(w.at[2]))
        run_b[...] += nt_dot(X[4][...], flat(w.at[3]))
        got["cv_w"] = load(wholes[6], w.at[1])
        got["activated"] = [load(saved["activated"].at[q], X[i]) for q, i in enumerate((0, 1, 5, 10))]
        norm_backward(run_c, run_b, 8, run_a, run_a)
        store(run_a, hidden_grad)
        got["late"] = load(saved["late"], run_c)
        for s in range(seqs):
            row = jnp.sum(run_a[pl.ds(s * length, length), :], axis=0, keepdims=True)
            for l in range(8):
                small_out[l : l + 1, :] += jnp.where(languages[s] == l, row, 0.0)

    def hidden_end():
        for q, i in enumerate((0, 1, 5, 10)):
            got["activated"][q].wait()
            get_wo[4 + q].wait()
            value = jnp.dot(X[i][...], wo[q % 2].reshape(width, width), preferred_element_type=FULL)
            if q < 2:
                get_wo.append(load(outer_chunk(q + 2), wo.at[q % 2]))
            if q == 0:
                got["late"].wait()
            if q < 3:
                run_c[...] += value
            else:
                X[2][...] = (run_c[...] + value).astype(LOW)
        store(X[2], hidden_out)

    def encoder_end():
        got["ck_w"].wait()
        got["cv_w"].wait()
        for e, run in ((0, run_b), (1, run_c)):
            run[...] = nt_dot(pool[8 + e], flat(w.at[0]))
            run[...] += nt_dot(pool[11 + e], flat(w.at[1]))
            store(run, encoder_grad.at[e])

    def bucket_sums():
        half = length // 2

        def pair(p, _):
            def bucket(c, _):
                here = ids[...] == c
                for h in range(2):
                    kept = jnp.where(here, score_sum[p, :, h * length : (h + 1) * length], 0.0)
                    lanes = jnp.sum(kept.reshape(length // 8, 8, length), axis=0)
                    row = jnp.sum(lanes[:, :half] + lanes[:, half:], axis=0, keepdims=True)
                    bucket_rows[pl.ds((2 * p + h) * 32 + c, 1), :] = row
                return 0

            return lax.fori_loop(0, 32, bucket, 0)

        lax.fori_loop(0, per_seq, pair, 0)
        ones = jnp.ones((8, 128), FULL)
        totals = lax.dot_general(
            ones, bucket_rows[...], (((1,), (1,)), ((), ())), precision=PRECISE, preferred_element_type=FULL
        )
        small_out[11:12, : bucket_rows.shape[0]] = totals[:1, :]

    small = []
    for dim in "cxyz":
        here, reach = place.at(dim), 1
        while reach < place.size(dim):
            small.append((dim, here + reach - 2 * reach * lax.rem(lax.div(here, reach), 2)))
            reach *= 2

    def small_copy(i):
        dim, partner = small[i]
        return pltpu.make_async_remote_copy(
            small_out, small_box.at[i], small_send.at[i], small_recv.at[i],
            device_id=place.device(dim, partner), device_id_type=MESH,
        )

    class Small:
        def start(self, i):
            small_copy(i).start()

        def finish(self, i):
            small_copy(i).wait()
            small_out[...] += small_box[i]

    tasks = dict(n3=third_backward, co=cross_out_grad, ccg=cross_context_grad, cq=cross_query_grad, n2=second_backward)
    tasks.update(so=self_out_grad, scg=self_context_grad, close=closing, bucket=bucket_sums, hid=hidden_end, enc=encoder_end)
    tasks["ck"] = functools.partial(source_grad, 6, 8)
    tasks["cv"] = functools.partial(source_grad, 7, 11)
    for i in range(4):
        tasks[f"in{i}"] = functools.partial(inner_grad, i)
    for i in range(3):
        tasks[f"ca{i}"] = functools.partial(cross_attention, 2 * i, 2 * i + 2)
        tasks[f"sa{i}"] = functools.partial(self_attention, 2 * i, 2 * i + 2)
        tasks["qkv"[i]] = functools.partial(self_grad, i)
    steps = [len(plan.stages) for plan in plans] + [len(small)]
    plans.append(Small())
    at = [0] * 17
    get_outers.wait()
    for entry in BACKWARD_ORDER:
        if isinstance(entry, str):
            tasks[entry]()
            continue
        step = at[entry]
        at[entry] += 1
        if step >= 1:
            plans[entry].finish(step - 1)
        if step < steps[entry]:
            plans[entry].start(step)
    for m, plan in enumerate(plans[:16]):
        packed[m] = plan.blocks(plan.own)[...].astype(FULL)
        plan.close()
    for copy in stores:
        copy.wait()


def backward(sizes, output_grad, encoder_states, language_ids, source_index, bucket_ids, forward_outs):
    ny, nz = sizes
    grid = (ny, 2, nz, 2)
    tokens, width = output_grad.shape
    length = bucket_ids.shape[0]
    part = width // (ny * nz * 4)
    outer_grads, wholes, score_weights = forward_outs[0], forward_outs[1:11], forward_outs[11:13]
    saved = dict(zip(SAVED, forward_outs[13:]))
    enc_count, enc_length = encoder_states.shape[:2]
    anywhere = pl.BlockSpec(memory_space=pl.ANY)
    vmem = pl.BlockSpec(memory_space=pltpu.VMEM)
    smem = pl.BlockSpec(memory_space=pltpu.SMEM)
    lead = [box_shapes(sizes, path) for path in BACK_PATHS]
    slots = slot_count(sizes)
    hops = (ny * nz * 4).bit_length() - 1
    pairs = tokens // length * (width // PAIR)
    row = (tokens, width)
    out_shape = [
        jax.ShapeDtypeStruct(row, LOW),
        jax.ShapeDtypeStruct(row, FULL),
        jax.ShapeDtypeStruct((enc_count, enc_length, width), FULL),
        jax.ShapeDtypeStruct((16, width), FULL),
        jax.ShapeDtypeStruct((16, part, width), FULL),
    ]
    outs = pl.pallas_call(
        functools.partial(backward_kernel, sizes, tuple(len(s) for s in lead)),
        out_shape=out_shape,
        in_specs=[anywhere, anywhere, smem, smem, vmem] + [anywhere] * (13 + len(SAVED)),
        out_specs=[anywhere] * 3 + [vmem] * 2,
        scratch_shapes=[
            pltpu.VMEM((12,) + grid + (part, width), LOW),
            pltpu.VMEM(grid + (4, part, width), LOW),
            pltpu.VMEM((2, 4, ny, nz, 2, part, width), LOW),
        ]
        + [pltpu.VMEM((2,) + s + (part, width), LOW) for one in lead for s in one]
        + [
            pltpu.VMEM((hops, 16, width), FULL),
            pltpu.VMEM((13,) + row, LOW),
            pltpu.VMEM((4,) + row, LOW),
            pltpu.VMEM(row, FULL),
            pltpu.VMEM(row, FULL),
            pltpu.VMEM(row, FULL),
            pltpu.VMEM((4,) + grid + (part, width), LOW),
            pltpu.VMEM((2, nz, 2, 4, part, width), LOW),
            pltpu.VMEM((2, enc_length, 2 * length), LOW),
            pltpu.VMEM((width // PAIR, length, 2 * length), FULL),
            pltpu.VMEM((32 * H, 128), FULL),
            pltpu.VMEM((16, width), FULL),
            pltpu.VMEM((pairs, 1, 2 * length), FULL),
            pltpu.VMEM((pairs, 1, 2 * length), FULL),
            pltpu.SemaphoreType.DMA((16, slots)),
            pltpu.SemaphoreType.DMA((16, slots)),
            pltpu.SemaphoreType.DMA((hops,)),
            pltpu.SemaphoreType.DMA((hops,)),
            pltpu.SemaphoreType.DMA((56,)),
            pltpu.SemaphoreType.DMA((2,)),
            pltpu.SemaphoreType.DMA((4,)),
        ],
        compiler_params=pltpu.CompilerParams(
            collective_id=3, has_side_effects=True, vmem_limit_bytes=63 * 1024 * 1024
        ),
    )(
        output_grad, encoder_states, language_ids, source_index, bucket_ids.T, outer_grads, *wholes, *score_weights,
        *[saved[name] for name in SAVED],
    )
    return finish(sizes, outs)


def finish_kernel(sizes, *refs):
    hidden_out, hidden_grad, encoder_grad, small, packed = refs[:5]
    outs = refs[5:18]
    language, bucket, gains = refs[18], refs[19], refs[20:23]
    staged, sem, in_sem = refs[23:26], refs[26], refs[27]
    part, width = packed.shape[1:]
    copies = []
    halves = []
    for i, source in enumerate((hidden_out, hidden_grad, encoder_grad)):
        for h in range(2):
            size = source.shape[0] // 2
            rows = pl.ds(h * size, size)
            halves.append((i, rows, pltpu.make_async_copy(source.at[rows], staged[i].at[rows], in_sem.at[2 * i + h])))
            halves[-1][2].start()

    def copy(source, target):
        copies.append(pltpu.make_async_copy(source, target, sem.at[len(copies)]))
        copies[-1].start()

    for q in range(4):
        copy(packed.at[q], outs[12].at[pl.ds(q * part, part)])
        copy(packed.at[4 + q], outs[11].at[:, pl.ds(q * width, width)])
    for i, m in enumerate((13, 14, 15, 12, 9, 10, 11, 8)):
        copy(packed.at[m], outs[3 + i])
    for i, rows, half in halves:
        half.wait()
        copy(staged[i].at[rows], outs[i].at[rows])
    place = Place(sizes)
    start = (place.dp * sizes[1] * 2 + place.fs) * part
    row = lax.broadcasted_iota(jnp.int32, (width, 128), 0)
    lane = lax.broadcasted_iota(jnp.int32, (width, 128), 1)
    chosen = jnp.where((row == lane + start) & (lane < part), 1.0, 0.0)
    own = jnp.dot(small[...], chosen, precision=PRECISE, preferred_element_type=FULL)
    language[...] = own[:8, :part]
    for i in range(3):
        gains[i][...] = own[8 + i, :part]
    row = lax.broadcasted_iota(jnp.int32, (32, width), 0)
    lane = lax.broadcasted_iota(jnp.int32, (32, width), 1)
    spread = jnp.where(lax.rem(lane, 32) == row, small[11:12, :], 0.0)
    row = lax.broadcasted_iota(jnp.int32, (width, 128), 0)
    lane = lax.broadcasted_iota(jnp.int32, (width, 128), 1)
    heads = jnp.where(lax.div(row, 32) == lane, 1.0, 0.0)
    bucket[...] = jnp.dot(spread, heads, precision=PRECISE, preferred_element_type=FULL)[:, :H]
    for c in copies:
        c.wait()


def finish(sizes, outs):
    part, width = outs[4].shape[1:]
    anywhere = pl.BlockSpec(memory_space=pl.ANY)
    vmem = pl.BlockSpec(memory_space=pltpu.VMEM)
    shapes = [o.shape for o in outs[:3]] + [(part, width)] * 8
    shapes += [(part, 4 * width), (4 * part, width)]
    out_shape = [jax.ShapeDtypeStruct(s, FULL) for s in shapes]
    out_shape[0] = jax.ShapeDtypeStruct(shapes[0], LOW)
    out_shape += [jax.ShapeDtypeStruct(s, FULL) for s in ((8, part), (32, H), (part,), (part,), (part,))]
    return pl.pallas_call(
        functools.partial(finish_kernel, sizes),
        out_shape=out_shape,
        in_specs=[pl.BlockSpec(memory_space=pltpu.HBM)] * 3 + [vmem, vmem],
        out_specs=[anywhere] * 13 + [vmem] * 5,
        scratch_shapes=[pltpu.VMEM(o.shape, o.dtype) for o in outs[:3]]
        + [pltpu.SemaphoreType.DMA((22,)), pltpu.SemaphoreType.DMA((6,))],
        compiler_params=pltpu.CompilerParams(vmem_limit_bytes=60 * 1024 * 1024),
    )(*outs)


def local_general(
    sizes,
    hidden_in,
    output_grad,
    encoder_states,
    language_ids,
    source_index,
    bucket_ids,
    language_table,
    bucket_table,
    self_gain,
    self_query,
    self_key,
    self_value,
    self_out,
    cross_gain,
    cross_query,
    cross_key,
    cross_value,
    cross_out,
    feed_gain,
    inner_weight,
    outer_weight,
):
    seq_count = language_ids.shape[0]
    length = bucket_ids.shape[0]
    tokens = seq_count * length
    enc_count = encoder_states.shape[0]
    enc_length = encoder_states.shape[1]
    width = hidden_in.shape[1]
    blocks = seq_count // SEQ_BLOCK
    (
        gain_one, gain_two, gain_three, table_whole, query_whole, key_whole, value_whole, out_whole,
        cquery_whole, ckey_whole, cvalue_whole, cout_whole, inner_whole, outer_whole,
    ) = gather_weights(
        sizes, language_table, (self_gain, cross_gain, feed_gain),
        (self_query, self_key, self_value, self_out, cross_query, cross_key, cross_value, cross_out),
        inner_weight, outer_weight,
    )

    def to_blocks(array, rows):
        return array.reshape(blocks, SEQ_BLOCK, rows, array.shape[-1])

    language_hot = (language_ids[:, None] == jnp.arange(table_whole.shape[0])[None, :]).astype(
        jnp.float32
    )
    language_rows = jnp.dot(language_hot, table_whole.astype(jnp.float32), precision=PRECISE)
    start_state = (
        hidden_in.astype(jnp.float32).reshape(seq_count, length, width) + language_rows[:, None, :]
    ).reshape(tokens, width)
    first_norm = to_low(norm_scale(start_state, gain_one.astype(jnp.float32)))
    self_queries = to_low(matmul(first_norm, query_whole))
    self_keys = to_low(matmul(first_norm, key_whole))
    self_values = to_low(matmul(first_norm, value_whole))
    bucket_hot = (
        bucket_ids[:, :, None] == jnp.arange(bucket_table.shape[0])[None, None, :]
    ).astype(jnp.float32)
    position_bias = jnp.einsum(
        "ijb,bh->hij", bucket_hot, bucket_table.astype(jnp.float32), precision=PRECISE
    )
    positions = jnp.arange(length)
    masked_bias = jnp.where(
        (positions[:, None] >= positions[None, :])[None], position_bias, NEGATIVE
    )

    def self_forward(block_items):
        return attend_forward(block_items[0], block_items[1], block_items[2], masked_bias)

    self_context, self_total = lax.map(
        self_forward,
        (
            to_blocks(self_queries, length),
            to_blocks(self_keys, length),
            to_blocks(self_values, length),
        ),
    )
    self_context = self_context.reshape(tokens, -1)
    mid_state = start_state + matmul(self_context, out_whole)
    second_norm = to_low(norm_scale(mid_state, gain_two.astype(jnp.float32)))
    cross_queries = to_low(matmul(second_norm, cquery_whole))
    encoder_flat = encoder_states.reshape(enc_count * enc_length, width)
    source_keys = to_low(matmul(encoder_flat, ckey_whole)).reshape(enc_count, enc_length, -1)
    source_values = to_low(matmul(encoder_flat, cvalue_whole)).reshape(enc_count, enc_length, -1)
    source_hot = (source_index[:, None] == jnp.arange(enc_count)[None, :]).astype(jnp.float32)
    source_low = to_low(source_hot)
    picked_keys = to_low(
        jnp.einsum("se,emc->smc", source_low, source_keys, preferred_element_type=jnp.float32)
    )
    picked_values = to_low(
        jnp.einsum("se,emc->smc", source_low, source_values, preferred_element_type=jnp.float32)
    )

    def cross_forward(block_items):
        return attend_forward(block_items[0], block_items[1], block_items[2], 0.0)

    cross_context, cross_total = lax.map(
        cross_forward,
        (
            to_blocks(cross_queries, length),
            picked_keys.reshape(blocks, SEQ_BLOCK, enc_length, -1),
            picked_values.reshape(blocks, SEQ_BLOCK, enc_length, -1),
        ),
    )
    cross_context = cross_context.reshape(tokens, -1)
    late_state = mid_state + matmul(cross_context, cout_whole)
    third_norm = to_low(norm_scale(late_state, gain_three.astype(jnp.float32)))
    expanded = matmul(third_norm, inner_whole)
    activated = to_low(jax.nn.gelu(expanded, approximate=True))
    hidden_out = (late_state + matmul(activated, outer_whole)).astype(jnp.bfloat16)
    top_grad = output_grad.astype(jnp.float32)
    outer_full = left_product(activated, output_grad)
    activated_grad = right_product(output_grad, outer_whole)
    gelu_value, gelu_back = jax.vjp(jax.nn.gelu, expanded)
    expanded_grad = to_low(gelu_back(activated_grad)[0])
    inner_full = left_product(third_norm, expanded_grad)
    third_grad = right_product(expanded_grad, inner_whole)
    norm_value, norm_back = jax.vjp(norm_scale, late_state, gain_three.astype(jnp.float32))
    state_back, feed_gain_full = norm_back(third_grad)
    late_grad = top_grad + state_back
    cross_low = to_low(late_grad)
    cout_full = left_product(cross_context, cross_low)
    cross_context_grad = to_low(right_product(cross_low, cout_whole))

    def cross_backward(block_items):
        return attend_backward(
            block_items[0],
            block_items[1],
            block_items[2],
            0.0,
            block_items[3],
            block_items[4],
            False,
        )

    cquery_part, ckey_part, cvalue_part = lax.map(
        cross_backward,
        (
            to_blocks(cross_queries, length),
            picked_keys.reshape(blocks, SEQ_BLOCK, enc_length, -1),
            picked_values.reshape(blocks, SEQ_BLOCK, enc_length, -1),
            cross_total,
            to_blocks(cross_context_grad, length),
        ),
    )
    cquery_low = to_low(cquery_part.reshape(tokens, -1))
    source_key_grad = to_low(
        jnp.einsum(
            "se,smc->emc",
            source_hot,
            ckey_part.reshape(seq_count, enc_length, -1),
            precision=PRECISE,
        ).reshape(enc_count * enc_length, -1)
    )
    source_value_grad = to_low(
        jnp.einsum(
            "se,smc->emc",
            source_hot,
            cvalue_part.reshape(seq_count, enc_length, -1),
            precision=PRECISE,
        ).reshape(enc_count * enc_length, -1)
    )
    cquery_full = left_product(second_norm, cquery_low)
    ckey_full = left_product(encoder_flat, source_key_grad)
    cvalue_full = left_product(encoder_flat, source_value_grad)
    encoder_grad = (
        right_product(source_key_grad, ckey_whole) + right_product(source_value_grad, cvalue_whole)
    ).reshape(enc_count, enc_length, width)
    second_grad = right_product(cquery_low, cquery_whole)
    norm_value, norm_back = jax.vjp(norm_scale, mid_state, gain_two.astype(jnp.float32))
    state_back, cross_gain_full = norm_back(second_grad)
    mid_grad = late_grad + state_back
    self_low = to_low(mid_grad)
    out_full = left_product(self_context, self_low)
    self_context_grad = to_low(right_product(self_low, out_whole))

    def self_backward(block_items):
        return attend_backward(
            block_items[0],
            block_items[1],
            block_items[2],
            masked_bias,
            block_items[3],
            block_items[4],
            True,
        )

    query_part, key_part, value_part, bias_part = lax.map(
        self_backward,
        (
            to_blocks(self_queries, length),
            to_blocks(self_keys, length),
            to_blocks(self_values, length),
            self_total,
            to_blocks(self_context_grad, length),
        ),
    )
    query_low = to_low(query_part.reshape(tokens, -1))
    key_low = to_low(key_part.reshape(tokens, -1))
    value_low = to_low(value_part.reshape(tokens, -1))
    table_full = jnp.einsum(
        "hij,ijb->bh", jnp.sum(bias_part, axis=0), bucket_hot, precision=PRECISE
    )
    query_full = left_product(first_norm, query_low)
    key_full = left_product(first_norm, key_low)
    value_full = left_product(first_norm, value_low)
    first_grad = (
        right_product(query_low, query_whole)
        + right_product(key_low, key_whole)
        + right_product(value_low, value_whole)
    )
    norm_value, norm_back = jax.vjp(norm_scale, start_state, gain_one.astype(jnp.float32))
    state_back, self_gain_full = norm_back(first_grad)
    hidden_in_grad = mid_grad + state_back
    sequence_sums = jnp.sum(hidden_in_grad.reshape(seq_count, length, width), axis=1)
    language_full = left_product(language_hot, sequence_sums)
    (
        language_part, bucket_table_grad, sgain_part, cgain_part, feed_gain_part, whole_parts, inner_part, outer_part,
    ) = reduce_grads(
        sizes, language_full, table_full, (self_gain_full, cross_gain_full, feed_gain_full),
        (query_full, key_full, value_full, out_full, cquery_full, ckey_full, cvalue_full, cout_full),
        inner_full, outer_full,
    )
    query_sum, key_sum, value_sum, out_part, cquery_part_sum, ckey_part_sum, cvalue_part_sum, cout_part = whole_parts
    return (
        hidden_out,
        hidden_in_grad,
        encoder_grad,
        language_part,
        bucket_table_grad,
        sgain_part,
        query_sum,
        key_sum,
        value_sum,
        out_part,
        cgain_part,
        cquery_part_sum,
        ckey_part_sum,
        cvalue_part_sum,
        cout_part,
        feed_gain_part,
        inner_part,
        outer_part,
    )


def local(sizes, *args):
    if sizes == (2, 4) and args[8].shape[0] % 8 == 0:
        return local_fused(sizes, *args)
    return local_general(sizes, *args)


def local_fused(
    sizes, hidden_in, output_grad, encoder_states, language_ids, source_index, bucket_ids, language_table,
    bucket_table, self_gain, self_query, self_key, self_value, self_out, cross_gain, cross_query, cross_key,
    cross_value, cross_out, feed_gain, inner_weight, outer_weight,
):
    kept = forward(
        sizes, hidden_in, output_grad, encoder_states, language_ids, source_index, bucket_ids, language_table,
        bucket_table, (self_gain, cross_gain, feed_gain),
        (self_query, self_key, self_value, self_out, cross_query, cross_key, cross_value, cross_out),
        inner_weight, outer_weight,
    )
    outs = backward(sizes, output_grad, encoder_states, language_ids, source_index, bucket_ids, kept)
    squares, inner, outer, language, bucket, gains = outs[3:11], outs[11], outs[12], outs[13], outs[14], outs[15:]
    return (
        *outs[:3], language, bucket, gains[0], *squares[:4], gains[1], *squares[4:], gains[2], inner, outer,
    )


def solution(mesh):
    sizes = (mesh.shape["dp"] // 2, mesh.shape["fsdp"] // 2)
    in_specs = (
        P(("dp", "fsdp"), None),
        P(("dp", "fsdp"), None),
        P(("dp", "fsdp"), None, None),
        P(("dp", "fsdp")),
        P(("dp", "fsdp")),
        P(),
        P(None, ("dp", "fsdp")),
        P(),
        P(("dp", "fsdp")),
        P(("dp", "fsdp"), None),
        P(("dp", "fsdp"), None),
        P(("dp", "fsdp"), None),
        P(("dp", "fsdp"), None),
        P(("dp", "fsdp")),
        P(("dp", "fsdp"), None),
        P(("dp", "fsdp"), None),
        P(("dp", "fsdp"), None),
        P(("dp", "fsdp"), None),
        P(("dp", "fsdp")),
        P(("dp", "fsdp"), None),
        P(("dp", "fsdp"), None),
    )
    out_specs = (
        P(("dp", "fsdp"), None),
        P(("dp", "fsdp"), None),
        P(("dp", "fsdp"), None, None),
        P(None, ("dp", "fsdp")),
        P(),
        P(("dp", "fsdp")),
        P(("dp", "fsdp"), None),
        P(("dp", "fsdp"), None),
        P(("dp", "fsdp"), None),
        P(("dp", "fsdp"), None),
        P(("dp", "fsdp")),
        P(("dp", "fsdp"), None),
        P(("dp", "fsdp"), None),
        P(("dp", "fsdp"), None),
        P(("dp", "fsdp"), None),
        P(("dp", "fsdp")),
        P(("dp", "fsdp"), None),
        P(("dp", "fsdp"), None),
    )
    return jax.shard_map(functools.partial(local, sizes), mesh=mesh, in_specs=in_specs, out_specs=out_specs, check_vma=False)
```

```python
import functools

import jax
import jax.numpy as jnp
from jax import lax
from jax.experimental import pallas as pl
from jax.experimental.pallas import tpu as pltpu
from jax.sharding import PartitionSpec as P

H = 12
HEAD = 64
SEQ_BLOCK = 2


EPSILON = 1e-06
PRECISE = lax.Precision.HIGHEST
NEGATIVE = -1e30


def to_low(value):
    return value.astype(jnp.bfloat16)


def norm_scale(hidden, gain):
    return hidden * lax.rsqrt(jnp.mean(hidden * hidden, axis=-1, keepdims=True) + EPSILON) * gain


def matmul(left, right):
    return jnp.dot(left, right, preferred_element_type=jnp.float32)


def left_product(left, right):
    return lax.dot_general(
        left, right, (((0,), (0,)), ((), ())), preferred_element_type=jnp.float32
    )


def right_product(left, right):
    return lax.dot_general(
        left, right, (((1,), (1,)), ((), ())), preferred_element_type=jnp.float32
    )


def split_heads(array):
    return array.reshape(array.shape[:-1] + (H, HEAD))


def score_block(queries, key_rows, offset):
    scores = jnp.einsum(
        "sqhe,skhe->shqk",
        split_heads(queries),
        split_heads(key_rows),
        preferred_element_type=jnp.float32,
    )
    return scores + offset


def attend_forward(queries, key_rows, value_rows, offset):
    scores = score_block(queries, key_rows, offset)
    top_score = jnp.max(scores, axis=-1, keepdims=True)
    log_total = top_score + jnp.log(jnp.sum(jnp.exp(scores - top_score), axis=-1, keepdims=True))
    weights = to_low(jnp.exp(scores - log_total))
    context = jnp.einsum(
        "shqk,skhe->sqhe", weights, split_heads(value_rows), preferred_element_type=jnp.float32
    )
    return (to_low(context).reshape(queries.shape), log_total)


def attend_backward(queries, key_rows, value_rows, offset, log_total, context_grad, with_bias):
    scores = score_block(queries, key_rows, offset)
    probs = jnp.exp(scores - log_total)
    weights = to_low(probs)
    grad_heads = split_heads(context_grad)
    value_grad = jnp.einsum(
        "shqk,sqhe->skhe", weights, grad_heads, preferred_element_type=jnp.float32
    )
    prob_grad = jnp.einsum(
        "sqhe,skhe->shqk", grad_heads, split_heads(value_rows), preferred_element_type=jnp.float32
    )
    score_grad = to_low(probs * (prob_grad - jnp.sum(probs * prob_grad, axis=-1, keepdims=True)))
    query_grad = jnp.einsum(
        "shqk,skhe->sqhe", score_grad, split_heads(key_rows), preferred_element_type=jnp.float32
    )
    key_grad = jnp.einsum(
        "shqk,sqhe->skhe", score_grad, split_heads(queries), preferred_element_type=jnp.float32
    )
    grads = (
        query_grad.reshape(queries.shape),
        key_grad.reshape(key_rows.shape),
        value_grad.reshape(value_rows.shape),
    )
    if with_bias:
        return grads + (jnp.sum(score_grad.astype(jnp.float32), axis=0),)
    return grads


MESH = pl.DeviceIdType.MESH
ALL = slice(None)


class Place:
    def __init__(self, sizes):
        self.ny, self.nz = sizes
        self.dp = lax.axis_index("dp")
        self.fs = lax.axis_index("fsdp")
        self.c, self.y = lax.rem(self.dp, 2), lax.div(self.dp, 2)
        self.x, self.z = lax.rem(self.fs, 2), lax.div(self.fs, 2)

    def size(self, dim):
        return {"c": 2, "x": 2, "y": self.ny, "z": self.nz}[dim]

    def at(self, dim):
        return {"c": self.c, "x": self.x, "y": self.y, "z": self.z}[dim]

    def device(self, dim, index):
        if dim == "c":
            return (self.y * 2 + index, self.fs)
        if dim == "y":
            return (index * 2 + self.c, self.fs)
        if dim == "x":
            return (self.dp, self.z * 2 + index)
        return (self.dp, index * 2 + self.x)


def neighbour_barrier(place, far=False):
    barrier = pltpu.get_barrier_semaphore()
    links = []
    for dim in "cxyz":
        here, size = place.at(dim), place.size(dim)
        reach = 1
        while reach < size and (reach == 1 or far):
            if size == 2:
                links.append((dim, 1 - here, None))
            elif reach == 1:
                for step in (1, -1):
                    links.append((dim, here + step, (here + step >= 0) & (here + step < size)))
            else:
                links.append((dim, here + reach - 2 * reach * lax.rem(lax.div(here, reach), 2), None))
            reach *= 2

    def signal(dim, there):
        pl.semaphore_signal(barrier, inc=1, device_id=place.device(dim, there), device_id_type=MESH)

    for dim, there, condition in links:
        if condition is None:
            signal(dim, there)
        else:
            pl.when(condition)(lambda dim=dim, there=there: signal(dim, there))
    peers = sum(1 if condition is None else condition.astype(jnp.int32) for _, _, condition in links)
    pl.semaphore_wait(barrier, peers)


PATHS = ("zxy", "zyx", "xzy", "yzx")


class Link:
    def __init__(self, copy, sends=None, receives=None):
        self.copy, self.sends, self.receives = copy, sends, receives

    @staticmethod
    def when(condition, run):
        if condition is None:
            run()
        else:
            pl.when(condition)(run)

    def start(self):
        self.when(self.sends, lambda: self.copy.start())

    def wait_send(self):
        self.when(self.sends, lambda: self.copy.wait_send())

    def wait_recv(self):
        self.when(self.receives, lambda: self.copy.wait_recv())


def pick(held, place, **fixed):
    return tuple(fixed.get(dim, ALL if dim in held else place.at(dim)) for dim in "yczx")


def gather_steps(place, blocks, path, sems):
    steps, slot, held = [], 0, ""
    for dim in path + "c":
        here, size = place.at(dim), place.size(dim)
        if size == 2:
            there = 1 - here
            index = pick(held, place)
            copy = pltpu.make_async_remote_copy(
                blocks(index), blocks(index), sems[0].at[slot], sems[1].at[slot],
                device_id=place.device(dim, there), device_id_type=MESH,
            )
            steps.append([Link(copy)])
            slot += 1
        else:
            for hop in range(1, size):
                links = []
                for way in (1, -1):
                    origin = here - way * (hop - 1)
                    there = here + way
                    source = here - way * hop
                    index = pick(held, place, **{dim: jnp.clip(origin, 0, size - 1)})
                    copy = pltpu.make_async_remote_copy(
                        blocks(index), blocks(index), sems[0].at[slot], sems[1].at[slot],
                        device_id=place.device(dim, jnp.clip(there, 0, size - 1)), device_id_type=MESH,
                    )
                    sends = (origin >= 0) & (origin < size) & (there >= 0) & (there < size)
                    links.append(Link(copy, sends, (source >= 0) & (source < size)))
                    slot += 1
                steps.append(links)
        held += dim
    return steps


def slot_count(sizes):
    ny, nz = sizes
    return 2 + (1 if ny == 2 else 2 * (ny - 1)) + (1 if nz == 2 else 2 * (nz - 1))


def run_steps(plans, lag):
    rounds = max(lag[i] + len(plan) for i, plan in enumerate(plans)) + 1
    for now in range(rounds):
        for offset, plan in zip(lag, plans):
            at = now - offset
            if 1 <= at <= len(plan):
                for link in plan[at - 1]:
                    link.wait_recv()
            if 0 <= at < len(plan):
                for link in plan[at]:
                    link.start()
    for plan in plans:
        for links in plan:
            for link in links:
                link.wait_send()


def gather_kernel(sizes, *refs):
    shards, wholes = refs[:11], refs[11:22]
    own_sem, send_sem, recv_sem = refs[22:]
    place = Place(sizes)
    own = (place.y, place.c, place.z, place.x)
    owns = [
        pltpu.make_async_copy(shard, whole.at[own], own_sem.at[i])
        for i, (shard, whole) in enumerate(zip(shards, wholes))
    ]
    for copy in owns:
        copy.start()
    neighbour_barrier(place)
    views = [lambda index, ref=ref: ref.at[index] for ref in wholes[:9]]
    width = wholes[8].shape[-1]
    for q in range(4):
        views.append(
            lambda index, q=q: wholes[9].at[index + (ALL, pl.ds(q * width, width))]
        )
    for q in range(4):
        views.append(lambda index, q=q: wholes[10].at[index + (q,)])
    plans, lag = [], []
    for i, view in enumerate(views):
        path = PATHS[0] if i == 0 else PATHS[(i - 1) % 4]
        plans.append(gather_steps(place, view, path, (send_sem.at[i], recv_sem.at[i])))
        lag.append(0 if i == 0 else 3 * ((i - 1) // 4))
    for copy in owns:
        copy.wait()
    run_steps(plans, lag)


def gather_weights(sizes, table, gains, squares, inner, outer):
    ny, nz = sizes
    grid = (ny, 2, nz, 2)
    part, width = squares[0].shape
    small = jnp.zeros((16, 128), table.dtype)
    small = small.at[: table.shape[0], :part].set(table)
    for i, gain in enumerate(gains):
        small = small.at[table.shape[0] + i, :part].set(gain)
    shards = (small,) + tuple(squares) + (inner, outer.reshape(4, part, width))
    anywhere = pl.BlockSpec(memory_space=pl.ANY)
    slots = slot_count(sizes)
    wholes = pl.pallas_call(
        functools.partial(gather_kernel, sizes),
        out_shape=[jax.ShapeDtypeStruct(grid + s.shape, s.dtype) for s in shards],
        in_specs=[anywhere] * 11,
        out_specs=[anywhere] * 11,
        scratch_shapes=[
            pltpu.SemaphoreType.DMA((11,)),
            pltpu.SemaphoreType.DMA((17, slots)),
            pltpu.SemaphoreType.DMA((17, slots)),
        ],
        compiler_params=pltpu.CompilerParams(collective_id=0, has_side_effects=True),
    )(*shards)
    count = ny * nz * 4
    tiny = wholes[0].reshape(count, 16, 128)[:, :, :part].transpose(1, 0, 2).reshape(16, count * part)
    rows = table.shape[0]
    return (
        (tiny[rows], tiny[rows + 1], tiny[rows + 2], tiny[:rows])
        + tuple(w.reshape(count * part, width) for w in wholes[1:9])
        + (wholes[9].reshape(count * part, 4 * width), wholes[10].reshape(4 * count * part, width))
    )


class Reduce:
    def __init__(self, place, path, source, total, core_in, boxes, out, sems):
        self.place, self.path, self.source, self.total = place, path, source, total
        self.core_in, self.boxes, self.out, self.sems = core_in, boxes, out, sems
        self.slot = 0
        self.sent = []

    def copy(self, source, target, dim, there):
        slot = self.slot
        self.slot += 1
        return pltpu.make_async_remote_copy(
            source, target, self.sems[0].at[slot], self.sems[1].at[slot],
            device_id=self.place.device(dim, there), device_id_type=MESH,
        )

    def index(self, fixed):
        return tuple(fixed.get(dim, ALL) for dim in "yzx")

    def add(self, target, box):
        shape = box.shape[:-2]
        count = 1
        for size in shape:
            count *= size
        free = [i for i, entry in enumerate(target) if entry is ALL]

        def body(n, _):
            spots, rest = [], n
            for size in reversed(shape):
                spots.append(lax.rem(rest, size))
                rest = lax.div(rest, size)
            spots = spots[::-1]
            full = list(target)
            for place_at, spot in zip(free, spots):
                full[place_at] = spot
            mine = self.total[tuple(full)].astype(jnp.float32)
            got = box[tuple(spots)].astype(jnp.float32)
            self.total[tuple(full)] = (mine + got).astype(jnp.bfloat16)
            return 0

        if count == 1:
            body(0, 0)
        else:
            lax.fori_loop(0, count, body, 0)

    def steps(self):
        place, listing = self.place, []
        own = pltpu.make_async_copy(self.source(place.c), self.total, self.sems[2])
        core = self.copy(self.source(1 - place.c), self.core_in, "c", 1 - place.c)

        def start():
            own.start()
            core.start()

        def finish():
            own.wait()
            core.wait_recv()
            self.add((ALL, ALL, ALL), self.core_in)

        self.sent.append(Link(core))
        listing.append((start, finish))
        fixed, box = {}, 0
        for dim in self.path:
            here, size = place.at(dim), place.size(dim)
            if size == 2:
                target = self.index({**fixed, dim: 1 - here})
                link = Link(self.copy(self.total.at[target], self.boxes[box], dim, 1 - here))
                self.sent.append(link)
                listing.append(self.pair([link], [(self.index({**fixed, dim: here}), box, None)]))
                box += 1
            else:
                for hop in range(size - 1, 0, -1):
                    links, adds = [], []
                    for way in (1, -1):
                        there = here - way
                        goal = here - way * hop
                        sends = (goal >= 0) & (goal < size)
                        source = here + way
                        got = source - way * hop
                        receives = (source >= 0) & (source < size) & (got >= 0) & (got < size)
                        target = self.index({**fixed, dim: jnp.clip(goal, 0, size - 1)})
                        copy = self.copy(
                            self.total.at[target], self.boxes[box], dim, jnp.clip(there, 0, size - 1)
                        )
                        link = Link(copy, sends, receives)
                        self.sent.append(link)
                        links.append(link)
                        adds.append((self.index({**fixed, dim: jnp.clip(got, 0, size - 1)}), box, receives))
                        box += 1
                    listing.append(self.pair(links, adds))
            fixed = {**fixed, dim: here}
        return listing

    def pair(self, links, adds):
        def start():
            for link in links:
                link.start()

        def finish():
            for link in links:
                link.wait_recv()
            for target, box, condition in adds:
                Link.when(condition, functools.partial(self.add, target, self.boxes[box]))

        return start, finish

    def close(self):
        own = (self.place.y, self.place.z, self.place.x)
        self.out(self.total[own].astype(jnp.float32))
        for link in self.sent:
            link.wait_send()


def box_shapes(sizes, path):
    ny, nz = sizes
    size = {"y": ny, "z": nz, "x": 2}
    left, shapes = "yzx", []
    for dim in path:
        left = left.replace(dim, "")
        lead = tuple(size[d] for d in left)
        shapes += [lead] * (1 if size[dim] == 2 else 2 * (size[dim] - 1))
    return shapes


BACK_PATHS = tuple(path[::-1] for path in PATHS)


def reduce_kernel(sizes, box_counts, *refs):
    sources, small_in = refs[:10], refs[10]
    outs, small_out = refs[11:21], refs[21]
    totals, core_boxes = refs[22], refs[23]
    at = 24
    boxes = []
    for count in box_counts:
        boxes.append(refs[at : at + count])
        at += count
    small_box, own_sem, send_sem, recv_sem, small_send, small_recv = refs[at:]
    place = Place(sizes)
    neighbour_barrier(place, far=True)
    width = outs[0].shape[-1]

    def square(ref):
        return lambda core: ref.at[:, core]

    def inner(q):
        return lambda core: sources[8].at[:, core, :, :, :, pl.ds(q * width, width)]

    def outer(q):
        return lambda core: sources[9].at[:, core, :, :, q]

    views = [inner(q) for q in range(4)] + [outer(q) for q in range(4)]
    views += [square(sources[i]) for i in (4, 5, 6, 7, 0, 1, 2, 3)]

    def store_square(i):
        def run(value):
            outs[i][...] = value

        return run

    def store_inner(q):
        def run(value):
            outs[8][:, q * width : (q + 1) * width] = value

        return run

    def store_outer(q):
        def run(value):
            outs[9][q] = value

        return run

    stores = [store_inner(q) for q in range(4)] + [store_outer(q) for q in range(4)]
    stores += [store_square(i) for i in (4, 5, 6, 7, 0, 1, 2, 3)]
    plans, lag = [], []
    reduces = []
    for m in range(16):
        group, kind = m // 4, m % 4
        reduce = Reduce(
            place, BACK_PATHS[kind], views[m], totals.at[m], core_boxes.at[m],
            [box.at[group] for box in boxes[kind]], stores[m],
            (send_sem.at[m], recv_sem.at[m], own_sem.at[m]),
        )
        reduces.append(reduce)
        plans.append(reduce.steps())
        lag.append(3 * group)
    small_out[...] = small_in[...]
    small = []
    moves = [("c", 1 - place.c), ("x", 1 - place.x), ("y", None), ("z", None)]
    for dim, there in moves:
        size, here, reach = place.size(dim), place.at(dim), 1
        while reach < size:
            partner = here + reach - 2 * reach * lax.rem(lax.div(here, reach), 2)
            small.append((dim, partner))
            reach *= 2
    rounds = max(max(lag[i] + len(plan) for i, plan in enumerate(plans)) + 1, len(small) + 1)
    copies = []
    for now in range(rounds):
        for offset, plan in zip(lag, plans):
            step = now - offset
            if 1 <= step <= len(plan):
                plan[step - 1][1]()
            if 0 <= step < len(plan):
                plan[step][0]()
        if 1 <= now <= len(small):
            copies[-1].wait()
            small_out[...] += small_box[now - 1]
        if now < len(small):
            dim, partner = small[now]
            copies.append(
                pltpu.make_async_remote_copy(
                    small_out, small_box.at[now], small_send.at[now], small_recv.at[now],
                    device_id=place.device(dim, partner), device_id_type=MESH,
                )
            )
            copies[-1].start()
    for reduce in reduces:
        reduce.close()


def reduce_grads(sizes, language, bucket, gains, squares, inner, outer):
    ny, nz = sizes
    grid = (ny, 2, nz, 2)
    count = ny * nz * 4
    width = squares[0].shape[1]
    part = squares[0].shape[0] // count
    langs = language.shape[0]
    flat = jnp.zeros((width,), jnp.float32).at[: bucket.size].set(bucket.reshape(-1))
    small = jnp.concatenate(
        [language] + [g.reshape(1, width) for g in gains] + [flat[None], jnp.zeros((4, width), jnp.float32)], axis=0
    )
    sources = [to_low(s).reshape(grid + (part, width)) for s in squares]
    sources += [
        to_low(inner).reshape(grid + (part, 4 * width)),
        to_low(outer).reshape(grid + (4, part, width)),
    ]
    anywhere = pl.BlockSpec(memory_space=pl.ANY)
    vmem = pl.BlockSpec(memory_space=pltpu.VMEM)
    shapes = [(part, width)] * 8 + [(part, 4 * width), (4, part, width), small.shape]
    lead = [box_shapes(sizes, path) for path in BACK_PATHS]
    slots = slot_count(sizes)
    hops = (ny * nz * 4).bit_length() - 1
    outs = pl.pallas_call(
        functools.partial(reduce_kernel, sizes, tuple(len(s) for s in lead)),
        out_shape=[jax.ShapeDtypeStruct(s, jnp.float32) for s in shapes],
        in_specs=[anywhere] * 10 + [vmem],
        out_specs=[vmem] * 11,
        scratch_shapes=[
            pltpu.VMEM((16, ny, nz, 2, part, width), jnp.bfloat16),
            pltpu.VMEM((16, ny, nz, 2, part, width), jnp.bfloat16),
        ]
        + [pltpu.VMEM((4,) + s + (part, width), jnp.bfloat16) for one in lead for s in one]
        + [
            pltpu.VMEM((hops,) + small.shape, jnp.float32),
            pltpu.SemaphoreType.DMA((16,)),
            pltpu.SemaphoreType.DMA((16, slots)),
            pltpu.SemaphoreType.DMA((16, slots)),
            pltpu.SemaphoreType.DMA((hops,)),
            pltpu.SemaphoreType.DMA((hops,)),
        ],
        compiler_params=pltpu.CompilerParams(
            collective_id=1, has_side_effects=True, vmem_limit_bytes=60 * 1024 * 1024
        ),
    )(*sources, small)
    start = (lax.axis_index("dp") * nz * 2 + lax.axis_index("fsdp")) * part
    total = outs[10]
    mine = lax.dynamic_slice(total, (0, start), (langs + 3, part))
    return (
        mine[:langs],
        total[langs + 3, : bucket.size].reshape(bucket.shape),
        mine[langs], mine[langs + 1], mine[langs + 2],
        outs[:8], outs[8], outs[9].reshape(4 * part, width),
    )


FORWARD_PATHS = (
    "yzx", "zxy", "zyx", "zxy", "zxy", "yxz", "zxy", "yzx", "yzx", "zxy", "xyz", "zyx", "zyx", "xyz", "zxy",
    "zyx", "xzy",
)
FORWARD_ORDER = (
    1, 2, 10, 16, 5, 6, 7, 8, 13, 5, 10, 1, 0, 2, 13, 3, 1, 1, 2, 2, 6, 4, 6, 12, 3, 6, 1, 3, 12, 11, 7, 3, 4,
    2, "b0", 9, 0, 7, 11, 3, 6, 4, 1, 0, 16, 0, 14, 7, 1, 12, 0, 4, "b1", 7, 9, 2, 14, 14, 9, 12, 8, 14, 0, 3,
    "b2", 2, 0, 5, "open", 11, 4, 6, 3, "q", 8, 9, "v", 6, "b3", 5, "k", 15, 12, "sa0", 11, "K", 8, 9, "sa1", 8,
    5, 4, 15, 7, 10, "sa2", "sa3", 4, 5, 15, 16, "send", 7, "V", 15, 5, "cq", 11, 10, 14, "ca0", 12, "ca1", 8,
    9, 16, 15, 10, 13, "ca2", 16, "ca3", 10, 8, "cend", 9, 11, "in0", 10, 13, 14, 12, "in1", 11, "in2", 13, 15,
    14, "og1", 16, "in3", 13, "og2", 15, "og0", 16, "og3", 13,
)
BACKWARD_PATHS = (
    "xyz", "yzx", "yxz", "xzy", "xzy", "xyz", "yzx", "yxz", "yzx", "xzy", "yxz", "xyz", "yxz", "yzx", "xyz",
    "xzy",
)
BACKWARD_ORDER = (
    3, 1, "in0", 3, 1, 0, 2, "in1", 0, 4, "in2", 6, 2, "in3", 7, "n3", 1, 4, 3, "co", 6, "ccg", 1, "ca0", 5, 7,
    3, 2, 8, "ca1", 1, "ca2", 5, "ca3", "ca4", 4, 6, "ca5", 3, "cq", 9, 4, 2, 0, "n2", "cv", 1, 7, 8, 11, 9, 4,
    "ck", 5, 10, "so", 0, "scg", 2, 6, "sa0", 7, 11, "sa1", 6, 0, "sa2", 7, 10, "q", 8, "v", 3, 5, 15, 6, 13,
    "k", 2, 7, 12, 9, 8, 0, "cl0", 1, 15, 2, 5, 13, 14, 4, 9, "bk0", 6, 8, 5, "cl1", 12, 9, 0, 10, 14, 11,
    "bk1", 15, 13, "bk2", 5, 3, 10, 15, "h0", 10, 13, 4, "h1", 16, 12, "h2", 16, 7, 15, "h3", 13, 10, 14, "e0",
    11, 12, 16, 8, 10, 14, 11, 9, 15, 12, 13, 16, 8, 14, 11, 15, 13, 9, 12, 16, 14, "e1", 11, 14, 16, 12,
)


LOW = jnp.bfloat16
FULL = jnp.float32
PAIR = 2 * HEAD


def nt_dot(left, right):
    return lax.dot_general(left, right, (((1,), (1,)), ((), ())), preferred_element_type=FULL)


def tn_dot(left, right):
    return lax.dot_general(left, right, (((0,), (0,)), ((), ())), preferred_element_type=FULL)


def flat(ref, *suffix):
    value = ref[(ALL,) * (len(ref.shape) - 1) + suffix] if suffix else ref[...]
    rows = 1
    for size in value.shape[:-1]:
        rows *= size
    return value.reshape(rows, value.shape[-1])


def each(count, body):
    def run(i, _):
        body(pl.ds(pl.multiple_of(i * 128, 128), 128))
        return 0

    lax.fori_loop(0, count, run, 0)


def unit_rows(hidden):
    return hidden * lax.rsqrt(jnp.mean(hidden * hidden, axis=-1, keepdims=True) + EPSILON)


def spread_small(tiny, table):
    part = table.shape[1] // (tiny.shape[0] * tiny.shape[2] * 4)
    table[...] = jnp.zeros_like(table)
    lane = lax.broadcasted_iota(jnp.int32, (16, 128), 1)
    at = 0
    for y in range(tiny.shape[0]):
        for core in range(2):
            for z in range(tiny.shape[2]):
                for x in range(2):
                    slab = jnp.where(lane < part, tiny[y, core, z, x], 0.0)
                    base, shift = at // 128 * 128, at % 128
                    if shift:
                        slab = pltpu.roll(slab, shift, 1)
                    if shift + part <= 128:
                        table[:, base : base + 128] += slab
                    else:
                        table[:, base : base + 128] += jnp.where(lane >= part, slab, 0.0)
                        table[:, base + 128 : base + 256] += jnp.where(lane < part, slab, 0.0)
                    at += part


def build_bias(ids, values, bias, heads):
    keys, queries = bias.shape[1:]
    rows = 64

    def block(n, _):
        at = pl.ds(pl.multiple_of(n * rows, rows), rows)
        bucket = ids[at, :]
        bits = [lax.bitwise_and(bucket, 1 << b) != 0 for b in range(5)]
        key = n * rows + lax.broadcasted_iota(jnp.int32, (rows, queries), 0)
        query = lax.broadcasted_iota(jnp.int32, (rows, queries), 1)
        hidden = key > query

        def head(h, _):
            row, first = 11 + lax.div(h, 4), lax.rem(h, 4) * 32
            level = [values[row, first + c] for c in range(32)]
            for bit in bits:
                level = [jnp.where(bit, level[i + 1], level[i]) for i in range(0, len(level), 2)]
            bias[h, at, :] = jnp.where(hidden, NEGATIVE, level[0]).astype(LOW)
            return 0

        return lax.fori_loop(*heads, head, 0)

    lax.fori_loop(0, keys // rows, block, 0)


def head_pair(value):
    lane = lax.broadcasted_iota(jnp.int32, value.shape, 1)
    zero = jnp.zeros_like(value)
    return jnp.concatenate([jnp.where(lane < HEAD, value, zero), jnp.where(lane < HEAD, zero, value)], axis=0)


def pairs_forward(items):
    scores = [nt_dot(keys, head_pair(queries)) for queries, keys, _, _ in items]
    scores = [s if item[3] is None else s + item[3] for s, item in zip(scores, items)]
    grown = [jnp.exp(s - jnp.max(s, axis=0, keepdims=True)) for s in scores]
    rows = [1.0 / jnp.sum(g, axis=0, keepdims=True) for g in grown]
    weights = [g.astype(LOW) for g in grown]
    results = []
    for (queries, _, values, _), low, row in zip(items, weights, rows):
        count = queries.shape[0]
        lane = lax.broadcasted_iota(jnp.int32, values.shape, 1)
        one = jnp.ones_like(values)
        first = tn_dot(low[:, :count], jnp.where(lane < HEAD, values, one))
        second = tn_dot(low[:, count:], jnp.where(lane < HEAD, one, values))
        lane = lax.broadcasted_iota(jnp.int32, first.shape, 1)
        inverse = 1.0 / pltpu.roll(jnp.where(lane < HEAD, second, first), HEAD, 1)
        results.append((jnp.where(lane < HEAD, first, second) * inverse, inverse, low, row))
    return results


def gelu_parts(u):
    a, b = 0.7978845608028654, 0.044715
    square = u * u
    t = jnp.tanh(a * u * (1.0 + b * square))
    half = 0.5 * (1.0 + t)
    slope = half + 0.5 * u * (1.0 - t * t) * (a * (1.0 + 3.0 * b * square))
    return u * half, slope


def gather_plans(place, wholes, small, sems):
    views = [lambda index, ref=ref: ref.at[index] for ref in [small] + list(wholes[:8])]
    width = wholes[0].shape[-1]
    for q in range(4):
        views.append(lambda index, q=q: wholes[8].at[index + (ALL, pl.ds(q * width, width))])
    for q in range(4):
        views.append(lambda index, q=q: wholes[9].at[index + (q,)])
    return [
        gather_steps(place, view, path, (sems[0].at[i], sems[1].at[i]))
        for i, (view, path) in enumerate(zip(views, FORWARD_PATHS))
    ]


def run_order(order, plans, tasks, done):
    at = [0] * len(plans)
    for entry in order:
        if isinstance(entry, str):
            tasks[entry]()
            continue
        step, plan = at[entry], plans[entry]
        at[entry] += 1
        if step >= 1:
            for link in plan[step - 1]:
                link.wait_recv()
        if step < len(plan):
            for link in plan[step]:
                link.start()
        else:
            done(entry)


SAVED = (
    "first_norm", "queries", "keys", "values", "self_context", "second_norm", "cross_queries",
    "source_keys", "source_values", "cross_context", "third_norm", "activated", "slope",
    "start", "mid", "late", "self_inverse", "cross_inverse", "self_rows", "cross_rows", "table",
)


def saved_shapes(tokens, sources, width, length):
    low, full = LOW, FULL
    row = (tokens, width)
    pairs = tokens // length * (width // PAIR)
    shapes = {name: (row, low) for name in SAVED}
    shapes["source_keys"] = shapes["source_values"] = ((2, sources // 2, width), low)
    shapes["activated"] = shapes["slope"] = ((4,) + row, low)
    for name in ("start", "mid", "late", "self_inverse", "cross_inverse"):
        shapes[name] = (row, full)
    shapes["self_rows"] = shapes["cross_rows"] = ((pairs, 1, 2 * length), full)
    shapes["table"] = ((16, width), full)
    return shapes


def forward_kernel(sizes, *refs):
    n = len(SAVED)
    small_shard, shards = refs[0], refs[1:11]
    hidden_in, upstream_in, encoder_in, languages, sources, ids, slab_values = refs[11:18]
    outer_grads, whole_outs = refs[18], refs[19:29]
    self_weights, cross_weights = refs[29:31]
    saved_outs = dict(zip(SAVED, refs[31 : 31 + n]))
    at = 31 + n
    tiny, wholes = refs[at], refs[at + 1 : at + 11]
    at += 11
    v = dict(zip(SAVED, refs[at : at + n]))
    at += n
    bias, stage, outer_blocks, hidden, upstream, encoder, ids_across = refs[at : at + 7]
    own_sem, send_sem, recv_sem, out_sem, stage_sem, in_sem = refs[at + 7 :]
    tokens, width = hidden.shape
    length = ids.shape[0]
    per_seq = width // PAIR
    seqs = tokens // length
    enc_length = encoder.shape[0] // 2
    blocks = tokens // 128

    place = Place(sizes)
    own = (place.y, place.c, place.z, place.x)
    owns = [
        pltpu.make_async_copy(shard, whole.at[own], own_sem.at[i])
        for i, (shard, whole) in enumerate(zip((small_shard,) + shards, (tiny,) + wholes))
    ]
    for copy in owns:
        copy.start()
    inputs = [
        pltpu.make_async_copy(source, target, in_sem.at[i])
        for i, (source, target) in enumerate(((hidden_in, hidden), (encoder_in, encoder), (upstream_in, upstream)))
    ]
    for copy in inputs:
        copy.start()
    neighbour_barrier(place)
    plans = gather_plans(place, wholes, tiny, (send_sem, recv_sem))
    for copy in owns:
        copy.wait()
    copies = []

    def keep(name):
        copy = pltpu.make_async_copy(v[name], saved_outs[name], out_sem.at[len(copies)])
        copy.start()
        copies.append(copy)

    def keep_whole(m):
        if m == 0:
            return
        if m < 9:
            source, target = wholes[m - 1], whole_outs[m - 1]
        elif m < 13:
            index = (ALL,) * 5 + (pl.ds((m - 9) * width, width),)
            source, target = wholes[8].at[index], whole_outs[8].at[index]
        else:
            index = (ALL,) * 4 + (m - 13,)
            source, target = wholes[9].at[index], whole_outs[9].at[index]
        copy = pltpu.make_async_copy(source, target, out_sem.at[len(copies)])
        copy.start()
        copies.append(copy)

    def opening():
        inputs.pop(0).wait()
        spread_small(tiny, v["table"])
        for s in range(seqs):
            row = jnp.zeros((1, width), FULL)
            for l in range(8):
                row = row + jnp.where(languages[s] == l, v["table"][l : l + 1, :], 0.0)

            def body(at):
                start = hidden[at, :].astype(FULL) + row
                v["start"][at, :] = start
                v["first_norm"][at, :] = (unit_rows(start) * v["table"][8:9, :]).astype(LOW)

            def run(i, _):
                body(pl.ds(pl.multiple_of(s * length + i * 128, 128), 128))
                return 0

            lax.fori_loop(0, length // 128, run, 0)
        keep("table")
        keep("start")
        keep("first_norm")

    def project(source, weight, target):
        target[...] = jnp.dot(source[...], flat(weight), preferred_element_type=FULL).astype(LOW)

    leaving = {}

    def attention(turn, queries, keys, values, context, inverse, rows, weights_out, seq, first, last, picked):
        row_at = pl.ds(seq * length, length)
        key_rows = length if picked is None else enc_length
        items = []
        for p in range(first, last):
            lanes = pl.ds(p * PAIR, PAIR)
            if picked is not None:
                items.append((queries[row_at, lanes], keys[picked, :, lanes], values[picked, :, lanes], None))
            else:
                offset = jnp.concatenate([bias[2 * p], bias[2 * p + 1]], axis=1).astype(FULL)
                items.append((queries[row_at, lanes], keys[row_at, lanes], values[row_at, lanes], offset))
        for n, (out, total, low, row) in enumerate(pairs_forward(items)):
            lanes = pl.ds((first + n) * PAIR, PAIR)
            index = seq * per_seq + first + n
            slot = turn % 2 * (last - first) + n
            if slot in leaving:
                leaving[slot].wait()
            part = stage.at[slot, pl.ds(0, key_rows)]
            part[...] = low
            rows[index] = row
            context[row_at, lanes] = out.astype(LOW)
            inverse[row_at, lanes] = total
            leaving[slot] = pltpu.make_async_copy(part, weights_out.at[index], stage_sem.at[slot])
            leaving[slot].start()

    def residual(context, weight, before, after, gain_row, norm):
        def body(at):
            state = before[at, :] + jnp.dot(context[at, :], flat(weight), preferred_element_type=FULL)
            after[at, :] = state
            norm[at, :] = (unit_rows(state) * v["table"][gain_row : gain_row + 1, :]).astype(LOW)

        each(blocks, body)

    def self_projection(i, name):
        project(v["first_norm"], wholes[i], v[name])
        keep(name)

    def self_attention(turn, s, first, last):
        attention(
            turn, v["queries"], v["keys"], v["values"], v["self_context"], v["self_inverse"], v["self_rows"],
            self_weights, s, first, last, None,
        )

    def self_end():
        for name in ("self_context", "self_inverse", "self_rows"):
            keep(name)
        residual(v["self_context"], wholes[3], v["start"], v["mid"], 9, v["second_norm"])
        keep("mid")
        keep("second_norm")

    def cross_source(i, name):
        if len(inputs) == 2:
            inputs.pop(0).wait()
        for half in range(2):
            v[name][half] = jnp.dot(
                encoder[pl.ds(half * enc_length, enc_length), :], flat(wholes[i]), preferred_element_type=FULL
            ).astype(LOW)
        keep(name)

    def cross_projection():
        project(v["second_norm"], wholes[4], v["cross_queries"])
        keep("cross_queries")

    def cross_attention(turn, s, first, last):
        attention(
            turn, v["cross_queries"], v["source_keys"], v["source_values"], v["cross_context"], v["cross_inverse"],
            v["cross_rows"], cross_weights, s, first, last, sources[s],
        )

    def cross_end():
        for name in ("cross_context", "cross_inverse", "cross_rows"):
            keep(name)
        residual(v["cross_context"], wholes[7], v["mid"], v["late"], 10, v["third_norm"])
        keep("late")
        keep("third_norm")

    def feed_inner(q):
        weight = flat(wholes[8], pl.ds(q * width, width))
        for half in range(2):
            at = pl.ds(half * tokens // 2, tokens // 2)
            expanded = jnp.dot(v["third_norm"][at, :], weight, preferred_element_type=FULL)
            value, slope = gelu_parts(expanded)
            v["activated"][q, at, :] = value.astype(LOW)
            v["slope"][q, at, :] = slope.astype(LOW)
        if q == 3:
            keep("activated")
            keep("slope")

    def bias_values(turn):
        if turn == 0:
            ids_across[...] = ids[...].astype(FULL).T.astype(jnp.int32)
        build_bias(ids_across, slab_values, bias, (3 * turn, 3 * turn + 3))

    def outer_grad(q):
        if inputs:
            inputs.pop(0).wait()
        value = tn_dot(v["activated"][q], upstream[...])
        outer_blocks[q // 2, q % 2] = value.reshape(outer_blocks.shape[2:]).astype(LOW)
        chunk = q // 2, q % 2
        copy = pltpu.make_async_copy(outer_blocks.at[chunk], outer_grads.at[chunk], out_sem.at[len(copies)])
        copy.start()
        copies.append(copy)

    tasks = {"open": opening, "send": self_end}
    tasks.update(cq=cross_projection, cend=cross_end)
    for i, (task, name) in enumerate((("q", "queries"), ("k", "keys"), ("v", "values"))):
        tasks[task] = functools.partial(self_projection, i, name)
    for i in range(4):
        first = per_seq // 2 * (i % 2)
        tasks[f"sa{i}"] = functools.partial(self_attention, i, i // 2, first, first + per_seq // 2)
        tasks[f"ca{i}"] = functools.partial(cross_attention, i, i // 2, first, first + per_seq // 2)
        tasks[f"in{i}"] = functools.partial(feed_inner, i)
        tasks[f"b{i}"] = functools.partial(bias_values, i)
        tasks[f"og{i}"] = functools.partial(outer_grad, i)
    tasks["K"] = functools.partial(cross_source, 5, "source_keys")
    tasks["V"] = functools.partial(cross_source, 6, "source_values")
    run_order(FORWARD_ORDER, plans, tasks, keep_whole)
    for plan in plans:
        for links in plan:
            for link in links:
                link.wait_send()
    for copy in copies + list(leaving.values()):
        copy.wait()


def small_slab(table, gains, bucket_table):
    part = table.shape[1]
    own = jnp.concatenate([table] + [g.reshape(1, part) for g in gains], axis=0)
    own = jnp.pad(own, ((0, 0), (0, 128 - part)))
    buckets = bucket_table.T.reshape(-1, 128)
    return jnp.pad(jnp.concatenate([own, buckets], axis=0), ((0, 2), (0, 0))).astype(FULL)


def forward(
    sizes, hidden_in, output_grad, encoder_states, language_ids, source_index, bucket_ids, language_table, bucket_table, gains,
    squares, inner, outer,
):
    ny, nz = sizes
    grid = (ny, 2, nz, 2)
    part, width = squares[0].shape
    tokens = hidden_in.shape[0]
    length = bucket_ids.shape[0]
    encoder = encoder_states.reshape(-1, width)
    enc_length = encoder_states.shape[1]
    slab = small_slab(language_table, gains, bucket_table)
    shards = [slab] + list(squares) + [inner, outer.reshape(4, part, width)]
    wholes = [jax.ShapeDtypeStruct(grid + s.shape, s.dtype) for s in shards]
    shapes = saved_shapes(tokens, encoder.shape[0], width, length)
    pairs = tokens // length * (width // PAIR)
    anywhere = pl.BlockSpec(memory_space=pl.ANY)
    vmem = pl.BlockSpec(memory_space=pltpu.VMEM)
    smem = pl.BlockSpec(memory_space=pltpu.SMEM)
    slots = slot_count(sizes)
    out_shape = [wholes[10]] + wholes[1:]
    out_shape += [jax.ShapeDtypeStruct((pairs, rows, 2 * length), LOW) for rows in (length, enc_length)]
    out_shape += [jax.ShapeDtypeStruct(*shapes[name]) for name in SAVED]
    outs = pl.pallas_call(
        functools.partial(forward_kernel, sizes),
        out_shape=out_shape,
        in_specs=[anywhere] * 11 + [anywhere] * 3 + [smem, smem, vmem, smem],
        out_specs=[anywhere] * len(out_shape),
        scratch_shapes=[pltpu.VMEM(w.shape, w.dtype) for w in wholes]
        + [pltpu.VMEM(*shapes[name]) for name in SAVED]
        + [
            pltpu.VMEM((H, length, length), LOW),
            pltpu.VMEM((6, enc_length, 2 * length), LOW),
            pltpu.VMEM(wholes[10].shape, LOW),
            pltpu.VMEM((tokens, width), LOW),
            pltpu.VMEM((tokens, width), LOW),
            pltpu.VMEM(encoder.shape, LOW),
            pltpu.VMEM((length, length), jnp.int32),
            pltpu.SemaphoreType.DMA((11,)),
            pltpu.SemaphoreType.DMA((17, slots)),
            pltpu.SemaphoreType.DMA((17, slots)),
            pltpu.SemaphoreType.DMA((len(SAVED) + 20,)),
            pltpu.SemaphoreType.DMA((6,)),
            pltpu.SemaphoreType.DMA((3,)),
        ],
        compiler_params=pltpu.CompilerParams(
            collective_id=2, has_side_effects=True, vmem_limit_bytes=62 * 1024 * 1024
        ),
    )(
        *shards, hidden_in, output_grad, encoder, language_ids, source_index, bucket_ids, slab,
    )
    return outs


class Summed:
    def __init__(self, place, path, blocks, leaving, core_in, boxes, sems):
        self.place, self.blocks, self.sems = place, blocks, sems
        self.slot, self.links, self.stages = 0, [], []
        c = place.c
        core = self.copy(leaving(1 - c), core_in, "c", 1 - c)
        self.stage([Link(core)], [((ALL, c, ALL, ALL), core_in, None)])
        fixed, box = {"c": c}, 0
        for dim in path:
            here, size = place.at(dim), place.size(dim)
            if size == 2:
                copy = self.copy(blocks(self.index({**fixed, dim: 1 - here})), boxes[box], dim, 1 - here)
                self.stage([Link(copy)], [(self.index({**fixed, dim: here}), boxes[box], None)])
                box += 1
            else:
                for hop in range(size - 1, 0, -1):
                    links, adds = [], []
                    for way in (1, -1):
                        there, goal = here - way, here - way * hop
                        sends = (goal >= 0) & (goal < size)
                        source = here + way
                        got = source - way * hop
                        receives = (source >= 0) & (source < size) & (got >= 0) & (got < size)
                        copy = self.copy(
                            blocks(self.index({**fixed, dim: jnp.clip(goal, 0, size - 1)})), boxes[box], dim,
                            jnp.clip(there, 0, size - 1),
                        )
                        links.append(Link(copy, sends, receives))
                        adds.append((self.index({**fixed, dim: jnp.clip(got, 0, size - 1)}), boxes[box], receives))
                        box += 1
                    self.stage(links, adds)
            fixed = {**fixed, dim: here}
        self.own = self.index(fixed)

    def index(self, fixed):
        return tuple(fixed.get(dim, ALL) for dim in "yczx")

    def copy(self, source, target, dim, there):
        slot = self.slot
        self.slot += 1
        return pltpu.make_async_remote_copy(
            source, target, self.sems[0].at[slot], self.sems[1].at[slot],
            device_id=self.place.device(dim, there), device_id_type=MESH,
        )

    def stage(self, links, adds):
        self.links += links
        self.stages.append((links, adds))

    def start(self, step):
        for link in self.stages[step][0]:
            link.start()

    def finish(self, step):
        links, adds = self.stages[step]
        for link in links:
            link.wait_recv()

        def add(target, box):
            view = self.blocks(target)
            view[...] = view[...] + box[...]

        for target, box, condition in adds:
            Link.when(condition, functools.partial(add, target, box))

    def close(self):
        for link in self.links:
            link.wait_send()


def pairs_backward(items):
    stacked = [head_pair(item[4]) for item in items]
    prob_grads = [nt_dot(item[3], grads) for item, grads in zip(items, stacked)]
    value_parts = [jnp.dot(item[0], grads, preferred_element_type=FULL) for item, grads in zip(items, stacked)]
    scaled = [item[0].astype(FULL) * grads for item, grads in zip(items, prob_grads)]
    centres = [jnp.sum(s, axis=0, keepdims=True) * item[5] for s, item in zip(scaled, items)]
    score_grads = [(s - item[0].astype(FULL) * c).astype(LOW) for s, c, item in zip(scaled, centres, items)]
    key_parts = [jnp.dot(s, head_pair(item[1]), preferred_element_type=FULL) for s, item in zip(score_grads, items)]
    results = []
    for item, value_part, key_part, score_grad in zip(items, value_parts, key_parts, score_grads):
        count = item[1].shape[0]
        lane = lax.broadcasted_iota(jnp.int32, (count, PAIR), 1)
        first, second = tn_dot(score_grad[:, :count], item[2]), tn_dot(score_grad[:, count:], item[2])
        results.append((jnp.where(lane < HEAD, first, second), key_part, value_part, score_grad))
    return results


def backward_kernel(sizes, box_counts, *refs):
    n = len(SAVED)
    grads, encoder, languages, sources, ids_in, outer_grads = refs[:6]
    wholes = refs[6:16]
    self_weights, cross_weights = refs[16:18]
    saved = dict(zip(SAVED, refs[18 : 18 + n]))
    at = 18 + n
    hidden_out, hidden_grad, encoder_grad, small_out, packed = refs[at : at + 5]
    at += 5
    squares, outers, core_boxes = refs[at : at + 3]
    at += 3
    boxes = []
    for count in box_counts:
        boxes.append(refs[at : at + count])
        at += count
    small_box, pool, pairs_in, run_a, run_b, run_c, w, wo, stage, score_sum, bucket_rows, table, self_rows, cross_rows, ids = refs[at : at + 15]
    send_sem, recv_sem, small_send, small_recv, load_sem, stage_sem, store_sem = refs[at + 15 :]
    place = Place(sizes)
    length = ids.shape[0]
    seqs, tokens = languages.shape[0], pool.shape[1]
    width = pool.shape[2]
    blocks = tokens // 128
    per_seq = width // PAIR
    loads = []

    def load(source, target):
        copy = pltpu.make_async_copy(source, target, load_sem.at[len(loads)])
        loads.append(copy)
        copy.start()
        return copy

    X = [pool.at[i] for i in range(11)] + [pairs_in.at[i] for i in range(4)]
    og, tn = X[0], X[1]
    get_outers = load(outer_grads.at[:, place.c], outers)
    get_og = load(grads, og)
    def outer_chunk(q):
        return wholes[9].at[q // 2, q % 2]

    def inner_chunk(q):
        return wholes[8].at[:, :, :, :, :, pl.ds(q * width, width)]

    arriving = {}

    def fetch(weights, pairs, key_rows, base):
        per_slot = stage.shape[1] // key_rows
        for n, p in enumerate(pairs):
            for s in range(seqs):
                at = base * per_slot + n * seqs + s
                part = stage.at[at // per_slot, pl.ds(at % per_slot * key_rows, key_rows)]
                copy = pltpu.make_async_copy(
                    weights.at[s * per_seq + p], part, stage_sem.at[base * 2 + n * seqs + s]
                )
                copy.start()
                arriving[key_rows, p, s] = copy, part

    get_wo = [load(outer_chunk(0), wo.at[0])]
    get_slope = [load(saved["slope"].at[0], X[6])]
    get_tn = load(saved["third_norm"], tn)
    get_wi = [load(inner_chunk(0), w.at[0])]
    got = {}

    def load_more(q):
        if q < 3:
            get_slope.append(load(saved["slope"].at[q + 1], X[7 + q]))
        if q == 0:
            get_wo.append(load(outer_chunk(1), wo.at[1]))
            get_wi.append(load(inner_chunk(1), w.at[1]))
            got["table"] = load(saved["table"], table)
            got["late"] = load(saved["late"], run_c)
        if q == 1:
            got["cross_context"] = load(saved["cross_context"], X[2])
            got["co"] = load(wholes[7], w.at[2])
            got["cross_rows"] = load(saved["cross_rows"], cross_rows)
            got["cross_queries"] = load(saved["cross_queries"], X[3])
        if q == 2:
            got["keys"] = load(saved["source_keys"], pairs_in.at[pl.ds(0, 2)])
            got["values"] = load(saved["source_values"], pairs_in.at[pl.ds(2, 2)])
            fetch(cross_weights, (0,), stage.shape[1], 0)
        if q == 3:
            got["cq_w"] = load(wholes[4], w.at[3])
            got["second_norm"] = load(saved["second_norm"], X[4])
            got["first_norm"] = load(saved["first_norm"], X[5])
            got["self_rows"] = load(saved["self_rows"], self_rows)

    neighbour_barrier(place, far=True)

    def view_of(m):
        if m < 4:
            return lambda index: outers.at[(index[0],) + index[2:] + (m,)]
        return lambda index: squares.at[(m - 4,) + index]

    def leaving_of(m):
        if m < 4:
            return lambda core: outer_grads.at[:, core, :, :, m]
        return lambda core: squares.at[m - 4, :, core]

    plans = []
    for m in range(16):
        group, kind = m // 4, BACK_PATHS.index(BACKWARD_PATHS[m])
        slot = group % 2
        plans.append(
            Summed(
                place, BACK_PATHS[kind], view_of(m), leaving_of(m), core_boxes.at[slot, kind], [box.at[slot] for box in boxes[kind]],
                (send_sem.at[m], recv_sem.at[m]),
            )
        )

    def put(i, value):
        squares[i] = value.reshape(squares.shape[1:]).astype(LOW)

    small_out[...] = jnp.zeros_like(small_out)

    def norm_backward(state, inflow, gain_row, before, after):
        def body(at):
            hidden, flow, gain = state[at, :], inflow[at, :], table[gain_row : gain_row + 1, :]
            scale = lax.rsqrt(jnp.mean(hidden * hidden, axis=-1, keepdims=True) + EPSILON)
            unit = hidden * scale
            small_out[gain_row : gain_row + 1, :] += jnp.sum(flow * unit, axis=0, keepdims=True)
            flow = flow * gain
            flow = (flow - unit * jnp.mean(unit * flow, axis=-1, keepdims=True)) * scale
            after[at, :] = before[at, :].astype(FULL) + flow

        each(blocks, body)

    branch = X[1]

    def inner_grad(q):
        eg = X[10]
        if q == 0:
            get_og.wait()
            get_tn.wait()
        get_wo[q].wait()
        get_slope[q].wait()
        out_w = wo[q % 2].reshape(width, width)
        eg[...] = (nt_dot(og[...], out_w) * X[6 + q][...].astype(FULL)).astype(LOW)
        load_more(q)
        get_wo.append(load(outer_chunk((q + 2) % 4), wo.at[q % 2]))
        put(q, tn_dot(tn[...], eg[...]))
        get_wi[q].wait()
        back = nt_dot(eg[...], flat(w.at[q % 2]))
        if q == 0:
            run_b[...] = back
        else:
            run_b[...] += back
        if q + 2 < 4:
            get_wi.append(load(inner_chunk(q + 2), w.at[q % 2]))
        if q == 3:
            got["so"] = load(wholes[3], w.at[0])
            got["q_w"] = load(wholes[0], w.at[1])
            got["encoder"] = load(encoder, pool.at[pl.ds(6, 2)])

    def third_backward():
        got["table"].wait()
        got["late"].wait()
        norm_backward(run_c, run_b, 10, og, run_a)
        got["inverse"] = load(saved["cross_inverse"], run_c)
        branch[...] = run_a[...].astype(LOW)

    def context_grad(weight, slot):
        got[weight].wait()
        got["inverse"].wait()
        X[0][...] = (nt_dot(branch[...], flat(w.at[slot])).astype(LOW).astype(FULL) * run_c[...]).astype(LOW)

    def cross_out_grad():
        got["cross_context"].wait()
        put(4, tn_dot(X[2][...], branch[...]))

    def cross_context_grad():
        context_grad("co", 2)
        got["k_w"] = load(wholes[1], w.at[2])
        got["mid"] = load(saved["mid"], run_c)

    def attention(rows, key_rows, pairs, one, finish_pair, ahead):
        for p in pairs:
            for s in range(seqs):
                arriving[key_rows, p, s][0].wait()
        ahead()
        items = []
        for p in pairs:
            for s in range(seqs):
                queries, keys, values, grad = one(s, pl.ds(p * PAIR, PAIR))
                items.append(
                    (arriving[key_rows, p, s][1][...], queries, keys, values, grad, rows[s * per_seq + p])
                )
        results = pairs_backward(items)
        for n, p in enumerate(pairs):
            finish_pair(p, pl.ds(p * PAIR, PAIR), results[n * seqs : (n + 1) * seqs])

    enc_length = pool.shape[1]

    def cross_attention(p):
        if p == 0:
            for name in ("cross_rows", "cross_queries", "keys", "values"):
                got[name].wait()

        def one(s, lanes):
            at = pl.ds(s * length, length)
            source = sources[s]
            return X[3][at, lanes], pairs_in[source, :, lanes], pairs_in[2 + source, :, lanes], X[0][at, lanes]

        def finish_pair(p, lanes, results):
            for s in range(seqs):
                X[1][pl.ds(s * length, length), lanes] = results[s][0].astype(LOW)
            for e in range(2):
                for target, part_at in ((8, 1), (11, 2)):
                    total = jnp.where(sources[0] == e, results[0][part_at], 0.0)
                    total = total + jnp.where(sources[1] == e, results[1][part_at], 0.0)
                    pool[target + e, :, lanes] = total.astype(LOW)

        def ahead():
            if p + 1 < per_seq:
                fetch(cross_weights, (p + 1,), enc_length, (p + 1) % 2 * 2)
            else:
                fetch(self_weights, (0, 1), length, 0)

        attention(cross_rows, enc_length, (p,), one, finish_pair, ahead)
        if p + 1 < per_seq:
            return
        got["queries"] = load(saved["queries"], X[11])
        got["keys"] = load(saved["keys"], X[12])
        got["values"] = load(saved["values"], X[13])
        got["self_context"] = load(saved["self_context"], X[14])

    def cross_query_grad():
        got["second_norm"].wait()
        put(5, tn_dot(X[4][...], X[1][...]))

    def source_grad(i, target):
        copy = got.pop("encoder", None)
        if copy is not None:
            copy.wait()
        put(i, tn_dot(pool[6], pool[target]) + tn_dot(pool[7], pool[target + 1]))

    def second_backward():
        got["cq_w"].wait()
        run_b[...] = nt_dot(X[1][...], flat(w.at[3]))
        got["v_w"] = load(wholes[2], w.at[3])
        got["mid"].wait()
        norm_backward(run_c, run_b, 9, run_a, run_a)
        got["inverse"] = load(saved["self_inverse"], run_c)
        branch[...] = run_a[...].astype(LOW)

    def self_out_grad():
        got["self_context"].wait()
        put(8, tn_dot(X[14][...], branch[...]))

    def self_context_grad():
        context_grad("so", 0)
        got["ck_w"] = load(wholes[5], w.at[0])
        got["start"] = load(saved["start"], run_c)

    def self_attention(turn):
        if turn == 0:
            for name in ("self_rows", "queries", "keys", "values"):
                got[name].wait()

        def one(s, lanes):
            at = pl.ds(s * length, length)
            return tuple(X[i][at, lanes] for i in (11, 12, 13, 0))

        def finish_pair(p, lanes, results):
            for s in range(seqs):
                for i in range(3):
                    X[2 + i][pl.ds(s * length, length), lanes] = results[s][i].astype(LOW)
            score_sum[p] = results[0][3].astype(FULL) + results[1][3].astype(FULL)

        def ahead():
            if turn < 2:
                fetch(self_weights, (2 * turn + 2, 2 * turn + 3), length, (turn + 1) % 2 * 2)

        attention(self_rows, length, (2 * turn, 2 * turn + 1), one, finish_pair, ahead)

    def self_grad(i):
        copy = got.pop("first_norm", None)
        if copy is not None:
            copy.wait()
        put(9 + i, tn_dot(X[5][...], X[2 + i][...]))

    stores = []

    def store(source, target):
        copy = pltpu.make_async_copy(source, target, store_sem.at[len(stores)])
        stores.append(copy)
        copy.start()

    def closing_product():
        for name in ("q_w", "k_w", "v_w", "start"):
            got[name].wait()
        run_b[...] = nt_dot(X[2][...], flat(w.at[1]))
        run_b[...] += nt_dot(X[3][...], flat(w.at[2]))
        run_b[...] += nt_dot(X[4][...], flat(w.at[3]))
        got["cv_w"] = load(wholes[6], w.at[1])

    def closing():
        got["activated"] = [load(saved["activated"].at[q], X[i]) for q, i in enumerate((0, 1, 5, 10))]
        norm_backward(run_c, run_b, 8, run_a, run_a)
        store(run_a, hidden_grad)
        got["late"] = load(saved["late"], run_c)
        for s in range(seqs):
            row = jnp.sum(run_a[pl.ds(s * length, length), :], axis=0, keepdims=True)
            for l in range(8):
                small_out[l : l + 1, :] += jnp.where(languages[s] == l, row, 0.0)

    def hidden_end(q):
        got["activated"][q].wait()
        get_wo[4 + q].wait()
        value = jnp.dot(X[(0, 1, 5, 10)[q]][...], wo[q % 2].reshape(width, width), preferred_element_type=FULL)
        if q < 2:
            get_wo.append(load(outer_chunk(q + 2), wo.at[q % 2]))
        if q == 0:
            got["late"].wait()
        if q < 3:
            run_c[...] += value
        else:
            X[2][...] = (run_c[...] + value).astype(LOW)
            store(X[2], hidden_out)

    def encoder_end(e):
        run = (run_b, run_c)[e]
        if e == 0:
            got["ck_w"].wait()
            got["cv_w"].wait()
        run[...] = nt_dot(pool[8 + e], flat(w.at[0]))
        run[...] += nt_dot(pool[11 + e], flat(w.at[1]))
        store(run, encoder_grad.at[e])

    def bucket_sums(turn):
        if turn == 0:
            ids[...] = ids_in[...].astype(FULL).T.astype(jnp.int32)
        half = length // 2
        rows = 32

        def pair(p, _):
            def bucket_group(first, count, spans):
                sums = [[jnp.zeros((8, half), FULL) for _ in range(2)] for _ in range(count)]
                for n, side in spans:
                    block = pl.ds(n * rows, rows)
                    bucket = ids[block, side * half : (side + 1) * half]
                    scores = [
                        score_sum[p, block, h * length + side * half : h * length + (side + 1) * half]
                        for h in range(2)
                    ]
                    for c in range(count):
                        here = bucket == first + c
                        for h in range(2):
                            kept = jnp.where(here, scores[h], 0.0).reshape(rows // 8, 8, half)
                            sums[c][h] = sums[c][h] + jnp.sum(kept, axis=0)
                for c in range(count):
                    for h in range(2):
                        row = (2 * p + h) * 32 + first + c
                        bucket_rows[pl.ds(row, 1), :] = jnp.sum(sums[c][h], axis=0, keepdims=True)

            blocks_of = length // rows
            every = [(n, side) for side in range(2) for n in range(blocks_of) if n * rows < (side + 1) * half]
            near = [(n, side) for n, side in every if n * rows + rows + 15 > side * half]
            for first in range(0, 32, 4):
                bucket_group(first, 4, near if first < 16 else every)
            return 0

        lax.fori_loop(2 * turn, 2 * turn + 2, pair, 0)
        if turn < 2:
            return
        ones = jnp.ones((8, 128), FULL)
        totals = lax.dot_general(
            ones, bucket_rows[...], (((1,), (1,)), ((), ())), precision=PRECISE, preferred_element_type=FULL
        )
        small_out[11:12, : bucket_rows.shape[0]] = totals[:1, :]

    small = []
    for dim in "cxyz":
        here, reach = place.at(dim), 1
        while reach < place.size(dim):
            small.append((dim, here + reach - 2 * reach * lax.rem(lax.div(here, reach), 2)))
            reach *= 2

    def small_copy(i):
        dim, partner = small[i]
        return pltpu.make_async_remote_copy(
            small_out, small_box.at[i], small_send.at[i], small_recv.at[i],
            device_id=place.device(dim, partner), device_id_type=MESH,
        )

    class Small:
        def start(self, i):
            small_copy(i).start()

        def finish(self, i):
            small_copy(i).wait()
            small_out[...] += small_box[i]

    tasks = dict(n3=third_backward, co=cross_out_grad, ccg=cross_context_grad, cq=cross_query_grad, n2=second_backward)
    tasks.update(so=self_out_grad, scg=self_context_grad, cl0=closing_product, cl1=closing)
    tasks["e0"], tasks["e1"] = functools.partial(encoder_end, 0), functools.partial(encoder_end, 1)
    tasks["ck"] = functools.partial(source_grad, 6, 8)
    tasks["cv"] = functools.partial(source_grad, 7, 11)
    for i in range(4):
        tasks[f"in{i}"] = functools.partial(inner_grad, i)
        tasks[f"h{i}"] = functools.partial(hidden_end, i)
    for i in range(per_seq):
        tasks[f"ca{i}"] = functools.partial(cross_attention, i)
    for i in range(3):
        tasks[f"sa{i}"] = functools.partial(self_attention, i)
        tasks[f"bk{i}"] = functools.partial(bucket_sums, i)
        tasks["qkv"[i]] = functools.partial(self_grad, i)
    steps = [len(plan.stages) for plan in plans] + [len(small)]
    plans.append(Small())
    at = [0] * 17
    get_outers.wait()
    for entry in BACKWARD_ORDER:
        if isinstance(entry, str):
            tasks[entry]()
            continue
        step = at[entry]
        at[entry] += 1
        if step >= 1:
            plans[entry].finish(step - 1)
        if step < steps[entry]:
            plans[entry].start(step)
    for m, plan in enumerate(plans[:16]):
        packed[m] = plan.blocks(plan.own)[...].astype(FULL)
        plan.close()
    for copy in stores:
        copy.wait()


def backward(sizes, output_grad, encoder_states, language_ids, source_index, bucket_ids, forward_outs):
    ny, nz = sizes
    grid = (ny, 2, nz, 2)
    tokens, width = output_grad.shape
    length = bucket_ids.shape[0]
    part = width // (ny * nz * 4)
    outer_grads, wholes, score_weights = forward_outs[0], forward_outs[1:11], forward_outs[11:13]
    saved = dict(zip(SAVED, forward_outs[13:]))
    enc_count, enc_length = encoder_states.shape[:2]
    anywhere = pl.BlockSpec(memory_space=pl.ANY)
    vmem = pl.BlockSpec(memory_space=pltpu.VMEM)
    smem = pl.BlockSpec(memory_space=pltpu.SMEM)
    lead = [box_shapes(sizes, path) for path in BACK_PATHS]
    slots = slot_count(sizes)
    hops = (ny * nz * 4).bit_length() - 1
    pairs = tokens // length * (width // PAIR)
    row = (tokens, width)
    out_shape = [
        jax.ShapeDtypeStruct(row, LOW),
        jax.ShapeDtypeStruct(row, FULL),
        jax.ShapeDtypeStruct((enc_count, enc_length, width), FULL),
        jax.ShapeDtypeStruct((16, width), FULL),
        jax.ShapeDtypeStruct((16, part, width), FULL),
    ]
    outs = pl.pallas_call(
        functools.partial(backward_kernel, sizes, tuple(len(s) for s in lead)),
        out_shape=out_shape,
        in_specs=[anywhere, anywhere, smem, smem, vmem] + [anywhere] * (13 + len(SAVED)),
        out_specs=[anywhere] * 3 + [vmem] * 2,
        scratch_shapes=[
            pltpu.VMEM((12,) + grid + (part, width), LOW),
            pltpu.VMEM((ny, nz, 2, 4, part, width), LOW),
            pltpu.VMEM((2, 4, ny, nz, 2, part, width), LOW),
        ]
        + [pltpu.VMEM((2,) + s + (part, width), LOW) for one in lead for s in one]
        + [
            pltpu.VMEM((hops, 16, width), FULL),
            pltpu.VMEM((13,) + row, LOW),
            pltpu.VMEM((4,) + row, LOW),
            pltpu.VMEM(row, FULL),
            pltpu.VMEM(row, FULL),
            pltpu.VMEM(row, FULL),
            pltpu.VMEM((4,) + grid + (part, width), LOW),
            pltpu.VMEM((2, nz, 2, 4, part, width), LOW),
            pltpu.VMEM((4, enc_length, 2 * length), LOW),
            pltpu.VMEM((width // PAIR, length, 2 * length), FULL),
            pltpu.VMEM((32 * H, 128), FULL),
            pltpu.VMEM((16, width), FULL),
            pltpu.VMEM((pairs, 1, 2 * length), FULL),
            pltpu.VMEM((pairs, 1, 2 * length), FULL),
            pltpu.VMEM((length, length), jnp.int32),
            pltpu.SemaphoreType.DMA((16, slots)),
            pltpu.SemaphoreType.DMA((16, slots)),
            pltpu.SemaphoreType.DMA((hops,)),
            pltpu.SemaphoreType.DMA((hops,)),
            pltpu.SemaphoreType.DMA((56,)),
            pltpu.SemaphoreType.DMA((8,)),
            pltpu.SemaphoreType.DMA((4,)),
        ],
        compiler_params=pltpu.CompilerParams(
            collective_id=3, has_side_effects=True, vmem_limit_bytes=63 * 1024 * 1024
        ),
    )(
        output_grad, encoder_states, language_ids, source_index, bucket_ids, outer_grads, *wholes, *score_weights,
        *[saved[name] for name in SAVED],
    )
    return finish(sizes, outs)


def finish_kernel(sizes, *refs):
    hidden_out, hidden_grad, encoder_grad, small, packed = refs[:5]
    outs = refs[5:18]
    language, bucket, gains = refs[18], refs[19], refs[20:23]
    staged, sem, in_sem = refs[23:26], refs[26], refs[27]
    part, width = packed.shape[1:]
    copies = []
    halves = []
    for i, source in enumerate((hidden_out, hidden_grad, encoder_grad)):
        for h in range(2):
            size = source.shape[0] // 2
            rows = pl.ds(h * size, size)
            halves.append((i, rows, pltpu.make_async_copy(source.at[rows], staged[i].at[rows], in_sem.at[2 * i + h])))
            halves[-1][2].start()

    def copy(source, target):
        copies.append(pltpu.make_async_copy(source, target, sem.at[len(copies)]))
        copies[-1].start()

    for q in range(4):
        copy(packed.at[q], outs[12].at[pl.ds(q * part, part)])
        copy(packed.at[4 + q], outs[11].at[:, pl.ds(q * width, width)])
    for i, m in enumerate((13, 14, 15, 12, 9, 10, 11, 8)):
        copy(packed.at[m], outs[3 + i])
    for i, rows, half in halves:
        half.wait()
        copy(staged[i].at[rows], outs[i].at[rows])
    place = Place(sizes)
    start = (place.dp * sizes[1] * 2 + place.fs) * part
    row = lax.broadcasted_iota(jnp.int32, (width, 128), 0)
    lane = lax.broadcasted_iota(jnp.int32, (width, 128), 1)
    chosen = jnp.where((row == lane + start) & (lane < part), 1.0, 0.0)
    own = jnp.dot(small[...], chosen, precision=PRECISE, preferred_element_type=FULL)
    language[...] = own[:8, :part]
    for i in range(3):
        gains[i][...] = own[8 + i, :part]
    row = lax.broadcasted_iota(jnp.int32, (16, width), 0)
    lane = lax.broadcasted_iota(jnp.int32, (16, width), 1)
    spread = jnp.where(lax.div(lane, 32) == row, small[11:12, :], 0.0)
    row = lax.broadcasted_iota(jnp.int32, (width, 128), 0)
    lane = lax.broadcasted_iota(jnp.int32, (width, 128), 1)
    places = jnp.where(lax.rem(row, 32) == lane, 1.0, 0.0)
    bucket[...] = jnp.dot(spread, places, precision=PRECISE, preferred_element_type=FULL)[:H, :32]
    for c in copies:
        c.wait()


def finish(sizes, outs):
    part, width = outs[4].shape[1:]
    anywhere = pl.BlockSpec(memory_space=pl.ANY)
    vmem = pl.BlockSpec(memory_space=pltpu.VMEM)
    shapes = [o.shape for o in outs[:3]] + [(part, width)] * 8
    shapes += [(part, 4 * width), (4 * part, width)]
    out_shape = [jax.ShapeDtypeStruct(s, FULL) for s in shapes]
    out_shape[0] = jax.ShapeDtypeStruct(shapes[0], LOW)
    out_shape += [jax.ShapeDtypeStruct(s, FULL) for s in ((8, part), (H, 32), (part,), (part,), (part,))]
    return pl.pallas_call(
        functools.partial(finish_kernel, sizes),
        out_shape=out_shape,
        in_specs=[pl.BlockSpec(memory_space=pltpu.HBM)] * 3 + [vmem, vmem],
        out_specs=[anywhere] * 13 + [vmem] * 5,
        scratch_shapes=[pltpu.VMEM(o.shape, o.dtype) for o in outs[:3]]
        + [pltpu.SemaphoreType.DMA((22,)), pltpu.SemaphoreType.DMA((6,))],
        compiler_params=pltpu.CompilerParams(vmem_limit_bytes=60 * 1024 * 1024),
    )(*outs)


def local_general(
    sizes,
    hidden_in,
    output_grad,
    encoder_states,
    language_ids,
    source_index,
    bucket_ids,
    language_table,
    bucket_table,
    self_gain,
    self_query,
    self_key,
    self_value,
    self_out,
    cross_gain,
    cross_query,
    cross_key,
    cross_value,
    cross_out,
    feed_gain,
    inner_weight,
    outer_weight,
):
    seq_count = language_ids.shape[0]
    length = bucket_ids.shape[0]
    tokens = seq_count * length
    enc_count = encoder_states.shape[0]
    enc_length = encoder_states.shape[1]
    width = hidden_in.shape[1]
    blocks = seq_count // SEQ_BLOCK
    (
        gain_one, gain_two, gain_three, table_whole, query_whole, key_whole, value_whole, out_whole,
        cquery_whole, ckey_whole, cvalue_whole, cout_whole, inner_whole, outer_whole,
    ) = gather_weights(
        sizes, language_table, (self_gain, cross_gain, feed_gain),
        (self_query, self_key, self_value, self_out, cross_query, cross_key, cross_value, cross_out),
        inner_weight, outer_weight,
    )

    def to_blocks(array, rows):
        return array.reshape(blocks, SEQ_BLOCK, rows, array.shape[-1])

    language_hot = (language_ids[:, None] == jnp.arange(table_whole.shape[0])[None, :]).astype(
        jnp.float32
    )
    language_rows = jnp.dot(language_hot, table_whole.astype(jnp.float32), precision=PRECISE)
    start_state = (
        hidden_in.astype(jnp.float32).reshape(seq_count, length, width) + language_rows[:, None, :]
    ).reshape(tokens, width)
    first_norm = to_low(norm_scale(start_state, gain_one.astype(jnp.float32)))
    self_queries = to_low(matmul(first_norm, query_whole))
    self_keys = to_low(matmul(first_norm, key_whole))
    self_values = to_low(matmul(first_norm, value_whole))
    bucket_hot = (
        bucket_ids[:, :, None] == jnp.arange(bucket_table.shape[0])[None, None, :]
    ).astype(jnp.float32)
    position_bias = jnp.einsum(
        "ijb,bh->hij", bucket_hot, bucket_table.astype(jnp.float32), precision=PRECISE
    )
    positions = jnp.arange(length)
    masked_bias = jnp.where(
        (positions[:, None] >= positions[None, :])[None], position_bias, NEGATIVE
    )

    def self_forward(block_items):
        return attend_forward(block_items[0], block_items[1], block_items[2], masked_bias)

    self_context, self_total = lax.map(
        self_forward,
        (
            to_blocks(self_queries, length),
            to_blocks(self_keys, length),
            to_blocks(self_values, length),
        ),
    )
    self_context = self_context.reshape(tokens, -1)
    mid_state = start_state + matmul(self_context, out_whole)
    second_norm = to_low(norm_scale(mid_state, gain_two.astype(jnp.float32)))
    cross_queries = to_low(matmul(second_norm, cquery_whole))
    encoder_flat = encoder_states.reshape(enc_count * enc_length, width)
    source_keys = to_low(matmul(encoder_flat, ckey_whole)).reshape(enc_count, enc_length, -1)
    source_values = to_low(matmul(encoder_flat, cvalue_whole)).reshape(enc_count, enc_length, -1)
    source_hot = (source_index[:, None] == jnp.arange(enc_count)[None, :]).astype(jnp.float32)
    source_low = to_low(source_hot)
    picked_keys = to_low(
        jnp.einsum("se,emc->smc", source_low, source_keys, preferred_element_type=jnp.float32)
    )
    picked_values = to_low(
        jnp.einsum("se,emc->smc", source_low, source_values, preferred_element_type=jnp.float32)
    )

    def cross_forward(block_items):
        return attend_forward(block_items[0], block_items[1], block_items[2], 0.0)

    cross_context, cross_total = lax.map(
        cross_forward,
        (
            to_blocks(cross_queries, length),
            picked_keys.reshape(blocks, SEQ_BLOCK, enc_length, -1),
            picked_values.reshape(blocks, SEQ_BLOCK, enc_length, -1),
        ),
    )
    cross_context = cross_context.reshape(tokens, -1)
    late_state = mid_state + matmul(cross_context, cout_whole)
    third_norm = to_low(norm_scale(late_state, gain_three.astype(jnp.float32)))
    expanded = matmul(third_norm, inner_whole)
    activated = to_low(jax.nn.gelu(expanded, approximate=True))
    hidden_out = (late_state + matmul(activated, outer_whole)).astype(jnp.bfloat16)
    top_grad = output_grad.astype(jnp.float32)
    outer_full = left_product(activated, output_grad)
    activated_grad = right_product(output_grad, outer_whole)
    gelu_value, gelu_back = jax.vjp(jax.nn.gelu, expanded)
    expanded_grad = to_low(gelu_back(activated_grad)[0])
    inner_full = left_product(third_norm, expanded_grad)
    third_grad = right_product(expanded_grad, inner_whole)
    norm_value, norm_back = jax.vjp(norm_scale, late_state, gain_three.astype(jnp.float32))
    state_back, feed_gain_full = norm_back(third_grad)
    late_grad = top_grad + state_back
    cross_low = to_low(late_grad)
    cout_full = left_product(cross_context, cross_low)
    cross_context_grad = to_low(right_product(cross_low, cout_whole))

    def cross_backward(block_items):
        return attend_backward(
            block_items[0],
            block_items[1],
            block_items[2],
            0.0,
            block_items[3],
            block_items[4],
            False,
        )

    cquery_part, ckey_part, cvalue_part = lax.map(
        cross_backward,
        (
            to_blocks(cross_queries, length),
            picked_keys.reshape(blocks, SEQ_BLOCK, enc_length, -1),
            picked_values.reshape(blocks, SEQ_BLOCK, enc_length, -1),
            cross_total,
            to_blocks(cross_context_grad, length),
        ),
    )
    cquery_low = to_low(cquery_part.reshape(tokens, -1))
    source_key_grad = to_low(
        jnp.einsum(
            "se,smc->emc",
            source_hot,
            ckey_part.reshape(seq_count, enc_length, -1),
            precision=PRECISE,
        ).reshape(enc_count * enc_length, -1)
    )
    source_value_grad = to_low(
        jnp.einsum(
            "se,smc->emc",
            source_hot,
            cvalue_part.reshape(seq_count, enc_length, -1),
            precision=PRECISE,
        ).reshape(enc_count * enc_length, -1)
    )
    cquery_full = left_product(second_norm, cquery_low)
    ckey_full = left_product(encoder_flat, source_key_grad)
    cvalue_full = left_product(encoder_flat, source_value_grad)
    encoder_grad = (
        right_product(source_key_grad, ckey_whole) + right_product(source_value_grad, cvalue_whole)
    ).reshape(enc_count, enc_length, width)
    second_grad = right_product(cquery_low, cquery_whole)
    norm_value, norm_back = jax.vjp(norm_scale, mid_state, gain_two.astype(jnp.float32))
    state_back, cross_gain_full = norm_back(second_grad)
    mid_grad = late_grad + state_back
    self_low = to_low(mid_grad)
    out_full = left_product(self_context, self_low)
    self_context_grad = to_low(right_product(self_low, out_whole))

    def self_backward(block_items):
        return attend_backward(
            block_items[0],
            block_items[1],
            block_items[2],
            masked_bias,
            block_items[3],
            block_items[4],
            True,
        )

    query_part, key_part, value_part, bias_part = lax.map(
        self_backward,
        (
            to_blocks(self_queries, length),
            to_blocks(self_keys, length),
            to_blocks(self_values, length),
            self_total,
            to_blocks(self_context_grad, length),
        ),
    )
    query_low = to_low(query_part.reshape(tokens, -1))
    key_low = to_low(key_part.reshape(tokens, -1))
    value_low = to_low(value_part.reshape(tokens, -1))
    table_full = jnp.einsum(
        "hij,ijb->bh", jnp.sum(bias_part, axis=0), bucket_hot, precision=PRECISE
    )
    query_full = left_product(first_norm, query_low)
    key_full = left_product(first_norm, key_low)
    value_full = left_product(first_norm, value_low)
    first_grad = (
        right_product(query_low, query_whole)
        + right_product(key_low, key_whole)
        + right_product(value_low, value_whole)
    )
    norm_value, norm_back = jax.vjp(norm_scale, start_state, gain_one.astype(jnp.float32))
    state_back, self_gain_full = norm_back(first_grad)
    hidden_in_grad = mid_grad + state_back
    sequence_sums = jnp.sum(hidden_in_grad.reshape(seq_count, length, width), axis=1)
    language_full = left_product(language_hot, sequence_sums)
    (
        language_part, bucket_table_grad, sgain_part, cgain_part, feed_gain_part, whole_parts, inner_part, outer_part,
    ) = reduce_grads(
        sizes, language_full, table_full, (self_gain_full, cross_gain_full, feed_gain_full),
        (query_full, key_full, value_full, out_full, cquery_full, ckey_full, cvalue_full, cout_full),
        inner_full, outer_full,
    )
    query_sum, key_sum, value_sum, out_part, cquery_part_sum, ckey_part_sum, cvalue_part_sum, cout_part = whole_parts
    return (
        hidden_out,
        hidden_in_grad,
        encoder_grad,
        language_part,
        bucket_table_grad,
        sgain_part,
        query_sum,
        key_sum,
        value_sum,
        out_part,
        cgain_part,
        cquery_part_sum,
        ckey_part_sum,
        cvalue_part_sum,
        cout_part,
        feed_gain_part,
        inner_part,
        outer_part,
    )


def local(sizes, *args):
    if sizes == (2, 4) and args[8].shape[0] % 8 == 0:
        return local_fused(sizes, *args)
    return local_general(sizes, *args)


def local_fused(
    sizes, hidden_in, output_grad, encoder_states, language_ids, source_index, bucket_ids, language_table,
    bucket_table, self_gain, self_query, self_key, self_value, self_out, cross_gain, cross_query, cross_key,
    cross_value, cross_out, feed_gain, inner_weight, outer_weight,
):
    kept = forward(
        sizes, hidden_in, output_grad, encoder_states, language_ids, source_index, bucket_ids, language_table,
        bucket_table, (self_gain, cross_gain, feed_gain),
        (self_query, self_key, self_value, self_out, cross_query, cross_key, cross_value, cross_out),
        inner_weight, outer_weight,
    )
    outs = backward(sizes, output_grad, encoder_states, language_ids, source_index, bucket_ids, kept)
    squares, inner, outer, language, bucket, gains = outs[3:11], outs[11], outs[12], outs[13], outs[14].T, outs[15:]
    return (
        *outs[:3], language, bucket, gains[0], *squares[:4], gains[1], *squares[4:], gains[2], inner, outer,
    )


def solution(mesh):
    sizes = (mesh.shape["dp"] // 2, mesh.shape["fsdp"] // 2)
    in_specs = (
        P(("dp", "fsdp"), None),
        P(("dp", "fsdp"), None),
        P(("dp", "fsdp"), None, None),
        P(("dp", "fsdp")),
        P(("dp", "fsdp")),
        P(),
        P(None, ("dp", "fsdp")),
        P(),
        P(("dp", "fsdp")),
        P(("dp", "fsdp"), None),
        P(("dp", "fsdp"), None),
        P(("dp", "fsdp"), None),
        P(("dp", "fsdp"), None),
        P(("dp", "fsdp")),
        P(("dp", "fsdp"), None),
        P(("dp", "fsdp"), None),
        P(("dp", "fsdp"), None),
        P(("dp", "fsdp"), None),
        P(("dp", "fsdp")),
        P(("dp", "fsdp"), None),
        P(("dp", "fsdp"), None),
    )
    out_specs = (
        P(("dp", "fsdp"), None),
        P(("dp", "fsdp"), None),
        P(("dp", "fsdp"), None, None),
        P(None, ("dp", "fsdp")),
        P(),
        P(("dp", "fsdp")),
        P(("dp", "fsdp"), None),
        P(("dp", "fsdp"), None),
        P(("dp", "fsdp"), None),
        P(("dp", "fsdp"), None),
        P(("dp", "fsdp")),
        P(("dp", "fsdp"), None),
        P(("dp", "fsdp"), None),
        P(("dp", "fsdp"), None),
        P(("dp", "fsdp"), None),
        P(("dp", "fsdp")),
        P(("dp", "fsdp"), None),
        P(("dp", "fsdp"), None),
    )
    return jax.shard_map(functools.partial(local, sizes), mesh=mesh, in_specs=in_specs, out_specs=out_specs, check_vma=False)
```

```python
import functools

import jax
import jax.numpy as jnp
from jax import lax
from jax.experimental import pallas as pl
from jax.experimental.pallas import tpu as pltpu
from jax.sharding import PartitionSpec as P

H = 12
HEAD = 64
SEQ_BLOCK = 2


EPSILON = 1e-06
PRECISE = lax.Precision.HIGHEST
NEGATIVE = -1e30


def to_low(value):
    return value.astype(jnp.bfloat16)


def norm_scale(hidden, gain):
    return hidden * lax.rsqrt(jnp.mean(hidden * hidden, axis=-1, keepdims=True) + EPSILON) * gain


def matmul(left, right):
    return jnp.dot(left, right, preferred_element_type=jnp.float32)


def left_product(left, right):
    return lax.dot_general(
        left, right, (((0,), (0,)), ((), ())), preferred_element_type=jnp.float32
    )


def right_product(left, right):
    return lax.dot_general(
        left, right, (((1,), (1,)), ((), ())), preferred_element_type=jnp.float32
    )


def split_heads(array):
    return array.reshape(array.shape[:-1] + (H, HEAD))


def score_block(queries, key_rows, offset):
    scores = jnp.einsum(
        "sqhe,skhe->shqk",
        split_heads(queries),
        split_heads(key_rows),
        preferred_element_type=jnp.float32,
    )
    return scores + offset


def attend_forward(queries, key_rows, value_rows, offset):
    scores = score_block(queries, key_rows, offset)
    top_score = jnp.max(scores, axis=-1, keepdims=True)
    log_total = top_score + jnp.log(jnp.sum(jnp.exp(scores - top_score), axis=-1, keepdims=True))
    weights = to_low(jnp.exp(scores - log_total))
    context = jnp.einsum(
        "shqk,skhe->sqhe", weights, split_heads(value_rows), preferred_element_type=jnp.float32
    )
    return (to_low(context).reshape(queries.shape), log_total)


def attend_backward(queries, key_rows, value_rows, offset, log_total, context_grad, with_bias):
    scores = score_block(queries, key_rows, offset)
    probs = jnp.exp(scores - log_total)
    weights = to_low(probs)
    grad_heads = split_heads(context_grad)
    value_grad = jnp.einsum(
        "shqk,sqhe->skhe", weights, grad_heads, preferred_element_type=jnp.float32
    )
    prob_grad = jnp.einsum(
        "sqhe,skhe->shqk", grad_heads, split_heads(value_rows), preferred_element_type=jnp.float32
    )
    score_grad = to_low(probs * (prob_grad - jnp.sum(probs * prob_grad, axis=-1, keepdims=True)))
    query_grad = jnp.einsum(
        "shqk,skhe->sqhe", score_grad, split_heads(key_rows), preferred_element_type=jnp.float32
    )
    key_grad = jnp.einsum(
        "shqk,sqhe->skhe", score_grad, split_heads(queries), preferred_element_type=jnp.float32
    )
    grads = (
        query_grad.reshape(queries.shape),
        key_grad.reshape(key_rows.shape),
        value_grad.reshape(value_rows.shape),
    )
    if with_bias:
        return grads + (jnp.sum(score_grad.astype(jnp.float32), axis=0),)
    return grads


MESH = pl.DeviceIdType.MESH
ALL = slice(None)


class Place:
    def __init__(self, sizes):
        self.ny, self.nz = sizes
        self.dp = lax.axis_index("dp")
        self.fs = lax.axis_index("fsdp")
        self.c, self.y = lax.rem(self.dp, 2), lax.div(self.dp, 2)
        self.x, self.z = lax.rem(self.fs, 2), lax.div(self.fs, 2)

    def size(self, dim):
        return {"c": 2, "x": 2, "y": self.ny, "z": self.nz}[dim]

    def at(self, dim):
        return {"c": self.c, "x": self.x, "y": self.y, "z": self.z}[dim]

    def device(self, dim, index):
        if dim == "c":
            return (self.y * 2 + index, self.fs)
        if dim == "y":
            return (index * 2 + self.c, self.fs)
        if dim == "x":
            return (self.dp, self.z * 2 + index)
        return (self.dp, index * 2 + self.x)


def neighbour_barrier(place, far=False):
    barrier = pltpu.get_barrier_semaphore()
    links = []
    for dim in "cxyz":
        here, size = place.at(dim), place.size(dim)
        reach = 1
        while reach < size and (reach == 1 or far):
            if size == 2:
                links.append((dim, 1 - here, None))
            elif reach == 1:
                for step in (1, -1):
                    links.append((dim, here + step, (here + step >= 0) & (here + step < size)))
            else:
                links.append((dim, here + reach - 2 * reach * lax.rem(lax.div(here, reach), 2), None))
            reach *= 2

    def signal(dim, there):
        pl.semaphore_signal(barrier, inc=1, device_id=place.device(dim, there), device_id_type=MESH)

    for dim, there, condition in links:
        if condition is None:
            signal(dim, there)
        else:
            pl.when(condition)(lambda dim=dim, there=there: signal(dim, there))
    peers = sum(1 if condition is None else condition.astype(jnp.int32) for _, _, condition in links)
    pl.semaphore_wait(barrier, peers)


PATHS = ("zxy", "zyx", "xzy", "yzx")


class Link:
    def __init__(self, copy, sends=None, receives=None):
        self.copy, self.sends, self.receives = copy, sends, receives

    @staticmethod
    def when(condition, run):
        if condition is None:
            run()
        else:
            pl.when(condition)(run)

    def start(self):
        self.when(self.sends, lambda: self.copy.start())

    def wait_send(self):
        self.when(self.sends, lambda: self.copy.wait_send())

    def wait_recv(self):
        self.when(self.receives, lambda: self.copy.wait_recv())


class Pool:
    def __init__(self, array, count):
        self.array, self.free, self.users = array, list(range(count)), []

    def take(self, user):
        if not self.free:
            self.users[0].release()
        self.users.append(user)
        return self.free.pop(0)

    def give(self, user, at):
        self.users.remove(user)
        self.free.append(at)

    def drain(self):
        while self.users:
            self.users[0].release()


class PooledLink(Link):
    def __init__(self, make, pool, sends=None, receives=None):
        self.make, self.pool, self.sends, self.receives = make, pool, sends, receives
        self.at = None

    def start(self):
        self.at = self.pool.take(self)
        copy = self.make(self.pool.array.at[self.at])
        self.when(self.sends, lambda: copy.start())

    def release(self):
        copy = self.make(self.pool.array.at[self.at])
        self.when(self.sends, lambda: copy.wait_send())
        self.pool.give(self, self.at)

    def wait_recv(self):
        copy = self.make(self.pool.array.at[0])
        self.when(self.receives, lambda: copy.wait_recv())


class PooledCopy:
    def __init__(self, pool, source, target):
        self.pool, self.done = pool, False
        self.at = pool.take(self)
        self.copy = pltpu.make_async_copy(source, target, pool.array.at[self.at])
        self.copy.start()

    def wait(self):
        if not self.done:
            self.copy.wait()
            self.done = True
            self.pool.give(self, self.at)

    release = wait


class Exchange:
    def __init__(self, place, pool, receive):
        self.place, self.pool, self.receive, self.count = place, pool, receive, 0

    def slot(self):
        self.count += 1
        return self.count - 1

    def link(self, source, target, dim, there, sends=None, receives=None, slot=None):
        slot = self.slot() if slot is None else slot
        device = self.place.device(dim, there)

        def make(send):
            return pltpu.make_async_remote_copy(
                source, target, send, self.receive.at[slot], device_id=device, device_id_type=MESH
            )

        return PooledLink(make, self.pool, sends, receives)


def pick(held, place, **fixed):
    return tuple(fixed.get(dim, ALL if dim in held else place.at(dim)) for dim in "yczx")


def gather_steps(place, blocks, path, sems):
    steps, slot, held = [], 0, ""
    for dim in path + "c":
        here, size = place.at(dim), place.size(dim)
        if size == 2:
            there = 1 - here
            index = pick(held, place)
            copy = pltpu.make_async_remote_copy(
                blocks(index), blocks(index), sems[0].at[slot], sems[1].at[slot],
                device_id=place.device(dim, there), device_id_type=MESH,
            )
            steps.append([Link(copy)])
            slot += 1
        else:
            for hop in range(1, size):
                links = []
                for way in (1, -1):
                    origin = here - way * (hop - 1)
                    there = here + way
                    source = here - way * hop
                    index = pick(held, place, **{dim: jnp.clip(origin, 0, size - 1)})
                    copy = pltpu.make_async_remote_copy(
                        blocks(index), blocks(index), sems[0].at[slot], sems[1].at[slot],
                        device_id=place.device(dim, jnp.clip(there, 0, size - 1)), device_id_type=MESH,
                    )
                    sends = (origin >= 0) & (origin < size) & (there >= 0) & (there < size)
                    links.append(Link(copy, sends, (source >= 0) & (source < size)))
                    slot += 1
                steps.append(links)
        held += dim
    return steps


def slot_count(sizes):
    ny, nz = sizes
    return 2 + (1 if ny == 2 else 2 * (ny - 1)) + (1 if nz == 2 else 2 * (nz - 1))


def run_steps(plans, lag):
    rounds = max(lag[i] + len(plan) for i, plan in enumerate(plans)) + 1
    for now in range(rounds):
        for offset, plan in zip(lag, plans):
            at = now - offset
            if 1 <= at <= len(plan):
                for link in plan[at - 1]:
                    link.wait_recv()
            if 0 <= at < len(plan):
                for link in plan[at]:
                    link.start()
    for plan in plans:
        for links in plan:
            for link in links:
                link.wait_send()


def gather_kernel(sizes, *refs):
    shards, wholes = refs[:11], refs[11:22]
    own_sem, send_sem, recv_sem = refs[22:]
    place = Place(sizes)
    own = (place.y, place.c, place.z, place.x)
    owns = [
        pltpu.make_async_copy(shard, whole.at[own], own_sem.at[i])
        for i, (shard, whole) in enumerate(zip(shards, wholes))
    ]
    for copy in owns:
        copy.start()
    neighbour_barrier(place)
    views = [lambda index, ref=ref: ref.at[index] for ref in wholes[:9]]
    width = wholes[8].shape[-1]
    for q in range(4):
        views.append(
            lambda index, q=q: wholes[9].at[index + (ALL, pl.ds(q * width, width))]
        )
    for q in range(4):
        views.append(lambda index, q=q: wholes[10].at[index + (q,)])
    plans, lag = [], []
    for i, view in enumerate(views):
        path = PATHS[0] if i == 0 else PATHS[(i - 1) % 4]
        plans.append(gather_steps(place, view, path, (send_sem.at[i], recv_sem.at[i])))
        lag.append(0 if i == 0 else 3 * ((i - 1) // 4))
    for copy in owns:
        copy.wait()
    run_steps(plans, lag)


def gather_weights(sizes, table, gains, squares, inner, outer):
    ny, nz = sizes
    grid = (ny, 2, nz, 2)
    part, width = squares[0].shape
    small = jnp.zeros((16, 128), table.dtype)
    small = small.at[: table.shape[0], :part].set(table)
    for i, gain in enumerate(gains):
        small = small.at[table.shape[0] + i, :part].set(gain)
    shards = (small,) + tuple(squares) + (inner, outer.reshape(4, part, width))
    anywhere = pl.BlockSpec(memory_space=pl.ANY)
    slots = slot_count(sizes)
    wholes = pl.pallas_call(
        functools.partial(gather_kernel, sizes),
        out_shape=[jax.ShapeDtypeStruct(grid + s.shape, s.dtype) for s in shards],
        in_specs=[anywhere] * 11,
        out_specs=[anywhere] * 11,
        scratch_shapes=[
            pltpu.SemaphoreType.DMA((11,)),
            pltpu.SemaphoreType.DMA((17, slots)),
            pltpu.SemaphoreType.DMA((17, slots)),
        ],
        compiler_params=pltpu.CompilerParams(collective_id=0, has_side_effects=True),
    )(*shards)
    count = ny * nz * 4
    tiny = wholes[0].reshape(count, 16, 128)[:, :, :part].transpose(1, 0, 2).reshape(16, count * part)
    rows = table.shape[0]
    return (
        (tiny[rows], tiny[rows + 1], tiny[rows + 2], tiny[:rows])
        + tuple(w.reshape(count * part, width) for w in wholes[1:9])
        + (wholes[9].reshape(count * part, 4 * width), wholes[10].reshape(4 * count * part, width))
    )


class Reduce:
    def __init__(self, place, path, source, total, core_in, boxes, out, sems):
        self.place, self.path, self.source, self.total = place, path, source, total
        self.core_in, self.boxes, self.out, self.sems = core_in, boxes, out, sems
        self.slot = 0
        self.sent = []

    def copy(self, source, target, dim, there):
        slot = self.slot
        self.slot += 1
        return pltpu.make_async_remote_copy(
            source, target, self.sems[0].at[slot], self.sems[1].at[slot],
            device_id=self.place.device(dim, there), device_id_type=MESH,
        )

    def index(self, fixed):
        return tuple(fixed.get(dim, ALL) for dim in "yzx")

    def add(self, target, box):
        shape = box.shape[:-2]
        count = 1
        for size in shape:
            count *= size
        free = [i for i, entry in enumerate(target) if entry is ALL]

        def body(n, _):
            spots, rest = [], n
            for size in reversed(shape):
                spots.append(lax.rem(rest, size))
                rest = lax.div(rest, size)
            spots = spots[::-1]
            full = list(target)
            for place_at, spot in zip(free, spots):
                full[place_at] = spot
            mine = self.total[tuple(full)].astype(jnp.float32)
            got = box[tuple(spots)].astype(jnp.float32)
            self.total[tuple(full)] = (mine + got).astype(jnp.bfloat16)
            return 0

        if count == 1:
            body(0, 0)
        else:
            lax.fori_loop(0, count, body, 0)

    def steps(self):
        place, listing = self.place, []
        own = pltpu.make_async_copy(self.source(place.c), self.total, self.sems[2])
        core = self.copy(self.source(1 - place.c), self.core_in, "c", 1 - place.c)

        def start():
            own.start()
            core.start()

        def finish():
            own.wait()
            core.wait_recv()
            self.add((ALL, ALL, ALL), self.core_in)

        self.sent.append(Link(core))
        listing.append((start, finish))
        fixed, box = {}, 0
        for dim in self.path:
            here, size = place.at(dim), place.size(dim)
            if size == 2:
                target = self.index({**fixed, dim: 1 - here})
                link = Link(self.copy(self.total.at[target], self.boxes[box], dim, 1 - here))
                self.sent.append(link)
                listing.append(self.pair([link], [(self.index({**fixed, dim: here}), box, None)]))
                box += 1
            else:
                for hop in range(size - 1, 0, -1):
                    links, adds = [], []
                    for way in (1, -1):
                        there = here - way
                        goal = here - way * hop
                        sends = (goal >= 0) & (goal < size)
                        source = here + way
                        got = source - way * hop
                        receives = (source >= 0) & (source < size) & (got >= 0) & (got < size)
                        target = self.index({**fixed, dim: jnp.clip(goal, 0, size - 1)})
                        copy = self.copy(
                            self.total.at[target], self.boxes[box], dim, jnp.clip(there, 0, size - 1)
                        )
                        link = Link(copy, sends, receives)
                        self.sent.append(link)
                        links.append(link)
                        adds.append((self.index({**fixed, dim: jnp.clip(got, 0, size - 1)}), box, receives))
                        box += 1
                    listing.append(self.pair(links, adds))
            fixed = {**fixed, dim: here}
        return listing

    def pair(self, links, adds):
        def start():
            for link in links:
                link.start()

        def finish():
            for link in links:
                link.wait_recv()
            for target, box, condition in adds:
                Link.when(condition, functools.partial(self.add, target, self.boxes[box]))

        return start, finish

    def close(self):
        own = (self.place.y, self.place.z, self.place.x)
        self.out(self.total[own].astype(jnp.float32))
        for link in self.sent:
            link.wait_send()


def box_shapes(sizes, path):
    ny, nz = sizes
    size = {"y": ny, "z": nz, "x": 2}
    left, shapes = "yzx", []
    for dim in path:
        left = left.replace(dim, "")
        lead = tuple(size[d] for d in left)
        shapes += [lead] * (1 if size[dim] == 2 else 2 * (size[dim] - 1))
    return shapes


BACK_PATHS = tuple(path[::-1] for path in PATHS)


def reduce_kernel(sizes, box_counts, *refs):
    sources, small_in = refs[:10], refs[10]
    outs, small_out = refs[11:21], refs[21]
    totals, core_boxes = refs[22], refs[23]
    at = 24
    boxes = []
    for count in box_counts:
        boxes.append(refs[at : at + count])
        at += count
    small_box, own_sem, send_sem, recv_sem, small_send, small_recv = refs[at:]
    place = Place(sizes)
    neighbour_barrier(place, far=True)
    width = outs[0].shape[-1]

    def square(ref):
        return lambda core: ref.at[:, core]

    def inner(q):
        return lambda core: sources[8].at[:, core, :, :, :, pl.ds(q * width, width)]

    def outer(q):
        return lambda core: sources[9].at[:, core, :, :, q]

    views = [inner(q) for q in range(4)] + [outer(q) for q in range(4)]
    views += [square(sources[i]) for i in (4, 5, 6, 7, 0, 1, 2, 3)]

    def store_square(i):
        def run(value):
            outs[i][...] = value

        return run

    def store_inner(q):
        def run(value):
            outs[8][:, q * width : (q + 1) * width] = value

        return run

    def store_outer(q):
        def run(value):
            outs[9][q] = value

        return run

    stores = [store_inner(q) for q in range(4)] + [store_outer(q) for q in range(4)]
    stores += [store_square(i) for i in (4, 5, 6, 7, 0, 1, 2, 3)]
    plans, lag = [], []
    reduces = []
    for m in range(16):
        group, kind = m // 4, m % 4
        reduce = Reduce(
            place, BACK_PATHS[kind], views[m], totals.at[m], core_boxes.at[m],
            [box.at[group] for box in boxes[kind]], stores[m],
            (send_sem.at[m], recv_sem.at[m], own_sem.at[m]),
        )
        reduces.append(reduce)
        plans.append(reduce.steps())
        lag.append(3 * group)
    small_out[...] = small_in[...]
    small = []
    moves = [("c", 1 - place.c), ("x", 1 - place.x), ("y", None), ("z", None)]
    for dim, there in moves:
        size, here, reach = place.size(dim), place.at(dim), 1
        while reach < size:
            partner = here + reach - 2 * reach * lax.rem(lax.div(here, reach), 2)
            small.append((dim, partner))
            reach *= 2
    rounds = max(max(lag[i] + len(plan) for i, plan in enumerate(plans)) + 1, len(small) + 1)
    copies = []
    for now in range(rounds):
        for offset, plan in zip(lag, plans):
            step = now - offset
            if 1 <= step <= len(plan):
                plan[step - 1][1]()
            if 0 <= step < len(plan):
                plan[step][0]()
        if 1 <= now <= len(small):
            copies[-1].wait()
            small_out[...] += small_box[now - 1]
        if now < len(small):
            dim, partner = small[now]
            copies.append(
                pltpu.make_async_remote_copy(
                    small_out, small_box.at[now], small_send.at[now], small_recv.at[now],
                    device_id=place.device(dim, partner), device_id_type=MESH,
                )
            )
            copies[-1].start()
    for reduce in reduces:
        reduce.close()


def reduce_grads(sizes, language, bucket, gains, squares, inner, outer):
    ny, nz = sizes
    grid = (ny, 2, nz, 2)
    count = ny * nz * 4
    width = squares[0].shape[1]
    part = squares[0].shape[0] // count
    langs = language.shape[0]
    flat = jnp.zeros((width,), jnp.float32).at[: bucket.size].set(bucket.reshape(-1))
    small = jnp.concatenate(
        [language] + [g.reshape(1, width) for g in gains] + [flat[None], jnp.zeros((4, width), jnp.float32)], axis=0
    )
    sources = [to_low(s).reshape(grid + (part, width)) for s in squares]
    sources += [
        to_low(inner).reshape(grid + (part, 4 * width)),
        to_low(outer).reshape(grid + (4, part, width)),
    ]
    anywhere = pl.BlockSpec(memory_space=pl.ANY)
    vmem = pl.BlockSpec(memory_space=pltpu.VMEM)
    shapes = [(part, width)] * 8 + [(part, 4 * width), (4, part, width), small.shape]
    lead = [box_shapes(sizes, path) for path in BACK_PATHS]
    slots = slot_count(sizes)
    hops = (ny * nz * 4).bit_length() - 1
    outs = pl.pallas_call(
        functools.partial(reduce_kernel, sizes, tuple(len(s) for s in lead)),
        out_shape=[jax.ShapeDtypeStruct(s, jnp.float32) for s in shapes],
        in_specs=[anywhere] * 10 + [vmem],
        out_specs=[vmem] * 11,
        scratch_shapes=[
            pltpu.VMEM((16, ny, nz, 2, part, width), jnp.bfloat16),
            pltpu.VMEM((16, ny, nz, 2, part, width), jnp.bfloat16),
        ]
        + [pltpu.VMEM((4,) + s + (part, width), jnp.bfloat16) for one in lead for s in one]
        + [
            pltpu.VMEM((hops,) + small.shape, jnp.float32),
            pltpu.SemaphoreType.DMA((16,)),
            pltpu.SemaphoreType.DMA((16, slots)),
            pltpu.SemaphoreType.DMA((16, slots)),
            pltpu.SemaphoreType.DMA((hops,)),
            pltpu.SemaphoreType.DMA((hops,)),
        ],
        compiler_params=pltpu.CompilerParams(
            collective_id=1, has_side_effects=True, vmem_limit_bytes=60 * 1024 * 1024
        ),
    )(*sources, small)
    start = (lax.axis_index("dp") * nz * 2 + lax.axis_index("fsdp")) * part
    total = outs[10]
    mine = lax.dynamic_slice(total, (0, start), (langs + 3, part))
    return (
        mine[:langs],
        total[langs + 3, : bucket.size].reshape(bucket.shape),
        mine[langs], mine[langs + 1], mine[langs + 2],
        outs[:8], outs[8], outs[9].reshape(4 * part, width),
    )


FORWARD_PATHS = (
    "zxy", "yzx", "zxy", "zyx", "zyx", "xzy", "zxy", "zxy", "zyx", "xyz", "zyx", "yxz", "zxy", "zxy", "zyx",
    "zyx", "xyz",
)
FORWARD_ORDER = (
    2, 11, 0, 9, 3, 1, 5, 16, 4, 2, 9, 3, 11, 0, 6, 16, 2, 5, 3, 1, 2, "b0", 4, 7, 0, 3, 1, 5, 0, 4, 13, 8, 6,
    2, "b1", 7, 3, 1, 4, 12, 6, 0, 10, "b2", 5, 1, 14, 6, 8, 3, 7, 2, 0, 10, 0, 1, 14, 12, 5, 9, 8, 2, 3, 13, 7,
    "b3", 4, 5, 12, "open", 6, 11, "k", 1, "q", "v", 5, 8, 15, 7, "sa0", 12, 10, 4, "sa1", 9, 6, "sa2", 8,
    "sa3", 14, 4, "send", 9, 13, 10, 6, 7, 16, "K", "cq", 14, 15, 7, 12, "V", 11, "ca0", 8, 9, 10, 13, "ca1",
    15, "ca2", "ca3", 10, 11, 16, 9, 8, 15, 14, "cend", "in0", 13, 12, "og0", 11, 10, "in1", 16, 12, 15, "og1",
    14, 13, 11, "in2", 16, "in3", 15, 14, "og3", 13, "og2", 16, 15,
)
BACKWARD_PATHS = (
    "xyz", "yzx", "yxz", "xzy", "xzy", "xyz", "yzx", "yxz", "yzx", "xzy", "yxz", "xyz", "yxz", "yzx", "xyz",
    "xzy",
)
BACKWARD_ORDER = (
    3, 1, "in0", 3, 1, 0, 2, "in1", 0, 4, "in2", 6, 2, "in3", 7, "n3", 1, 4, 3, "co", 6, "ccg", 1, "ca0", 5, 7,
    3, 2, 8, "ca1", 1, "ca2", 5, "ca3", "ca4", 4, 6, "ca5", 3, "cq", 9, 4, 2, 0, "n2", "cv", 1, 7, 8, 11, 9, 4,
    "ck", 5, 10, "so", 0, "scg", 2, 6, "sa0", 7, 11, "sa1", 6, 0, "sa2", 7, 10, "q", 8, "v", 3, 5, 15, 6, 13,
    "k", 2, 7, 12, 9, 8, 0, "cl0", 1, 15, 2, 5, 13, 14, 4, 9, "bk0", 6, 8, 5, "cl1", 12, 9, 0, 10, 14, 11,
    "bk1", 15, 13, "bk2", 5, 3, 10, 15, "h0", 10, 13, 4, "h1", 16, 12, "h2", 16, 7, 15, "h3", 13, 10, 14, "e0",
    11, 12, 16, 8, 10, 14, 11, 9, 15, 12, 13, 16, 8, 14, 11, 15, 13, 9, 12, 16, 14, "e1", 11, 14, 16, 12,
)


LOW = jnp.bfloat16
FULL = jnp.float32
PAIR = 2 * HEAD


def nt_dot(left, right):
    return lax.dot_general(left, right, (((1,), (1,)), ((), ())), preferred_element_type=FULL)


def tn_dot(left, right):
    return lax.dot_general(left, right, (((0,), (0,)), ((), ())), preferred_element_type=FULL)


def flat(ref, *suffix):
    value = ref[(ALL,) * (len(ref.shape) - 1) + suffix] if suffix else ref[...]
    rows = 1
    for size in value.shape[:-1]:
        rows *= size
    return value.reshape(rows, value.shape[-1])


def each(count, body):
    def run(i, _):
        body(pl.ds(pl.multiple_of(i * 128, 128), 128))
        return 0

    lax.fori_loop(0, count, run, 0)


def unit_rows(hidden):
    return hidden * lax.rsqrt(jnp.mean(hidden * hidden, axis=-1, keepdims=True) + EPSILON)


def spread_small(tiny, table):
    part = table.shape[1] // (tiny.shape[0] * tiny.shape[2] * 4)
    table[...] = jnp.zeros_like(table)
    lane = lax.broadcasted_iota(jnp.int32, (16, 128), 1)
    at = 0
    for y in range(tiny.shape[0]):
        for core in range(2):
            for z in range(tiny.shape[2]):
                for x in range(2):
                    slab = jnp.where(lane < part, tiny[y, core, z, x], 0.0)
                    base, shift = at // 128 * 128, at % 128
                    if shift:
                        slab = pltpu.roll(slab, shift, 1)
                    if shift + part <= 128:
                        table[:, base : base + 128] += slab
                    else:
                        table[:, base : base + 128] += jnp.where(lane >= part, slab, 0.0)
                        table[:, base + 128 : base + 256] += jnp.where(lane < part, slab, 0.0)
                    at += part


def build_bias(ids, values, bias, heads):
    keys, queries = bias.shape[1:]
    rows = 64

    def block(n, _):
        at = pl.ds(pl.multiple_of(n * rows, rows), rows)
        bucket = ids[at, :]
        bits = [lax.bitwise_and(bucket, 1 << b) != 0 for b in range(5)]
        key = n * rows + lax.broadcasted_iota(jnp.int32, (rows, queries), 0)
        query = lax.broadcasted_iota(jnp.int32, (rows, queries), 1)
        hidden = key > query

        def head(h, _):
            row, first = 11 + lax.div(h, 4), lax.rem(h, 4) * 32
            level = [values[row, first + c] for c in range(32)]
            for bit in bits:
                level = [jnp.where(bit, level[i + 1], level[i]) for i in range(0, len(level), 2)]
            bias[h, at, :] = jnp.where(hidden, NEGATIVE, level[0]).astype(LOW)
            return 0

        return lax.fori_loop(*heads, head, 0)

    lax.fori_loop(0, keys // rows, block, 0)


def head_pair(value):
    lane = lax.broadcasted_iota(jnp.int32, value.shape, 1)
    zero = jnp.zeros_like(value)
    return jnp.concatenate([jnp.where(lane < HEAD, value, zero), jnp.where(lane < HEAD, zero, value)], axis=0)


def pairs_forward(items):
    scores = [nt_dot(keys, head_pair(queries)) for queries, keys, _, _ in items]
    scores = [s if item[3] is None else s + item[3] for s, item in zip(scores, items)]
    grown = [jnp.exp(s - jnp.max(s, axis=0, keepdims=True)) for s in scores]
    rows = [1.0 / jnp.sum(g, axis=0, keepdims=True) for g in grown]
    weights = [g.astype(LOW) for g in grown]
    results = []
    for (queries, _, values, _), low, row in zip(items, weights, rows):
        count = queries.shape[0]
        lane = lax.broadcasted_iota(jnp.int32, values.shape, 1)
        one = jnp.ones_like(values)
        first = tn_dot(low[:, :count], jnp.where(lane < HEAD, values, one))
        second = tn_dot(low[:, count:], jnp.where(lane < HEAD, one, values))
        lane = lax.broadcasted_iota(jnp.int32, first.shape, 1)
        inverse = 1.0 / pltpu.roll(jnp.where(lane < HEAD, second, first), HEAD, 1)
        results.append((jnp.where(lane < HEAD, first, second) * inverse, inverse, low, row))
    return results


def gelu_parts(u):
    a, b = 0.7978845608028654, 0.044715
    square = u * u
    t = jnp.tanh(a * u * (1.0 + b * square))
    half = 0.5 * (1.0 + t)
    slope = half + 0.5 * u * (1.0 - t * t) * (a * (1.0 + 3.0 * b * square))
    return u * half, slope


def gather_plans(place, wholes, small, exchange):
    views = [lambda index, ref=ref: ref.at[index] for ref in [small] + list(wholes[:8])]
    width = wholes[0].shape[-1]
    for q in range(4):
        views.append(lambda index, q=q: wholes[8].at[index + (ALL, pl.ds(q * width, width))])
    for q in range(4):
        views.append(lambda index, q=q: wholes[9].at[index + (q,)])
    return [gather_early(place, view, path, exchange) for view, path in zip(views, FORWARD_PATHS)]


def gather_early(place, blocks, path, exchange):
    steps = []
    at = {dim: place.at(dim) for dim in "yczx"}

    def link(dim, there, where, sends=None, receives=None, slot=None):
        view = blocks(tuple(where.get(d, at[d]) for d in "yczx"))
        return exchange.link(view, view, dim, there, sends, receives, slot)

    def swap(dim, where):
        return link(dim, 1 - at[dim], where)

    def slots(hop):
        first = exchange.slot()
        return first, first if 2 * hop >= place.nz else exchange.slot()

    def hops(hop, where):
        here, size, links = at["z"], place.nz, []
        for way, slot in zip((1, -1), slots(hop)):
            origin, there, source = here - way * (hop - 1), here + way, here - way * hop
            sends = (origin >= 0) & (origin < size) & (there >= 0) & (there < size)
            receives = (source >= 0) & (source < size)
            spot = {**where, "z": jnp.clip(origin, 0, size - 1)}
            links.append(link("z", jnp.clip(there, 0, size - 1), spot, sends, receives, slot))
        return links

    def swap_arrived(dim, hop, where):
        here, size, links = at["z"], place.nz, []
        for way, slot in zip((1, -1), slots(hop)):
            source = here - way * hop
            here_now = (source >= 0) & (source < size)
            spot = {**where, "z": jnp.clip(source, 0, size - 1)}
            links.append(link(dim, 1 - at[dim], spot, here_now, here_now, slot))
        return links

    last = path[2]
    if last == "z":
        first, second = path[0], path[1]
        steps = [[swap(first, {})], [swap(second, {first: ALL})]]
        steps += [hops(hop, {first: ALL, second: ALL}) for hop in range(1, place.nz)]
        steps.append([swap("c", {"y": ALL, "z": ALL, "x": ALL})])
        return steps
    if path[0] == "z":
        first = path[1]
        steps = [hops(hop, {}) for hop in range(1, place.nz)]
        steps.append([swap(first, {"z": ALL}), swap(last, {"z": ALL})])
        steps.append([swap(last, {"z": ALL, first: 1 - at[first]})])
    else:
        first = path[0]
        steps.append([swap(first, {})])
        steps.append(hops(1, {first: ALL}) + [swap(last, {first: ALL})])
        for hop in range(2, place.nz):
            steps.append(hops(hop, {first: ALL}) + swap_arrived(last, hop - 1, {first: ALL}))
        steps.append(swap_arrived(last, place.nz - 1, {first: ALL}))
    steps[-1].append(swap("c", {"z": ALL, first: ALL}))
    steps.append([swap("c", {"z": ALL, first: ALL, last: 1 - at[last]})])
    return steps


def run_order(order, plans, tasks, done):
    at = [0] * len(plans)
    for entry in order:
        if isinstance(entry, str):
            tasks[entry]()
            continue
        step, plan = at[entry], plans[entry]
        at[entry] += 1
        if step >= 1:
            for link in plan[step - 1]:
                link.wait_recv()
        if step < len(plan):
            for link in plan[step]:
                link.start()
        else:
            done(entry)


SAVED = (
    "first_norm", "queries", "keys", "values", "self_context", "second_norm", "cross_queries",
    "source_keys", "source_values", "cross_context", "third_norm", "activated", "slope",
    "start", "mid", "late", "self_inverse", "cross_inverse", "self_rows", "cross_rows", "table",
)


def saved_shapes(tokens, sources, width, length):
    low, full = LOW, FULL
    row = (tokens, width)
    pairs = tokens // length * (width // PAIR)
    shapes = {name: (row, low) for name in SAVED}
    shapes["source_keys"] = shapes["source_values"] = ((2, sources // 2, width), low)
    shapes["activated"] = shapes["slope"] = ((4,) + row, low)
    for name in ("start", "mid", "late", "self_inverse", "cross_inverse"):
        shapes[name] = (row, full)
    shapes["self_rows"] = shapes["cross_rows"] = ((pairs, 1, 2 * length), full)
    shapes["table"] = ((16, width), full)
    return shapes


def forward_kernel(sizes, *refs):
    n = len(SAVED)
    small_shard, shards = refs[0], refs[1:11]
    hidden_in, upstream_in, encoder_in, languages, sources, ids, slab_values = refs[11:18]
    outer_grads, whole_outs = refs[18], refs[19:29]
    self_weights, cross_weights = refs[29:31]
    saved_outs = dict(zip(SAVED, refs[31 : 31 + n]))
    at = 31 + n
    tiny, wholes = refs[at], refs[at + 1 : at + 11]
    at += 11
    v = dict(zip(SAVED, refs[at : at + n]))
    at += n
    bias, stage, outer_blocks, hidden, upstream, encoder, ids_across = refs[at : at + 7]
    send_sem, recv_sem, copy_sem = refs[at + 7 :]
    tokens, width = hidden.shape
    length = ids.shape[0]
    per_seq = width // PAIR
    seqs = tokens // length
    enc_length = encoder.shape[0] // 2
    blocks = tokens // 128

    place = Place(sizes)
    own = (place.y, place.c, place.z, place.x)
    moving = Pool(copy_sem, copy_sem.shape[0])
    sending = Pool(send_sem, send_sem.shape[0])
    owns = [
        PooledCopy(moving, shard, whole.at[own])
        for shard, whole in zip((small_shard,) + shards, (tiny,) + wholes)
    ]
    inputs = [
        PooledCopy(moving, source, target)
        for source, target in ((hidden_in, hidden), (encoder_in, encoder), (upstream_in, upstream))
    ]
    neighbour_barrier(place)
    plans = gather_plans(place, wholes, tiny, Exchange(place, sending, recv_sem))
    for copy in owns:
        copy.wait()

    def keep(name):
        PooledCopy(moving, v[name], saved_outs[name])

    def keep_whole(m):
        if m == 0:
            return
        if m < 9:
            source, target = wholes[m - 1], whole_outs[m - 1]
        elif m < 13:
            index = (ALL,) * 5 + (pl.ds((m - 9) * width, width),)
            source, target = wholes[8].at[index], whole_outs[8].at[index]
        else:
            index = (ALL,) * 4 + (m - 13,)
            source, target = wholes[9].at[index], whole_outs[9].at[index]
        PooledCopy(moving, source, target)

    def opening():
        inputs.pop(0).wait()
        spread_small(tiny, v["table"])
        for s in range(seqs):
            row = jnp.zeros((1, width), FULL)
            for l in range(8):
                row = row + jnp.where(languages[s] == l, v["table"][l : l + 1, :], 0.0)

            def body(at):
                start = hidden[at, :].astype(FULL) + row
                v["start"][at, :] = start
                v["first_norm"][at, :] = (unit_rows(start) * v["table"][8:9, :]).astype(LOW)

            def run(i, _):
                body(pl.ds(pl.multiple_of(s * length + i * 128, 128), 128))
                return 0

            lax.fori_loop(0, length // 128, run, 0)
        keep("table")
        keep("start")
        keep("first_norm")

    def project(source, weight, target):
        target[...] = jnp.dot(source[...], flat(weight), preferred_element_type=FULL).astype(LOW)

    leaving = {}

    def attention(turn, queries, keys, values, context, inverse, rows, weights_out, seq, first, last, picked):
        row_at = pl.ds(seq * length, length)
        key_rows = length if picked is None else enc_length
        items = []
        for p in range(first, last):
            lanes = pl.ds(p * PAIR, PAIR)
            if picked is not None:
                items.append((queries[row_at, lanes], keys[picked, :, lanes], values[picked, :, lanes], None))
            else:
                offset = jnp.concatenate([bias[2 * p], bias[2 * p + 1]], axis=1).astype(FULL)
                items.append((queries[row_at, lanes], keys[row_at, lanes], values[row_at, lanes], offset))
        for n, (out, total, low, row) in enumerate(pairs_forward(items)):
            lanes = pl.ds((first + n) * PAIR, PAIR)
            index = seq * per_seq + first + n
            slot = turn % 2 * (last - first) + n
            if slot in leaving:
                leaving[slot].wait()
            part = stage.at[slot, pl.ds(0, key_rows)]
            part[...] = low
            rows[index] = row
            context[row_at, lanes] = out.astype(LOW)
            inverse[row_at, lanes] = total
            leaving[slot] = PooledCopy(moving, part, weights_out.at[index])

    def residual(context, weight, before, after, gain_row, norm):
        def body(at):
            state = before[at, :] + jnp.dot(context[at, :], flat(weight), preferred_element_type=FULL)
            after[at, :] = state
            norm[at, :] = (unit_rows(state) * v["table"][gain_row : gain_row + 1, :]).astype(LOW)

        each(blocks, body)

    def self_projection(i, name):
        project(v["first_norm"], wholes[i], v[name])
        keep(name)

    def self_attention(turn, s, first, last):
        attention(
            turn, v["queries"], v["keys"], v["values"], v["self_context"], v["self_inverse"], v["self_rows"],
            self_weights, s, first, last, None,
        )

    def self_end():
        for name in ("self_context", "self_inverse", "self_rows"):
            keep(name)
        residual(v["self_context"], wholes[3], v["start"], v["mid"], 9, v["second_norm"])
        keep("mid")
        keep("second_norm")

    def cross_source(i, name):
        if len(inputs) == 2:
            inputs.pop(0).wait()
        for half in range(2):
            v[name][half] = jnp.dot(
                encoder[pl.ds(half * enc_length, enc_length), :], flat(wholes[i]), preferred_element_type=FULL
            ).astype(LOW)
        keep(name)

    def cross_projection():
        project(v["second_norm"], wholes[4], v["cross_queries"])
        keep("cross_queries")

    def cross_attention(turn, s, first, last):
        attention(
            turn, v["cross_queries"], v["source_keys"], v["source_values"], v["cross_context"], v["cross_inverse"],
            v["cross_rows"], cross_weights, s, first, last, sources[s],
        )

    def cross_end():
        for name in ("cross_context", "cross_inverse", "cross_rows"):
            keep(name)
        residual(v["cross_context"], wholes[7], v["mid"], v["late"], 10, v["third_norm"])
        keep("late")
        keep("third_norm")

    def feed_inner(q):
        weight = flat(wholes[8], pl.ds(q * width, width))
        for half in range(2):
            at = pl.ds(half * tokens // 2, tokens // 2)
            expanded = jnp.dot(v["third_norm"][at, :], weight, preferred_element_type=FULL)
            value, slope = gelu_parts(expanded)
            v["activated"][q, at, :] = value.astype(LOW)
            v["slope"][q, at, :] = slope.astype(LOW)
        for name in ("activated", "slope"):
            PooledCopy(moving, v[name].at[q], saved_outs[name].at[q])

    def bias_values(turn):
        if turn == 0:
            ids_across[...] = ids[...].astype(FULL).T.astype(jnp.int32)
        build_bias(ids_across, slab_values, bias, (3 * turn, 3 * turn + 3))

    def outer_grad(q):
        if inputs:
            inputs.pop(0).wait()
        value = tn_dot(v["activated"][q], upstream[...])
        outer_blocks[q // 2, q % 2] = value.reshape(outer_blocks.shape[2:]).astype(LOW)
        chunk = q // 2, q % 2
        PooledCopy(moving, outer_blocks.at[chunk], outer_grads.at[chunk])

    tasks = {"open": opening, "send": self_end}
    tasks.update(cq=cross_projection, cend=cross_end)
    for i, (task, name) in enumerate((("q", "queries"), ("k", "keys"), ("v", "values"))):
        tasks[task] = functools.partial(self_projection, i, name)
    for i in range(4):
        first = per_seq // 2 * (i % 2)
        tasks[f"sa{i}"] = functools.partial(self_attention, i, i // 2, first, first + per_seq // 2)
        tasks[f"ca{i}"] = functools.partial(cross_attention, i, i // 2, first, first + per_seq // 2)
        tasks[f"in{i}"] = functools.partial(feed_inner, i)
        tasks[f"b{i}"] = functools.partial(bias_values, i)
        tasks[f"og{i}"] = functools.partial(outer_grad, i)
    tasks["K"] = functools.partial(cross_source, 5, "source_keys")
    tasks["V"] = functools.partial(cross_source, 6, "source_values")
    run_order(FORWARD_ORDER, plans, tasks, keep_whole)
    sending.drain()
    moving.drain()


RECEIVES = {"xyz": 7, "yxz": 7, "zxy": 9, "zyx": 9, "xzy": 12, "yzx": 12}


def small_slab(table, gains, bucket_table):
    part = table.shape[1]
    own = jnp.concatenate([table] + [g.reshape(1, part) for g in gains], axis=0)
    own = jnp.pad(own, ((0, 0), (0, 128 - part)))
    buckets = bucket_table.T.reshape(-1, 128)
    return jnp.pad(jnp.concatenate([own, buckets], axis=0), ((0, 2), (0, 0))).astype(FULL)


def forward(
    sizes, hidden_in, output_grad, encoder_states, language_ids, source_index, bucket_ids, language_table, bucket_table, gains,
    squares, inner, outer,
):
    ny, nz = sizes
    grid = (ny, 2, nz, 2)
    part, width = squares[0].shape
    tokens = hidden_in.shape[0]
    length = bucket_ids.shape[0]
    encoder = encoder_states.reshape(-1, width)
    enc_length = encoder_states.shape[1]
    slab = small_slab(language_table, gains, bucket_table)
    shards = [slab] + list(squares) + [inner, outer.reshape(4, part, width)]
    wholes = [jax.ShapeDtypeStruct(grid + s.shape, s.dtype) for s in shards]
    shapes = saved_shapes(tokens, encoder.shape[0], width, length)
    pairs = tokens // length * (width // PAIR)
    anywhere = pl.BlockSpec(memory_space=pl.ANY)
    vmem = pl.BlockSpec(memory_space=pltpu.VMEM)
    smem = pl.BlockSpec(memory_space=pltpu.SMEM)
    out_shape = [wholes[10]] + wholes[1:]
    out_shape += [jax.ShapeDtypeStruct((pairs, rows, 2 * length), LOW) for rows in (length, enc_length)]
    out_shape += [jax.ShapeDtypeStruct(*shapes[name]) for name in SAVED]
    outs = pl.pallas_call(
        functools.partial(forward_kernel, sizes),
        out_shape=out_shape,
        in_specs=[anywhere] * 11 + [anywhere] * 3 + [smem, smem, vmem, smem],
        out_specs=[anywhere] * len(out_shape),
        scratch_shapes=[pltpu.VMEM(w.shape, w.dtype) for w in wholes]
        + [pltpu.VMEM(*shapes[name]) for name in SAVED]
        + [
            pltpu.VMEM((H, length, length), LOW),
            pltpu.VMEM((6, enc_length, 2 * length), LOW),
            pltpu.VMEM(wholes[10].shape, LOW),
            pltpu.VMEM((tokens, width), LOW),
            pltpu.VMEM((tokens, width), LOW),
            pltpu.VMEM(encoder.shape, LOW),
            pltpu.VMEM((length, length), jnp.int32),
            pltpu.SemaphoreType.DMA((48,)),
            pltpu.SemaphoreType.DMA((sum(RECEIVES[path] for path in FORWARD_PATHS),)),
            pltpu.SemaphoreType.DMA((28,)),
        ],
        compiler_params=pltpu.CompilerParams(
            collective_id=2, has_side_effects=True, vmem_limit_bytes=62 * 1024 * 1024
        ),
    )(
        *shards, hidden_in, output_grad, encoder, language_ids, source_index, bucket_ids, slab,
    )
    return outs


class Summed:
    def __init__(self, place, path, blocks, leaving, core_in, boxes, exchange):
        self.blocks, self.stages = blocks, []
        c = place.c
        core = exchange.link(leaving(1 - c), core_in, "c", 1 - c)
        self.stages.append(([core], [((ALL, c, ALL, ALL), core_in, None)]))
        fixed, box = {"c": c}, 0
        for dim in path:
            here, size = place.at(dim), place.size(dim)
            if size == 2:
                link = exchange.link(blocks(self.index({**fixed, dim: 1 - here})), boxes[box], dim, 1 - here)
                self.stages.append(([link], [(self.index({**fixed, dim: here}), boxes[box], None)]))
                box += 1
            else:
                for hop in range(size - 1, 0, -1):
                    links, adds = [], []
                    first = exchange.slot()
                    second = first if 2 * hop > size + 1 else exchange.slot()
                    for way, slot in ((1, first), (-1, second)):
                        there, goal = here - way, here - way * hop
                        sends = (goal >= 0) & (goal < size)
                        source = here + way
                        got = source - way * hop
                        receives = (source >= 0) & (source < size) & (got >= 0) & (got < size)
                        goal_at = self.index({**fixed, dim: jnp.clip(goal, 0, size - 1)})
                        there = jnp.clip(there, 0, size - 1)
                        links.append(exchange.link(blocks(goal_at), boxes[box], dim, there, sends, receives, slot))
                        adds.append((self.index({**fixed, dim: jnp.clip(got, 0, size - 1)}), boxes[box], receives))
                        box += 1
                    self.stages.append((links, adds))
            fixed = {**fixed, dim: here}
        self.own = self.index(fixed)

    def index(self, fixed):
        return tuple(fixed.get(dim, ALL) for dim in "yczx")

    def start(self, step):
        for link in self.stages[step][0]:
            link.start()

    def finish(self, step):
        links, adds = self.stages[step]
        for link in links:
            link.wait_recv()

        def add(target, box):
            view = self.blocks(target)
            view[...] = view[...] + box[...]

        for target, box, condition in adds:
            Link.when(condition, functools.partial(add, target, box))


def pairs_backward(items):
    stacked = [head_pair(item[4]) for item in items]
    prob_grads = [nt_dot(item[3], grads) for item, grads in zip(items, stacked)]
    value_parts = [jnp.dot(item[0], grads, preferred_element_type=FULL) for item, grads in zip(items, stacked)]
    scaled = [item[0].astype(FULL) * grads for item, grads in zip(items, prob_grads)]
    centres = [jnp.sum(s, axis=0, keepdims=True) * item[5] for s, item in zip(scaled, items)]
    score_grads = [(s - item[0].astype(FULL) * c).astype(LOW) for s, c, item in zip(scaled, centres, items)]
    key_parts = [jnp.dot(s, head_pair(item[1]), preferred_element_type=FULL) for s, item in zip(score_grads, items)]
    results = []
    for item, value_part, key_part, score_grad in zip(items, value_parts, key_parts, score_grads):
        count = item[1].shape[0]
        lane = lax.broadcasted_iota(jnp.int32, (count, PAIR), 1)
        first, second = tn_dot(score_grad[:, :count], item[2]), tn_dot(score_grad[:, count:], item[2])
        results.append((jnp.where(lane < HEAD, first, second), key_part, value_part, score_grad))
    return results


def backward_kernel(sizes, box_counts, *refs):
    n = len(SAVED)
    grads, encoder, languages, sources, ids_in, outer_grads = refs[:6]
    wholes = refs[6:16]
    self_weights, cross_weights = refs[16:18]
    saved = dict(zip(SAVED, refs[18 : 18 + n]))
    at = 18 + n
    hidden_out, hidden_grad, encoder_grad, small_out, packed_out = refs[at : at + 5]
    at += 5
    squares, outers, core_boxes = refs[at : at + 3]
    at += 3
    boxes = []
    for count in box_counts:
        boxes.append(refs[at : at + count])
        at += count
    small_box, pool, pairs_in, run_a, run_b, run_c, w, wo, stage, score_sum, bucket_rows, table, self_rows, cross_rows, ids, packed = refs[at : at + 16]
    send_sem, recv_sem, small_send, small_recv, load_sem, store_sem = refs[at + 16 :]
    place = Place(sizes)
    length = ids.shape[0]
    seqs, tokens = languages.shape[0], pool.shape[1]
    width = pool.shape[2]
    blocks = tokens // 128
    per_seq = width // PAIR
    sending = Pool(send_sem, send_sem.shape[0])
    loading = Pool(load_sem, load_sem.shape[0])
    storing = Pool(store_sem, store_sem.shape[0])

    def load(source, target):
        return PooledCopy(loading, source, target)

    def store(source, target):
        PooledCopy(storing, source, target)

    X = [pool.at[i] for i in range(11)] + [pairs_in.at[i] for i in range(4)]
    og, tn = X[0], X[1]
    get_og = load(grads, og)
    def outer_chunk(q):
        return wholes[9].at[q // 2, q % 2]

    def inner_chunk(q):
        return wholes[8].at[:, :, :, :, :, pl.ds(q * width, width)]

    arriving = {}

    def fetch(weights, pairs, key_rows, base):
        per_slot = stage.shape[1] // key_rows
        for n, p in enumerate(pairs):
            for s in range(seqs):
                at = base * per_slot + n * seqs + s
                part = stage.at[at // per_slot, pl.ds(at % per_slot * key_rows, key_rows)]
                arriving[key_rows, p, s] = load(weights.at[s * per_seq + p], part), part

    get_wo = [load(outer_chunk(0), wo.at[0])]
    get_slope = [load(saved["slope"].at[0], X[6])]
    get_tn = load(saved["third_norm"], tn)
    get_wi = [load(inner_chunk(0), w.at[0])]
    get_outers = load(outer_grads.at[:, place.c], outers)
    got = {}

    def load_more(q):
        if q < 3:
            get_slope.append(load(saved["slope"].at[q + 1], X[7 + q]))
        if q == 0:
            get_wo.append(load(outer_chunk(1), wo.at[1]))
            get_wi.append(load(inner_chunk(1), w.at[1]))
            got["table"] = load(saved["table"], table)
            got["late"] = load(saved["late"], run_c)
        if q == 1:
            got["cross_context"] = load(saved["cross_context"], X[2])
            got["co"] = load(wholes[7], w.at[2])
            got["cross_rows"] = load(saved["cross_rows"], cross_rows)
            got["cross_queries"] = load(saved["cross_queries"], X[3])
        if q == 2:
            got["keys"] = load(saved["source_keys"], pairs_in.at[pl.ds(0, 2)])
            got["values"] = load(saved["source_values"], pairs_in.at[pl.ds(2, 2)])
            fetch(cross_weights, (0,), stage.shape[1], 0)
        if q == 3:
            got["cq_w"] = load(wholes[4], w.at[3])
            got["second_norm"] = load(saved["second_norm"], X[4])
            got["first_norm"] = load(saved["first_norm"], X[5])
            got["self_rows"] = load(saved["self_rows"], self_rows)

    neighbour_barrier(place, far=True)

    def view_of(m):
        if m < 4:
            return lambda index: outers.at[(index[0],) + index[2:] + (m,)]
        return lambda index: squares.at[(m - 4,) + index]

    def leaving_of(m):
        if m < 4:
            return lambda core: outer_grads.at[:, core, :, :, m]
        return lambda core: squares.at[m - 4, :, core]

    exchange = Exchange(place, sending, recv_sem)
    plans = []
    for m in range(16):
        group, kind = m // 4, BACK_PATHS.index(BACKWARD_PATHS[m])
        slot = group % 2
        plans.append(
            Summed(
                place, BACK_PATHS[kind], view_of(m), leaving_of(m), core_boxes.at[slot, kind], [box.at[slot] for box in boxes[kind]],
                exchange,
            )
        )

    def put(i, value):
        squares[i] = value.reshape(squares.shape[1:]).astype(LOW)

    small_out[...] = jnp.zeros_like(small_out)

    def norm_backward(state, inflow, gain_row, before, after):
        def body(at):
            hidden, flow, gain = state[at, :], inflow[at, :], table[gain_row : gain_row + 1, :]
            scale = lax.rsqrt(jnp.mean(hidden * hidden, axis=-1, keepdims=True) + EPSILON)
            unit = hidden * scale
            small_out[gain_row : gain_row + 1, :] += jnp.sum(flow * unit, axis=0, keepdims=True)
            flow = flow * gain
            flow = (flow - unit * jnp.mean(unit * flow, axis=-1, keepdims=True)) * scale
            after[at, :] = before[at, :].astype(FULL) + flow

        each(blocks, body)

    branch = X[1]

    def inner_grad(q):
        eg = X[10]
        if q == 0:
            get_og.wait()
            get_tn.wait()
        get_wo[q].wait()
        get_slope[q].wait()
        out_w = wo[q % 2].reshape(width, width)
        eg[...] = (nt_dot(og[...], out_w) * X[6 + q][...].astype(FULL)).astype(LOW)
        load_more(q)
        get_wo.append(load(outer_chunk((q + 2) % 4), wo.at[q % 2]))
        put(q, tn_dot(tn[...], eg[...]))
        get_wi[q].wait()
        back = nt_dot(eg[...], flat(w.at[q % 2]))
        if q == 0:
            run_b[...] = back
        else:
            run_b[...] += back
        if q + 2 < 4:
            get_wi.append(load(inner_chunk(q + 2), w.at[q % 2]))
        if q == 3:
            got["so"] = load(wholes[3], w.at[0])
            got["q_w"] = load(wholes[0], w.at[1])
            got["encoder"] = load(encoder, pool.at[pl.ds(6, 2)])

    def third_backward():
        got["table"].wait()
        got["late"].wait()
        norm_backward(run_c, run_b, 10, og, run_a)
        got["inverse"] = load(saved["cross_inverse"], run_c)
        branch[...] = run_a[...].astype(LOW)

    def context_grad(weight, slot):
        got[weight].wait()
        got["inverse"].wait()
        X[0][...] = (nt_dot(branch[...], flat(w.at[slot])).astype(LOW).astype(FULL) * run_c[...]).astype(LOW)

    def cross_out_grad():
        got["cross_context"].wait()
        put(4, tn_dot(X[2][...], branch[...]))

    def cross_context_grad():
        context_grad("co", 2)
        got["k_w"] = load(wholes[1], w.at[2])
        got["mid"] = load(saved["mid"], run_c)

    def attention(rows, key_rows, pairs, one, finish_pair, ahead):
        for p in pairs:
            for s in range(seqs):
                arriving[key_rows, p, s][0].wait()
        ahead()
        items = []
        for p in pairs:
            for s in range(seqs):
                queries, keys, values, grad = one(s, pl.ds(p * PAIR, PAIR))
                items.append(
                    (arriving[key_rows, p, s][1][...], queries, keys, values, grad, rows[s * per_seq + p])
                )
        results = pairs_backward(items)
        for n, p in enumerate(pairs):
            finish_pair(p, pl.ds(p * PAIR, PAIR), results[n * seqs : (n + 1) * seqs])

    enc_length = pool.shape[1]

    def cross_attention(p):
        if p == 0:
            for name in ("cross_rows", "cross_queries", "keys", "values"):
                got[name].wait()

        def one(s, lanes):
            at = pl.ds(s * length, length)
            source = sources[s]
            return X[3][at, lanes], pairs_in[source, :, lanes], pairs_in[2 + source, :, lanes], X[0][at, lanes]

        def finish_pair(p, lanes, results):
            for s in range(seqs):
                X[1][pl.ds(s * length, length), lanes] = results[s][0].astype(LOW)
            for e in range(2):
                for target, part_at in ((8, 1), (11, 2)):
                    total = jnp.where(sources[0] == e, results[0][part_at], 0.0)
                    total = total + jnp.where(sources[1] == e, results[1][part_at], 0.0)
                    pool[target + e, :, lanes] = total.astype(LOW)

        def ahead():
            if p + 1 < per_seq:
                fetch(cross_weights, (p + 1,), enc_length, (p + 1) % 2 * 2)
            else:
                fetch(self_weights, (0, 1), length, 0)

        attention(cross_rows, enc_length, (p,), one, finish_pair, ahead)
        if p + 1 < per_seq:
            return
        got["queries"] = load(saved["queries"], X[11])
        got["keys"] = load(saved["keys"], X[12])
        got["values"] = load(saved["values"], X[13])
        got["self_context"] = load(saved["self_context"], X[14])

    def cross_query_grad():
        got["second_norm"].wait()
        put(5, tn_dot(X[4][...], X[1][...]))

    def source_grad(i, target):
        copy = got.pop("encoder", None)
        if copy is not None:
            copy.wait()
        put(i, tn_dot(pool[6], pool[target]) + tn_dot(pool[7], pool[target + 1]))

    def second_backward():
        got["cq_w"].wait()
        run_b[...] = nt_dot(X[1][...], flat(w.at[3]))
        got["v_w"] = load(wholes[2], w.at[3])
        got["mid"].wait()
        norm_backward(run_c, run_b, 9, run_a, run_a)
        got["inverse"] = load(saved["self_inverse"], run_c)
        branch[...] = run_a[...].astype(LOW)

    def self_out_grad():
        got["self_context"].wait()
        put(8, tn_dot(X[14][...], branch[...]))

    def self_context_grad():
        context_grad("so", 0)
        got["ck_w"] = load(wholes[5], w.at[0])
        got["start"] = load(saved["start"], run_c)

    def self_attention(turn):
        if turn == 0:
            for name in ("self_rows", "queries", "keys", "values"):
                got[name].wait()

        def one(s, lanes):
            at = pl.ds(s * length, length)
            return tuple(X[i][at, lanes] for i in (11, 12, 13, 0))

        def finish_pair(p, lanes, results):
            for s in range(seqs):
                for i in range(3):
                    X[2 + i][pl.ds(s * length, length), lanes] = results[s][i].astype(LOW)
            score_sum[p] = results[0][3].astype(FULL) + results[1][3].astype(FULL)

        def ahead():
            if turn < 2:
                fetch(self_weights, (2 * turn + 2, 2 * turn + 3), length, (turn + 1) % 2 * 2)

        attention(self_rows, length, (2 * turn, 2 * turn + 1), one, finish_pair, ahead)

    def self_grad(i):
        copy = got.pop("first_norm", None)
        if copy is not None:
            copy.wait()
        put(9 + i, tn_dot(X[5][...], X[2 + i][...]))

    def closing_product():
        for name in ("q_w", "k_w", "v_w", "start"):
            got[name].wait()
        run_b[...] = nt_dot(X[2][...], flat(w.at[1]))
        run_b[...] += nt_dot(X[3][...], flat(w.at[2]))
        run_b[...] += nt_dot(X[4][...], flat(w.at[3]))
        got["cv_w"] = load(wholes[6], w.at[1])

    def closing():
        got["activated"] = [load(saved["activated"].at[q], X[i]) for q, i in enumerate((0, 1, 5, 10))]
        norm_backward(run_c, run_b, 8, run_a, run_a)
        store(run_a, hidden_grad)
        got["late"] = load(saved["late"], run_c)
        for s in range(seqs):
            row = jnp.sum(run_a[pl.ds(s * length, length), :], axis=0, keepdims=True)
            for l in range(8):
                small_out[l : l + 1, :] += jnp.where(languages[s] == l, row, 0.0)

    def hidden_end(q):
        got["activated"][q].wait()
        get_wo[4 + q].wait()
        value = jnp.dot(X[(0, 1, 5, 10)[q]][...], wo[q % 2].reshape(width, width), preferred_element_type=FULL)
        if q < 2:
            get_wo.append(load(outer_chunk(q + 2), wo.at[q % 2]))
        if q == 0:
            got["late"].wait()
        if q < 3:
            run_c[...] += value
        else:
            X[2][...] = (run_c[...] + value).astype(LOW)
            store(X[2], hidden_out)

    def encoder_end(e):
        run = (run_b, run_c)[e]
        if e == 0:
            got["ck_w"].wait()
            got["cv_w"].wait()
        run[...] = nt_dot(pool[8 + e], flat(w.at[0]))
        run[...] += nt_dot(pool[11 + e], flat(w.at[1]))
        store(run, encoder_grad.at[e])

    def bucket_sums(turn):
        if turn == 0:
            ids[...] = ids_in[...].astype(FULL).T.astype(jnp.int32)
        half = length // 2
        rows = 32

        def pair(p, _):
            def bucket_group(first, count, spans):
                sums = [[jnp.zeros((8, half), FULL) for _ in range(2)] for _ in range(count)]
                for n, side in spans:
                    block = pl.ds(n * rows, rows)
                    bucket = ids[block, side * half : (side + 1) * half]
                    scores = [
                        score_sum[p, block, h * length + side * half : h * length + (side + 1) * half]
                        for h in range(2)
                    ]
                    for c in range(count):
                        here = bucket == first + c
                        for h in range(2):
                            kept = jnp.where(here, scores[h], 0.0).reshape(rows // 8, 8, half)
                            sums[c][h] = sums[c][h] + jnp.sum(kept, axis=0)
                for c in range(count):
                    for h in range(2):
                        row = (2 * p + h) * 32 + first + c
                        bucket_rows[pl.ds(row, 1), :] = jnp.sum(sums[c][h], axis=0, keepdims=True)

            blocks_of = length // rows
            every = [(n, side) for side in range(2) for n in range(blocks_of) if n * rows < (side + 1) * half]
            near = [(n, side) for n, side in every if n * rows + rows + 15 > side * half]
            for first in range(0, 32, 4):
                bucket_group(first, 4, near if first < 16 else every)
            return 0

        lax.fori_loop(2 * turn, 2 * turn + 2, pair, 0)
        if turn < 2:
            return
        ones = jnp.ones((8, 128), FULL)
        totals = lax.dot_general(
            ones, bucket_rows[...], (((1,), (1,)), ((), ())), precision=PRECISE, preferred_element_type=FULL
        )
        small_out[11:12, : bucket_rows.shape[0]] = totals[:1, :]

    small = []
    for dim in "cxyz":
        here, reach = place.at(dim), 1
        while reach < place.size(dim):
            small.append((dim, here + reach - 2 * reach * lax.rem(lax.div(here, reach), 2)))
            reach *= 2

    def small_copy(i):
        dim, partner = small[i]
        return pltpu.make_async_remote_copy(
            small_out, small_box.at[i], small_send.at[i], small_recv.at[i],
            device_id=place.device(dim, partner), device_id_type=MESH,
        )

    class Small:
        def start(self, i):
            small_copy(i).start()

        def finish(self, i):
            small_copy(i).wait()
            small_out[...] += small_box[i]

    tasks = dict(n3=third_backward, co=cross_out_grad, ccg=cross_context_grad, cq=cross_query_grad, n2=second_backward)
    tasks.update(so=self_out_grad, scg=self_context_grad, cl0=closing_product, cl1=closing)
    tasks["e0"], tasks["e1"] = functools.partial(encoder_end, 0), functools.partial(encoder_end, 1)
    tasks["ck"] = functools.partial(source_grad, 6, 8)
    tasks["cv"] = functools.partial(source_grad, 7, 11)
    for i in range(4):
        tasks[f"in{i}"] = functools.partial(inner_grad, i)
        tasks[f"h{i}"] = functools.partial(hidden_end, i)
    for i in range(per_seq):
        tasks[f"ca{i}"] = functools.partial(cross_attention, i)
    for i in range(3):
        tasks[f"sa{i}"] = functools.partial(self_attention, i)
        tasks[f"bk{i}"] = functools.partial(bucket_sums, i)
        tasks["qkv"[i]] = functools.partial(self_grad, i)
    steps = [len(plan.stages) for plan in plans] + [len(small)]
    plans.append(Small())
    at = [0] * 17
    def keep_sum(m):
        plan = plans[m]
        packed[m] = plan.blocks(plan.own)[...].astype(FULL)
        store(packed.at[m], packed_out.at[m])

    get_outers.wait()
    for entry in BACKWARD_ORDER:
        if isinstance(entry, str):
            tasks[entry]()
            continue
        step = at[entry]
        at[entry] += 1
        if step >= 1:
            plans[entry].finish(step - 1)
        if step < steps[entry]:
            plans[entry].start(step)
        elif entry < 16:
            keep_sum(entry)
    sending.drain()
    storing.drain()


def backward(sizes, output_grad, encoder_states, language_ids, source_index, bucket_ids, forward_outs):
    ny, nz = sizes
    grid = (ny, 2, nz, 2)
    tokens, width = output_grad.shape
    length = bucket_ids.shape[0]
    part = width // (ny * nz * 4)
    outer_grads, wholes, score_weights = forward_outs[0], forward_outs[1:11], forward_outs[11:13]
    saved = dict(zip(SAVED, forward_outs[13:]))
    enc_count, enc_length = encoder_states.shape[:2]
    anywhere = pl.BlockSpec(memory_space=pl.ANY)
    vmem = pl.BlockSpec(memory_space=pltpu.VMEM)
    smem = pl.BlockSpec(memory_space=pltpu.SMEM)
    lead = [box_shapes(sizes, path) for path in BACK_PATHS]
    hops = (ny * nz * 4).bit_length() - 1
    pairs = tokens // length * (width // PAIR)
    row = (tokens, width)
    out_shape = [
        jax.ShapeDtypeStruct(row, LOW),
        jax.ShapeDtypeStruct(row, FULL),
        jax.ShapeDtypeStruct((enc_count, enc_length, width), FULL),
        jax.ShapeDtypeStruct((16, width), FULL),
        jax.ShapeDtypeStruct((16, part, width), FULL),
    ]
    outs = pl.pallas_call(
        functools.partial(backward_kernel, sizes, tuple(len(s) for s in lead)),
        out_shape=out_shape,
        in_specs=[anywhere, anywhere, smem, smem, vmem] + [anywhere] * (13 + len(SAVED)),
        out_specs=[anywhere] * 3 + [vmem, anywhere],
        scratch_shapes=[
            pltpu.VMEM((12,) + grid + (part, width), LOW),
            pltpu.VMEM((ny, nz, 2, 4, part, width), LOW),
            pltpu.VMEM((2, 4, ny, nz, 2, part, width), LOW),
        ]
        + [pltpu.VMEM((2,) + s + (part, width), LOW) for one in lead for s in one]
        + [
            pltpu.VMEM((hops, 16, width), FULL),
            pltpu.VMEM((13,) + row, LOW),
            pltpu.VMEM((4,) + row, LOW),
            pltpu.VMEM(row, FULL),
            pltpu.VMEM(row, FULL),
            pltpu.VMEM(row, FULL),
            pltpu.VMEM((4,) + grid + (part, width), LOW),
            pltpu.VMEM((2, nz, 2, 4, part, width), LOW),
            pltpu.VMEM((4, enc_length, 2 * length), LOW),
            pltpu.VMEM((width // PAIR, length, 2 * length), FULL),
            pltpu.VMEM((32 * H, 128), FULL),
            pltpu.VMEM((16, width), FULL),
            pltpu.VMEM((pairs, 1, 2 * length), FULL),
            pltpu.VMEM((pairs, 1, 2 * length), FULL),
            pltpu.VMEM((length, length), jnp.int32),
            pltpu.VMEM((16, part, width), FULL),
            pltpu.SemaphoreType.DMA((40,)),
            pltpu.SemaphoreType.DMA((16 * 8,)),
            pltpu.SemaphoreType.DMA((hops,)),
            pltpu.SemaphoreType.DMA((hops,)),
            pltpu.SemaphoreType.DMA((28,)),
            pltpu.SemaphoreType.DMA((8,)),
        ],
        compiler_params=pltpu.CompilerParams(
            collective_id=3, has_side_effects=True, vmem_limit_bytes=63 * 1024 * 1024
        ),
    )(
        output_grad, encoder_states, language_ids, source_index, bucket_ids, outer_grads, *wholes, *score_weights,
        *[saved[name] for name in SAVED],
    )
    return finish(sizes, outs)


def finish_kernel(sizes, *refs):
    hidden_out, hidden_grad, encoder_grad, small_in, packed_in = refs[:5]
    outs = refs[5:18]
    language, bucket, gains = refs[18], refs[19], refs[20:23]
    staged_hidden, staged_grad, staged_encoder, small, packed, sem, in_sem = refs[23:]
    part, width = packed.shape[1:]
    copies, arriving = [], []

    def copy(source, target):
        copies.append(pltpu.make_async_copy(source, target, sem.at[len(copies)]))
        copies[-1].start()

    def arrive(source, target):
        arriving.append(pltpu.make_async_copy(source, target, in_sem.at[len(arriving)]))
        arriving[-1].start()
        return arriving[-1]

    get_small = arrive(small_in, small)
    blocks = []
    for source, target, out, pieces in (
        (encoder_grad, staged_encoder, outs[2], 4), (hidden_grad, staged_grad, outs[1], 2),
        (hidden_out, staged_hidden, outs[0], 1),
    ):
        size = source.shape[-2]
        for n in range(pieces):
            if len(source.shape) == 3:
                half = size // 2
                index = (n // 2, pl.ds(n % 2 * half, half))
            else:
                index = pl.ds(n * (size // pieces), size // pieces)
            blocks.append((arrive(source.at[index], target.at[index]), target.at[index], out.at[index]))
    groups = [arrive(packed_in.at[pl.ds(4 * n, 4)], packed.at[pl.ds(4 * n, 4)]) for n in range(4)]
    for ready, source, target in blocks:
        ready.wait()
        copy(source, target)
    for group in groups:
        group.wait()
    for q in range(4):
        copy(packed.at[q], outs[12].at[pl.ds(q * part, part)])
        copy(packed.at[4 + q], outs[11].at[:, pl.ds(q * width, width)])
    for i, m in enumerate((13, 14, 15, 12, 9, 10, 11, 8)):
        copy(packed.at[m], outs[3 + i])
    get_small.wait()
    place = Place(sizes)
    start = (place.dp * sizes[1] * 2 + place.fs) * part
    row = lax.broadcasted_iota(jnp.int32, (width, 128), 0)
    lane = lax.broadcasted_iota(jnp.int32, (width, 128), 1)
    chosen = jnp.where((row == lane + start) & (lane < part), 1.0, 0.0)
    own = jnp.dot(small[...], chosen, precision=PRECISE, preferred_element_type=FULL)
    language[...] = own[:8, :part]
    for i in range(3):
        gains[i][...] = own[8 + i, :part]
    row = lax.broadcasted_iota(jnp.int32, (16, width), 0)
    lane = lax.broadcasted_iota(jnp.int32, (16, width), 1)
    spread = jnp.where(lax.div(lane, 32) == row, small[11:12, :], 0.0)
    row = lax.broadcasted_iota(jnp.int32, (width, 128), 0)
    lane = lax.broadcasted_iota(jnp.int32, (width, 128), 1)
    places = jnp.where(lax.rem(row, 32) == lane, 1.0, 0.0)
    bucket[...] = jnp.dot(spread, places, precision=PRECISE, preferred_element_type=FULL)[:H, :32]
    for c in copies:
        c.wait()


def finish(sizes, outs):
    part, width = outs[4].shape[1:]
    anywhere = pl.BlockSpec(memory_space=pl.ANY)
    hbm = pl.BlockSpec(memory_space=pltpu.HBM)
    vmem = pl.BlockSpec(memory_space=pltpu.VMEM)
    shapes = [o.shape for o in outs[:3]] + [(part, width)] * 8
    shapes += [(part, 4 * width), (4 * part, width)]
    out_shape = [jax.ShapeDtypeStruct(s, FULL) for s in shapes]
    out_shape[0] = jax.ShapeDtypeStruct(shapes[0], LOW)
    out_shape += [jax.ShapeDtypeStruct(s, FULL) for s in ((8, part), (H, 32), (part,), (part,), (part,))]
    return pl.pallas_call(
        functools.partial(finish_kernel, sizes),
        out_shape=out_shape,
        in_specs=[hbm] * 5,
        out_specs=[anywhere] * 13 + [vmem] * 5,
        scratch_shapes=[pltpu.VMEM(o.shape, o.dtype) for o in outs]
        + [pltpu.SemaphoreType.DMA((23,)), pltpu.SemaphoreType.DMA((12,))],
        compiler_params=pltpu.CompilerParams(vmem_limit_bytes=60 * 1024 * 1024),
    )(*outs)


def local_general(
    sizes,
    hidden_in,
    output_grad,
    encoder_states,
    language_ids,
    source_index,
    bucket_ids,
    language_table,
    bucket_table,
    self_gain,
    self_query,
    self_key,
    self_value,
    self_out,
    cross_gain,
    cross_query,
    cross_key,
    cross_value,
    cross_out,
    feed_gain,
    inner_weight,
    outer_weight,
):
    seq_count = language_ids.shape[0]
    length = bucket_ids.shape[0]
    tokens = seq_count * length
    enc_count = encoder_states.shape[0]
    enc_length = encoder_states.shape[1]
    width = hidden_in.shape[1]
    blocks = seq_count // SEQ_BLOCK
    (
        gain_one, gain_two, gain_three, table_whole, query_whole, key_whole, value_whole, out_whole,
        cquery_whole, ckey_whole, cvalue_whole, cout_whole, inner_whole, outer_whole,
    ) = gather_weights(
        sizes, language_table, (self_gain, cross_gain, feed_gain),
        (self_query, self_key, self_value, self_out, cross_query, cross_key, cross_value, cross_out),
        inner_weight, outer_weight,
    )

    def to_blocks(array, rows):
        return array.reshape(blocks, SEQ_BLOCK, rows, array.shape[-1])

    language_hot = (language_ids[:, None] == jnp.arange(table_whole.shape[0])[None, :]).astype(
        jnp.float32
    )
    language_rows = jnp.dot(language_hot, table_whole.astype(jnp.float32), precision=PRECISE)
    start_state = (
        hidden_in.astype(jnp.float32).reshape(seq_count, length, width) + language_rows[:, None, :]
    ).reshape(tokens, width)
    first_norm = to_low(norm_scale(start_state, gain_one.astype(jnp.float32)))
    self_queries = to_low(matmul(first_norm, query_whole))
    self_keys = to_low(matmul(first_norm, key_whole))
    self_values = to_low(matmul(first_norm, value_whole))
    bucket_hot = (
        bucket_ids[:, :, None] == jnp.arange(bucket_table.shape[0])[None, None, :]
    ).astype(jnp.float32)
    position_bias = jnp.einsum(
        "ijb,bh->hij", bucket_hot, bucket_table.astype(jnp.float32), precision=PRECISE
    )
    positions = jnp.arange(length)
    masked_bias = jnp.where(
        (positions[:, None] >= positions[None, :])[None], position_bias, NEGATIVE
    )

    def self_forward(block_items):
        return attend_forward(block_items[0], block_items[1], block_items[2], masked_bias)

    self_context, self_total = lax.map(
        self_forward,
        (
            to_blocks(self_queries, length),
            to_blocks(self_keys, length),
            to_blocks(self_values, length),
        ),
    )
    self_context = self_context.reshape(tokens, -1)
    mid_state = start_state + matmul(self_context, out_whole)
    second_norm = to_low(norm_scale(mid_state, gain_two.astype(jnp.float32)))
    cross_queries = to_low(matmul(second_norm, cquery_whole))
    encoder_flat = encoder_states.reshape(enc_count * enc_length, width)
    source_keys = to_low(matmul(encoder_flat, ckey_whole)).reshape(enc_count, enc_length, -1)
    source_values = to_low(matmul(encoder_flat, cvalue_whole)).reshape(enc_count, enc_length, -1)
    source_hot = (source_index[:, None] == jnp.arange(enc_count)[None, :]).astype(jnp.float32)
    source_low = to_low(source_hot)
    picked_keys = to_low(
        jnp.einsum("se,emc->smc", source_low, source_keys, preferred_element_type=jnp.float32)
    )
    picked_values = to_low(
        jnp.einsum("se,emc->smc", source_low, source_values, preferred_element_type=jnp.float32)
    )

    def cross_forward(block_items):
        return attend_forward(block_items[0], block_items[1], block_items[2], 0.0)

    cross_context, cross_total = lax.map(
        cross_forward,
        (
            to_blocks(cross_queries, length),
            picked_keys.reshape(blocks, SEQ_BLOCK, enc_length, -1),
            picked_values.reshape(blocks, SEQ_BLOCK, enc_length, -1),
        ),
    )
    cross_context = cross_context.reshape(tokens, -1)
    late_state = mid_state + matmul(cross_context, cout_whole)
    third_norm = to_low(norm_scale(late_state, gain_three.astype(jnp.float32)))
    expanded = matmul(third_norm, inner_whole)
    activated = to_low(jax.nn.gelu(expanded, approximate=True))
    hidden_out = (late_state + matmul(activated, outer_whole)).astype(jnp.bfloat16)
    top_grad = output_grad.astype(jnp.float32)
    outer_full = left_product(activated, output_grad)
    activated_grad = right_product(output_grad, outer_whole)
    gelu_value, gelu_back = jax.vjp(jax.nn.gelu, expanded)
    expanded_grad = to_low(gelu_back(activated_grad)[0])
    inner_full = left_product(third_norm, expanded_grad)
    third_grad = right_product(expanded_grad, inner_whole)
    norm_value, norm_back = jax.vjp(norm_scale, late_state, gain_three.astype(jnp.float32))
    state_back, feed_gain_full = norm_back(third_grad)
    late_grad = top_grad + state_back
    cross_low = to_low(late_grad)
    cout_full = left_product(cross_context, cross_low)
    cross_context_grad = to_low(right_product(cross_low, cout_whole))

    def cross_backward(block_items):
        return attend_backward(
            block_items[0],
            block_items[1],
            block_items[2],
            0.0,
            block_items[3],
            block_items[4],
            False,
        )

    cquery_part, ckey_part, cvalue_part = lax.map(
        cross_backward,
        (
            to_blocks(cross_queries, length),
            picked_keys.reshape(blocks, SEQ_BLOCK, enc_length, -1),
            picked_values.reshape(blocks, SEQ_BLOCK, enc_length, -1),
            cross_total,
            to_blocks(cross_context_grad, length),
        ),
    )
    cquery_low = to_low(cquery_part.reshape(tokens, -1))
    source_key_grad = to_low(
        jnp.einsum(
            "se,smc->emc",
            source_hot,
            ckey_part.reshape(seq_count, enc_length, -1),
            precision=PRECISE,
        ).reshape(enc_count * enc_length, -1)
    )
    source_value_grad = to_low(
        jnp.einsum(
            "se,smc->emc",
            source_hot,
            cvalue_part.reshape(seq_count, enc_length, -1),
            precision=PRECISE,
        ).reshape(enc_count * enc_length, -1)
    )
    cquery_full = left_product(second_norm, cquery_low)
    ckey_full = left_product(encoder_flat, source_key_grad)
    cvalue_full = left_product(encoder_flat, source_value_grad)
    encoder_grad = (
        right_product(source_key_grad, ckey_whole) + right_product(source_value_grad, cvalue_whole)
    ).reshape(enc_count, enc_length, width)
    second_grad = right_product(cquery_low, cquery_whole)
    norm_value, norm_back = jax.vjp(norm_scale, mid_state, gain_two.astype(jnp.float32))
    state_back, cross_gain_full = norm_back(second_grad)
    mid_grad = late_grad + state_back
    self_low = to_low(mid_grad)
    out_full = left_product(self_context, self_low)
    self_context_grad = to_low(right_product(self_low, out_whole))

    def self_backward(block_items):
        return attend_backward(
            block_items[0],
            block_items[1],
            block_items[2],
            masked_bias,
            block_items[3],
            block_items[4],
            True,
        )

    query_part, key_part, value_part, bias_part = lax.map(
        self_backward,
        (
            to_blocks(self_queries, length),
            to_blocks(self_keys, length),
            to_blocks(self_values, length),
            self_total,
            to_blocks(self_context_grad, length),
        ),
    )
    query_low = to_low(query_part.reshape(tokens, -1))
    key_low = to_low(key_part.reshape(tokens, -1))
    value_low = to_low(value_part.reshape(tokens, -1))
    table_full = jnp.einsum(
        "hij,ijb->bh", jnp.sum(bias_part, axis=0), bucket_hot, precision=PRECISE
    )
    query_full = left_product(first_norm, query_low)
    key_full = left_product(first_norm, key_low)
    value_full = left_product(first_norm, value_low)
    first_grad = (
        right_product(query_low, query_whole)
        + right_product(key_low, key_whole)
        + right_product(value_low, value_whole)
    )
    norm_value, norm_back = jax.vjp(norm_scale, start_state, gain_one.astype(jnp.float32))
    state_back, self_gain_full = norm_back(first_grad)
    hidden_in_grad = mid_grad + state_back
    sequence_sums = jnp.sum(hidden_in_grad.reshape(seq_count, length, width), axis=1)
    language_full = left_product(language_hot, sequence_sums)
    (
        language_part, bucket_table_grad, sgain_part, cgain_part, feed_gain_part, whole_parts, inner_part, outer_part,
    ) = reduce_grads(
        sizes, language_full, table_full, (self_gain_full, cross_gain_full, feed_gain_full),
        (query_full, key_full, value_full, out_full, cquery_full, ckey_full, cvalue_full, cout_full),
        inner_full, outer_full,
    )
    query_sum, key_sum, value_sum, out_part, cquery_part_sum, ckey_part_sum, cvalue_part_sum, cout_part = whole_parts
    return (
        hidden_out,
        hidden_in_grad,
        encoder_grad,
        language_part,
        bucket_table_grad,
        sgain_part,
        query_sum,
        key_sum,
        value_sum,
        out_part,
        cgain_part,
        cquery_part_sum,
        ckey_part_sum,
        cvalue_part_sum,
        cout_part,
        feed_gain_part,
        inner_part,
        outer_part,
    )


def local(sizes, *args):
    if sizes == (2, 4) and args[8].shape[0] % 8 == 0:
        return local_fused(sizes, *args)
    return local_general(sizes, *args)


def local_fused(
    sizes, hidden_in, output_grad, encoder_states, language_ids, source_index, bucket_ids, language_table,
    bucket_table, self_gain, self_query, self_key, self_value, self_out, cross_gain, cross_query, cross_key,
    cross_value, cross_out, feed_gain, inner_weight, outer_weight,
):
    kept = forward(
        sizes, hidden_in, output_grad, encoder_states, language_ids, source_index, bucket_ids, language_table,
        bucket_table, (self_gain, cross_gain, feed_gain),
        (self_query, self_key, self_value, self_out, cross_query, cross_key, cross_value, cross_out),
        inner_weight, outer_weight,
    )
    outs = backward(sizes, output_grad, encoder_states, language_ids, source_index, bucket_ids, kept)
    squares, inner, outer, language, bucket, gains = outs[3:11], outs[11], outs[12], outs[13], outs[14].T, outs[15:]
    return (
        *outs[:3], language, bucket, gains[0], *squares[:4], gains[1], *squares[4:], gains[2], inner, outer,
    )


def solution(mesh):
    sizes = (mesh.shape["dp"] // 2, mesh.shape["fsdp"] // 2)
    in_specs = (
        P(("dp", "fsdp"), None),
        P(("dp", "fsdp"), None),
        P(("dp", "fsdp"), None, None),
        P(("dp", "fsdp")),
        P(("dp", "fsdp")),
        P(),
        P(None, ("dp", "fsdp")),
        P(),
        P(("dp", "fsdp")),
        P(("dp", "fsdp"), None),
        P(("dp", "fsdp"), None),
        P(("dp", "fsdp"), None),
        P(("dp", "fsdp"), None),
        P(("dp", "fsdp")),
        P(("dp", "fsdp"), None),
        P(("dp", "fsdp"), None),
        P(("dp", "fsdp"), None),
        P(("dp", "fsdp"), None),
        P(("dp", "fsdp")),
        P(("dp", "fsdp"), None),
        P(("dp", "fsdp"), None),
    )
    out_specs = (
        P(("dp", "fsdp"), None),
        P(("dp", "fsdp"), None),
        P(("dp", "fsdp"), None, None),
        P(None, ("dp", "fsdp")),
        P(),
        P(("dp", "fsdp")),
        P(("dp", "fsdp"), None),
        P(("dp", "fsdp"), None),
        P(("dp", "fsdp"), None),
        P(("dp", "fsdp"), None),
        P(("dp", "fsdp")),
        P(("dp", "fsdp"), None),
        P(("dp", "fsdp"), None),
        P(("dp", "fsdp"), None),
        P(("dp", "fsdp"), None),
        P(("dp", "fsdp")),
        P(("dp", "fsdp"), None),
        P(("dp", "fsdp"), None),
    )
    return jax.shard_map(functools.partial(local, sizes), mesh=mesh, in_specs=in_specs, out_specs=out_specs, check_vma=False)
```

```python
import functools

import jax
import jax.numpy as jnp
from jax import lax
from jax.experimental import pallas as pl
from jax.experimental.pallas import tpu as pltpu
from jax.sharding import PartitionSpec as P

H = 12
HEAD = 64
SEQ_BLOCK = 2


EPSILON = 1e-06
PRECISE = lax.Precision.HIGHEST
NEGATIVE = -1e30


def to_low(value):
    return value.astype(jnp.bfloat16)


def norm_scale(hidden, gain):
    return hidden * lax.rsqrt(jnp.mean(hidden * hidden, axis=-1, keepdims=True) + EPSILON) * gain


def matmul(left, right):
    return jnp.dot(left, right, preferred_element_type=jnp.float32)


def left_product(left, right):
    return lax.dot_general(
        left, right, (((0,), (0,)), ((), ())), preferred_element_type=jnp.float32
    )


def right_product(left, right):
    return lax.dot_general(
        left, right, (((1,), (1,)), ((), ())), preferred_element_type=jnp.float32
    )


def split_heads(array):
    return array.reshape(array.shape[:-1] + (H, HEAD))


def score_block(queries, key_rows, offset):
    scores = jnp.einsum(
        "sqhe,skhe->shqk",
        split_heads(queries),
        split_heads(key_rows),
        preferred_element_type=jnp.float32,
    )
    return scores + offset


def attend_forward(queries, key_rows, value_rows, offset):
    scores = score_block(queries, key_rows, offset)
    top_score = jnp.max(scores, axis=-1, keepdims=True)
    log_total = top_score + jnp.log(jnp.sum(jnp.exp(scores - top_score), axis=-1, keepdims=True))
    weights = to_low(jnp.exp(scores - log_total))
    context = jnp.einsum(
        "shqk,skhe->sqhe", weights, split_heads(value_rows), preferred_element_type=jnp.float32
    )
    return (to_low(context).reshape(queries.shape), log_total)


def attend_backward(queries, key_rows, value_rows, offset, log_total, context_grad, with_bias):
    scores = score_block(queries, key_rows, offset)
    probs = jnp.exp(scores - log_total)
    weights = to_low(probs)
    grad_heads = split_heads(context_grad)
    value_grad = jnp.einsum(
        "shqk,sqhe->skhe", weights, grad_heads, preferred_element_type=jnp.float32
    )
    prob_grad = jnp.einsum(
        "sqhe,skhe->shqk", grad_heads, split_heads(value_rows), preferred_element_type=jnp.float32
    )
    score_grad = to_low(probs * (prob_grad - jnp.sum(probs * prob_grad, axis=-1, keepdims=True)))
    query_grad = jnp.einsum(
        "shqk,skhe->sqhe", score_grad, split_heads(key_rows), preferred_element_type=jnp.float32
    )
    key_grad = jnp.einsum(
        "shqk,sqhe->skhe", score_grad, split_heads(queries), preferred_element_type=jnp.float32
    )
    grads = (
        query_grad.reshape(queries.shape),
        key_grad.reshape(key_rows.shape),
        value_grad.reshape(value_rows.shape),
    )
    if with_bias:
        return grads + (jnp.sum(score_grad.astype(jnp.float32), axis=0),)
    return grads


MESH = pl.DeviceIdType.MESH
ALL = slice(None)


class Place:
    def __init__(self, sizes):
        self.ny, self.nz = sizes
        self.dp = lax.axis_index("dp")
        self.fs = lax.axis_index("fsdp")
        self.c, self.y = lax.rem(self.dp, 2), lax.div(self.dp, 2)
        self.x, self.z = lax.rem(self.fs, 2), lax.div(self.fs, 2)

    def size(self, dim):
        return {"c": 2, "x": 2, "y": self.ny, "z": self.nz}[dim]

    def at(self, dim):
        return {"c": self.c, "x": self.x, "y": self.y, "z": self.z}[dim]

    def device(self, dim, index):
        if dim == "c":
            return (self.y * 2 + index, self.fs)
        if dim == "y":
            return (index * 2 + self.c, self.fs)
        if dim == "x":
            return (self.dp, self.z * 2 + index)
        return (self.dp, index * 2 + self.x)


def neighbour_barrier(place, far=False):
    barrier = pltpu.get_barrier_semaphore()
    links = []
    for dim in "cxyz":
        here, size = place.at(dim), place.size(dim)
        reach = 1
        while reach < size and (reach == 1 or far):
            if size == 2:
                links.append((dim, 1 - here, None))
            elif reach == 1:
                for step in (1, -1):
                    links.append((dim, here + step, (here + step >= 0) & (here + step < size)))
            else:
                links.append((dim, here + reach - 2 * reach * lax.rem(lax.div(here, reach), 2), None))
            reach *= 2

    def signal(dim, there):
        pl.semaphore_signal(barrier, inc=1, device_id=place.device(dim, there), device_id_type=MESH)

    for dim, there, condition in links:
        if condition is None:
            signal(dim, there)
        else:
            pl.when(condition)(lambda dim=dim, there=there: signal(dim, there))
    peers = sum(1 if condition is None else condition.astype(jnp.int32) for _, _, condition in links)
    pl.semaphore_wait(barrier, peers)


PATHS = ("zxy", "zyx", "xzy", "yzx")


class Link:
    def __init__(self, copy, sends=None, receives=None):
        self.copy, self.sends, self.receives = copy, sends, receives

    @staticmethod
    def when(condition, run):
        if condition is None:
            run()
        else:
            pl.when(condition)(run)

    def start(self):
        self.when(self.sends, lambda: self.copy.start())

    def wait_send(self):
        self.when(self.sends, lambda: self.copy.wait_send())

    def wait_recv(self):
        self.when(self.receives, lambda: self.copy.wait_recv())


class Pool:
    def __init__(self, array, count):
        self.array, self.free, self.users = array, list(range(count)), []

    def take(self, user):
        if not self.free:
            self.users[0].release()
        self.users.append(user)
        return self.free.pop(0)

    def give(self, user, at):
        self.users.remove(user)
        self.free.append(at)

    def drain(self):
        while self.users:
            self.users[0].release()


class PooledLink(Link):
    def __init__(self, make, pool, sends=None, receives=None):
        self.make, self.pool, self.sends, self.receives = make, pool, sends, receives
        self.at = None

    def start(self):
        self.at = self.pool.take(self)
        copy = self.make(self.pool.array.at[self.at])
        self.when(self.sends, lambda: copy.start())

    def release(self):
        copy = self.make(self.pool.array.at[self.at])
        self.when(self.sends, lambda: copy.wait_send())
        self.pool.give(self, self.at)

    def wait_recv(self):
        copy = self.make(self.pool.array.at[0])
        self.when(self.receives, lambda: copy.wait_recv())


class PooledCopy:
    def __init__(self, pool, source, target):
        self.pool, self.done = pool, False
        self.at = pool.take(self)
        self.copy = pltpu.make_async_copy(source, target, pool.array.at[self.at])
        self.copy.start()

    def wait(self):
        if not self.done:
            self.copy.wait()
            self.done = True
            self.pool.give(self, self.at)

    release = wait


class Exchange:
    def __init__(self, place, pool, receive):
        self.place, self.pool, self.receive, self.count = place, pool, receive, 0

    def slot(self):
        self.count += 1
        return self.count - 1

    def link(self, source, target, dim, there, sends=None, receives=None, slot=None):
        slot = self.slot() if slot is None else slot
        device = self.place.device(dim, there)

        def make(send):
            return pltpu.make_async_remote_copy(
                source, target, send, self.receive.at[slot], device_id=device, device_id_type=MESH
            )

        return PooledLink(make, self.pool, sends, receives)


def pick(held, place, **fixed):
    return tuple(fixed.get(dim, ALL if dim in held else place.at(dim)) for dim in "yczx")


def gather_steps(place, blocks, path, sems):
    steps, slot, held = [], 0, ""
    for dim in path + "c":
        here, size = place.at(dim), place.size(dim)
        if size == 2:
            there = 1 - here
            index = pick(held, place)
            copy = pltpu.make_async_remote_copy(
                blocks(index), blocks(index), sems[0].at[slot], sems[1].at[slot],
                device_id=place.device(dim, there), device_id_type=MESH,
            )
            steps.append([Link(copy)])
            slot += 1
        else:
            for hop in range(1, size):
                links = []
                for way in (1, -1):
                    origin = here - way * (hop - 1)
                    there = here + way
                    source = here - way * hop
                    index = pick(held, place, **{dim: jnp.clip(origin, 0, size - 1)})
                    copy = pltpu.make_async_remote_copy(
                        blocks(index), blocks(index), sems[0].at[slot], sems[1].at[slot],
                        device_id=place.device(dim, jnp.clip(there, 0, size - 1)), device_id_type=MESH,
                    )
                    sends = (origin >= 0) & (origin < size) & (there >= 0) & (there < size)
                    links.append(Link(copy, sends, (source >= 0) & (source < size)))
                    slot += 1
                steps.append(links)
        held += dim
    return steps


def slot_count(sizes):
    ny, nz = sizes
    return 2 + (1 if ny == 2 else 2 * (ny - 1)) + (1 if nz == 2 else 2 * (nz - 1))


def run_steps(plans, lag):
    rounds = max(lag[i] + len(plan) for i, plan in enumerate(plans)) + 1
    for now in range(rounds):
        for offset, plan in zip(lag, plans):
            at = now - offset
            if 1 <= at <= len(plan):
                for link in plan[at - 1]:
                    link.wait_recv()
            if 0 <= at < len(plan):
                for link in plan[at]:
                    link.start()
    for plan in plans:
        for links in plan:
            for link in links:
                link.wait_send()


def gather_kernel(sizes, *refs):
    shards, wholes = refs[:11], refs[11:22]
    own_sem, send_sem, recv_sem = refs[22:]
    place = Place(sizes)
    own = (place.y, place.c, place.z, place.x)
    owns = [
        pltpu.make_async_copy(shard, whole.at[own], own_sem.at[i])
        for i, (shard, whole) in enumerate(zip(shards, wholes))
    ]
    for copy in owns:
        copy.start()
    neighbour_barrier(place)
    views = [lambda index, ref=ref: ref.at[index] for ref in wholes[:9]]
    width = wholes[8].shape[-1]
    for q in range(4):
        views.append(
            lambda index, q=q: wholes[9].at[index + (ALL, pl.ds(q * width, width))]
        )
    for q in range(4):
        views.append(lambda index, q=q: wholes[10].at[index + (q,)])
    plans, lag = [], []
    for i, view in enumerate(views):
        path = PATHS[0] if i == 0 else PATHS[(i - 1) % 4]
        plans.append(gather_steps(place, view, path, (send_sem.at[i], recv_sem.at[i])))
        lag.append(0 if i == 0 else 3 * ((i - 1) // 4))
    for copy in owns:
        copy.wait()
    run_steps(plans, lag)


def gather_weights(sizes, table, gains, squares, inner, outer):
    ny, nz = sizes
    grid = (ny, 2, nz, 2)
    part, width = squares[0].shape
    small = jnp.zeros((16, 128), table.dtype)
    small = small.at[: table.shape[0], :part].set(table)
    for i, gain in enumerate(gains):
        small = small.at[table.shape[0] + i, :part].set(gain)
    shards = (small,) + tuple(squares) + (inner, outer.reshape(4, part, width))
    anywhere = pl.BlockSpec(memory_space=pl.ANY)
    slots = slot_count(sizes)
    wholes = pl.pallas_call(
        functools.partial(gather_kernel, sizes),
        out_shape=[jax.ShapeDtypeStruct(grid + s.shape, s.dtype) for s in shards],
        in_specs=[anywhere] * 11,
        out_specs=[anywhere] * 11,
        scratch_shapes=[
            pltpu.SemaphoreType.DMA((11,)),
            pltpu.SemaphoreType.DMA((17, slots)),
            pltpu.SemaphoreType.DMA((17, slots)),
        ],
        compiler_params=pltpu.CompilerParams(collective_id=0, has_side_effects=True),
    )(*shards)
    count = ny * nz * 4
    tiny = wholes[0].reshape(count, 16, 128)[:, :, :part].transpose(1, 0, 2).reshape(16, count * part)
    rows = table.shape[0]
    return (
        (tiny[rows], tiny[rows + 1], tiny[rows + 2], tiny[:rows])
        + tuple(w.reshape(count * part, width) for w in wholes[1:9])
        + (wholes[9].reshape(count * part, 4 * width), wholes[10].reshape(4 * count * part, width))
    )


class Reduce:
    def __init__(self, place, path, source, total, core_in, boxes, out, sems):
        self.place, self.path, self.source, self.total = place, path, source, total
        self.core_in, self.boxes, self.out, self.sems = core_in, boxes, out, sems
        self.slot = 0
        self.sent = []

    def copy(self, source, target, dim, there):
        slot = self.slot
        self.slot += 1
        return pltpu.make_async_remote_copy(
            source, target, self.sems[0].at[slot], self.sems[1].at[slot],
            device_id=self.place.device(dim, there), device_id_type=MESH,
        )

    def index(self, fixed):
        return tuple(fixed.get(dim, ALL) for dim in "yzx")

    def add(self, target, box):
        shape = box.shape[:-2]
        count = 1
        for size in shape:
            count *= size
        free = [i for i, entry in enumerate(target) if entry is ALL]

        def body(n, _):
            spots, rest = [], n
            for size in reversed(shape):
                spots.append(lax.rem(rest, size))
                rest = lax.div(rest, size)
            spots = spots[::-1]
            full = list(target)
            for place_at, spot in zip(free, spots):
                full[place_at] = spot
            mine = self.total[tuple(full)].astype(jnp.float32)
            got = box[tuple(spots)].astype(jnp.float32)
            self.total[tuple(full)] = (mine + got).astype(jnp.bfloat16)
            return 0

        if count == 1:
            body(0, 0)
        else:
            lax.fori_loop(0, count, body, 0)

    def steps(self):
        place, listing = self.place, []
        own = pltpu.make_async_copy(self.source(place.c), self.total, self.sems[2])
        core = self.copy(self.source(1 - place.c), self.core_in, "c", 1 - place.c)

        def start():
            own.start()
            core.start()

        def finish():
            own.wait()
            core.wait_recv()
            self.add((ALL, ALL, ALL), self.core_in)

        self.sent.append(Link(core))
        listing.append((start, finish))
        fixed, box = {}, 0
        for dim in self.path:
            here, size = place.at(dim), place.size(dim)
            if size == 2:
                target = self.index({**fixed, dim: 1 - here})
                link = Link(self.copy(self.total.at[target], self.boxes[box], dim, 1 - here))
                self.sent.append(link)
                listing.append(self.pair([link], [(self.index({**fixed, dim: here}), box, None)]))
                box += 1
            else:
                for hop in range(size - 1, 0, -1):
                    links, adds = [], []
                    for way in (1, -1):
                        there = here - way
                        goal = here - way * hop
                        sends = (goal >= 0) & (goal < size)
                        source = here + way
                        got = source - way * hop
                        receives = (source >= 0) & (source < size) & (got >= 0) & (got < size)
                        target = self.index({**fixed, dim: jnp.clip(goal, 0, size - 1)})
                        copy = self.copy(
                            self.total.at[target], self.boxes[box], dim, jnp.clip(there, 0, size - 1)
                        )
                        link = Link(copy, sends, receives)
                        self.sent.append(link)
                        links.append(link)
                        adds.append((self.index({**fixed, dim: jnp.clip(got, 0, size - 1)}), box, receives))
                        box += 1
                    listing.append(self.pair(links, adds))
            fixed = {**fixed, dim: here}
        return listing

    def pair(self, links, adds):
        def start():
            for link in links:
                link.start()

        def finish():
            for link in links:
                link.wait_recv()
            for target, box, condition in adds:
                Link.when(condition, functools.partial(self.add, target, self.boxes[box]))

        return start, finish

    def close(self):
        own = (self.place.y, self.place.z, self.place.x)
        self.out(self.total[own].astype(jnp.float32))
        for link in self.sent:
            link.wait_send()


def box_shapes(sizes, path):
    ny, nz = sizes
    size = {"y": ny, "z": nz, "x": 2}
    left, shapes = "yzx", []
    for dim in path:
        left = left.replace(dim, "")
        lead = tuple(size[d] for d in left)
        shapes += [lead] * (1 if size[dim] == 2 else 2 * (size[dim] - 1))
    return shapes


BACK_PATHS = tuple(path[::-1] for path in PATHS)


def reduce_kernel(sizes, box_counts, *refs):
    sources, small_in = refs[:10], refs[10]
    outs, small_out = refs[11:21], refs[21]
    totals, core_boxes = refs[22], refs[23]
    at = 24
    boxes = []
    for count in box_counts:
        boxes.append(refs[at : at + count])
        at += count
    small_box, own_sem, send_sem, recv_sem, small_send, small_recv = refs[at:]
    place = Place(sizes)
    neighbour_barrier(place, far=True)
    width = outs[0].shape[-1]

    def square(ref):
        return lambda core: ref.at[:, core]

    def inner(q):
        return lambda core: sources[8].at[:, core, :, :, :, pl.ds(q * width, width)]

    def outer(q):
        return lambda core: sources[9].at[:, core, :, :, q]

    views = [inner(q) for q in range(4)] + [outer(q) for q in range(4)]
    views += [square(sources[i]) for i in (4, 5, 6, 7, 0, 1, 2, 3)]

    def store_square(i):
        def run(value):
            outs[i][...] = value

        return run

    def store_inner(q):
        def run(value):
            outs[8][:, q * width : (q + 1) * width] = value

        return run

    def store_outer(q):
        def run(value):
            outs[9][q] = value

        return run

    stores = [store_inner(q) for q in range(4)] + [store_outer(q) for q in range(4)]
    stores += [store_square(i) for i in (4, 5, 6, 7, 0, 1, 2, 3)]
    plans, lag = [], []
    reduces = []
    for m in range(16):
        group, kind = m // 4, m % 4
        reduce = Reduce(
            place, BACK_PATHS[kind], views[m], totals.at[m], core_boxes.at[m],
            [box.at[group] for box in boxes[kind]], stores[m],
            (send_sem.at[m], recv_sem.at[m], own_sem.at[m]),
        )
        reduces.append(reduce)
        plans.append(reduce.steps())
        lag.append(3 * group)
    small_out[...] = small_in[...]
    small = []
    moves = [("c", 1 - place.c), ("x", 1 - place.x), ("y", None), ("z", None)]
    for dim, there in moves:
        size, here, reach = place.size(dim), place.at(dim), 1
        while reach < size:
            partner = here + reach - 2 * reach * lax.rem(lax.div(here, reach), 2)
            small.append((dim, partner))
            reach *= 2
    rounds = max(max(lag[i] + len(plan) for i, plan in enumerate(plans)) + 1, len(small) + 1)
    copies = []
    for now in range(rounds):
        for offset, plan in zip(lag, plans):
            step = now - offset
            if 1 <= step <= len(plan):
                plan[step - 1][1]()
            if 0 <= step < len(plan):
                plan[step][0]()
        if 1 <= now <= len(small):
            copies[-1].wait()
            small_out[...] += small_box[now - 1]
        if now < len(small):
            dim, partner = small[now]
            copies.append(
                pltpu.make_async_remote_copy(
                    small_out, small_box.at[now], small_send.at[now], small_recv.at[now],
                    device_id=place.device(dim, partner), device_id_type=MESH,
                )
            )
            copies[-1].start()
    for reduce in reduces:
        reduce.close()


def reduce_grads(sizes, language, bucket, gains, squares, inner, outer):
    ny, nz = sizes
    grid = (ny, 2, nz, 2)
    count = ny * nz * 4
    width = squares[0].shape[1]
    part = squares[0].shape[0] // count
    langs = language.shape[0]
    flat = jnp.zeros((width,), jnp.float32).at[: bucket.size].set(bucket.reshape(-1))
    small = jnp.concatenate(
        [language] + [g.reshape(1, width) for g in gains] + [flat[None], jnp.zeros((4, width), jnp.float32)], axis=0
    )
    sources = [to_low(s).reshape(grid + (part, width)) for s in squares]
    sources += [
        to_low(inner).reshape(grid + (part, 4 * width)),
        to_low(outer).reshape(grid + (4, part, width)),
    ]
    anywhere = pl.BlockSpec(memory_space=pl.ANY)
    vmem = pl.BlockSpec(memory_space=pltpu.VMEM)
    shapes = [(part, width)] * 8 + [(part, 4 * width), (4, part, width), small.shape]
    lead = [box_shapes(sizes, path) for path in BACK_PATHS]
    slots = slot_count(sizes)
    hops = (ny * nz * 4).bit_length() - 1
    outs = pl.pallas_call(
        functools.partial(reduce_kernel, sizes, tuple(len(s) for s in lead)),
        out_shape=[jax.ShapeDtypeStruct(s, jnp.float32) for s in shapes],
        in_specs=[anywhere] * 10 + [vmem],
        out_specs=[vmem] * 11,
        scratch_shapes=[
            pltpu.VMEM((16, ny, nz, 2, part, width), jnp.bfloat16),
            pltpu.VMEM((16, ny, nz, 2, part, width), jnp.bfloat16),
        ]
        + [pltpu.VMEM((4,) + s + (part, width), jnp.bfloat16) for one in lead for s in one]
        + [
            pltpu.VMEM((hops,) + small.shape, jnp.float32),
            pltpu.SemaphoreType.DMA((16,)),
            pltpu.SemaphoreType.DMA((16, slots)),
            pltpu.SemaphoreType.DMA((16, slots)),
            pltpu.SemaphoreType.DMA((hops,)),
            pltpu.SemaphoreType.DMA((hops,)),
        ],
        compiler_params=pltpu.CompilerParams(
            collective_id=1, has_side_effects=True, vmem_limit_bytes=60 * 1024 * 1024
        ),
    )(*sources, small)
    start = (lax.axis_index("dp") * nz * 2 + lax.axis_index("fsdp")) * part
    total = outs[10]
    mine = lax.dynamic_slice(total, (0, start), (langs + 3, part))
    return (
        mine[:langs],
        total[langs + 3, : bucket.size].reshape(bucket.shape),
        mine[langs], mine[langs + 1], mine[langs + 2],
        outs[:8], outs[8], outs[9].reshape(4 * part, width),
    )


FORWARD_PATHS = (
    "zxy", "yzx", "zxy", "zyx", "zyx", "xzy", "zxy", "zxy", "zyx", "xyz", "zyx", "yxz", "zxy", "zxy", "zyx",
    "zyx", "xyz",
)
FORWARD_ORDER = (
    2, 11, 0, 9, 3, 1, 5, 16, 4, 2, 9, 3, 11, 0, 6, 16, 2, 5, 3, 1, 2, "b0", 4, 7, 0, 3, 1, 5, 0, 4, 13, 8, 6,
    2, "b1", 7, 3, 1, 4, 12, 6, 0, 10, "b2", 5, 1, 14, 6, 8, 3, 7, 2, 0, 10, 0, 1, 14, 12, 5, 9, 8, 2, 3, 13, 7,
    "b3", 4, 5, 12, "open", 6, 11, "k", 1, "q", "v", 5, 8, 15, 7, "sa0", 12, 10, 4, "sa1", 9, 6, "sa2", 8,
    "sa3", 14, 4, "se0", "se1", 9, 13, 10, 6, 7, 16, "K", "cq", 14, 15, 7, 12, "V", 11, "ca0", 8, 9, 10, 13,
    "ca1", 15, "ca2", "ca3", 10, 11, 16, 9, 8, 15, 14, "ce0", "ce1", "in0", 13, 12, "og0", 11, 10, "in1", 16,
    12, 15, "og1", 14, 13, 11, "in2", 16, "in3", 15, 14, "og3", 13, "og2", 16, 15,
)
BACKWARD_PATHS = (
    "xzy", "yzx", "yxz", "xyz", "xzy", "xyz", "yxz", "yzx", "yzx", "yxz", "xyz", "xzy", "xyz", "xzy", "yzx",
    "yxz",
)
BACKWARD_ORDER = (
    3, "x0", 2, "in0", 0, 4, 3, "t0", 2, "x1", 0, "in1", 1, 3, "t1", "x2", 0, 1, 5, 4, "in2", 2, "t2", 6, "x3",
    3, "in3", 1, 0, "t3", 7, 4, 6, "n3", 5, "co", 1, "ccg", 2, 7, 0, "ca0", 6, "ca1", "ca2", "ca3", 4, 8, 7, 1,
    "ca4", "ca5", 5, "cv", 11, "cq", 7, 9, "ck", 10, 11, 4, 8, "n2a", 1, 9, "n2", 10, 6, 3, "so", 5, 8, 2,
    "scg", 12, 0, 11, "sa0", 9, 5, "sa1", 6, 10, 2, 8, "sa2", 3, 4, "k", 7, 14, "v", 11, 15, "cp0", "q", 3, 14,
    12, 13, 5, 2, "cp1", 9, 10, 15, 1, "bk0", 13, 11, "bk1", 9, 4, 0, 14, 7, "bk2", 10, 12, 6, "cp2", "cl1", 13,
    "bk3", 15, 14, "bk4", 8, "bk5", 16, 12, "h0", 5, 7, 16, 6, 13, "h1", 9, "h2", 12, "h3", 15, 16, 14, "e0k",
    13, 9, "e0v", 16, 15, 10, 11, 12, "e1k", 13, 14, 8, 11, 16, 15, "e1v", 13, 8, 10, 12, 15, 14, 16,
)


LOW = jnp.bfloat16
FULL = jnp.float32
PAIR = 2 * HEAD


def nt_dot(left, right):
    return lax.dot_general(left, right, (((1,), (1,)), ((), ())), preferred_element_type=FULL)


def tn_dot(left, right):
    return lax.dot_general(left, right, (((0,), (0,)), ((), ())), preferred_element_type=FULL)


def flat(ref, *suffix):
    value = ref[(ALL,) * (len(ref.shape) - 1) + suffix] if suffix else ref[...]
    rows = 1
    for size in value.shape[:-1]:
        rows *= size
    return value.reshape(rows, value.shape[-1])


def each(count, body):
    def run(i, _):
        body(pl.ds(pl.multiple_of(i * 128, 128), 128))
        return 0

    lax.fori_loop(0, count, run, 0)


def unit_rows(hidden):
    return hidden * lax.rsqrt(jnp.mean(hidden * hidden, axis=-1, keepdims=True) + EPSILON)


def spread_small(tiny, table):
    part = table.shape[1] // (tiny.shape[0] * tiny.shape[2] * 4)
    table[...] = jnp.zeros_like(table)
    lane = lax.broadcasted_iota(jnp.int32, (16, 128), 1)
    at = 0
    for y in range(tiny.shape[0]):
        for core in range(2):
            for z in range(tiny.shape[2]):
                for x in range(2):
                    slab = jnp.where(lane < part, tiny[y, core, z, x], 0.0)
                    base, shift = at // 128 * 128, at % 128
                    if shift:
                        slab = pltpu.roll(slab, shift, 1)
                    if shift + part <= 128:
                        table[:, base : base + 128] += slab
                    else:
                        table[:, base : base + 128] += jnp.where(lane >= part, slab, 0.0)
                        table[:, base + 128 : base + 256] += jnp.where(lane < part, slab, 0.0)
                    at += part


def build_bias(ids, values, bias, heads):
    keys, queries = bias.shape[1:]
    rows = 64

    def block(n, _):
        at = pl.ds(pl.multiple_of(n * rows, rows), rows)
        bucket = ids[at, :]
        bits = [lax.bitwise_and(bucket, 1 << b) != 0 for b in range(5)]
        key = n * rows + lax.broadcasted_iota(jnp.int32, (rows, queries), 0)
        query = lax.broadcasted_iota(jnp.int32, (rows, queries), 1)
        hidden = key > query

        def head(h, _):
            level = [values[16 + h, c] for c in range(32)]
            for bit in bits:
                level = [jnp.where(bit, level[i + 1], level[i]) for i in range(0, len(level), 2)]
            bias[h, at, :] = jnp.where(hidden, NEGATIVE, level[0]).astype(LOW)
            return 0

        return lax.fori_loop(*heads, head, 0)

    lax.fori_loop(0, keys // rows, block, 0)


def head_pair(value):
    lane = lax.broadcasted_iota(jnp.int32, value.shape, 1)
    zero = jnp.zeros_like(value)
    return jnp.concatenate([jnp.where(lane < HEAD, value, zero), jnp.where(lane < HEAD, zero, value)], axis=0)


def pairs_forward(items):
    scores = [nt_dot(keys, head_pair(queries)) for queries, keys, _, _ in items]
    scores = [s if item[3] is None else s + item[3] for s, item in zip(scores, items)]
    grown = [jnp.exp(s - jnp.max(s, axis=0, keepdims=True)) for s in scores]
    rows = [1.0 / jnp.sum(g, axis=0, keepdims=True) for g in grown]
    weights = [g.astype(LOW) for g in grown]
    results = []
    for (queries, _, values, _), low, row in zip(items, weights, rows):
        count = queries.shape[0]
        lane = lax.broadcasted_iota(jnp.int32, values.shape, 1)
        one = jnp.ones_like(values)
        first = tn_dot(low[:, :count], jnp.where(lane < HEAD, values, one))
        second = tn_dot(low[:, count:], jnp.where(lane < HEAD, one, values))
        lane = lax.broadcasted_iota(jnp.int32, first.shape, 1)
        inverse = 1.0 / pltpu.roll(jnp.where(lane < HEAD, second, first), HEAD, 1)
        results.append((jnp.where(lane < HEAD, first, second) * inverse, inverse, low, row))
    return results


def gelu_parts(u):
    a, b = 0.7978845608028654, 0.044715
    square = u * u
    t = jnp.tanh(a * u * (1.0 + b * square))
    half = 0.5 * (1.0 + t)
    slope = half + 0.5 * u * (1.0 - t * t) * (a * (1.0 + 3.0 * b * square))
    return u * half, slope


def gather_plans(place, wholes, small, exchange):
    views = [lambda index, ref=ref: ref.at[index] for ref in [small] + list(wholes[:8])]
    width = wholes[0].shape[-1]
    for q in range(4):
        views.append(lambda index, q=q: wholes[8].at[index + (ALL, pl.ds(q * width, width))])
    for q in range(4):
        views.append(lambda index, q=q: wholes[9].at[index + (q,)])
    return [gather_early(place, view, path, exchange) for view, path in zip(views, FORWARD_PATHS)]


def gather_early(place, blocks, path, exchange):
    steps = []
    at = {dim: place.at(dim) for dim in "yczx"}

    def link(dim, there, where, sends=None, receives=None, slot=None):
        view = blocks(tuple(where.get(d, at[d]) for d in "yczx"))
        return exchange.link(view, view, dim, there, sends, receives, slot)

    def swap(dim, where):
        return link(dim, 1 - at[dim], where)

    def slots(hop):
        first = exchange.slot()
        return first, first if 2 * hop >= place.nz else exchange.slot()

    def hops(hop, where):
        here, size, links = at["z"], place.nz, []
        for way, slot in zip((1, -1), slots(hop)):
            origin, there, source = here - way * (hop - 1), here + way, here - way * hop
            sends = (origin >= 0) & (origin < size) & (there >= 0) & (there < size)
            receives = (source >= 0) & (source < size)
            spot = {**where, "z": jnp.clip(origin, 0, size - 1)}
            links.append(link("z", jnp.clip(there, 0, size - 1), spot, sends, receives, slot))
        return links

    def swap_arrived(dim, hop, where):
        here, size, links = at["z"], place.nz, []
        for way, slot in zip((1, -1), slots(hop)):
            source = here - way * hop
            here_now = (source >= 0) & (source < size)
            spot = {**where, "z": jnp.clip(source, 0, size - 1)}
            links.append(link(dim, 1 - at[dim], spot, here_now, here_now, slot))
        return links

    last = path[2]
    if last == "z":
        first, second = path[0], path[1]
        steps = [[swap(first, {})], [swap(second, {first: ALL})]]
        steps += [hops(hop, {first: ALL, second: ALL}) for hop in range(1, place.nz)]
        steps.append([swap("c", {"y": ALL, "z": ALL, "x": ALL})])
        return steps
    if path[0] == "z":
        first = path[1]
        steps = [hops(hop, {}) for hop in range(1, place.nz)]
        steps.append([swap(first, {"z": ALL}), swap(last, {"z": ALL})])
        steps.append([swap(last, {"z": ALL, first: 1 - at[first]})])
    else:
        first = path[0]
        steps.append([swap(first, {})])
        steps.append(hops(1, {first: ALL}) + [swap(last, {first: ALL})])
        for hop in range(2, place.nz):
            steps.append(hops(hop, {first: ALL}) + swap_arrived(last, hop - 1, {first: ALL}))
        steps.append(swap_arrived(last, place.nz - 1, {first: ALL}))
    steps[-1].append(swap("c", {"z": ALL, first: ALL}))
    steps.append([swap("c", {"z": ALL, first: ALL, last: 1 - at[last]})])
    return steps


def run_order(order, plans, tasks, done):
    at = [0] * len(plans)
    for entry in order:
        if isinstance(entry, str):
            tasks[entry]()
            continue
        step, plan = at[entry], plans[entry]
        at[entry] += 1
        if step >= 1:
            for link in plan[step - 1]:
                link.wait_recv()
        if step < len(plan):
            for link in plan[step]:
                link.start()
        else:
            done(entry)


SAVED = (
    "first_norm", "queries", "keys", "values", "self_context", "second_norm", "cross_queries",
    "source_keys", "source_values", "cross_context", "third_norm", "activated", "slope",
    "start", "mid", "late", "self_inverse", "cross_inverse", "self_rows", "cross_rows", "table",
)


def saved_shapes(tokens, sources, width, length):
    low, full = LOW, FULL
    row = (tokens, width)
    pairs = tokens // length * (width // PAIR)
    shapes = {name: (row, low) for name in SAVED}
    shapes["source_keys"] = shapes["source_values"] = ((2, sources // 2, width), low)
    shapes["activated"] = shapes["slope"] = ((4,) + row, low)
    for name in ("start", "mid", "late", "self_inverse", "cross_inverse"):
        shapes[name] = (row, full)
    shapes["self_rows"] = shapes["cross_rows"] = ((pairs, 1, 2 * length), full)
    shapes["table"] = ((16, width), full)
    return shapes


def forward_kernel(sizes, *refs):
    n = len(SAVED)
    small_shard, shards = refs[0], refs[1:11]
    hidden_in, upstream_in, encoder_in, languages, sources, ids, slab_values = refs[11:18]
    outer_grads, whole_outs = refs[18], refs[19:29]
    self_weights, cross_weights = refs[29:31]
    saved_outs = dict(zip(SAVED, refs[31 : 31 + n]))
    at = 31 + n
    tiny, wholes = refs[at], refs[at + 1 : at + 11]
    at += 11
    v = dict(zip(SAVED, refs[at : at + n]))
    at += n
    bias, stage, outer_blocks, hidden, upstream, encoder, ids_across = refs[at : at + 7]
    send_sem, recv_sem, copy_sem = refs[at + 7 :]
    tokens, width = hidden.shape
    length = ids.shape[0]
    per_seq = width // PAIR
    seqs = tokens // length
    enc_length = encoder.shape[0] // 2
    blocks = tokens // 128

    place = Place(sizes)
    own = (place.y, place.c, place.z, place.x)
    moving = Pool(copy_sem, copy_sem.shape[0])
    sending = Pool(send_sem, send_sem.shape[0])
    owns = [
        PooledCopy(moving, shard, whole.at[own])
        for shard, whole in zip((small_shard.at[pl.ds(0, 16)],) + shards, (tiny,) + wholes)
    ]
    inputs = [
        PooledCopy(moving, source, target)
        for source, target in ((hidden_in, hidden), (encoder_in, encoder), (upstream_in, upstream))
    ]
    neighbour_barrier(place)
    plans = gather_plans(place, wholes, tiny, Exchange(place, sending, recv_sem))
    for copy in owns:
        copy.wait()

    def keep(name):
        PooledCopy(moving, v[name], saved_outs[name])

    def keep_whole(m):
        if m == 0:
            return
        if m < 9:
            source, target = wholes[m - 1], whole_outs[m - 1]
        elif m < 13:
            index = (ALL,) * 5 + (pl.ds((m - 9) * width, width),)
            source, target = wholes[8].at[index], whole_outs[8].at[index]
        else:
            index = (ALL,) * 4 + (m - 13,)
            source, target = wholes[9].at[index], whole_outs[9].at[index]
        PooledCopy(moving, source, target)

    def opening():
        inputs.pop(0).wait()
        spread_small(tiny, v["table"])
        for s in range(seqs):
            row = jnp.zeros((1, width), FULL)
            for l in range(8):
                row = row + jnp.where(languages[s] == l, v["table"][l : l + 1, :], 0.0)

            def body(at):
                start = hidden[at, :].astype(FULL) + row
                v["start"][at, :] = start
                v["first_norm"][at, :] = (unit_rows(start) * v["table"][8:9, :]).astype(LOW)

            def run(i, _):
                body(pl.ds(pl.multiple_of(s * length + i * 128, 128), 128))
                return 0

            lax.fori_loop(0, length // 128, run, 0)
        keep("table")
        keep("start")
        keep("first_norm")

    def project(source, weight, target):
        target[...] = jnp.dot(source[...], flat(weight), preferred_element_type=FULL).astype(LOW)

    leaving = {}

    def attention(turn, queries, keys, values, context, inverse, rows, weights_out, seq, first, last, picked):
        row_at = pl.ds(seq * length, length)
        key_rows = length if picked is None else enc_length
        items = []
        for p in range(first, last):
            lanes = pl.ds(p * PAIR, PAIR)
            if picked is not None:
                items.append((queries[row_at, lanes], keys[picked, :, lanes], values[picked, :, lanes], None))
            else:
                offset = jnp.concatenate([bias[2 * p], bias[2 * p + 1]], axis=1).astype(FULL)
                items.append((queries[row_at, lanes], keys[row_at, lanes], values[row_at, lanes], offset))
        for n, (out, total, low, row) in enumerate(pairs_forward(items)):
            lanes = pl.ds((first + n) * PAIR, PAIR)
            index = seq * per_seq + first + n
            slot = turn % 2 * (last - first) + n
            if slot in leaving:
                leaving[slot].wait()
            part = stage.at[slot, pl.ds(0, key_rows)]
            part[...] = low
            rows[index] = row
            context[row_at, lanes] = out.astype(LOW)
            inverse[row_at, lanes] = total
            leaving[slot] = PooledCopy(moving, part, weights_out.at[index])

    def residual(half, context, weight, before, after, gain_row, norm):
        at = pl.ds(half * (tokens // 2), tokens // 2)
        state = before[at, :] + jnp.dot(context[at, :], flat(weight), preferred_element_type=FULL)
        after[at, :] = state
        norm[at, :] = (unit_rows(state) * v["table"][gain_row : gain_row + 1, :]).astype(LOW)

    def self_projection(i, name):
        project(v["first_norm"], wholes[i], v[name])
        keep(name)

    def self_attention(turn, s, first, last):
        attention(
            turn, v["queries"], v["keys"], v["values"], v["self_context"], v["self_inverse"], v["self_rows"],
            self_weights, s, first, last, None,
        )

    def self_end(half):
        if half == 0:
            for name in ("self_context", "self_inverse", "self_rows"):
                keep(name)
        residual(half, v["self_context"], wholes[3], v["start"], v["mid"], 9, v["second_norm"])
        if half:
            keep("mid")
            keep("second_norm")

    def cross_source(i, name):
        if len(inputs) == 2:
            inputs.pop(0).wait()
        for half in range(2):
            v[name][half] = jnp.dot(
                encoder[pl.ds(half * enc_length, enc_length), :], flat(wholes[i]), preferred_element_type=FULL
            ).astype(LOW)
        keep(name)

    def cross_projection():
        project(v["second_norm"], wholes[4], v["cross_queries"])
        keep("cross_queries")

    def cross_attention(turn, s, first, last):
        attention(
            turn, v["cross_queries"], v["source_keys"], v["source_values"], v["cross_context"], v["cross_inverse"],
            v["cross_rows"], cross_weights, s, first, last, sources[s],
        )

    def cross_end(half):
        if half == 0:
            for name in ("cross_context", "cross_inverse", "cross_rows"):
                keep(name)
        residual(half, v["cross_context"], wholes[7], v["mid"], v["late"], 10, v["third_norm"])
        if half:
            keep("late")
            keep("third_norm")

    def feed_inner(q):
        weight = flat(wholes[8], pl.ds(q * width, width))
        for half in range(2):
            at = pl.ds(half * tokens // 2, tokens // 2)
            expanded = jnp.dot(v["third_norm"][at, :], weight, preferred_element_type=FULL)
            value, slope = gelu_parts(expanded)
            v["activated"][q, at, :] = value.astype(LOW)
            v["slope"][q, at, :] = slope.astype(LOW)
        for name in ("activated", "slope"):
            PooledCopy(moving, v[name].at[q], saved_outs[name].at[q])

    def bias_values(turn):
        if turn == 0:
            ids_across[...] = ids[...].astype(FULL).T.astype(jnp.int32)
        build_bias(ids_across, slab_values, bias, (3 * turn, 3 * turn + 3))

    def outer_grad(q):
        if inputs:
            inputs.pop(0).wait()
        value = tn_dot(v["activated"][q], upstream[...])
        outer_blocks[q // 2, q % 2] = value.reshape(outer_blocks.shape[2:]).astype(LOW)
        chunk = q // 2, q % 2
        PooledCopy(moving, outer_blocks.at[chunk], outer_grads.at[chunk])

    tasks = {"open": opening, "cq": cross_projection}
    for half in range(2):
        tasks[f"se{half}"] = functools.partial(self_end, half)
        tasks[f"ce{half}"] = functools.partial(cross_end, half)
    for i, (task, name) in enumerate((("q", "queries"), ("k", "keys"), ("v", "values"))):
        tasks[task] = functools.partial(self_projection, i, name)
    for i in range(4):
        first = per_seq // 2 * (i % 2)
        tasks[f"sa{i}"] = functools.partial(self_attention, i, i // 2, first, first + per_seq // 2)
        tasks[f"ca{i}"] = functools.partial(cross_attention, i, i // 2, first, first + per_seq // 2)
        tasks[f"in{i}"] = functools.partial(feed_inner, i)
        tasks[f"b{i}"] = functools.partial(bias_values, i)
        tasks[f"og{i}"] = functools.partial(outer_grad, i)
    tasks["K"] = functools.partial(cross_source, 5, "source_keys")
    tasks["V"] = functools.partial(cross_source, 6, "source_values")
    run_order(FORWARD_ORDER, plans, tasks, keep_whole)
    sending.drain()
    moving.drain()


RECEIVES = {"xyz": 7, "yxz": 7, "zxy": 9, "zyx": 9, "xzy": 12, "yzx": 12}


def small_slab(table, gains, bucket_table):
    part = table.shape[1]
    own = jnp.concatenate([table] + [g.reshape(1, part) for g in gains], axis=0).astype(FULL)
    buckets = bucket_table.T.astype(FULL)
    own = jnp.pad(own, ((0, 32 - own.shape[0]), (0, 128 - part)))
    heads, count = buckets.shape
    return own + jnp.pad(buckets, ((16, 16 - heads), (0, 128 - count)))


def forward(
    sizes, hidden_in, output_grad, encoder_states, language_ids, source_index, bucket_ids, language_table, bucket_table, gains,
    squares, inner, outer,
):
    ny, nz = sizes
    grid = (ny, 2, nz, 2)
    part, width = squares[0].shape
    tokens = hidden_in.shape[0]
    length = bucket_ids.shape[0]
    encoder = encoder_states.reshape(-1, width)
    enc_length = encoder_states.shape[1]
    slab = small_slab(language_table, gains, bucket_table)
    shards = [slab] + list(squares) + [inner, outer.reshape(4, part, width)]
    wholes = [jax.ShapeDtypeStruct(grid + s.shape, s.dtype) for s in shards]
    wholes[0] = jax.ShapeDtypeStruct(grid + (16, 128), FULL)
    shapes = saved_shapes(tokens, encoder.shape[0], width, length)
    pairs = tokens // length * (width // PAIR)
    anywhere = pl.BlockSpec(memory_space=pl.ANY)
    vmem = pl.BlockSpec(memory_space=pltpu.VMEM)
    smem = pl.BlockSpec(memory_space=pltpu.SMEM)
    out_shape = [wholes[10]] + wholes[1:]
    out_shape += [jax.ShapeDtypeStruct((pairs, rows, 2 * length), LOW) for rows in (length, enc_length)]
    out_shape += [jax.ShapeDtypeStruct(*shapes[name]) for name in SAVED]
    outs = pl.pallas_call(
        functools.partial(forward_kernel, sizes),
        out_shape=out_shape,
        in_specs=[anywhere] * 11 + [anywhere] * 3 + [smem, smem, vmem, smem],
        out_specs=[anywhere] * len(out_shape),
        scratch_shapes=[pltpu.VMEM(w.shape, w.dtype) for w in wholes]
        + [pltpu.VMEM(*shapes[name]) for name in SAVED]
        + [
            pltpu.VMEM((H, length, length), LOW),
            pltpu.VMEM((6, enc_length, 2 * length), LOW),
            pltpu.VMEM(wholes[10].shape, LOW),
            pltpu.VMEM((tokens, width), LOW),
            pltpu.VMEM((tokens, width), LOW),
            pltpu.VMEM(encoder.shape, LOW),
            pltpu.VMEM((length, length), jnp.int32),
            pltpu.SemaphoreType.DMA((48,)),
            pltpu.SemaphoreType.DMA((sum(RECEIVES[path] for path in FORWARD_PATHS),)),
            pltpu.SemaphoreType.DMA((28,)),
        ],
        compiler_params=pltpu.CompilerParams(
            collective_id=2, has_side_effects=True, vmem_limit_bytes=62 * 1024 * 1024
        ),
    )(
        *shards, hidden_in, output_grad, encoder, language_ids, source_index, bucket_ids, slab,
    )
    return outs


class Summed:
    def __init__(self, place, path, blocks, leaving, core_in, boxes, exchange):
        self.blocks, self.stages = blocks, []
        c = place.c
        core = exchange.link(leaving(1 - c), core_in, "c", 1 - c)
        self.stages.append(([core], [((ALL, c, ALL, ALL), core_in, None)]))
        self.box, self.boxes, self.exchange, self.place = 0, boxes, exchange, place
        first, last = path[0], path[2]
        fixed = {"c": c}
        if last == "z":
            second = path[1]
            self.stages.append(self.join(self.swap(first, {**fixed, second: 1 - place.at(second)})))
            fixed[first] = place.at(first)
            here = self.swap(first, {"c": c, second: place.at(second)})
            self.stages.append(self.join(self.swap(second, fixed), here))
            fixed[second] = place.at(second)
            for hop in range(place.nz - 1, 0, -1):
                self.stages.append(self.join(self.hops(hop, fixed)))
        else:
            after = {**fixed, first: place.at(first)}
            self.stages.append(self.join(self.swap_goals(first, place.nz - 1, fixed)))
            for hop in range(place.nz - 1, 1, -1):
                self.stages.append(self.join(self.hops(hop, after), self.swap_goals(first, hop - 1, fixed)))
            own = self.swap(first, {**fixed, "z": place.z})
            self.stages.append(self.join(self.hops(1, after), own))
            self.stages.append(self.join(self.swap(last, {**after, "z": place.z})))
        fixed = {"c": c, "y": place.y, "z": place.z, "x": place.x}
        self.own = self.index(fixed)

    def index(self, fixed):
        return tuple(fixed.get(dim, ALL) for dim in "yczx")

    @staticmethod
    def join(*parts):
        return [link for part in parts for link, _ in part], [add for part in parts for _, add in part]

    def next_box(self):
        self.box += 1
        return self.boxes[self.box - 1]

    def swap(self, dim, where):
        box, here = self.next_box(), self.place.at(dim)
        link = self.exchange.link(self.blocks(self.index({**where, dim: 1 - here})), box, dim, 1 - here)
        return [(link, (self.index({**where, dim: here}), box, None))]

    def swap_goals(self, dim, hop, where):
        pairs, here = [], self.place.at(dim)
        first = self.exchange.slot()
        second = first if 2 * hop >= self.place.nz else self.exchange.slot()
        for way, slot in ((1, first), (-1, second)):
            goal = self.place.z - way * hop
            there = (goal >= 0) & (goal < self.place.nz)
            spot = {**where, "z": jnp.clip(goal, 0, self.place.nz - 1)}
            box = self.next_box()
            source = self.blocks(self.index({**spot, dim: 1 - here}))
            link = self.exchange.link(source, box, dim, 1 - here, there, there, slot)
            pairs.append((link, (self.index({**spot, dim: here}), box, there)))
        return pairs

    def hops(self, hop, where):
        pairs, here, size = [], self.place.z, self.place.nz
        first = self.exchange.slot()
        second = first if 2 * hop > size + 1 else self.exchange.slot()
        for way, slot in ((1, first), (-1, second)):
            there, goal = here - way, here - way * hop
            sends = (goal >= 0) & (goal < size)
            source = here + way
            got = source - way * hop
            receives = (source >= 0) & (source < size) & (got >= 0) & (got < size)
            box = self.next_box()
            view = self.blocks(self.index({**where, "z": jnp.clip(goal, 0, size - 1)}))
            link = self.exchange.link(view, box, "z", jnp.clip(there, 0, size - 1), sends, receives, slot)
            pairs.append((link, (self.index({**where, "z": jnp.clip(got, 0, size - 1)}), box, receives)))
        return pairs

    def start(self, step):
        for link in self.stages[step][0]:
            link.start()

    def finish(self, step):
        links, adds = self.stages[step]
        for link in links:
            link.wait_recv()

        def add(target, box):
            view = self.blocks(target)
            view[...] = view[...] + box[...]

        for target, box, condition in adds:
            Link.when(condition, functools.partial(add, target, box))


def sum_boxes(sizes, path):
    size = {"y": sizes[0], "z": sizes[1], "x": 2}
    hops = 2 * (size["z"] - 1)
    if path[2] == "z":
        return [(size["z"],)] * 3 + [()] * hops, 9
    wide = (size[path[2]],)
    steps = [wide, wide]
    shapes = steps[:]
    for _ in range(size["z"] - 2):
        shapes += [wide] * 4
    return shapes + [wide] * 3 + [()], 12


def pairs_backward(items):
    stacked = [head_pair(item[4]) for item in items]
    prob_grads = [nt_dot(item[3], grads) for item, grads in zip(items, stacked)]
    value_parts = [jnp.dot(item[0], grads, preferred_element_type=FULL) for item, grads in zip(items, stacked)]
    scaled = [item[0].astype(FULL) * grads for item, grads in zip(items, prob_grads)]
    centres = [jnp.sum(s, axis=0, keepdims=True) * item[5] for s, item in zip(scaled, items)]
    score_grads = [(s - item[0].astype(FULL) * c).astype(LOW) for s, c, item in zip(scaled, centres, items)]
    key_parts = [jnp.dot(s, head_pair(item[1]), preferred_element_type=FULL) for s, item in zip(score_grads, items)]
    results = []
    for item, value_part, key_part, score_grad in zip(items, value_parts, key_parts, score_grads):
        count = item[1].shape[0]
        lane = lax.broadcasted_iota(jnp.int32, (count, PAIR), 1)
        first, second = tn_dot(score_grad[:, :count], item[2]), tn_dot(score_grad[:, count:], item[2])
        results.append((jnp.where(lane < HEAD, first, second), key_part, value_part, score_grad))
    return results


def backward_kernel(sizes, box_counts, *refs):
    n = len(SAVED)
    grads, encoder, languages, sources, ids_in, outer_grads = refs[:6]
    wholes = refs[6:16]
    self_weights, cross_weights = refs[16:18]
    saved = dict(zip(SAVED, refs[18 : 18 + n]))
    at = 18 + n
    hidden_out, hidden_grad, encoder_grad, small_out, packed_out = refs[at : at + 5]
    at += 5
    squares, outers, core_boxes = refs[at : at + 3]
    at += 3
    boxes = []
    for count in box_counts:
        boxes.append(refs[at : at + count])
        at += count
    small_box, pool, pairs_in, run_a, run_b, run_c, w, wo, stage, score_sum, bucket_rows, table, self_rows, cross_rows, ids, packed = refs[at : at + 16]
    send_sem, recv_sem, small_send, small_recv, load_sem, store_sem = refs[at + 16 :]
    place = Place(sizes)
    length = ids.shape[0]
    seqs, tokens = languages.shape[0], pool.shape[1]
    width = pool.shape[2]
    blocks = tokens // 128
    per_seq = width // PAIR
    sending = Pool(send_sem, send_sem.shape[0])
    loading = Pool(load_sem, load_sem.shape[0])
    storing = Pool(store_sem, store_sem.shape[0])

    def load(source, target):
        return PooledCopy(loading, source, target)

    def store(source, target):
        PooledCopy(storing, source, target)

    X = [pool.at[i] for i in range(11)] + [pairs_in.at[i] for i in range(4)]
    og, tn = X[0], X[1]
    get_og = load(grads, og)
    def outer_chunk(q):
        return wholes[9].at[q // 2, q % 2]

    def inner_chunk(q):
        return wholes[8].at[:, :, :, :, :, pl.ds(q * width, width)]

    arriving = {}

    def fetch(weights, pairs, key_rows, base):
        per_slot = stage.shape[1] // key_rows
        for n, p in enumerate(pairs):
            for s in range(seqs):
                at = base * per_slot + n * seqs + s
                part = stage.at[at // per_slot, pl.ds(at % per_slot * key_rows, key_rows)]
                arriving[key_rows, p, s] = load(weights.at[s * per_seq + p], part), part

    get_wo = [load(outer_chunk(0), wo.at[0])]
    get_slope = [load(saved["slope"].at[0], X[6])]
    get_tn = load(saved["third_norm"], tn)
    get_wi = [load(inner_chunk(0), w.at[0])]
    get_outers = load(outer_grads.at[:, place.c], outers)
    got = {}

    def load_more(q):
        if q < 3:
            get_slope.append(load(saved["slope"].at[q + 1], X[7 + q]))
        if q == 0:
            get_wo.append(load(outer_chunk(1), wo.at[1]))
            get_wi.append(load(inner_chunk(1), w.at[1]))
            got["table"] = load(saved["table"], table)
            got["late"] = load(saved["late"], run_c)
        if q == 1:
            got["cross_context"] = load(saved["cross_context"], X[2])
            got["co"] = load(wholes[7], w.at[2])
            got["cross_rows"] = load(saved["cross_rows"], cross_rows)
            got["cross_queries"] = load(saved["cross_queries"], X[3])
        if q == 2:
            got["keys"] = load(saved["source_keys"], pairs_in.at[pl.ds(0, 2)])
            got["values"] = load(saved["source_values"], pairs_in.at[pl.ds(2, 2)])
            fetch(cross_weights, (0,), stage.shape[1], 0)
        if q == 3:
            got["cq_w"] = load(wholes[4], w.at[3])
            got["second_norm"] = load(saved["second_norm"], X[4])
            got["first_norm"] = load(saved["first_norm"], X[5])
            got["self_rows"] = load(saved["self_rows"], self_rows)

    neighbour_barrier(place, far=True)

    def view_of(m):
        if m < 4:
            return lambda index: outers.at[(index[0],) + index[2:] + (m,)]
        return lambda index: squares.at[(m - 4,) + index]

    def leaving_of(m):
        if m < 4:
            return lambda core: outer_grads.at[:, core, :, :, m]
        return lambda core: squares.at[m - 4, :, core]

    exchange = Exchange(place, sending, recv_sem)
    plans = []
    for m in range(16):
        group, kind = m // 4, BACK_PATHS.index(BACKWARD_PATHS[m])
        slot = group % 2
        plans.append(
            Summed(
                place, BACK_PATHS[kind], view_of(m), leaving_of(m), core_boxes.at[slot, kind], [box.at[slot] for box in boxes[kind]],
                exchange,
            )
        )

    def put(i, value):
        squares[i] = value.reshape(squares.shape[1:]).astype(LOW)

    small_out[...] = jnp.zeros_like(small_out)

    def norm_backward(state, inflow, gain_row, before, after):
        def body(at):
            hidden, flow, gain = state[at, :], inflow[at, :], table[gain_row : gain_row + 1, :]
            scale = lax.rsqrt(jnp.mean(hidden * hidden, axis=-1, keepdims=True) + EPSILON)
            unit = hidden * scale
            small_out[gain_row : gain_row + 1, :] += jnp.sum(flow * unit, axis=0, keepdims=True)
            flow = flow * gain
            flow = (flow - unit * jnp.mean(unit * flow, axis=-1, keepdims=True)) * scale
            after[at, :] = before[at, :].astype(FULL) + flow

        each(blocks, body)

    branch = X[1]

    eg = X[10]

    def expanded_grad(q):
        if q == 0:
            get_og.wait()
        get_wo[q].wait()
        get_slope[q].wait()
        out_w = wo[q % 2].reshape(width, width)
        eg[...] = (nt_dot(og[...], out_w) * X[6 + q][...].astype(FULL)).astype(LOW)
        load_more(q)
        get_wo.append(load(outer_chunk((q + 2) % 4), wo.at[q % 2]))

    def inner_grad(q):
        get_tn.wait()
        put(q, tn_dot(tn[...], eg[...]))

    def third_grad(q):
        get_wi[q].wait()
        back = nt_dot(eg[...], flat(w.at[q % 2]))
        if q == 0:
            run_b[...] = back
        else:
            run_b[...] += back
        if q + 2 < 4:
            get_wi.append(load(inner_chunk(q + 2), w.at[q % 2]))
        if q == 3:
            got["so"] = load(wholes[3], w.at[0])
            got["q_w"] = load(wholes[0], w.at[1])
            got["encoder"] = load(encoder, pool.at[pl.ds(6, 2)])

    def third_backward():
        got["table"].wait()
        got["late"].wait()
        norm_backward(run_c, run_b, 10, og, run_a)
        got["inverse"] = load(saved["cross_inverse"], run_c)
        branch[...] = run_a[...].astype(LOW)

    def context_grad(weight, slot):
        got[weight].wait()
        got["inverse"].wait()
        X[0][...] = (nt_dot(branch[...], flat(w.at[slot])).astype(LOW).astype(FULL) * run_c[...]).astype(LOW)

    def cross_out_grad():
        got["cross_context"].wait()
        put(4, tn_dot(X[2][...], branch[...]))

    def cross_context_grad():
        context_grad("co", 2)
        got["k_w"] = load(wholes[1], w.at[2])
        got["mid"] = load(saved["mid"], run_c)

    def attention(rows, key_rows, pairs, one, finish_pair, ahead):
        for p in pairs:
            for s in range(seqs):
                arriving[key_rows, p, s][0].wait()
        ahead()
        items = []
        for p in pairs:
            for s in range(seqs):
                queries, keys, values, grad = one(s, pl.ds(p * PAIR, PAIR))
                items.append(
                    (arriving[key_rows, p, s][1][...], queries, keys, values, grad, rows[s * per_seq + p])
                )
        results = pairs_backward(items)
        for n, p in enumerate(pairs):
            finish_pair(p, pl.ds(p * PAIR, PAIR), results[n * seqs : (n + 1) * seqs])

    enc_length = pool.shape[1]

    def cross_attention(p):
        if p == 0:
            for name in ("cross_rows", "cross_queries", "keys", "values"):
                got[name].wait()

        def one(s, lanes):
            at = pl.ds(s * length, length)
            source = sources[s]
            return X[3][at, lanes], pairs_in[source, :, lanes], pairs_in[2 + source, :, lanes], X[0][at, lanes]

        def finish_pair(p, lanes, results):
            for s in range(seqs):
                X[1][pl.ds(s * length, length), lanes] = results[s][0].astype(LOW)
            for e in range(2):
                for target, part_at in ((8, 1), (11, 2)):
                    total = jnp.where(sources[0] == e, results[0][part_at], 0.0)
                    total = total + jnp.where(sources[1] == e, results[1][part_at], 0.0)
                    pool[target + e, :, lanes] = total.astype(LOW)

        def ahead():
            if p + 1 < per_seq:
                fetch(cross_weights, (p + 1,), enc_length, (p + 1) % 2 * 2)
            else:
                fetch(self_weights, (0, 1), length, 0)

        attention(cross_rows, enc_length, (p,), one, finish_pair, ahead)
        if p + 1 < per_seq:
            return
        got["queries"] = load(saved["queries"], X[11])
        got["keys"] = load(saved["keys"], X[12])
        got["values"] = load(saved["values"], X[13])
        got["self_context"] = load(saved["self_context"], X[14])

    def cross_query_grad():
        got["second_norm"].wait()
        put(5, tn_dot(X[4][...], X[1][...]))

    def source_grad(i, target):
        copy = got.pop("encoder", None)
        if copy is not None:
            copy.wait()
        put(i, tn_dot(pool[6], pool[target]) + tn_dot(pool[7], pool[target + 1]))

    def second_grad():
        got["cq_w"].wait()
        run_b[...] = nt_dot(X[1][...], flat(w.at[3]))
        got["v_w"] = load(wholes[2], w.at[3])

    def second_backward():
        got["mid"].wait()
        norm_backward(run_c, run_b, 9, run_a, run_a)
        got["inverse"] = load(saved["self_inverse"], run_c)
        branch[...] = run_a[...].astype(LOW)

    def self_out_grad():
        got["self_context"].wait()
        put(8, tn_dot(X[14][...], branch[...]))

    def self_context_grad():
        context_grad("so", 0)
        got["ck_w"] = load(wholes[5], w.at[0])
        got["start"] = load(saved["start"], run_c)

    def self_attention(turn):
        if turn == 0:
            for name in ("self_rows", "queries", "keys", "values"):
                got[name].wait()

        def one(s, lanes):
            at = pl.ds(s * length, length)
            return tuple(X[i][at, lanes] for i in (11, 12, 13, 0))

        def finish_pair(p, lanes, results):
            for s in range(seqs):
                for i in range(3):
                    X[2 + i][pl.ds(s * length, length), lanes] = results[s][i].astype(LOW)
            score_sum[p] = (results[0][3].astype(FULL) + results[1][3].astype(FULL)).astype(LOW)

        def ahead():
            if turn < 2:
                fetch(self_weights, (2 * turn + 2, 2 * turn + 3), length, (turn + 1) % 2 * 2)

        attention(self_rows, length, (2 * turn, 2 * turn + 1), one, finish_pair, ahead)

    def self_grad(i):
        copy = got.pop("first_norm", None)
        if copy is not None:
            copy.wait()
        put(9 + i, tn_dot(X[5][...], X[2 + i][...]))

    def closing_product(i):
        got[("q_w", "k_w", "v_w")[i]].wait()
        back = nt_dot(X[2 + i][...], flat(w.at[1 + i]))
        if i == 0:
            run_b[...] = back
            got["cv_w"] = load(wholes[6], w.at[1])
        else:
            run_b[...] += back

    def closing():
        got["start"].wait()
        got["activated"] = [load(saved["activated"].at[q], X[i]) for q, i in enumerate((0, 1, 5, 10))]
        norm_backward(run_c, run_b, 8, run_a, run_a)
        store(run_a, hidden_grad)
        got["late"] = load(saved["late"], run_c)
        for s in range(seqs):
            row = jnp.sum(run_a[pl.ds(s * length, length), :], axis=0, keepdims=True)
            for l in range(8):
                small_out[l : l + 1, :] += jnp.where(languages[s] == l, row, 0.0)

    def hidden_end(q):
        got["activated"][q].wait()
        get_wo[4 + q].wait()
        value = jnp.dot(X[(0, 1, 5, 10)[q]][...], wo[q % 2].reshape(width, width), preferred_element_type=FULL)
        if q < 2:
            get_wo.append(load(outer_chunk(q + 2), wo.at[q % 2]))
        if q == 0:
            got["late"].wait()
        if q < 3:
            run_c[...] += value
        else:
            X[2][...] = (run_c[...] + value).astype(LOW)
            store(X[2], hidden_out)

    def encoder_end(e, value):
        run = (run_b, run_c)[e]
        if value:
            got["cv_w"].wait()
            run[...] += nt_dot(pool[11 + e], flat(w.at[1]))
            store(run, encoder_grad.at[e])
        else:
            got["ck_w"].wait()
            run[...] = nt_dot(pool[8 + e], flat(w.at[0]))

    def bucket_sums(turn):
        if turn == 0:
            ids[...] = ids_in[...].astype(FULL).T.astype(jnp.int32)
        half = length // 2
        rows = 32

        def pair(p, _):
            def bucket_group(first, count, spans):
                sums = [[jnp.zeros((8, half), FULL) for _ in range(2)] for _ in range(count)]
                for n, side in spans:
                    block = pl.ds(n * rows, rows)
                    bucket = ids[block, side * half : (side + 1) * half]
                    scores = [
                        score_sum[p, block, h * length + side * half : h * length + (side + 1) * half].astype(FULL)
                        for h in range(2)
                    ]
                    for c in range(count):
                        here = bucket == first + c
                        for h in range(2):
                            kept = jnp.where(here, scores[h], 0.0).reshape(rows // 8, 8, half)
                            sums[c][h] = sums[c][h] + jnp.sum(kept, axis=0)
                for c in range(count):
                    for h in range(2):
                        row = (2 * p + h) * 32 + first + c
                        bucket_rows[pl.ds(row, 1), :] = jnp.sum(sums[c][h], axis=0, keepdims=True)

            blocks_of = length // rows
            every = [(n, side) for side in range(2) for n in range(blocks_of) if n * rows < (side + 1) * half]
            near = [(n, side) for n, side in every if n * rows + rows + 15 > side * half]
            for first in range(0, 32, 4):
                bucket_group(first, 4, near if first < 16 else every)
            return 0

        pair(turn, 0)
        if turn + 1 < per_seq:
            return
        ones = jnp.ones((8, 128), FULL)
        totals = lax.dot_general(
            ones, bucket_rows[...], (((1,), (1,)), ((), ())), precision=PRECISE, preferred_element_type=FULL
        )
        small_out[11:12, : bucket_rows.shape[0]] = totals[:1, :]

    small = []
    for dim in "cxyz":
        here, reach = place.at(dim), 1
        while reach < place.size(dim):
            small.append((dim, here + reach - 2 * reach * lax.rem(lax.div(here, reach), 2)))
            reach *= 2

    def small_copy(i):
        dim, partner = small[i]
        return pltpu.make_async_remote_copy(
            small_out, small_box.at[i], small_send.at[i], small_recv.at[i],
            device_id=place.device(dim, partner), device_id_type=MESH,
        )

    class Small:
        def start(self, i):
            small_copy(i).start()

        def finish(self, i):
            small_copy(i).wait()
            small_out[...] += small_box[i]

    tasks = dict(n3=third_backward, co=cross_out_grad, ccg=cross_context_grad, cq=cross_query_grad, n2a=second_grad, n2=second_backward)
    tasks.update(so=self_out_grad, scg=self_context_grad, cl1=closing)
    for e in range(2):
        tasks[f"e{e}k"] = functools.partial(encoder_end, e, False)
        tasks[f"e{e}v"] = functools.partial(encoder_end, e, True)
    tasks["ck"] = functools.partial(source_grad, 6, 8)
    tasks["cv"] = functools.partial(source_grad, 7, 11)
    for i in range(4):
        tasks[f"x{i}"] = functools.partial(expanded_grad, i)
        tasks[f"in{i}"] = functools.partial(inner_grad, i)
        tasks[f"t{i}"] = functools.partial(third_grad, i)
        tasks[f"h{i}"] = functools.partial(hidden_end, i)
    for i in range(per_seq):
        tasks[f"ca{i}"] = functools.partial(cross_attention, i)
        tasks[f"bk{i}"] = functools.partial(bucket_sums, i)
    for i in range(3):
        tasks[f"sa{i}"] = functools.partial(self_attention, i)
        tasks[f"cp{i}"] = functools.partial(closing_product, i)
        tasks["qkv"[i]] = functools.partial(self_grad, i)
    steps = [len(plan.stages) for plan in plans] + [len(small)]
    plans.append(Small())
    at = [0] * 17
    def keep_sum(m):
        plan = plans[m]
        packed[m] = plan.blocks(plan.own)[...].astype(FULL)
        store(packed.at[m], packed_out.at[m])

    for entry in BACKWARD_ORDER:
        if isinstance(entry, str):
            tasks[entry]()
            continue
        step = at[entry]
        at[entry] += 1
        if step >= 1:
            if entry < 4:
                get_outers.wait()
            plans[entry].finish(step - 1)
        if step < steps[entry]:
            plans[entry].start(step)
        elif entry < 16:
            keep_sum(entry)
    sending.drain()
    storing.drain()


def backward(sizes, output_grad, encoder_states, language_ids, source_index, bucket_ids, forward_outs):
    ny, nz = sizes
    grid = (ny, 2, nz, 2)
    tokens, width = output_grad.shape
    length = bucket_ids.shape[0]
    part = width // (ny * nz * 4)
    outer_grads, wholes, score_weights = forward_outs[0], forward_outs[1:11], forward_outs[11:13]
    saved = dict(zip(SAVED, forward_outs[13:]))
    enc_count, enc_length = encoder_states.shape[:2]
    anywhere = pl.BlockSpec(memory_space=pl.ANY)
    vmem = pl.BlockSpec(memory_space=pltpu.VMEM)
    smem = pl.BlockSpec(memory_space=pltpu.SMEM)
    lead = [sum_boxes(sizes, path)[0] for path in BACK_PATHS]
    receives = sum(sum_boxes(sizes, path)[1] for path in BACKWARD_PATHS)
    hops = (ny * nz * 4).bit_length() - 1
    pairs = tokens // length * (width // PAIR)
    row = (tokens, width)
    out_shape = [
        jax.ShapeDtypeStruct(row, LOW),
        jax.ShapeDtypeStruct(row, FULL),
        jax.ShapeDtypeStruct((enc_count, enc_length, width), FULL),
        jax.ShapeDtypeStruct((16, width), FULL),
        jax.ShapeDtypeStruct((16, part, width), FULL),
    ]
    outs = pl.pallas_call(
        functools.partial(backward_kernel, sizes, tuple(len(s) for s in lead)),
        out_shape=out_shape,
        in_specs=[anywhere, anywhere, smem, smem, vmem] + [anywhere] * (13 + len(SAVED)),
        out_specs=[anywhere] * 3 + [vmem, anywhere],
        scratch_shapes=[
            pltpu.VMEM((12,) + grid + (part, width), LOW),
            pltpu.VMEM((ny, nz, 2, 4, part, width), LOW),
            pltpu.VMEM((2, 4, ny, nz, 2, part, width), LOW),
        ]
        + [pltpu.VMEM((2,) + s + (part, width), LOW) for one in lead for s in one]
        + [
            pltpu.VMEM((hops, 16, width), FULL),
            pltpu.VMEM((13,) + row, LOW),
            pltpu.VMEM((4,) + row, LOW),
            pltpu.VMEM(row, FULL),
            pltpu.VMEM(row, FULL),
            pltpu.VMEM(row, FULL),
            pltpu.VMEM((4,) + grid + (part, width), LOW),
            pltpu.VMEM((2, nz, 2, 4, part, width), LOW),
            pltpu.VMEM((4, enc_length, 2 * length), LOW),
            pltpu.VMEM((width // PAIR, length, 2 * length), LOW),
            pltpu.VMEM((32 * H, 128), FULL),
            pltpu.VMEM((16, width), FULL),
            pltpu.VMEM((pairs, 1, 2 * length), FULL),
            pltpu.VMEM((pairs, 1, 2 * length), FULL),
            pltpu.VMEM((length, length), jnp.int32),
            pltpu.VMEM((16, part, width), FULL),
            pltpu.SemaphoreType.DMA((40,)),
            pltpu.SemaphoreType.DMA((receives,)),
            pltpu.SemaphoreType.DMA((hops,)),
            pltpu.SemaphoreType.DMA((hops,)),
            pltpu.SemaphoreType.DMA((28,)),
            pltpu.SemaphoreType.DMA((8,)),
        ],
        compiler_params=pltpu.CompilerParams(
            collective_id=3, has_side_effects=True, vmem_limit_bytes=63 * 1024 * 1024
        ),
    )(
        output_grad, encoder_states, language_ids, source_index, bucket_ids, outer_grads, *wholes, *score_weights,
        *[saved[name] for name in SAVED],
    )
    return finish(sizes, outs)


def finish_kernel(sizes, *refs):
    hidden_out, hidden_grad, encoder_grad, small_in, packed_in = refs[:5]
    outs = refs[5:18]
    language, bucket, gains = refs[18], refs[19], refs[20:23]
    staged_hidden, staged_grad, staged_encoder, small, packed, sem, in_sem = refs[23:]
    part, width = packed.shape[1:]
    copies, arriving = [], []

    def copy(source, target):
        copies.append(pltpu.make_async_copy(source, target, sem.at[len(copies)]))
        copies[-1].start()

    def arrive(source, target):
        arriving.append(pltpu.make_async_copy(source, target, in_sem.at[len(arriving)]))
        arriving[-1].start()
        return arriving[-1]

    get_small = arrive(small_in, small)
    blocks = []
    for source, target, out, pieces in (
        (encoder_grad, staged_encoder, outs[2], 4), (hidden_grad, staged_grad, outs[1], 2),
        (hidden_out, staged_hidden, outs[0], 1),
    ):
        size = source.shape[-2]
        for n in range(pieces):
            if len(source.shape) == 3:
                half = size // 2
                index = (n // 2, pl.ds(n % 2 * half, half))
            else:
                index = pl.ds(n * (size // pieces), size // pieces)
            blocks.append((arrive(source.at[index], target.at[index]), target.at[index], out.at[index]))
    groups = [arrive(packed_in.at[pl.ds(4 * n, 4)], packed.at[pl.ds(4 * n, 4)]) for n in range(4)]
    for ready, source, target in blocks:
        ready.wait()
        copy(source, target)
    for group in groups:
        group.wait()
    for q in range(4):
        copy(packed.at[q], outs[12].at[pl.ds(q * part, part)])
        copy(packed.at[4 + q], outs[11].at[:, pl.ds(q * width, width)])
    for i, m in enumerate((13, 14, 15, 12, 9, 10, 11, 8)):
        copy(packed.at[m], outs[3 + i])
    get_small.wait()
    place = Place(sizes)
    start = (place.dp * sizes[1] * 2 + place.fs) * part
    row = lax.broadcasted_iota(jnp.int32, (width, 128), 0)
    lane = lax.broadcasted_iota(jnp.int32, (width, 128), 1)
    chosen = jnp.where((row == lane + start) & (lane < part), 1.0, 0.0)
    own = jnp.dot(small[...], chosen, precision=PRECISE, preferred_element_type=FULL)
    language[...] = own[:8, :part]
    for i in range(3):
        gains[i][...] = own[8 + i, :part]
    row = lax.broadcasted_iota(jnp.int32, (16, width), 0)
    lane = lax.broadcasted_iota(jnp.int32, (16, width), 1)
    spread = jnp.where(lax.div(lane, 32) == row, small[11:12, :], 0.0)
    row = lax.broadcasted_iota(jnp.int32, (width, 128), 0)
    lane = lax.broadcasted_iota(jnp.int32, (width, 128), 1)
    places = jnp.where(lax.rem(row, 32) == lane, 1.0, 0.0)
    bucket[...] = jnp.dot(spread, places, precision=PRECISE, preferred_element_type=FULL)[:H, :32]
    for c in copies:
        c.wait()


def finish(sizes, outs):
    part, width = outs[4].shape[1:]
    anywhere = pl.BlockSpec(memory_space=pl.ANY)
    hbm = pl.BlockSpec(memory_space=pltpu.HBM)
    vmem = pl.BlockSpec(memory_space=pltpu.VMEM)
    shapes = [o.shape for o in outs[:3]] + [(part, width)] * 8
    shapes += [(part, 4 * width), (4 * part, width)]
    out_shape = [jax.ShapeDtypeStruct(s, FULL) for s in shapes]
    out_shape[0] = jax.ShapeDtypeStruct(shapes[0], LOW)
    out_shape += [jax.ShapeDtypeStruct(s, FULL) for s in ((8, part), (H, 32), (part,), (part,), (part,))]
    return pl.pallas_call(
        functools.partial(finish_kernel, sizes),
        out_shape=out_shape,
        in_specs=[hbm] * 5,
        out_specs=[anywhere] * 13 + [vmem] * 5,
        scratch_shapes=[pltpu.VMEM(o.shape, o.dtype) for o in outs]
        + [pltpu.SemaphoreType.DMA((23,)), pltpu.SemaphoreType.DMA((12,))],
        compiler_params=pltpu.CompilerParams(vmem_limit_bytes=60 * 1024 * 1024),
    )(*outs)


def local_general(
    sizes,
    hidden_in,
    output_grad,
    encoder_states,
    language_ids,
    source_index,
    bucket_ids,
    language_table,
    bucket_table,
    self_gain,
    self_query,
    self_key,
    self_value,
    self_out,
    cross_gain,
    cross_query,
    cross_key,
    cross_value,
    cross_out,
    feed_gain,
    inner_weight,
    outer_weight,
):
    seq_count = language_ids.shape[0]
    length = bucket_ids.shape[0]
    tokens = seq_count * length
    enc_count = encoder_states.shape[0]
    enc_length = encoder_states.shape[1]
    width = hidden_in.shape[1]
    blocks = seq_count // SEQ_BLOCK
    (
        gain_one, gain_two, gain_three, table_whole, query_whole, key_whole, value_whole, out_whole,
        cquery_whole, ckey_whole, cvalue_whole, cout_whole, inner_whole, outer_whole,
    ) = gather_weights(
        sizes, language_table, (self_gain, cross_gain, feed_gain),
        (self_query, self_key, self_value, self_out, cross_query, cross_key, cross_value, cross_out),
        inner_weight, outer_weight,
    )

    def to_blocks(array, rows):
        return array.reshape(blocks, SEQ_BLOCK, rows, array.shape[-1])

    language_hot = (language_ids[:, None] == jnp.arange(table_whole.shape[0])[None, :]).astype(
        jnp.float32
    )
    language_rows = jnp.dot(language_hot, table_whole.astype(jnp.float32), precision=PRECISE)
    start_state = (
        hidden_in.astype(jnp.float32).reshape(seq_count, length, width) + language_rows[:, None, :]
    ).reshape(tokens, width)
    first_norm = to_low(norm_scale(start_state, gain_one.astype(jnp.float32)))
    self_queries = to_low(matmul(first_norm, query_whole))
    self_keys = to_low(matmul(first_norm, key_whole))
    self_values = to_low(matmul(first_norm, value_whole))
    bucket_hot = (
        bucket_ids[:, :, None] == jnp.arange(bucket_table.shape[0])[None, None, :]
    ).astype(jnp.float32)
    position_bias = jnp.einsum(
        "ijb,bh->hij", bucket_hot, bucket_table.astype(jnp.float32), precision=PRECISE
    )
    positions = jnp.arange(length)
    masked_bias = jnp.where(
        (positions[:, None] >= positions[None, :])[None], position_bias, NEGATIVE
    )

    def self_forward(block_items):
        return attend_forward(block_items[0], block_items[1], block_items[2], masked_bias)

    self_context, self_total = lax.map(
        self_forward,
        (
            to_blocks(self_queries, length),
            to_blocks(self_keys, length),
            to_blocks(self_values, length),
        ),
    )
    self_context = self_context.reshape(tokens, -1)
    mid_state = start_state + matmul(self_context, out_whole)
    second_norm = to_low(norm_scale(mid_state, gain_two.astype(jnp.float32)))
    cross_queries = to_low(matmul(second_norm, cquery_whole))
    encoder_flat = encoder_states.reshape(enc_count * enc_length, width)
    source_keys = to_low(matmul(encoder_flat, ckey_whole)).reshape(enc_count, enc_length, -1)
    source_values = to_low(matmul(encoder_flat, cvalue_whole)).reshape(enc_count, enc_length, -1)
    source_hot = (source_index[:, None] == jnp.arange(enc_count)[None, :]).astype(jnp.float32)
    source_low = to_low(source_hot)
    picked_keys = to_low(
        jnp.einsum("se,emc->smc", source_low, source_keys, preferred_element_type=jnp.float32)
    )
    picked_values = to_low(
        jnp.einsum("se,emc->smc", source_low, source_values, preferred_element_type=jnp.float32)
    )

    def cross_forward(block_items):
        return attend_forward(block_items[0], block_items[1], block_items[2], 0.0)

    cross_context, cross_total = lax.map(
        cross_forward,
        (
            to_blocks(cross_queries, length),
            picked_keys.reshape(blocks, SEQ_BLOCK, enc_length, -1),
            picked_values.reshape(blocks, SEQ_BLOCK, enc_length, -1),
        ),
    )
    cross_context = cross_context.reshape(tokens, -1)
    late_state = mid_state + matmul(cross_context, cout_whole)
    third_norm = to_low(norm_scale(late_state, gain_three.astype(jnp.float32)))
    expanded = matmul(third_norm, inner_whole)
    activated = to_low(jax.nn.gelu(expanded, approximate=True))
    hidden_out = (late_state + matmul(activated, outer_whole)).astype(jnp.bfloat16)
    top_grad = output_grad.astype(jnp.float32)
    outer_full = left_product(activated, output_grad)
    activated_grad = right_product(output_grad, outer_whole)
    gelu_value, gelu_back = jax.vjp(jax.nn.gelu, expanded)
    expanded_grad = to_low(gelu_back(activated_grad)[0])
    inner_full = left_product(third_norm, expanded_grad)
    third_grad = right_product(expanded_grad, inner_whole)
    norm_value, norm_back = jax.vjp(norm_scale, late_state, gain_three.astype(jnp.float32))
    state_back, feed_gain_full = norm_back(third_grad)
    late_grad = top_grad + state_back
    cross_low = to_low(late_grad)
    cout_full = left_product(cross_context, cross_low)
    cross_context_grad = to_low(right_product(cross_low, cout_whole))

    def cross_backward(block_items):
        return attend_backward(
            block_items[0],
            block_items[1],
            block_items[2],
            0.0,
            block_items[3],
            block_items[4],
            False,
        )

    cquery_part, ckey_part, cvalue_part = lax.map(
        cross_backward,
        (
            to_blocks(cross_queries, length),
            picked_keys.reshape(blocks, SEQ_BLOCK, enc_length, -1),
            picked_values.reshape(blocks, SEQ_BLOCK, enc_length, -1),
            cross_total,
            to_blocks(cross_context_grad, length),
        ),
    )
    cquery_low = to_low(cquery_part.reshape(tokens, -1))
    source_key_grad = to_low(
        jnp.einsum(
            "se,smc->emc",
            source_hot,
            ckey_part.reshape(seq_count, enc_length, -1),
            precision=PRECISE,
        ).reshape(enc_count * enc_length, -1)
    )
    source_value_grad = to_low(
        jnp.einsum(
            "se,smc->emc",
            source_hot,
            cvalue_part.reshape(seq_count, enc_length, -1),
            precision=PRECISE,
        ).reshape(enc_count * enc_length, -1)
    )
    cquery_full = left_product(second_norm, cquery_low)
    ckey_full = left_product(encoder_flat, source_key_grad)
    cvalue_full = left_product(encoder_flat, source_value_grad)
    encoder_grad = (
        right_product(source_key_grad, ckey_whole) + right_product(source_value_grad, cvalue_whole)
    ).reshape(enc_count, enc_length, width)
    second_grad = right_product(cquery_low, cquery_whole)
    norm_value, norm_back = jax.vjp(norm_scale, mid_state, gain_two.astype(jnp.float32))
    state_back, cross_gain_full = norm_back(second_grad)
    mid_grad = late_grad + state_back
    self_low = to_low(mid_grad)
    out_full = left_product(self_context, self_low)
    self_context_grad = to_low(right_product(self_low, out_whole))

    def self_backward(block_items):
        return attend_backward(
            block_items[0],
            block_items[1],
            block_items[2],
            masked_bias,
            block_items[3],
            block_items[4],
            True,
        )

    query_part, key_part, value_part, bias_part = lax.map(
        self_backward,
        (
            to_blocks(self_queries, length),
            to_blocks(self_keys, length),
            to_blocks(self_values, length),
            self_total,
            to_blocks(self_context_grad, length),
        ),
    )
    query_low = to_low(query_part.reshape(tokens, -1))
    key_low = to_low(key_part.reshape(tokens, -1))
    value_low = to_low(value_part.reshape(tokens, -1))
    table_full = jnp.einsum(
        "hij,ijb->bh", jnp.sum(bias_part, axis=0), bucket_hot, precision=PRECISE
    )
    query_full = left_product(first_norm, query_low)
    key_full = left_product(first_norm, key_low)
    value_full = left_product(first_norm, value_low)
    first_grad = (
        right_product(query_low, query_whole)
        + right_product(key_low, key_whole)
        + right_product(value_low, value_whole)
    )
    norm_value, norm_back = jax.vjp(norm_scale, start_state, gain_one.astype(jnp.float32))
    state_back, self_gain_full = norm_back(first_grad)
    hidden_in_grad = mid_grad + state_back
    sequence_sums = jnp.sum(hidden_in_grad.reshape(seq_count, length, width), axis=1)
    language_full = left_product(language_hot, sequence_sums)
    (
        language_part, bucket_table_grad, sgain_part, cgain_part, feed_gain_part, whole_parts, inner_part, outer_part,
    ) = reduce_grads(
        sizes, language_full, table_full, (self_gain_full, cross_gain_full, feed_gain_full),
        (query_full, key_full, value_full, out_full, cquery_full, ckey_full, cvalue_full, cout_full),
        inner_full, outer_full,
    )
    query_sum, key_sum, value_sum, out_part, cquery_part_sum, ckey_part_sum, cvalue_part_sum, cout_part = whole_parts
    return (
        hidden_out,
        hidden_in_grad,
        encoder_grad,
        language_part,
        bucket_table_grad,
        sgain_part,
        query_sum,
        key_sum,
        value_sum,
        out_part,
        cgain_part,
        cquery_part_sum,
        ckey_part_sum,
        cvalue_part_sum,
        cout_part,
        feed_gain_part,
        inner_part,
        outer_part,
    )


def local(sizes, *args):
    if sizes == (2, 4) and args[8].shape[0] % 8 == 0:
        return local_fused(sizes, *args)
    return local_general(sizes, *args)


def local_fused(
    sizes, hidden_in, output_grad, encoder_states, language_ids, source_index, bucket_ids, language_table,
    bucket_table, self_gain, self_query, self_key, self_value, self_out, cross_gain, cross_query, cross_key,
    cross_value, cross_out, feed_gain, inner_weight, outer_weight,
):
    kept = forward(
        sizes, hidden_in, output_grad, encoder_states, language_ids, source_index, bucket_ids, language_table,
        bucket_table, (self_gain, cross_gain, feed_gain),
        (self_query, self_key, self_value, self_out, cross_query, cross_key, cross_value, cross_out),
        inner_weight, outer_weight,
    )
    outs = backward(sizes, output_grad, encoder_states, language_ids, source_index, bucket_ids, kept)
    squares, inner, outer, language, bucket, gains = outs[3:11], outs[11], outs[12], outs[13], outs[14].T, outs[15:]
    return (
        *outs[:3], language, bucket, gains[0], *squares[:4], gains[1], *squares[4:], gains[2], inner, outer,
    )


def solution(mesh):
    sizes = (mesh.shape["dp"] // 2, mesh.shape["fsdp"] // 2)
    in_specs = (
        P(("dp", "fsdp"), None),
        P(("dp", "fsdp"), None),
        P(("dp", "fsdp"), None, None),
        P(("dp", "fsdp")),
        P(("dp", "fsdp")),
        P(),
        P(None, ("dp", "fsdp")),
        P(),
        P(("dp", "fsdp")),
        P(("dp", "fsdp"), None),
        P(("dp", "fsdp"), None),
        P(("dp", "fsdp"), None),
        P(("dp", "fsdp"), None),
        P(("dp", "fsdp")),
        P(("dp", "fsdp"), None),
        P(("dp", "fsdp"), None),
        P(("dp", "fsdp"), None),
        P(("dp", "fsdp"), None),
        P(("dp", "fsdp")),
        P(("dp", "fsdp"), None),
        P(("dp", "fsdp"), None),
    )
    out_specs = (
        P(("dp", "fsdp"), None),
        P(("dp", "fsdp"), None),
        P(("dp", "fsdp"), None, None),
        P(None, ("dp", "fsdp")),
        P(),
        P(("dp", "fsdp")),
        P(("dp", "fsdp"), None),
        P(("dp", "fsdp"), None),
        P(("dp", "fsdp"), None),
        P(("dp", "fsdp"), None),
        P(("dp", "fsdp")),
        P(("dp", "fsdp"), None),
        P(("dp", "fsdp"), None),
        P(("dp", "fsdp"), None),
        P(("dp", "fsdp"), None),
        P(("dp", "fsdp")),
        P(("dp", "fsdp"), None),
        P(("dp", "fsdp"), None),
    )
    return jax.shard_map(functools.partial(local, sizes), mesh=mesh, in_specs=in_specs, out_specs=out_specs, check_vma=False)
```

```python
import functools

import jax
import jax.numpy as jnp
from jax import lax
from jax.experimental import pallas as pl
from jax.experimental.pallas import tpu as pltpu
from jax.sharding import PartitionSpec as P

H = 12
HEAD = 64
SEQ_BLOCK = 2


EPSILON = 1e-06
PRECISE = lax.Precision.HIGHEST
NEGATIVE = -1e30


def to_low(value):
    return value.astype(jnp.bfloat16)


def norm_scale(hidden, gain):
    return hidden * lax.rsqrt(jnp.mean(hidden * hidden, axis=-1, keepdims=True) + EPSILON) * gain


def matmul(left, right):
    return jnp.dot(left, right, preferred_element_type=jnp.float32)


def left_product(left, right):
    return lax.dot_general(
        left, right, (((0,), (0,)), ((), ())), preferred_element_type=jnp.float32
    )


def right_product(left, right):
    return lax.dot_general(
        left, right, (((1,), (1,)), ((), ())), preferred_element_type=jnp.float32
    )


def split_heads(array):
    return array.reshape(array.shape[:-1] + (H, HEAD))


def score_block(queries, key_rows, offset):
    scores = jnp.einsum(
        "sqhe,skhe->shqk",
        split_heads(queries),
        split_heads(key_rows),
        preferred_element_type=jnp.float32,
    )
    return scores + offset


def attend_forward(queries, key_rows, value_rows, offset):
    scores = score_block(queries, key_rows, offset)
    top_score = jnp.max(scores, axis=-1, keepdims=True)
    log_total = top_score + jnp.log(jnp.sum(jnp.exp(scores - top_score), axis=-1, keepdims=True))
    weights = to_low(jnp.exp(scores - log_total))
    context = jnp.einsum(
        "shqk,skhe->sqhe", weights, split_heads(value_rows), preferred_element_type=jnp.float32
    )
    return (to_low(context).reshape(queries.shape), log_total)


def attend_backward(queries, key_rows, value_rows, offset, log_total, context_grad, with_bias):
    scores = score_block(queries, key_rows, offset)
    probs = jnp.exp(scores - log_total)
    weights = to_low(probs)
    grad_heads = split_heads(context_grad)
    value_grad = jnp.einsum(
        "shqk,sqhe->skhe", weights, grad_heads, preferred_element_type=jnp.float32
    )
    prob_grad = jnp.einsum(
        "sqhe,skhe->shqk", grad_heads, split_heads(value_rows), preferred_element_type=jnp.float32
    )
    score_grad = to_low(probs * (prob_grad - jnp.sum(probs * prob_grad, axis=-1, keepdims=True)))
    query_grad = jnp.einsum(
        "shqk,skhe->sqhe", score_grad, split_heads(key_rows), preferred_element_type=jnp.float32
    )
    key_grad = jnp.einsum(
        "shqk,sqhe->skhe", score_grad, split_heads(queries), preferred_element_type=jnp.float32
    )
    grads = (
        query_grad.reshape(queries.shape),
        key_grad.reshape(key_rows.shape),
        value_grad.reshape(value_rows.shape),
    )
    if with_bias:
        return grads + (jnp.sum(score_grad.astype(jnp.float32), axis=0),)
    return grads


MESH = pl.DeviceIdType.MESH
ALL = slice(None)


class Place:
    def __init__(self, sizes):
        self.ny, self.nz = sizes
        self.dp = lax.axis_index("dp")
        self.fs = lax.axis_index("fsdp")
        self.c, self.y = lax.rem(self.dp, 2), lax.div(self.dp, 2)
        self.x, self.z = lax.rem(self.fs, 2), lax.div(self.fs, 2)

    def size(self, dim):
        return {"c": 2, "x": 2, "y": self.ny, "z": self.nz}[dim]

    def at(self, dim):
        return {"c": self.c, "x": self.x, "y": self.y, "z": self.z}[dim]

    def device(self, dim, index):
        if dim == "c":
            return (self.y * 2 + index, self.fs)
        if dim == "y":
            return (index * 2 + self.c, self.fs)
        if dim == "x":
            return (self.dp, self.z * 2 + index)
        return (self.dp, index * 2 + self.x)


def neighbour_barrier(place, far=False):
    barrier = pltpu.get_barrier_semaphore()
    links = []
    for dim in "cxyz":
        here, size = place.at(dim), place.size(dim)
        reach = 1
        while reach < size and (reach == 1 or far):
            if size == 2:
                links.append((dim, 1 - here, None))
            elif reach == 1:
                for step in (1, -1):
                    links.append((dim, here + step, (here + step >= 0) & (here + step < size)))
            else:
                links.append((dim, here + reach - 2 * reach * lax.rem(lax.div(here, reach), 2), None))
            reach *= 2

    def signal(dim, there):
        pl.semaphore_signal(barrier, inc=1, device_id=place.device(dim, there), device_id_type=MESH)

    for dim, there, condition in links:
        if condition is None:
            signal(dim, there)
        else:
            pl.when(condition)(lambda dim=dim, there=there: signal(dim, there))
    peers = sum(1 if condition is None else condition.astype(jnp.int32) for _, _, condition in links)
    pl.semaphore_wait(barrier, peers)


PATHS = ("zxy", "zyx", "xzy", "yzx")


class Link:
    def __init__(self, copy, sends=None, receives=None):
        self.copy, self.sends, self.receives = copy, sends, receives

    @staticmethod
    def when(condition, run):
        if condition is None:
            run()
        else:
            pl.when(condition)(run)

    def start(self):
        self.when(self.sends, lambda: self.copy.start())

    def wait_send(self):
        self.when(self.sends, lambda: self.copy.wait_send())

    def wait_recv(self):
        self.when(self.receives, lambda: self.copy.wait_recv())


class Pool:
    def __init__(self, array, count):
        self.array, self.free, self.users = array, list(range(count)), []

    def take(self, user):
        if not self.free:
            self.users[0].release()
        self.users.append(user)
        return self.free.pop(0)

    def give(self, user, at):
        self.users.remove(user)
        self.free.append(at)

    def drain(self):
        while self.users:
            self.users[0].release()


class PooledLink(Link):
    def __init__(self, make, pool, sends=None, receives=None):
        self.make, self.pool, self.sends, self.receives = make, pool, sends, receives
        self.at = None

    def start(self):
        self.at = self.pool.take(self)
        copy = self.make(self.pool.array.at[self.at])
        self.when(self.sends, lambda: copy.start())

    def release(self):
        copy = self.make(self.pool.array.at[self.at])
        self.when(self.sends, lambda: copy.wait_send())
        self.pool.give(self, self.at)

    def wait_recv(self):
        copy = self.make(self.pool.array.at[0])
        self.when(self.receives, lambda: copy.wait_recv())


class PooledCopy:
    def __init__(self, pool, source, target):
        self.pool, self.done = pool, False
        self.at = pool.take(self)
        self.copy = pltpu.make_async_copy(source, target, pool.array.at[self.at])
        self.copy.start()

    def wait(self):
        if not self.done:
            self.copy.wait()
            self.done = True
            self.pool.give(self, self.at)

    release = wait


class Exchange:
    def __init__(self, place, pool, receive):
        self.place, self.pool, self.receive, self.count = place, pool, receive, 0

    def slot(self):
        self.count += 1
        return self.count - 1

    def link(self, source, target, dim, there, sends=None, receives=None, slot=None):
        slot = self.slot() if slot is None else slot
        device = self.place.device(dim, there)

        def make(send):
            return pltpu.make_async_remote_copy(
                source, target, send, self.receive.at[slot], device_id=device, device_id_type=MESH
            )

        return PooledLink(make, self.pool, sends, receives)


def pick(held, place, **fixed):
    return tuple(fixed.get(dim, ALL if dim in held else place.at(dim)) for dim in "yczx")


def gather_steps(place, blocks, path, sems):
    steps, slot, held = [], 0, ""
    for dim in path + "c":
        here, size = place.at(dim), place.size(dim)
        if size == 2:
            there = 1 - here
            index = pick(held, place)
            copy = pltpu.make_async_remote_copy(
                blocks(index), blocks(index), sems[0].at[slot], sems[1].at[slot],
                device_id=place.device(dim, there), device_id_type=MESH,
            )
            steps.append([Link(copy)])
            slot += 1
        else:
            for hop in range(1, size):
                links = []
                for way in (1, -1):
                    origin = here - way * (hop - 1)
                    there = here + way
                    source = here - way * hop
                    index = pick(held, place, **{dim: jnp.clip(origin, 0, size - 1)})
                    copy = pltpu.make_async_remote_copy(
                        blocks(index), blocks(index), sems[0].at[slot], sems[1].at[slot],
                        device_id=place.device(dim, jnp.clip(there, 0, size - 1)), device_id_type=MESH,
                    )
                    sends = (origin >= 0) & (origin < size) & (there >= 0) & (there < size)
                    links.append(Link(copy, sends, (source >= 0) & (source < size)))
                    slot += 1
                steps.append(links)
        held += dim
    return steps


def slot_count(sizes):
    ny, nz = sizes
    return 2 + (1 if ny == 2 else 2 * (ny - 1)) + (1 if nz == 2 else 2 * (nz - 1))


def run_steps(plans, lag):
    rounds = max(lag[i] + len(plan) for i, plan in enumerate(plans)) + 1
    for now in range(rounds):
        for offset, plan in zip(lag, plans):
            at = now - offset
            if 1 <= at <= len(plan):
                for link in plan[at - 1]:
                    link.wait_recv()
            if 0 <= at < len(plan):
                for link in plan[at]:
                    link.start()
    for plan in plans:
        for links in plan:
            for link in links:
                link.wait_send()


def gather_kernel(sizes, *refs):
    shards, wholes = refs[:11], refs[11:22]
    own_sem, send_sem, recv_sem = refs[22:]
    place = Place(sizes)
    own = (place.y, place.c, place.z, place.x)
    owns = [
        pltpu.make_async_copy(shard, whole.at[own], own_sem.at[i])
        for i, (shard, whole) in enumerate(zip(shards, wholes))
    ]
    for copy in owns:
        copy.start()
    neighbour_barrier(place)
    views = [lambda index, ref=ref: ref.at[index] for ref in wholes[:9]]
    width = wholes[8].shape[-1]
    for q in range(4):
        views.append(
            lambda index, q=q: wholes[9].at[index + (ALL, pl.ds(q * width, width))]
        )
    for q in range(4):
        views.append(lambda index, q=q: wholes[10].at[index + (q,)])
    plans, lag = [], []
    for i, view in enumerate(views):
        path = PATHS[0] if i == 0 else PATHS[(i - 1) % 4]
        plans.append(gather_steps(place, view, path, (send_sem.at[i], recv_sem.at[i])))
        lag.append(0 if i == 0 else 3 * ((i - 1) // 4))
    for copy in owns:
        copy.wait()
    run_steps(plans, lag)


def gather_weights(sizes, table, gains, squares, inner, outer):
    ny, nz = sizes
    grid = (ny, 2, nz, 2)
    part, width = squares[0].shape
    small = jnp.zeros((16, 128), table.dtype)
    small = small.at[: table.shape[0], :part].set(table)
    for i, gain in enumerate(gains):
        small = small.at[table.shape[0] + i, :part].set(gain)
    shards = (small,) + tuple(squares) + (inner, outer.reshape(4, part, width))
    anywhere = pl.BlockSpec(memory_space=pl.ANY)
    slots = slot_count(sizes)
    wholes = pl.pallas_call(
        functools.partial(gather_kernel, sizes),
        out_shape=[jax.ShapeDtypeStruct(grid + s.shape, s.dtype) for s in shards],
        in_specs=[anywhere] * 11,
        out_specs=[anywhere] * 11,
        scratch_shapes=[
            pltpu.SemaphoreType.DMA((11,)),
            pltpu.SemaphoreType.DMA((17, slots)),
            pltpu.SemaphoreType.DMA((17, slots)),
        ],
        compiler_params=pltpu.CompilerParams(collective_id=0, has_side_effects=True),
    )(*shards)
    count = ny * nz * 4
    tiny = wholes[0].reshape(count, 16, 128)[:, :, :part].transpose(1, 0, 2).reshape(16, count * part)
    rows = table.shape[0]
    return (
        (tiny[rows], tiny[rows + 1], tiny[rows + 2], tiny[:rows])
        + tuple(w.reshape(count * part, width) for w in wholes[1:9])
        + (wholes[9].reshape(count * part, 4 * width), wholes[10].reshape(4 * count * part, width))
    )


class Reduce:
    def __init__(self, place, path, source, total, core_in, boxes, out, sems):
        self.place, self.path, self.source, self.total = place, path, source, total
        self.core_in, self.boxes, self.out, self.sems = core_in, boxes, out, sems
        self.slot = 0
        self.sent = []

    def copy(self, source, target, dim, there):
        slot = self.slot
        self.slot += 1
        return pltpu.make_async_remote_copy(
            source, target, self.sems[0].at[slot], self.sems[1].at[slot],
            device_id=self.place.device(dim, there), device_id_type=MESH,
        )

    def index(self, fixed):
        return tuple(fixed.get(dim, ALL) for dim in "yzx")

    def add(self, target, box):
        shape = box.shape[:-2]
        count = 1
        for size in shape:
            count *= size
        free = [i for i, entry in enumerate(target) if entry is ALL]

        def body(n, _):
            spots, rest = [], n
            for size in reversed(shape):
                spots.append(lax.rem(rest, size))
                rest = lax.div(rest, size)
            spots = spots[::-1]
            full = list(target)
            for place_at, spot in zip(free, spots):
                full[place_at] = spot
            mine = self.total[tuple(full)].astype(jnp.float32)
            got = box[tuple(spots)].astype(jnp.float32)
            self.total[tuple(full)] = (mine + got).astype(jnp.bfloat16)
            return 0

        if count == 1:
            body(0, 0)
        else:
            lax.fori_loop(0, count, body, 0)

    def steps(self):
        place, listing = self.place, []
        own = pltpu.make_async_copy(self.source(place.c), self.total, self.sems[2])
        core = self.copy(self.source(1 - place.c), self.core_in, "c", 1 - place.c)

        def start():
            own.start()
            core.start()

        def finish():
            own.wait()
            core.wait_recv()
            self.add((ALL, ALL, ALL), self.core_in)

        self.sent.append(Link(core))
        listing.append((start, finish))
        fixed, box = {}, 0
        for dim in self.path:
            here, size = place.at(dim), place.size(dim)
            if size == 2:
                target = self.index({**fixed, dim: 1 - here})
                link = Link(self.copy(self.total.at[target], self.boxes[box], dim, 1 - here))
                self.sent.append(link)
                listing.append(self.pair([link], [(self.index({**fixed, dim: here}), box, None)]))
                box += 1
            else:
                for hop in range(size - 1, 0, -1):
                    links, adds = [], []
                    for way in (1, -1):
                        there = here - way
                        goal = here - way * hop
                        sends = (goal >= 0) & (goal < size)
                        source = here + way
                        got = source - way * hop
                        receives = (source >= 0) & (source < size) & (got >= 0) & (got < size)
                        target = self.index({**fixed, dim: jnp.clip(goal, 0, size - 1)})
                        copy = self.copy(
                            self.total.at[target], self.boxes[box], dim, jnp.clip(there, 0, size - 1)
                        )
                        link = Link(copy, sends, receives)
                        self.sent.append(link)
                        links.append(link)
                        adds.append((self.index({**fixed, dim: jnp.clip(got, 0, size - 1)}), box, receives))
                        box += 1
                    listing.append(self.pair(links, adds))
            fixed = {**fixed, dim: here}
        return listing

    def pair(self, links, adds):
        def start():
            for link in links:
                link.start()

        def finish():
            for link in links:
                link.wait_recv()
            for target, box, condition in adds:
                Link.when(condition, functools.partial(self.add, target, self.boxes[box]))

        return start, finish

    def close(self):
        own = (self.place.y, self.place.z, self.place.x)
        self.out(self.total[own].astype(jnp.float32))
        for link in self.sent:
            link.wait_send()


def box_shapes(sizes, path):
    ny, nz = sizes
    size = {"y": ny, "z": nz, "x": 2}
    left, shapes = "yzx", []
    for dim in path:
        left = left.replace(dim, "")
        lead = tuple(size[d] for d in left)
        shapes += [lead] * (1 if size[dim] == 2 else 2 * (size[dim] - 1))
    return shapes


BACK_PATHS = tuple(path[::-1] for path in PATHS)


def reduce_kernel(sizes, box_counts, *refs):
    sources, small_in = refs[:10], refs[10]
    outs, small_out = refs[11:21], refs[21]
    totals, core_boxes = refs[22], refs[23]
    at = 24
    boxes = []
    for count in box_counts:
        boxes.append(refs[at : at + count])
        at += count
    small_box, own_sem, send_sem, recv_sem, small_send, small_recv = refs[at:]
    place = Place(sizes)
    neighbour_barrier(place, far=True)
    width = outs[0].shape[-1]

    def square(ref):
        return lambda core: ref.at[:, core]

    def inner(q):
        return lambda core: sources[8].at[:, core, :, :, :, pl.ds(q * width, width)]

    def outer(q):
        return lambda core: sources[9].at[:, core, :, :, q]

    views = [inner(q) for q in range(4)] + [outer(q) for q in range(4)]
    views += [square(sources[i]) for i in (4, 5, 6, 7, 0, 1, 2, 3)]

    def store_square(i):
        def run(value):
            outs[i][...] = value

        return run

    def store_inner(q):
        def run(value):
            outs[8][:, q * width : (q + 1) * width] = value

        return run

    def store_outer(q):
        def run(value):
            outs[9][q] = value

        return run

    stores = [store_inner(q) for q in range(4)] + [store_outer(q) for q in range(4)]
    stores += [store_square(i) for i in (4, 5, 6, 7, 0, 1, 2, 3)]
    plans, lag = [], []
    reduces = []
    for m in range(16):
        group, kind = m // 4, m % 4
        reduce = Reduce(
            place, BACK_PATHS[kind], views[m], totals.at[m], core_boxes.at[m],
            [box.at[group] for box in boxes[kind]], stores[m],
            (send_sem.at[m], recv_sem.at[m], own_sem.at[m]),
        )
        reduces.append(reduce)
        plans.append(reduce.steps())
        lag.append(3 * group)
    small_out[...] = small_in[...]
    small = []
    moves = [("c", 1 - place.c), ("x", 1 - place.x), ("y", None), ("z", None)]
    for dim, there in moves:
        size, here, reach = place.size(dim), place.at(dim), 1
        while reach < size:
            partner = here + reach - 2 * reach * lax.rem(lax.div(here, reach), 2)
            small.append((dim, partner))
            reach *= 2
    rounds = max(max(lag[i] + len(plan) for i, plan in enumerate(plans)) + 1, len(small) + 1)
    copies = []
    for now in range(rounds):
        for offset, plan in zip(lag, plans):
            step = now - offset
            if 1 <= step <= len(plan):
                plan[step - 1][1]()
            if 0 <= step < len(plan):
                plan[step][0]()
        if 1 <= now <= len(small):
            copies[-1].wait()
            small_out[...] += small_box[now - 1]
        if now < len(small):
            dim, partner = small[now]
            copies.append(
                pltpu.make_async_remote_copy(
                    small_out, small_box.at[now], small_send.at[now], small_recv.at[now],
                    device_id=place.device(dim, partner), device_id_type=MESH,
                )
            )
            copies[-1].start()
    for reduce in reduces:
        reduce.close()


def reduce_grads(sizes, language, bucket, gains, squares, inner, outer):
    ny, nz = sizes
    grid = (ny, 2, nz, 2)
    count = ny * nz * 4
    width = squares[0].shape[1]
    part = squares[0].shape[0] // count
    langs = language.shape[0]
    flat = jnp.zeros((width,), jnp.float32).at[: bucket.size].set(bucket.reshape(-1))
    small = jnp.concatenate(
        [language] + [g.reshape(1, width) for g in gains] + [flat[None], jnp.zeros((4, width), jnp.float32)], axis=0
    )
    sources = [to_low(s).reshape(grid + (part, width)) for s in squares]
    sources += [
        to_low(inner).reshape(grid + (part, 4 * width)),
        to_low(outer).reshape(grid + (4, part, width)),
    ]
    anywhere = pl.BlockSpec(memory_space=pl.ANY)
    vmem = pl.BlockSpec(memory_space=pltpu.VMEM)
    shapes = [(part, width)] * 8 + [(part, 4 * width), (4, part, width), small.shape]
    lead = [box_shapes(sizes, path) for path in BACK_PATHS]
    slots = slot_count(sizes)
    hops = (ny * nz * 4).bit_length() - 1
    outs = pl.pallas_call(
        functools.partial(reduce_kernel, sizes, tuple(len(s) for s in lead)),
        out_shape=[jax.ShapeDtypeStruct(s, jnp.float32) for s in shapes],
        in_specs=[anywhere] * 10 + [vmem],
        out_specs=[vmem] * 11,
        scratch_shapes=[
            pltpu.VMEM((16, ny, nz, 2, part, width), jnp.bfloat16),
            pltpu.VMEM((16, ny, nz, 2, part, width), jnp.bfloat16),
        ]
        + [pltpu.VMEM((4,) + s + (part, width), jnp.bfloat16) for one in lead for s in one]
        + [
            pltpu.VMEM((hops,) + small.shape, jnp.float32),
            pltpu.SemaphoreType.DMA((16,)),
            pltpu.SemaphoreType.DMA((16, slots)),
            pltpu.SemaphoreType.DMA((16, slots)),
            pltpu.SemaphoreType.DMA((hops,)),
            pltpu.SemaphoreType.DMA((hops,)),
        ],
        compiler_params=pltpu.CompilerParams(
            collective_id=1, has_side_effects=True, vmem_limit_bytes=60 * 1024 * 1024
        ),
    )(*sources, small)
    start = (lax.axis_index("dp") * nz * 2 + lax.axis_index("fsdp")) * part
    total = outs[10]
    mine = lax.dynamic_slice(total, (0, start), (langs + 3, part))
    return (
        mine[:langs],
        total[langs + 3, : bucket.size].reshape(bucket.shape),
        mine[langs], mine[langs + 1], mine[langs + 2],
        outs[:8], outs[8], outs[9].reshape(4 * part, width),
    )


FORWARD_PATHS = (
    "zxy", "yzx", "zxy", "zyx", "zyx", "xzy", "zxy", "zxy", "zyx", "xyz", "zyx", "yxz", "zxy", "zxy", "zyx",
    "zyx", "xyz",
)
FORWARD_ORDER = (
    2, 11, 0, 9, 3, 1, 5, 16, 4, 2, 9, 3, 11, 0, 6, 16, 2, 5, 3, 1, 2, "b0", 4, 7, 0, 3, 1, 5, 0, 4, 13, 8, 6,
    2, "b1", 7, 3, 1, 4, 12, 6, 0, 10, "b2", 5, 1, 14, 6, 8, 3, 7, 2, 0, 10, 0, 1, 14, 12, 5, 9, 8, 2, 3, 13, 7,
    "b3", 4, 5, 12, "open", 6, 11, "k", 1, "q", "v", 5, 8, 15, 7, "sa0", 12, 10, 4, "sa1", 9, 6, "sa2", 8,
    "sa3", 14, 4, "se0", "se1", 9, 13, 10, 6, 7, 16, "K", "cq", 14, 15, 7, 12, "V", 11, "ca0", 8, 9, 10, 13,
    "ca1", 15, "ca2", "ca3", 10, 11, 16, 9, 8, 15, 14, "ce0", "ce1", "in0", 13, 12, "og0", 11, 10, "in1", 16,
    12, 15, "og1", 14, 13, 11, "in2", 16, "in3", 15, 14, "og3", 13, "og2", 16, 15,
)
BACKWARD_PATHS = (
    "xzy", "yzx", "yxz", "xyz", "xzy", "xyz", "yxz", "yzx", "yzx", "yxz", "xyz", "xzy", "xyz", "xzy", "yzx",
    "yxz",
)
BACKWARD_ORDER = (
    3, "x0", 2, "in0", 0, 4, 3, "t0", 2, "x1", 0, "in1", 1, 3, "t1", "x2", 0, 1, 5, 4, "in2", 2, "t2", 6, "x3",
    3, "in3", 1, 0, "t3", 7, 4, 6, "n3", 5, "co", 1, "ccg", 2, 7, 0, "ca0", 6, "ca1", "ca2", "ca3", 4, 8, 7, 1,
    "ca4", "ca5", 5, "cv", 11, "cq", 7, 9, "ck", 10, 11, 4, 8, "n2a", 1, 9, "n2", 10, 6, 3, "so", 5, 8, 2,
    "scg", 12, 0, 11, "sa0", 9, 5, "sa1", 6, 10, 2, 8, "sa2", 3, 4, "k", 7, 14, "v", 11, 15, "cp0", "q", 3, 14,
    12, 13, 5, 2, "cp1", 9, 10, 15, 1, "bk0", 13, 11, "bk1", 9, 4, 0, 14, 7, "bk2", 10, 12, 6, "cp2", "cl1", 13,
    "bk3", 15, 14, "bk4", 8, "bk5", 16, 12, "h0", 5, 7, 16, 6, 13, "h1", 9, "h2", 12, "h3", 15, 16, 14, "e0k",
    13, 9, "e0v", 16, 15, 10, 11, 12, "e1k", 13, 14, 8, 11, 16, 15, "e1v", 13, 8, 10, 12, 15, 14, 16,
)


LOW = jnp.bfloat16
FULL = jnp.float32
PAIR = 2 * HEAD


def nt_dot(left, right):
    return lax.dot_general(left, right, (((1,), (1,)), ((), ())), preferred_element_type=FULL)


def tn_dot(left, right):
    return lax.dot_general(left, right, (((0,), (0,)), ((), ())), preferred_element_type=FULL)


def flat(ref, *suffix):
    value = ref[(ALL,) * (len(ref.shape) - 1) + suffix] if suffix else ref[...]
    rows = 1
    for size in value.shape[:-1]:
        rows *= size
    return value.reshape(rows, value.shape[-1])


def each(count, body):
    def run(i, _):
        body(pl.ds(pl.multiple_of(i * 128, 128), 128))
        return 0

    lax.fori_loop(0, count, run, 0)


def unit_rows(hidden):
    return hidden * lax.rsqrt(jnp.mean(hidden * hidden, axis=-1, keepdims=True) + EPSILON)


def spread_small(tiny, table):
    part = table.shape[1] // (tiny.shape[0] * tiny.shape[2] * 4)
    table[...] = jnp.zeros_like(table)
    lane = lax.broadcasted_iota(jnp.int32, (16, 128), 1)
    at = 0
    for y in range(tiny.shape[0]):
        for core in range(2):
            for z in range(tiny.shape[2]):
                for x in range(2):
                    slab = jnp.where(lane < part, tiny[y, core, z, x], 0.0)
                    base, shift = at // 128 * 128, at % 128
                    if shift:
                        slab = pltpu.roll(slab, shift, 1)
                    if shift + part <= 128:
                        table[:, base : base + 128] += slab
                    else:
                        table[:, base : base + 128] += jnp.where(lane >= part, slab, 0.0)
                        table[:, base + 128 : base + 256] += jnp.where(lane < part, slab, 0.0)
                    at += part


def build_bias(ids, values, bias, heads):
    keys, queries = bias.shape[1:]
    rows = 64

    def block(n, _):
        at = pl.ds(pl.multiple_of(n * rows, rows), rows)
        bucket = ids[at, :]
        bits = [lax.bitwise_and(bucket, 1 << b) != 0 for b in range(5)]
        key = n * rows + lax.broadcasted_iota(jnp.int32, (rows, queries), 0)
        query = lax.broadcasted_iota(jnp.int32, (rows, queries), 1)
        hidden = key > query

        def head(h, _):
            level = [values[16 + h, c] for c in range(32)]
            for bit in bits:
                level = [jnp.where(bit, level[i + 1], level[i]) for i in range(0, len(level), 2)]
            bias[h, at, :] = jnp.where(hidden, NEGATIVE, level[0]).astype(LOW)
            return 0

        return lax.fori_loop(*heads, head, 0)

    lax.fori_loop(0, keys // rows, block, 0)


def head_pair(value):
    lane = lax.broadcasted_iota(jnp.int32, value.shape, 1)
    zero = jnp.zeros_like(value)
    return jnp.concatenate([jnp.where(lane < HEAD, value, zero), jnp.where(lane < HEAD, zero, value)], axis=0)


def pairs_forward(items):
    scores = [nt_dot(keys, head_pair(queries)) for queries, keys, _, _ in items]
    scores = [s if item[3] is None else s + item[3] for s, item in zip(scores, items)]
    grown = [jnp.exp(s - jnp.max(s, axis=0, keepdims=True)) for s in scores]
    rows = [1.0 / jnp.sum(g, axis=0, keepdims=True) for g in grown]
    weights = [g.astype(LOW) for g in grown]
    results = []
    for (queries, _, values, _), low, row in zip(items, weights, rows):
        count = queries.shape[0]
        lane = lax.broadcasted_iota(jnp.int32, values.shape, 1)
        one = jnp.ones_like(values)
        first = tn_dot(low[:, :count], jnp.where(lane < HEAD, values, one))
        second = tn_dot(low[:, count:], jnp.where(lane < HEAD, one, values))
        lane = lax.broadcasted_iota(jnp.int32, first.shape, 1)
        inverse = 1.0 / pltpu.roll(jnp.where(lane < HEAD, second, first), HEAD, 1)
        results.append((jnp.where(lane < HEAD, first, second) * inverse, inverse, low, row))
    return results


def gelu_parts(u):
    a, b = 0.7978845608028654, 0.044715
    square = u * u
    t = jnp.tanh(a * u * (1.0 + b * square))
    half = 0.5 * (1.0 + t)
    slope = half + 0.5 * u * (1.0 - t * t) * (a * (1.0 + 3.0 * b * square))
    return u * half, slope


def gather_plans(place, wholes, small, exchange):
    views = [lambda index, ref=ref: ref.at[index] for ref in [small] + list(wholes[:8])]
    width = wholes[0].shape[-1]
    for q in range(4):
        views.append(lambda index, q=q: wholes[8].at[index + (ALL, pl.ds(q * width, width))])
    for q in range(4):
        views.append(lambda index, q=q: wholes[9].at[index + (q,)])
    return [gather_early(place, view, path, exchange) for view, path in zip(views, FORWARD_PATHS)]


def gather_early(place, blocks, path, exchange):
    steps = []
    at = {dim: place.at(dim) for dim in "yczx"}

    def link(dim, there, where, sends=None, receives=None, slot=None):
        view = blocks(tuple(where.get(d, at[d]) for d in "yczx"))
        return exchange.link(view, view, dim, there, sends, receives, slot)

    def swap(dim, where):
        return link(dim, 1 - at[dim], where)

    def slots(hop):
        first = exchange.slot()
        return first, first if 2 * hop >= place.nz else exchange.slot()

    def hops(hop, where):
        here, size, links = at["z"], place.nz, []
        for way, slot in zip((1, -1), slots(hop)):
            origin, there, source = here - way * (hop - 1), here + way, here - way * hop
            sends = (origin >= 0) & (origin < size) & (there >= 0) & (there < size)
            receives = (source >= 0) & (source < size)
            spot = {**where, "z": jnp.clip(origin, 0, size - 1)}
            links.append(link("z", jnp.clip(there, 0, size - 1), spot, sends, receives, slot))
        return links

    def swap_arrived(dim, hop, where):
        here, size, links = at["z"], place.nz, []
        for way, slot in zip((1, -1), slots(hop)):
            source = here - way * hop
            here_now = (source >= 0) & (source < size)
            spot = {**where, "z": jnp.clip(source, 0, size - 1)}
            links.append(link(dim, 1 - at[dim], spot, here_now, here_now, slot))
        return links

    last = path[2]
    if last == "z":
        first, second = path[0], path[1]
        steps = [[swap(first, {})], [swap(second, {first: ALL})]]
        steps += [hops(hop, {first: ALL, second: ALL}) for hop in range(1, place.nz)]
        steps.append([swap("c", {"y": ALL, "z": ALL, "x": ALL})])
        return steps
    if path[0] == "z":
        first = path[1]
        steps = [hops(hop, {}) for hop in range(1, place.nz)]
        steps.append([swap(first, {"z": ALL}), swap(last, {"z": ALL})])
        steps.append([swap(last, {"z": ALL, first: 1 - at[first]})])
    else:
        first = path[0]
        steps.append([swap(first, {})])
        steps.append(hops(1, {first: ALL}) + [swap(last, {first: ALL})])
        for hop in range(2, place.nz):
            steps.append(hops(hop, {first: ALL}) + swap_arrived(last, hop - 1, {first: ALL}))
        steps.append(swap_arrived(last, place.nz - 1, {first: ALL}))
    steps[-1].append(swap("c", {"z": ALL, first: ALL}))
    steps.append([swap("c", {"z": ALL, first: ALL, last: 1 - at[last]})])
    return steps


def run_order(order, plans, tasks, done):
    at = [0] * len(plans)
    for entry in order:
        if isinstance(entry, str):
            tasks[entry]()
            continue
        step, plan = at[entry], plans[entry]
        at[entry] += 1
        if step >= 1:
            for link in plan[step - 1]:
                link.wait_recv()
        if step < len(plan):
            for link in plan[step]:
                link.start()
        else:
            done(entry)


SAVED = (
    "first_norm", "queries", "keys", "values", "self_context", "second_norm", "cross_queries",
    "source_keys", "source_values", "cross_context", "third_norm", "activated", "slope",
    "start", "mid", "late", "self_inverse", "cross_inverse", "self_rows", "cross_rows", "table",
)


def saved_shapes(tokens, sources, width, length):
    low, full = LOW, FULL
    row = (tokens, width)
    pairs = tokens // length * (width // PAIR)
    shapes = {name: (row, low) for name in SAVED}
    shapes["source_keys"] = shapes["source_values"] = ((2, sources // 2, width), low)
    shapes["activated"] = shapes["slope"] = ((4,) + row, low)
    for name in ("start", "mid", "late", "self_inverse", "cross_inverse"):
        shapes[name] = (row, full)
    shapes["self_rows"] = shapes["cross_rows"] = ((pairs, 1, 2 * length), full)
    shapes["table"] = ((16, width), full)
    return shapes


def forward_kernel(sizes, *refs):
    n = len(SAVED)
    small_shard, shards = refs[0], refs[1:11]
    hidden_in, upstream_in, encoder_in, languages, sources, ids, slab_values = refs[11:18]
    outer_grads, whole_outs = refs[18], refs[19:29]
    self_weights, cross_weights = refs[29:31]
    saved_outs = dict(zip(SAVED, refs[31 : 31 + n]))
    at = 31 + n
    tiny, wholes = refs[at], refs[at + 1 : at + 11]
    at += 11
    v = dict(zip(SAVED, refs[at : at + n]))
    at += n
    bias, stage, outer_blocks, hidden, upstream, encoder, ids_across = refs[at : at + 7]
    send_sem, recv_sem, copy_sem = refs[at + 7 :]
    tokens, width = hidden.shape
    length = ids.shape[0]
    per_seq = width // PAIR
    seqs = tokens // length
    enc_length = encoder.shape[0] // 2
    blocks = tokens // 128

    place = Place(sizes)
    own = (place.y, place.c, place.z, place.x)
    moving = Pool(copy_sem, copy_sem.shape[0])
    sending = Pool(send_sem, send_sem.shape[0])
    owns = [
        PooledCopy(moving, shard, whole.at[own])
        for shard, whole in zip((small_shard.at[pl.ds(0, 16)],) + shards, (tiny,) + wholes)
    ]
    inputs = [
        PooledCopy(moving, source, target)
        for source, target in ((hidden_in, hidden), (encoder_in, encoder), (upstream_in, upstream))
    ]
    get_ids = PooledCopy(moving, ids, ids_across)
    neighbour_barrier(place)
    plans = gather_plans(place, wholes, tiny, Exchange(place, sending, recv_sem))
    for copy in owns:
        copy.wait()

    def keep(name):
        PooledCopy(moving, v[name], saved_outs[name])

    def keep_whole(m):
        if m == 0:
            return
        if m < 9:
            source, target = wholes[m - 1], whole_outs[m - 1]
        elif m < 13:
            index = (ALL,) * 5 + (pl.ds((m - 9) * width, width),)
            source, target = wholes[8].at[index], whole_outs[8].at[index]
        else:
            index = (ALL,) * 4 + (m - 13,)
            source, target = wholes[9].at[index], whole_outs[9].at[index]
        PooledCopy(moving, source, target)

    def opening():
        inputs.pop(0).wait()
        spread_small(tiny, v["table"])
        for s in range(seqs):
            row = jnp.zeros((1, width), FULL)
            for l in range(8):
                row = row + jnp.where(languages[s] == l, v["table"][l : l + 1, :], 0.0)

            def body(at):
                start = hidden[at, :].astype(FULL) + row
                v["start"][at, :] = start
                v["first_norm"][at, :] = (unit_rows(start) * v["table"][8:9, :]).astype(LOW)

            def run(i, _):
                body(pl.ds(pl.multiple_of(s * length + i * 128, 128), 128))
                return 0

            lax.fori_loop(0, length // 128, run, 0)
        keep("table")
        keep("start")
        keep("first_norm")

    def project(source, weight, target):
        target[...] = jnp.dot(source[...], flat(weight), preferred_element_type=FULL).astype(LOW)

    leaving = {}

    def attention(turn, queries, keys, values, context, inverse, rows, weights_out, seq, first, last, picked):
        row_at = pl.ds(seq * length, length)
        key_rows = length if picked is None else enc_length
        items = []
        for p in range(first, last):
            lanes = pl.ds(p * PAIR, PAIR)
            if picked is not None:
                items.append((queries[row_at, lanes], keys[picked, :, lanes], values[picked, :, lanes], None))
            else:
                offset = jnp.concatenate([bias[2 * p], bias[2 * p + 1]], axis=1).astype(FULL)
                items.append((queries[row_at, lanes], keys[row_at, lanes], values[row_at, lanes], offset))
        for n, (out, total, low, row) in enumerate(pairs_forward(items)):
            lanes = pl.ds((first + n) * PAIR, PAIR)
            index = seq * per_seq + first + n
            slot = turn % 2 * (last - first) + n
            if slot in leaving:
                leaving[slot].wait()
            part = stage.at[slot, pl.ds(0, key_rows)]
            part[...] = low
            rows[index] = row
            context[row_at, lanes] = out.astype(LOW)
            inverse[row_at, lanes] = total
            leaving[slot] = PooledCopy(moving, part, weights_out.at[index])

    def residual(half, context, weight, before, after, gain_row, norm):
        at = pl.ds(half * (tokens // 2), tokens // 2)
        state = before[at, :] + jnp.dot(context[at, :], flat(weight), preferred_element_type=FULL)
        after[at, :] = state
        norm[at, :] = (unit_rows(state) * v["table"][gain_row : gain_row + 1, :]).astype(LOW)

    def self_projection(i, name):
        project(v["first_norm"], wholes[i], v[name])
        keep(name)

    def self_attention(turn, s, first, last):
        attention(
            turn, v["queries"], v["keys"], v["values"], v["self_context"], v["self_inverse"], v["self_rows"],
            self_weights, s, first, last, None,
        )

    def self_end(half):
        if half == 0:
            for name in ("self_context", "self_inverse", "self_rows"):
                keep(name)
        residual(half, v["self_context"], wholes[3], v["start"], v["mid"], 9, v["second_norm"])
        if half:
            keep("mid")
            keep("second_norm")

    def cross_source(i, name):
        if len(inputs) == 2:
            inputs.pop(0).wait()
        for half in range(2):
            v[name][half] = jnp.dot(
                encoder[pl.ds(half * enc_length, enc_length), :], flat(wholes[i]), preferred_element_type=FULL
            ).astype(LOW)
        keep(name)

    def cross_projection():
        project(v["second_norm"], wholes[4], v["cross_queries"])
        keep("cross_queries")

    def cross_attention(turn, s, first, last):
        attention(
            turn, v["cross_queries"], v["source_keys"], v["source_values"], v["cross_context"], v["cross_inverse"],
            v["cross_rows"], cross_weights, s, first, last, sources[s],
        )

    def cross_end(half):
        if half == 0:
            for name in ("cross_context", "cross_inverse", "cross_rows"):
                keep(name)
        residual(half, v["cross_context"], wholes[7], v["mid"], v["late"], 10, v["third_norm"])
        if half:
            keep("late")
            keep("third_norm")

    def feed_inner(q):
        weight = flat(wholes[8], pl.ds(q * width, width))
        for half in range(2):
            at = pl.ds(half * tokens // 2, tokens // 2)
            expanded = jnp.dot(v["third_norm"][at, :], weight, preferred_element_type=FULL)
            value, slope = gelu_parts(expanded)
            v["activated"][q, at, :] = value.astype(LOW)
            v["slope"][q, at, :] = slope.astype(LOW)
        for name in ("activated", "slope"):
            PooledCopy(moving, v[name].at[q], saved_outs[name].at[q])

    def bias_values(turn):
        if turn == 0:
            get_ids.wait()
            ids_across[...] = ids_across[...].astype(FULL).T.astype(jnp.int32)
        build_bias(ids_across, slab_values, bias, (3 * turn, 3 * turn + 3))

    def outer_grad(q):
        if inputs:
            inputs.pop(0).wait()
        value = tn_dot(v["activated"][q], upstream[...])
        outer_blocks[q // 2, q % 2] = value.reshape(outer_blocks.shape[2:]).astype(LOW)
        chunk = q // 2, q % 2
        PooledCopy(moving, outer_blocks.at[chunk], outer_grads.at[chunk])

    tasks = {"open": opening, "cq": cross_projection}
    for half in range(2):
        tasks[f"se{half}"] = functools.partial(self_end, half)
        tasks[f"ce{half}"] = functools.partial(cross_end, half)
    for i, (task, name) in enumerate((("q", "queries"), ("k", "keys"), ("v", "values"))):
        tasks[task] = functools.partial(self_projection, i, name)
    for i in range(4):
        first = per_seq // 2 * (i % 2)
        tasks[f"sa{i}"] = functools.partial(self_attention, i, i // 2, first, first + per_seq // 2)
        tasks[f"ca{i}"] = functools.partial(cross_attention, i, i // 2, first, first + per_seq // 2)
        tasks[f"in{i}"] = functools.partial(feed_inner, i)
        tasks[f"b{i}"] = functools.partial(bias_values, i)
        tasks[f"og{i}"] = functools.partial(outer_grad, i)
    tasks["K"] = functools.partial(cross_source, 5, "source_keys")
    tasks["V"] = functools.partial(cross_source, 6, "source_values")
    run_order(FORWARD_ORDER, plans, tasks, keep_whole)
    sending.drain()
    moving.drain()


RECEIVES = {"xyz": 7, "yxz": 7, "zxy": 9, "zyx": 9, "xzy": 12, "yzx": 12}


def small_slab(table, gains, bucket_table):
    part = table.shape[1]
    own = jnp.concatenate([table] + [g.reshape(1, part) for g in gains], axis=0).astype(FULL)
    buckets = bucket_table.T.astype(FULL)
    own = jnp.pad(own, ((0, 32 - own.shape[0]), (0, 128 - part)))
    heads, count = buckets.shape
    return own + jnp.pad(buckets, ((16, 16 - heads), (0, 128 - count)))


def forward(
    sizes, hidden_in, output_grad, encoder_states, language_ids, source_index, bucket_ids, language_table, bucket_table, gains,
    squares, inner, outer,
):
    ny, nz = sizes
    grid = (ny, 2, nz, 2)
    part, width = squares[0].shape
    tokens = hidden_in.shape[0]
    length = bucket_ids.shape[0]
    encoder = encoder_states.reshape(-1, width)
    enc_length = encoder_states.shape[1]
    slab = small_slab(language_table, gains, bucket_table)
    shards = [slab] + list(squares) + [inner, outer.reshape(4, part, width)]
    wholes = [jax.ShapeDtypeStruct(grid + s.shape, s.dtype) for s in shards]
    wholes[0] = jax.ShapeDtypeStruct(grid + (16, 128), FULL)
    shapes = saved_shapes(tokens, encoder.shape[0], width, length)
    pairs = tokens // length * (width // PAIR)
    anywhere = pl.BlockSpec(memory_space=pl.ANY)
    vmem = pl.BlockSpec(memory_space=pltpu.VMEM)
    smem = pl.BlockSpec(memory_space=pltpu.SMEM)
    out_shape = [wholes[10]] + wholes[1:]
    out_shape += [jax.ShapeDtypeStruct((pairs, rows, 2 * length), LOW) for rows in (length, enc_length)]
    out_shape += [jax.ShapeDtypeStruct(*shapes[name]) for name in SAVED]
    outs = pl.pallas_call(
        functools.partial(forward_kernel, sizes),
        out_shape=out_shape,
        in_specs=[anywhere] * 11 + [anywhere] * 3 + [smem, smem, anywhere, smem],
        out_specs=[anywhere] * len(out_shape),
        scratch_shapes=[pltpu.VMEM(w.shape, w.dtype) for w in wholes]
        + [pltpu.VMEM(*shapes[name]) for name in SAVED]
        + [
            pltpu.VMEM((H, length, length), LOW),
            pltpu.VMEM((6, enc_length, 2 * length), LOW),
            pltpu.VMEM(wholes[10].shape, LOW),
            pltpu.VMEM((tokens, width), LOW),
            pltpu.VMEM((tokens, width), LOW),
            pltpu.VMEM(encoder.shape, LOW),
            pltpu.VMEM((length, length), jnp.int32),
            pltpu.SemaphoreType.DMA((36,)),
            pltpu.SemaphoreType.DMA((sum(RECEIVES[path] for path in FORWARD_PATHS),)),
            pltpu.SemaphoreType.DMA((28,)),
        ],
        compiler_params=pltpu.CompilerParams(
            collective_id=2, has_side_effects=True, vmem_limit_bytes=62 * 1024 * 1024
        ),
    )(
        *shards, hidden_in, output_grad, encoder, language_ids, source_index, bucket_ids, slab,
    )
    return outs


class Summed:
    def __init__(self, place, path, blocks, leaving, core_in, boxes, exchange):
        self.blocks, self.stages = blocks, []
        c = place.c
        core = exchange.link(leaving(1 - c), core_in, "c", 1 - c)
        self.stages.append(([core], [((ALL, c, ALL, ALL), core_in, None)]))
        self.box, self.boxes, self.exchange, self.place = 0, boxes, exchange, place
        first, last = path[0], path[2]
        fixed = {"c": c}
        if last == "z":
            second = path[1]
            self.stages.append(self.join(self.swap(first, {**fixed, second: 1 - place.at(second)})))
            fixed[first] = place.at(first)
            here = self.swap(first, {"c": c, second: place.at(second)})
            self.stages.append(self.join(self.swap(second, fixed), here))
            fixed[second] = place.at(second)
            for hop in range(place.nz - 1, 0, -1):
                self.stages.append(self.join(self.hops(hop, fixed)))
        else:
            after = {**fixed, first: place.at(first)}
            self.stages.append(self.join(self.swap_goals(first, place.nz - 1, fixed)))
            for hop in range(place.nz - 1, 1, -1):
                self.stages.append(self.join(self.hops(hop, after), self.swap_goals(first, hop - 1, fixed)))
            own = self.swap(first, {**fixed, "z": place.z})
            self.stages.append(self.join(self.hops(1, after), own))
            self.stages.append(self.join(self.swap(last, {**after, "z": place.z})))
        fixed = {"c": c, "y": place.y, "z": place.z, "x": place.x}
        self.own = self.index(fixed)

    def index(self, fixed):
        return tuple(fixed.get(dim, ALL) for dim in "yczx")

    @staticmethod
    def join(*parts):
        return [link for part in parts for link, _ in part], [add for part in parts for _, add in part]

    def next_box(self):
        self.box += 1
        return self.boxes[self.box - 1]

    def swap(self, dim, where):
        box, here = self.next_box(), self.place.at(dim)
        link = self.exchange.link(self.blocks(self.index({**where, dim: 1 - here})), box, dim, 1 - here)
        return [(link, (self.index({**where, dim: here}), box, None))]

    def swap_goals(self, dim, hop, where):
        pairs, here = [], self.place.at(dim)
        first = self.exchange.slot()
        second = first if 2 * hop >= self.place.nz else self.exchange.slot()
        for way, slot in ((1, first), (-1, second)):
            goal = self.place.z - way * hop
            there = (goal >= 0) & (goal < self.place.nz)
            spot = {**where, "z": jnp.clip(goal, 0, self.place.nz - 1)}
            box = self.next_box()
            source = self.blocks(self.index({**spot, dim: 1 - here}))
            link = self.exchange.link(source, box, dim, 1 - here, there, there, slot)
            pairs.append((link, (self.index({**spot, dim: here}), box, there)))
        return pairs

    def hops(self, hop, where):
        pairs, here, size = [], self.place.z, self.place.nz
        first = self.exchange.slot()
        second = first if 2 * hop > size + 1 else self.exchange.slot()
        for way, slot in ((1, first), (-1, second)):
            there, goal = here - way, here - way * hop
            sends = (goal >= 0) & (goal < size)
            source = here + way
            got = source - way * hop
            receives = (source >= 0) & (source < size) & (got >= 0) & (got < size)
            box = self.next_box()
            view = self.blocks(self.index({**where, "z": jnp.clip(goal, 0, size - 1)}))
            link = self.exchange.link(view, box, "z", jnp.clip(there, 0, size - 1), sends, receives, slot)
            pairs.append((link, (self.index({**where, "z": jnp.clip(got, 0, size - 1)}), box, receives)))
        return pairs

    def start(self, step):
        for link in self.stages[step][0]:
            link.start()

    def finish(self, step):
        links, adds = self.stages[step]
        for link in links:
            link.wait_recv()

        def add(target, box):
            view = self.blocks(target)
            view[...] = view[...] + box[...]

        for target, box, condition in adds:
            Link.when(condition, functools.partial(add, target, box))


def sum_boxes(sizes, path):
    size = {"y": sizes[0], "z": sizes[1], "x": 2}
    hops = 2 * (size["z"] - 1)
    if path[2] == "z":
        return [(size["z"],)] * 3 + [()] * hops, 9
    wide = (size[path[2]],)
    steps = [wide, wide]
    shapes = steps[:]
    for _ in range(size["z"] - 2):
        shapes += [wide] * 4
    return shapes + [wide] * 3 + [()], 12


def pairs_backward(items):
    stacked = [head_pair(item[4]) for item in items]
    prob_grads = [nt_dot(item[3], grads) for item, grads in zip(items, stacked)]
    value_parts = [jnp.dot(item[0], grads, preferred_element_type=FULL) for item, grads in zip(items, stacked)]
    scaled = [item[0].astype(FULL) * grads for item, grads in zip(items, prob_grads)]
    centres = [jnp.sum(s, axis=0, keepdims=True) * item[5] for s, item in zip(scaled, items)]
    score_grads = [(s - item[0].astype(FULL) * c).astype(LOW) for s, c, item in zip(scaled, centres, items)]
    key_parts = [jnp.dot(s, head_pair(item[1]), preferred_element_type=FULL) for s, item in zip(score_grads, items)]
    results = []
    for item, value_part, key_part, score_grad in zip(items, value_parts, key_parts, score_grads):
        count = item[1].shape[0]
        lane = lax.broadcasted_iota(jnp.int32, (count, PAIR), 1)
        first, second = tn_dot(score_grad[:, :count], item[2]), tn_dot(score_grad[:, count:], item[2])
        results.append((jnp.where(lane < HEAD, first, second), key_part, value_part, score_grad))
    return results


def backward_kernel(sizes, box_counts, *refs):
    n = len(SAVED)
    grads, encoder, languages, sources, ids_in, outer_grads = refs[:6]
    wholes = refs[6:16]
    self_weights, cross_weights = refs[16:18]
    saved = dict(zip(SAVED, refs[18 : 18 + n]))
    at = 18 + n
    hidden_out, hidden_grad, encoder_grad, small_out, packed_out = refs[at : at + 5]
    at += 5
    squares, outers, core_boxes = refs[at : at + 3]
    at += 3
    boxes = []
    for count in box_counts:
        boxes.append(refs[at : at + count])
        at += count
    small_box, pool, pairs_in, run_a, run_b, run_c, w, wo, stage, score_sum, bucket_rows, table, self_rows, cross_rows, ids, packed = refs[at : at + 16]
    send_sem, recv_sem, small_send, small_recv, load_sem, store_sem = refs[at + 16 :]
    place = Place(sizes)
    length = ids.shape[0]
    seqs, tokens = languages.shape[0], pool.shape[1]
    width = pool.shape[2]
    blocks = tokens // 128
    per_seq = width // PAIR
    sending = Pool(send_sem, send_sem.shape[0])
    loading = Pool(load_sem, load_sem.shape[0])
    storing = Pool(store_sem, store_sem.shape[0])

    def load(source, target):
        return PooledCopy(loading, source, target)

    def store(source, target):
        PooledCopy(storing, source, target)

    X = [pool.at[i] for i in range(11)] + [pairs_in.at[i] for i in range(4)]
    og, tn = X[0], X[1]
    get_og = load(grads, og)
    def outer_chunk(q):
        return wholes[9].at[q // 2, q % 2]

    def inner_chunk(q):
        return wholes[8].at[:, :, :, :, :, pl.ds(q * width, width)]

    arriving = {}

    def fetch(weights, pairs, key_rows, base):
        per_slot = stage.shape[1] // key_rows
        for n, p in enumerate(pairs):
            for s in range(seqs):
                at = base * per_slot + n * seqs + s
                part = stage.at[at // per_slot, pl.ds(at % per_slot * key_rows, key_rows)]
                arriving[key_rows, p, s] = load(weights.at[s * per_seq + p], part), part

    get_wo = [load(outer_chunk(0), wo.at[0])]
    get_slope = [load(saved["slope"].at[0], X[6])]
    get_tn = load(saved["third_norm"], tn)
    get_wi = [load(inner_chunk(0), w.at[0])]
    get_outers = load(outer_grads.at[:, place.c], outers)
    got = {}

    def load_more(q):
        if q < 3:
            get_slope.append(load(saved["slope"].at[q + 1], X[7 + q]))
        if q == 0:
            get_wo.append(load(outer_chunk(1), wo.at[1]))
            get_wi.append(load(inner_chunk(1), w.at[1]))
            got["table"] = load(saved["table"], table)
            got["late"] = load(saved["late"], run_c)
        if q == 1:
            got["cross_context"] = load(saved["cross_context"], X[2])
            got["co"] = load(wholes[7], w.at[2])
            got["cross_rows"] = load(saved["cross_rows"], cross_rows)
            got["cross_queries"] = load(saved["cross_queries"], X[3])
        if q == 2:
            got["keys"] = load(saved["source_keys"], pairs_in.at[pl.ds(0, 2)])
            got["values"] = load(saved["source_values"], pairs_in.at[pl.ds(2, 2)])
            fetch(cross_weights, (0,), stage.shape[1], 0)
        if q == 3:
            got["cq_w"] = load(wholes[4], w.at[3])
            got["second_norm"] = load(saved["second_norm"], X[4])
            got["first_norm"] = load(saved["first_norm"], X[5])
            got["self_rows"] = load(saved["self_rows"], self_rows)
            got["ids"] = load(ids_in, ids)

    neighbour_barrier(place, far=True)

    def view_of(m):
        if m < 4:
            return lambda index: outers.at[(index[0],) + index[2:] + (m,)]
        return lambda index: squares.at[(m - 4,) + index]

    def leaving_of(m):
        if m < 4:
            return lambda core: outer_grads.at[:, core, :, :, m]
        return lambda core: squares.at[m - 4, :, core]

    exchange = Exchange(place, sending, recv_sem)
    plans = []
    for m in range(16):
        group, kind = m // 4, BACK_PATHS.index(BACKWARD_PATHS[m])
        slot = group % 2
        plans.append(
            Summed(
                place, BACK_PATHS[kind], view_of(m), leaving_of(m), core_boxes.at[slot, kind], [box.at[slot] for box in boxes[kind]],
                exchange,
            )
        )

    def put(i, value):
        squares[i] = value.reshape(squares.shape[1:]).astype(LOW)

    small_out[...] = jnp.zeros_like(small_out)

    def norm_backward(state, inflow, gain_row, before, after):
        def body(at):
            hidden, flow, gain = state[at, :], inflow[at, :], table[gain_row : gain_row + 1, :]
            scale = lax.rsqrt(jnp.mean(hidden * hidden, axis=-1, keepdims=True) + EPSILON)
            unit = hidden * scale
            small_out[gain_row : gain_row + 1, :] += jnp.sum(flow * unit, axis=0, keepdims=True)
            flow = flow * gain
            flow = (flow - unit * jnp.mean(unit * flow, axis=-1, keepdims=True)) * scale
            after[at, :] = before[at, :].astype(FULL) + flow

        each(blocks, body)

    branch = X[1]

    eg = X[10]

    def expanded_grad(q):
        if q == 0:
            get_og.wait()
        get_wo[q].wait()
        get_slope[q].wait()
        out_w = wo[q % 2].reshape(width, width)
        eg[...] = (nt_dot(og[...], out_w) * X[6 + q][...].astype(FULL)).astype(LOW)
        load_more(q)
        get_wo.append(load(outer_chunk((q + 2) % 4), wo.at[q % 2]))

    def inner_grad(q):
        get_tn.wait()
        put(q, tn_dot(tn[...], eg[...]))

    def third_grad(q):
        get_wi[q].wait()
        back = nt_dot(eg[...], flat(w.at[q % 2]))
        if q == 0:
            run_b[...] = back
        else:
            run_b[...] += back
        if q + 2 < 4:
            get_wi.append(load(inner_chunk(q + 2), w.at[q % 2]))
        if q == 3:
            got["so"] = load(wholes[3], w.at[0])
            got["q_w"] = load(wholes[0], w.at[1])
            got["encoder"] = load(encoder, pool.at[pl.ds(6, 2)])

    def third_backward():
        got["table"].wait()
        got["late"].wait()
        norm_backward(run_c, run_b, 10, og, run_a)
        got["inverse"] = load(saved["cross_inverse"], run_c)
        branch[...] = run_a[...].astype(LOW)

    def context_grad(weight, slot):
        got[weight].wait()
        got["inverse"].wait()
        X[0][...] = (nt_dot(branch[...], flat(w.at[slot])).astype(LOW).astype(FULL) * run_c[...]).astype(LOW)

    def cross_out_grad():
        got["cross_context"].wait()
        put(4, tn_dot(X[2][...], branch[...]))

    def cross_context_grad():
        context_grad("co", 2)
        got["k_w"] = load(wholes[1], w.at[2])
        got["mid"] = load(saved["mid"], run_c)

    def attention(rows, key_rows, pairs, one, finish_pair, ahead):
        for p in pairs:
            for s in range(seqs):
                arriving[key_rows, p, s][0].wait()
        ahead()
        items = []
        for p in pairs:
            for s in range(seqs):
                queries, keys, values, grad = one(s, pl.ds(p * PAIR, PAIR))
                items.append(
                    (arriving[key_rows, p, s][1][...], queries, keys, values, grad, rows[s * per_seq + p])
                )
        results = pairs_backward(items)
        for n, p in enumerate(pairs):
            finish_pair(p, pl.ds(p * PAIR, PAIR), results[n * seqs : (n + 1) * seqs])

    enc_length = pool.shape[1]

    def cross_attention(p):
        if p == 0:
            for name in ("cross_rows", "cross_queries", "keys", "values"):
                got[name].wait()

        def one(s, lanes):
            at = pl.ds(s * length, length)
            source = sources[s]
            return X[3][at, lanes], pairs_in[source, :, lanes], pairs_in[2 + source, :, lanes], X[0][at, lanes]

        def finish_pair(p, lanes, results):
            for s in range(seqs):
                X[1][pl.ds(s * length, length), lanes] = results[s][0].astype(LOW)
            for e in range(2):
                for target, part_at in ((8, 1), (11, 2)):
                    total = jnp.where(sources[0] == e, results[0][part_at], 0.0)
                    total = total + jnp.where(sources[1] == e, results[1][part_at], 0.0)
                    pool[target + e, :, lanes] = total.astype(LOW)

        def ahead():
            if p + 1 < per_seq:
                fetch(cross_weights, (p + 1,), enc_length, (p + 1) % 2 * 2)
            else:
                fetch(self_weights, (0, 1), length, 0)

        attention(cross_rows, enc_length, (p,), one, finish_pair, ahead)
        if p + 1 < per_seq:
            return
        got["queries"] = load(saved["queries"], X[11])
        got["keys"] = load(saved["keys"], X[12])
        got["values"] = load(saved["values"], X[13])
        got["self_context"] = load(saved["self_context"], X[14])

    def cross_query_grad():
        got["second_norm"].wait()
        put(5, tn_dot(X[4][...], X[1][...]))

    def source_grad(i, target):
        copy = got.pop("encoder", None)
        if copy is not None:
            copy.wait()
        put(i, tn_dot(pool[6], pool[target]) + tn_dot(pool[7], pool[target + 1]))

    def second_grad():
        got["cq_w"].wait()
        run_b[...] = nt_dot(X[1][...], flat(w.at[3]))
        got["v_w"] = load(wholes[2], w.at[3])

    def second_backward():
        got["mid"].wait()
        norm_backward(run_c, run_b, 9, run_a, run_a)
        got["inverse"] = load(saved["self_inverse"], run_c)
        branch[...] = run_a[...].astype(LOW)

    def self_out_grad():
        got["self_context"].wait()
        put(8, tn_dot(X[14][...], branch[...]))

    def self_context_grad():
        context_grad("so", 0)
        got["ck_w"] = load(wholes[5], w.at[0])
        got["start"] = load(saved["start"], run_c)

    def self_attention(turn):
        if turn == 0:
            for name in ("self_rows", "queries", "keys", "values"):
                got[name].wait()

        def one(s, lanes):
            at = pl.ds(s * length, length)
            return tuple(X[i][at, lanes] for i in (11, 12, 13, 0))

        def finish_pair(p, lanes, results):
            for s in range(seqs):
                for i in range(3):
                    X[2 + i][pl.ds(s * length, length), lanes] = results[s][i].astype(LOW)
            score_sum[p] = (results[0][3].astype(FULL) + results[1][3].astype(FULL)).astype(LOW)

        def ahead():
            if turn < 2:
                fetch(self_weights, (2 * turn + 2, 2 * turn + 3), length, (turn + 1) % 2 * 2)

        attention(self_rows, length, (2 * turn, 2 * turn + 1), one, finish_pair, ahead)

    def self_grad(i):
        copy = got.pop("first_norm", None)
        if copy is not None:
            copy.wait()
        put(9 + i, tn_dot(X[5][...], X[2 + i][...]))

    def closing_product(i):
        got[("q_w", "k_w", "v_w")[i]].wait()
        back = nt_dot(X[2 + i][...], flat(w.at[1 + i]))
        if i == 0:
            run_b[...] = back
            got["cv_w"] = load(wholes[6], w.at[1])
        else:
            run_b[...] += back

    def closing():
        got["start"].wait()
        got["activated"] = [load(saved["activated"].at[q], X[i]) for q, i in enumerate((0, 1, 5, 10))]
        norm_backward(run_c, run_b, 8, run_a, run_a)
        store(run_a, hidden_grad)
        got["late"] = load(saved["late"], run_c)
        for s in range(seqs):
            row = jnp.sum(run_a[pl.ds(s * length, length), :], axis=0, keepdims=True)
            for l in range(8):
                small_out[l : l + 1, :] += jnp.where(languages[s] == l, row, 0.0)

    def hidden_end(q):
        got["activated"][q].wait()
        get_wo[4 + q].wait()
        value = jnp.dot(X[(0, 1, 5, 10)[q]][...], wo[q % 2].reshape(width, width), preferred_element_type=FULL)
        if q < 2:
            get_wo.append(load(outer_chunk(q + 2), wo.at[q % 2]))
        if q == 0:
            got["late"].wait()
        if q < 3:
            run_c[...] += value
        else:
            X[2][...] = (run_c[...] + value).astype(LOW)
            store(X[2], hidden_out)

    def encoder_end(e, value):
        run = (run_b, run_c)[e]
        if value:
            got["cv_w"].wait()
            run[...] += nt_dot(pool[11 + e], flat(w.at[1]))
            store(run, encoder_grad.at[e])
        else:
            got["ck_w"].wait()
            run[...] = nt_dot(pool[8 + e], flat(w.at[0]))

    def bucket_sums(turn):
        if turn == 0:
            got["ids"].wait()
            ids[...] = ids[...].astype(FULL).T.astype(jnp.int32)
        half = length // 2
        rows = 32

        def pair(p, _):
            def bucket_group(first, count, spans):
                sums = [[jnp.zeros((8, half), FULL) for _ in range(2)] for _ in range(count)]
                for n, side in spans:
                    block = pl.ds(n * rows, rows)
                    bucket = ids[block, side * half : (side + 1) * half]
                    scores = [
                        score_sum[p, block, h * length + side * half : h * length + (side + 1) * half].astype(FULL)
                        for h in range(2)
                    ]
                    for c in range(count):
                        here = bucket == first + c
                        for h in range(2):
                            kept = jnp.where(here, scores[h], 0.0).reshape(rows // 8, 8, half)
                            sums[c][h] = sums[c][h] + jnp.sum(kept, axis=0)
                for c in range(count):
                    for h in range(2):
                        row = (2 * p + h) * 32 + first + c
                        bucket_rows[pl.ds(row, 1), :] = jnp.sum(sums[c][h], axis=0, keepdims=True)

            blocks_of = length // rows
            every = [(n, side) for side in range(2) for n in range(blocks_of) if n * rows < (side + 1) * half]
            near = [(n, side) for n, side in every if n * rows + rows + 15 > side * half]
            for first in range(0, 32, 4):
                bucket_group(first, 4, near if first < 16 else every)
            return 0

        pair(turn, 0)
        if turn + 1 < per_seq:
            return
        ones = jnp.ones((8, 128), FULL)
        totals = lax.dot_general(
            ones, bucket_rows[...], (((1,), (1,)), ((), ())), precision=PRECISE, preferred_element_type=FULL
        )
        small_out[11:12, : bucket_rows.shape[0]] = totals[:1, :]

    small = []
    for dim in "cxyz":
        here, reach = place.at(dim), 1
        while reach < place.size(dim):
            small.append((dim, here + reach - 2 * reach * lax.rem(lax.div(here, reach), 2)))
            reach *= 2

    def small_copy(i):
        dim, partner = small[i]
        return pltpu.make_async_remote_copy(
            small_out, small_box.at[i], small_send.at[i], small_recv.at[i],
            device_id=place.device(dim, partner), device_id_type=MESH,
        )

    class Small:
        def start(self, i):
            small_copy(i).start()

        def finish(self, i):
            small_copy(i).wait()
            small_out[...] += small_box[i]

    tasks = dict(n3=third_backward, co=cross_out_grad, ccg=cross_context_grad, cq=cross_query_grad, n2a=second_grad, n2=second_backward)
    tasks.update(so=self_out_grad, scg=self_context_grad, cl1=closing)
    for e in range(2):
        tasks[f"e{e}k"] = functools.partial(encoder_end, e, False)
        tasks[f"e{e}v"] = functools.partial(encoder_end, e, True)
    tasks["ck"] = functools.partial(source_grad, 6, 8)
    tasks["cv"] = functools.partial(source_grad, 7, 11)
    for i in range(4):
        tasks[f"x{i}"] = functools.partial(expanded_grad, i)
        tasks[f"in{i}"] = functools.partial(inner_grad, i)
        tasks[f"t{i}"] = functools.partial(third_grad, i)
        tasks[f"h{i}"] = functools.partial(hidden_end, i)
    for i in range(per_seq):
        tasks[f"ca{i}"] = functools.partial(cross_attention, i)
        tasks[f"bk{i}"] = functools.partial(bucket_sums, i)
    for i in range(3):
        tasks[f"sa{i}"] = functools.partial(self_attention, i)
        tasks[f"cp{i}"] = functools.partial(closing_product, i)
        tasks["qkv"[i]] = functools.partial(self_grad, i)
    steps = [len(plan.stages) for plan in plans] + [len(small)]
    plans.append(Small())
    at = [0] * 17
    def keep_sum(m):
        plan = plans[m]
        packed[m] = plan.blocks(plan.own)[...].astype(FULL)
        store(packed.at[m], packed_out.at[m])

    for entry in BACKWARD_ORDER:
        if isinstance(entry, str):
            tasks[entry]()
            continue
        step = at[entry]
        at[entry] += 1
        if step >= 1:
            if entry < 4:
                get_outers.wait()
            plans[entry].finish(step - 1)
        if step < steps[entry]:
            plans[entry].start(step)
        elif entry < 16:
            keep_sum(entry)
    sending.drain()
    storing.drain()


def backward(sizes, output_grad, encoder_states, language_ids, source_index, bucket_ids, forward_outs):
    ny, nz = sizes
    grid = (ny, 2, nz, 2)
    tokens, width = output_grad.shape
    length = bucket_ids.shape[0]
    part = width // (ny * nz * 4)
    outer_grads, wholes, score_weights = forward_outs[0], forward_outs[1:11], forward_outs[11:13]
    saved = dict(zip(SAVED, forward_outs[13:]))
    enc_count, enc_length = encoder_states.shape[:2]
    anywhere = pl.BlockSpec(memory_space=pl.ANY)
    vmem = pl.BlockSpec(memory_space=pltpu.VMEM)
    smem = pl.BlockSpec(memory_space=pltpu.SMEM)
    lead = [sum_boxes(sizes, path)[0] for path in BACK_PATHS]
    receives = sum(sum_boxes(sizes, path)[1] for path in BACKWARD_PATHS)
    hops = (ny * nz * 4).bit_length() - 1
    pairs = tokens // length * (width // PAIR)
    row = (tokens, width)
    out_shape = [
        jax.ShapeDtypeStruct(row, LOW),
        jax.ShapeDtypeStruct(row, FULL),
        jax.ShapeDtypeStruct((enc_count, enc_length, width), FULL),
        jax.ShapeDtypeStruct((16, width), FULL),
        jax.ShapeDtypeStruct((16, part, width), FULL),
    ]
    outs = pl.pallas_call(
        functools.partial(backward_kernel, sizes, tuple(len(s) for s in lead)),
        out_shape=out_shape,
        in_specs=[anywhere, anywhere, smem, smem, anywhere] + [anywhere] * (13 + len(SAVED)),
        out_specs=[anywhere] * 3 + [vmem, anywhere],
        scratch_shapes=[
            pltpu.VMEM((12,) + grid + (part, width), LOW),
            pltpu.VMEM((ny, nz, 2, 4, part, width), LOW),
            pltpu.VMEM((2, 4, ny, nz, 2, part, width), LOW),
        ]
        + [pltpu.VMEM((2,) + s + (part, width), LOW) for one in lead for s in one]
        + [
            pltpu.VMEM((hops, 16, width), FULL),
            pltpu.VMEM((13,) + row, LOW),
            pltpu.VMEM((4,) + row, LOW),
            pltpu.VMEM(row, FULL),
            pltpu.VMEM(row, FULL),
            pltpu.VMEM(row, FULL),
            pltpu.VMEM((4,) + grid + (part, width), LOW),
            pltpu.VMEM((2, nz, 2, 4, part, width), LOW),
            pltpu.VMEM((4, enc_length, 2 * length), LOW),
            pltpu.VMEM((width // PAIR, length, 2 * length), LOW),
            pltpu.VMEM((32 * H, 128), FULL),
            pltpu.VMEM((16, width), FULL),
            pltpu.VMEM((pairs, 1, 2 * length), FULL),
            pltpu.VMEM((pairs, 1, 2 * length), FULL),
            pltpu.VMEM((length, length), jnp.int32),
            pltpu.VMEM((16, part, width), FULL),
            pltpu.SemaphoreType.DMA((30,)),
            pltpu.SemaphoreType.DMA((receives,)),
            pltpu.SemaphoreType.DMA((hops,)),
            pltpu.SemaphoreType.DMA((hops,)),
            pltpu.SemaphoreType.DMA((24,)),
            pltpu.SemaphoreType.DMA((8,)),
        ],
        compiler_params=pltpu.CompilerParams(
            collective_id=3, has_side_effects=True, vmem_limit_bytes=63 * 1024 * 1024
        ),
    )(
        output_grad, encoder_states, language_ids, source_index, bucket_ids, outer_grads, *wholes, *score_weights,
        *[saved[name] for name in SAVED],
    )
    return finish(sizes, outs)


def finish_kernel(sizes, *refs):
    hidden_out, hidden_grad, encoder_grad, small_in, packed_in = refs[:5]
    outs = refs[5:18]
    language, bucket, gains = refs[18], refs[19], refs[20:23]
    staged_hidden, staged_grad, staged_encoder, small, packed, sem, in_sem = refs[23:]
    part, width = packed.shape[1:]
    copies, arriving = [], []

    def copy(source, target):
        copies.append(pltpu.make_async_copy(source, target, sem.at[len(copies)]))
        copies[-1].start()

    def arrive(source, target):
        arriving.append(pltpu.make_async_copy(source, target, in_sem.at[len(arriving)]))
        arriving[-1].start()
        return arriving[-1]

    get_small = arrive(small_in, small)
    blocks = []
    for source, target, out, pieces in (
        (encoder_grad, staged_encoder, outs[2], 4), (hidden_grad, staged_grad, outs[1], 2),
        (hidden_out, staged_hidden, outs[0], 1),
    ):
        size = source.shape[-2]
        for n in range(pieces):
            if len(source.shape) == 3:
                half = size // 2
                index = (n // 2, pl.ds(n % 2 * half, half))
            else:
                index = pl.ds(n * (size // pieces), size // pieces)
            blocks.append((arrive(source.at[index], target.at[index]), target.at[index], out.at[index]))
    groups = [arrive(packed_in.at[pl.ds(4 * n, 4)], packed.at[pl.ds(4 * n, 4)]) for n in range(4)]
    for ready, source, target in blocks:
        ready.wait()
        copy(source, target)
    for group in groups:
        group.wait()
    for q in range(4):
        copy(packed.at[q], outs[12].at[pl.ds(q * part, part)])
        copy(packed.at[4 + q], outs[11].at[:, pl.ds(q * width, width)])
    for i, m in enumerate((13, 14, 15, 12, 9, 10, 11, 8)):
        copy(packed.at[m], outs[3 + i])
    get_small.wait()
    place = Place(sizes)
    start = (place.dp * sizes[1] * 2 + place.fs) * part
    row = lax.broadcasted_iota(jnp.int32, (width, 128), 0)
    lane = lax.broadcasted_iota(jnp.int32, (width, 128), 1)
    chosen = jnp.where((row == lane + start) & (lane < part), 1.0, 0.0)
    own = jnp.dot(small[...], chosen, precision=PRECISE, preferred_element_type=FULL)
    language[...] = own[:8, :part]
    for i in range(3):
        gains[i][...] = own[8 + i, :part]
    row = lax.broadcasted_iota(jnp.int32, (16, width), 0)
    lane = lax.broadcasted_iota(jnp.int32, (16, width), 1)
    spread = jnp.where(lax.div(lane, 32) == row, small[11:12, :], 0.0)
    row = lax.broadcasted_iota(jnp.int32, (width, 128), 0)
    lane = lax.broadcasted_iota(jnp.int32, (width, 128), 1)
    places = jnp.where(lax.rem(row, 32) == lane, 1.0, 0.0)
    bucket[...] = jnp.dot(spread, places, precision=PRECISE, preferred_element_type=FULL)[:H, :32]
    for c in copies:
        c.wait()


def finish(sizes, outs):
    part, width = outs[4].shape[1:]
    anywhere = pl.BlockSpec(memory_space=pl.ANY)
    hbm = pl.BlockSpec(memory_space=pltpu.HBM)
    vmem = pl.BlockSpec(memory_space=pltpu.VMEM)
    shapes = [o.shape for o in outs[:3]] + [(part, width)] * 8
    shapes += [(part, 4 * width), (4 * part, width)]
    out_shape = [jax.ShapeDtypeStruct(s, FULL) for s in shapes]
    out_shape[0] = jax.ShapeDtypeStruct(shapes[0], LOW)
    out_shape += [jax.ShapeDtypeStruct(s, FULL) for s in ((8, part), (H, 32), (part,), (part,), (part,))]
    return pl.pallas_call(
        functools.partial(finish_kernel, sizes),
        out_shape=out_shape,
        in_specs=[hbm] * 5,
        out_specs=[anywhere] * 13 + [vmem] * 5,
        scratch_shapes=[pltpu.VMEM(o.shape, o.dtype) for o in outs]
        + [pltpu.SemaphoreType.DMA((23,)), pltpu.SemaphoreType.DMA((12,))],
        compiler_params=pltpu.CompilerParams(vmem_limit_bytes=60 * 1024 * 1024),
    )(*outs)


def local_general(
    sizes,
    hidden_in,
    output_grad,
    encoder_states,
    language_ids,
    source_index,
    bucket_ids,
    language_table,
    bucket_table,
    self_gain,
    self_query,
    self_key,
    self_value,
    self_out,
    cross_gain,
    cross_query,
    cross_key,
    cross_value,
    cross_out,
    feed_gain,
    inner_weight,
    outer_weight,
):
    seq_count = language_ids.shape[0]
    length = bucket_ids.shape[0]
    tokens = seq_count * length
    enc_count = encoder_states.shape[0]
    enc_length = encoder_states.shape[1]
    width = hidden_in.shape[1]
    blocks = seq_count // SEQ_BLOCK
    (
        gain_one, gain_two, gain_three, table_whole, query_whole, key_whole, value_whole, out_whole,
        cquery_whole, ckey_whole, cvalue_whole, cout_whole, inner_whole, outer_whole,
    ) = gather_weights(
        sizes, language_table, (self_gain, cross_gain, feed_gain),
        (self_query, self_key, self_value, self_out, cross_query, cross_key, cross_value, cross_out),
        inner_weight, outer_weight,
    )

    def to_blocks(array, rows):
        return array.reshape(blocks, SEQ_BLOCK, rows, array.shape[-1])

    language_hot = (language_ids[:, None] == jnp.arange(table_whole.shape[0])[None, :]).astype(
        jnp.float32
    )
    language_rows = jnp.dot(language_hot, table_whole.astype(jnp.float32), precision=PRECISE)
    start_state = (
        hidden_in.astype(jnp.float32).reshape(seq_count, length, width) + language_rows[:, None, :]
    ).reshape(tokens, width)
    first_norm = to_low(norm_scale(start_state, gain_one.astype(jnp.float32)))
    self_queries = to_low(matmul(first_norm, query_whole))
    self_keys = to_low(matmul(first_norm, key_whole))
    self_values = to_low(matmul(first_norm, value_whole))
    bucket_hot = (
        bucket_ids[:, :, None] == jnp.arange(bucket_table.shape[0])[None, None, :]
    ).astype(jnp.float32)
    position_bias = jnp.einsum(
        "ijb,bh->hij", bucket_hot, bucket_table.astype(jnp.float32), precision=PRECISE
    )
    positions = jnp.arange(length)
    masked_bias = jnp.where(
        (positions[:, None] >= positions[None, :])[None], position_bias, NEGATIVE
    )

    def self_forward(block_items):
        return attend_forward(block_items[0], block_items[1], block_items[2], masked_bias)

    self_context, self_total = lax.map(
        self_forward,
        (
            to_blocks(self_queries, length),
            to_blocks(self_keys, length),
            to_blocks(self_values, length),
        ),
    )
    self_context = self_context.reshape(tokens, -1)
    mid_state = start_state + matmul(self_context, out_whole)
    second_norm = to_low(norm_scale(mid_state, gain_two.astype(jnp.float32)))
    cross_queries = to_low(matmul(second_norm, cquery_whole))
    encoder_flat = encoder_states.reshape(enc_count * enc_length, width)
    source_keys = to_low(matmul(encoder_flat, ckey_whole)).reshape(enc_count, enc_length, -1)
    source_values = to_low(matmul(encoder_flat, cvalue_whole)).reshape(enc_count, enc_length, -1)
    source_hot = (source_index[:, None] == jnp.arange(enc_count)[None, :]).astype(jnp.float32)
    source_low = to_low(source_hot)
    picked_keys = to_low(
        jnp.einsum("se,emc->smc", source_low, source_keys, preferred_element_type=jnp.float32)
    )
    picked_values = to_low(
        jnp.einsum("se,emc->smc", source_low, source_values, preferred_element_type=jnp.float32)
    )

    def cross_forward(block_items):
        return attend_forward(block_items[0], block_items[1], block_items[2], 0.0)

    cross_context, cross_total = lax.map(
        cross_forward,
        (
            to_blocks(cross_queries, length),
            picked_keys.reshape(blocks, SEQ_BLOCK, enc_length, -1),
            picked_values.reshape(blocks, SEQ_BLOCK, enc_length, -1),
        ),
    )
    cross_context = cross_context.reshape(tokens, -1)
    late_state = mid_state + matmul(cross_context, cout_whole)
    third_norm = to_low(norm_scale(late_state, gain_three.astype(jnp.float32)))
    expanded = matmul(third_norm, inner_whole)
    activated = to_low(jax.nn.gelu(expanded, approximate=True))
    hidden_out = (late_state + matmul(activated, outer_whole)).astype(jnp.bfloat16)
    top_grad = output_grad.astype(jnp.float32)
    outer_full = left_product(activated, output_grad)
    activated_grad = right_product(output_grad, outer_whole)
    gelu_value, gelu_back = jax.vjp(jax.nn.gelu, expanded)
    expanded_grad = to_low(gelu_back(activated_grad)[0])
    inner_full = left_product(third_norm, expanded_grad)
    third_grad = right_product(expanded_grad, inner_whole)
    norm_value, norm_back = jax.vjp(norm_scale, late_state, gain_three.astype(jnp.float32))
    state_back, feed_gain_full = norm_back(third_grad)
    late_grad = top_grad + state_back
    cross_low = to_low(late_grad)
    cout_full = left_product(cross_context, cross_low)
    cross_context_grad = to_low(right_product(cross_low, cout_whole))

    def cross_backward(block_items):
        return attend_backward(
            block_items[0],
            block_items[1],
            block_items[2],
            0.0,
            block_items[3],
            block_items[4],
            False,
        )

    cquery_part, ckey_part, cvalue_part = lax.map(
        cross_backward,
        (
            to_blocks(cross_queries, length),
            picked_keys.reshape(blocks, SEQ_BLOCK, enc_length, -1),
            picked_values.reshape(blocks, SEQ_BLOCK, enc_length, -1),
            cross_total,
            to_blocks(cross_context_grad, length),
        ),
    )
    cquery_low = to_low(cquery_part.reshape(tokens, -1))
    source_key_grad = to_low(
        jnp.einsum(
            "se,smc->emc",
            source_hot,
            ckey_part.reshape(seq_count, enc_length, -1),
            precision=PRECISE,
        ).reshape(enc_count * enc_length, -1)
    )
    source_value_grad = to_low(
        jnp.einsum(
            "se,smc->emc",
            source_hot,
            cvalue_part.reshape(seq_count, enc_length, -1),
            precision=PRECISE,
        ).reshape(enc_count * enc_length, -1)
    )
    cquery_full = left_product(second_norm, cquery_low)
    ckey_full = left_product(encoder_flat, source_key_grad)
    cvalue_full = left_product(encoder_flat, source_value_grad)
    encoder_grad = (
        right_product(source_key_grad, ckey_whole) + right_product(source_value_grad, cvalue_whole)
    ).reshape(enc_count, enc_length, width)
    second_grad = right_product(cquery_low, cquery_whole)
    norm_value, norm_back = jax.vjp(norm_scale, mid_state, gain_two.astype(jnp.float32))
    state_back, cross_gain_full = norm_back(second_grad)
    mid_grad = late_grad + state_back
    self_low = to_low(mid_grad)
    out_full = left_product(self_context, self_low)
    self_context_grad = to_low(right_product(self_low, out_whole))

    def self_backward(block_items):
        return attend_backward(
            block_items[0],
            block_items[1],
            block_items[2],
            masked_bias,
            block_items[3],
            block_items[4],
            True,
        )

    query_part, key_part, value_part, bias_part = lax.map(
        self_backward,
        (
            to_blocks(self_queries, length),
            to_blocks(self_keys, length),
            to_blocks(self_values, length),
            self_total,
            to_blocks(self_context_grad, length),
        ),
    )
    query_low = to_low(query_part.reshape(tokens, -1))
    key_low = to_low(key_part.reshape(tokens, -1))
    value_low = to_low(value_part.reshape(tokens, -1))
    table_full = jnp.einsum(
        "hij,ijb->bh", jnp.sum(bias_part, axis=0), bucket_hot, precision=PRECISE
    )
    query_full = left_product(first_norm, query_low)
    key_full = left_product(first_norm, key_low)
    value_full = left_product(first_norm, value_low)
    first_grad = (
        right_product(query_low, query_whole)
        + right_product(key_low, key_whole)
        + right_product(value_low, value_whole)
    )
    norm_value, norm_back = jax.vjp(norm_scale, start_state, gain_one.astype(jnp.float32))
    state_back, self_gain_full = norm_back(first_grad)
    hidden_in_grad = mid_grad + state_back
    sequence_sums = jnp.sum(hidden_in_grad.reshape(seq_count, length, width), axis=1)
    language_full = left_product(language_hot, sequence_sums)
    (
        language_part, bucket_table_grad, sgain_part, cgain_part, feed_gain_part, whole_parts, inner_part, outer_part,
    ) = reduce_grads(
        sizes, language_full, table_full, (self_gain_full, cross_gain_full, feed_gain_full),
        (query_full, key_full, value_full, out_full, cquery_full, ckey_full, cvalue_full, cout_full),
        inner_full, outer_full,
    )
    query_sum, key_sum, value_sum, out_part, cquery_part_sum, ckey_part_sum, cvalue_part_sum, cout_part = whole_parts
    return (
        hidden_out,
        hidden_in_grad,
        encoder_grad,
        language_part,
        bucket_table_grad,
        sgain_part,
        query_sum,
        key_sum,
        value_sum,
        out_part,
        cgain_part,
        cquery_part_sum,
        ckey_part_sum,
        cvalue_part_sum,
        cout_part,
        feed_gain_part,
        inner_part,
        outer_part,
    )


def local(sizes, *args):
    if sizes == (2, 4) and args[8].shape[0] % 8 == 0:
        return local_fused(sizes, *args)
    return local_general(sizes, *args)


def local_fused(
    sizes, hidden_in, output_grad, encoder_states, language_ids, source_index, bucket_ids, language_table,
    bucket_table, self_gain, self_query, self_key, self_value, self_out, cross_gain, cross_query, cross_key,
    cross_value, cross_out, feed_gain, inner_weight, outer_weight,
):
    kept = forward(
        sizes, hidden_in, output_grad, encoder_states, language_ids, source_index, bucket_ids, language_table,
        bucket_table, (self_gain, cross_gain, feed_gain),
        (self_query, self_key, self_value, self_out, cross_query, cross_key, cross_value, cross_out),
        inner_weight, outer_weight,
    )
    outs = backward(sizes, output_grad, encoder_states, language_ids, source_index, bucket_ids, kept)
    squares, inner, outer, language, bucket, gains = outs[3:11], outs[11], outs[12], outs[13], outs[14].T, outs[15:]
    return (
        *outs[:3], language, bucket, gains[0], *squares[:4], gains[1], *squares[4:], gains[2], inner, outer,
    )


def solution(mesh):
    sizes = (mesh.shape["dp"] // 2, mesh.shape["fsdp"] // 2)
    in_specs = (
        P(("dp", "fsdp"), None),
        P(("dp", "fsdp"), None),
        P(("dp", "fsdp"), None, None),
        P(("dp", "fsdp")),
        P(("dp", "fsdp")),
        P(),
        P(None, ("dp", "fsdp")),
        P(),
        P(("dp", "fsdp")),
        P(("dp", "fsdp"), None),
        P(("dp", "fsdp"), None),
        P(("dp", "fsdp"), None),
        P(("dp", "fsdp"), None),
        P(("dp", "fsdp")),
        P(("dp", "fsdp"), None),
        P(("dp", "fsdp"), None),
        P(("dp", "fsdp"), None),
        P(("dp", "fsdp"), None),
        P(("dp", "fsdp")),
        P(("dp", "fsdp"), None),
        P(("dp", "fsdp"), None),
    )
    out_specs = (
        P(("dp", "fsdp"), None),
        P(("dp", "fsdp"), None),
        P(("dp", "fsdp"), None, None),
        P(None, ("dp", "fsdp")),
        P(),
        P(("dp", "fsdp")),
        P(("dp", "fsdp"), None),
        P(("dp", "fsdp"), None),
        P(("dp", "fsdp"), None),
        P(("dp", "fsdp"), None),
        P(("dp", "fsdp")),
        P(("dp", "fsdp"), None),
        P(("dp", "fsdp"), None),
        P(("dp", "fsdp"), None),
        P(("dp", "fsdp"), None),
        P(("dp", "fsdp")),
        P(("dp", "fsdp"), None),
        P(("dp", "fsdp"), None),
    )
    return jax.shard_map(functools.partial(local, sizes), mesh=mesh, in_specs=in_specs, out_specs=out_specs, check_vma=False)
```
